32 devices in a mesh: seq: 2 (over core), ctx: 4 (over y, x), fsdp: 4 (over z).
Axes of the slice: x: 2, y: 2, z: 4, core: 2. Of those that a mesh axis runs over, the one named last changes fastest.
Arguments:
- tokens: bfloat16 [2, 3072, 896], P('seq', ('ctx', 'fsdp')), may hold values from -6 to 6
- out_grad: bfloat16 [2, 3072, 896], P('seq', ('ctx', 'fsdp')), may hold values from -6 to 6
- block_order: int32 [2, 4], P('seq'), may hold values from 0 to 3, each once within a row
- norm1_gain: bfloat16 [896], P('fsdp'), may hold values from 0.5 to 1.5
- q_weight: bfloat16 [896, 896], P('fsdp'), may hold values from -0.25 to 0.25
- q_bias: bfloat16 [896], P('fsdp'), may hold values from -1.25 to 1.25
- k_weight: bfloat16 [896, 128], P('fsdp'), may hold values from -0.25 to 0.25
- k_bias: bfloat16 [128], P('fsdp'), may hold values from -1.25 to 1.25
- v_weight: bfloat16 [896, 128], P('fsdp'), may hold values from -0.1875 to 0.1875
- v_bias: bfloat16 [128], P('fsdp'), may hold values from -1.25 to 1.25
- o_weight: bfloat16 [896, 896], P('fsdp'), may hold values from -0.375 to 0.375
- norm2_gain: bfloat16 [896], P('fsdp'), may hold values from 0.5 to 1.5
- gate_weight: bfloat16 [896, 4864], P('fsdp'), may hold values from -0.1875 to 0.1875
- up_weight: bfloat16 [896, 4864], P('fsdp'), may hold values from -0.1875 to 0.1875
- down_weight: bfloat16 [4864, 896], P('fsdp'), may hold values from -0.078125 to 0.078125
Outputs:
- layer_out: bfloat16 [2, 3072, 896], P('seq', ('ctx', 'fsdp'))
- tokens_grad: float32 [2, 3072, 896], P('seq', ('ctx', 'fsdp'))
- norm1_gain_grad: float32 [896], P('fsdp')
- q_weight_grad: float32 [896, 896], P('fsdp')
- q_bias_grad: float32 [896], P('fsdp')
- k_weight_grad: float32 [896, 128], P('fsdp')
- k_bias_grad: float32 [128], P('fsdp')
- v_weight_grad: float32 [896, 128], P('fsdp')
- v_bias_grad: float32 [128], P('fsdp')
- o_weight_grad: float32 [896, 896], P('fsdp')
- norm2_gain_grad: float32 [896], P('fsdp')
- gate_weight_grad: float32 [896, 4864], P('fsdp')
- up_weight_grad: float32 [896, 4864], P('fsdp')
- down_weight_grad: float32 [4864, 896], P('fsdp')
The draws below stay inside these ranges and needn't reach their ends.
Inputs may be any that keep to these rules, and one draw needn't show every extreme that they name: `block_order`: each row is a permutation of 0 to 3.
All inputs are finite; a program needn't handle non-finite values.
Results may differ from the reference program's by a relative error of at most 0.04.
Values may be sent and summed in bfloat16 or wider, within the bound.
No kernel may reach another device: no remote copies, remote signals or barrier semaphores. Data moves between devices by JAX's collectives and lax.ppermute only.
A program may use at most 256 MiB of HBM per device.

```python
import math
import jax
import jax.numpy as jnp
from jax import lax

D = 896
HEADS = 14
KV_HEADS = 2
HEAD = 64
FF = 4864
SEQS = 2
BLOCK = 768
LENGTH = 3072
N_CTX = 4


def block_levels(rng, shape, shards, low, high):
    factor_of, own = 1.0, jax.random.fold_in(rng, 6)
    for position, shards_of in shards:
        steps = jnp.exp(jax.random.uniform(jax.random.fold_in(own, position), (shards_of,), jnp.float32, low / len(shards), high / len(shards)))
        factor_of = factor_of * jnp.repeat(steps, shape[position] // shards_of).reshape([-1 if axis == position else 1 for axis in range(len(shape))])
    return factor_of


def gaussian(own_key, extent, width, most, shards=(), kind=jnp.bfloat16):
    values = jax.random.normal(own_key, extent, jnp.float32) * width
    if len(shards) > 0:
        values = block_levels(own_key, extent, shards, -0.22, 0.18) * values
    return jnp.clip(values, min=-most, max=most).astype(kind)


def setup_inputs(seed: int = 0) -> dict:
    seeds = jax.random.split(jax.random.key(seed), 16)
    tokens = gaussian(seeds[0], (SEQS, LENGTH, D), 1.0, 6.0, ((0, 2), (1, 16)))
    out_grad = gaussian(seeds[1], (SEQS, LENGTH, D), 1.0, 6.0, ((0, 2), (1, 16)))
    block_order = jax.vmap(lambda own: jax.random.permutation(own, N_CTX))(jax.random.split(seeds[2], SEQS)).reshape((SEQS, N_CTX)).astype(jnp.int32)
    norm1_gain = jnp.clip(1.0 + 0.1 * jax.random.normal(seeds[3], (D,), jnp.float32), 0.5, 1.5).astype(jnp.bfloat16)
    q_weight = gaussian(seeds[4], (D, HEADS * HEAD), (D // 2) ** -0.5, 0.25, ((0, 4),))
    q_bias = gaussian(seeds[5], (HEADS * HEAD,), 0.2, 1.25, ((0, 4),))
    k_weight = gaussian(seeds[6], (D, KV_HEADS * HEAD), (D // 2) ** -0.5, 0.25, ((0, 4),))
    k_bias = gaussian(seeds[7], (KV_HEADS * HEAD,), 0.2, 1.25, ((0, 4),))
    v_weight = gaussian(seeds[8], (D, KV_HEADS * HEAD), D ** -0.5, 0.1875, ((0, 4),))
    v_bias = gaussian(seeds[9], (KV_HEADS * HEAD,), 0.2, 1.25, ((0, 4),))
    o_weight = gaussian(seeds[10], (HEADS * HEAD, D), (HEADS * HEAD // 4) ** -0.5, 0.375, ((0, 4),))
    norm2_gain = jnp.clip(1.0 + 0.1 * jax.random.normal(seeds[11], (D,), jnp.float32), 0.5, 1.5).astype(jnp.bfloat16)
    gate_weight = gaussian(seeds[12], (D, FF), D ** -0.5, 0.1875, ((0, 4),))
    up_weight = gaussian(seeds[13], (D, FF), D ** -0.5, 0.1875, ((0, 4),))
    down_weight = gaussian(seeds[14], (FF, D), FF ** -0.5, 0.078125, ((0, 4),))
    return dict(tokens=tokens, out_grad=out_grad, block_order=block_order, norm1_gain=norm1_gain, q_weight=q_weight, q_bias=q_bias, k_weight=k_weight, k_bias=k_bias, v_weight=v_weight, v_bias=v_bias, o_weight=o_weight, norm2_gain=norm2_gain, gate_weight=gate_weight, up_weight=up_weight, down_weight=down_weight)


NORM_EPS = 1e-06
ROPE_BASE = 1000000.0
MASKED = -1e+30

@jax.custom_vjp
def low(v):
    return lax.optimization_barrier(v.astype(jnp.bfloat16)).astype(jnp.float32)

@jax.custom_vjp
def low_back(v):
    return v

def low_keep(v):
    return (low(v), None)

def low_pass(kept, grad):
    return (grad,)

def back_keep(v):
    return (v, None)

def back_low(kept, grad):
    return (low(grad),)
low.defvjp(low_keep, low_pass)
low_back.defvjp(back_keep, back_low)

def matmul(left_side, right_side):
    return jnp.dot(left_side, right_side, precision=lax.Precision.HIGHEST)

def largest_divisor(length, upper_limit):
    chosen = 1
    for candidate in range(1, min(length, upper_limit) + 1):
        if length % candidate == 0:
            chosen = candidate
    return chosen

def rope_tables(positions, head_dim):
    half_dim = head_dim // 2
    inverse = jnp.exp(jnp.arange(half_dim, dtype=jnp.float32) * (-math.log(ROPE_BASE) * 2.0 / head_dim))
    angles = positions.astype(jnp.float32)[:, None] * inverse[None, :]
    return (jnp.cos(angles)[:, None, :], jnp.sin(angles)[:, None, :])

def rotate(values, cosine_table, sine_table):
    half_dim = values.shape[-1] // 2
    front_half = values[..., :half_dim]
    back_half = values[..., half_dim:]
    return jnp.concatenate([front_half * cosine_table - back_half * sine_table, back_half * cosine_table + front_half * sine_table], -1)

def one_layer(inputs, positions, gain_one, w_query, b_query, w_key, b_key, w_value, b_value, w_out, gain_two, w_gate, w_up, w_down):
    length_all = inputs.shape[0]
    hidden_one = low(inputs * lax.rsqrt(lax.optimization_barrier(jnp.mean(inputs * inputs, -1, keepdims=True)) + NORM_EPS) * gain_one)
    cosine_table, sine_table = rope_tables(positions, HEAD)
    query_pre = low_back(matmul(hidden_one, w_query) + b_query).reshape(length_all, HEADS, HEAD)
    key_pre = low_back(matmul(hidden_one, w_key) + b_key).reshape(length_all, KV_HEADS, HEAD)
    values = low(low_back(matmul(hidden_one, w_value) + b_value)).reshape(length_all, KV_HEADS, HEAD)
    queries = low(rotate(query_pre, cosine_table, sine_table))
    keys = low(rotate(key_pre, cosine_table, sine_table))
    group_size = HEADS // KV_HEADS
    keys_wide = jnp.repeat(keys, group_size, axis=1)
    values_wide = jnp.repeat(values, group_size, axis=1)
    query_block = largest_divisor(length_all, 512)
    block_count = length_all // query_block

    def attend(block_pair):
        query_rows, query_pos = block_pair
        raw_scores = jnp.einsum('qhd,khd->hqk', query_rows, keys_wide, precision=lax.Precision.HIGHEST)
        allowed = positions[None, None, :] <= query_pos[None, :, None]
        scores = jnp.where(allowed, low_back(raw_scores) * HEAD ** (-0.5), MASKED)
        prob_values = low(jax.nn.softmax(scores, axis=-1))
        return jnp.einsum('hqk,khd->qhd', prob_values, values_wide, precision=lax.Precision.HIGHEST)
    attention = lax.map(jax.checkpoint(attend), (queries.reshape(block_count, query_block, HEADS, HEAD), positions.reshape(block_count, query_block)))
    attended = low(low_back(attention.reshape(length_all, HEADS * HEAD)))
    resid = inputs + low_back(matmul(attended, w_out))
    hidden_two = low(resid * lax.rsqrt(lax.optimization_barrier(jnp.mean(resid * resid, -1, keepdims=True)) + NORM_EPS) * gain_two)
    gate_proj = low_back(matmul(hidden_two, w_gate))
    up_proj = low_back(matmul(hidden_two, w_up))
    activated = low(jax.nn.silu(gate_proj) * up_proj)
    return resid + low_back(matmul(activated, w_down))

def reference(tokens, out_grad, block_order, norm1_gain, q_weight, q_bias, k_weight, k_bias, v_weight, v_bias, o_weight, norm2_gain, gate_weight, up_weight, down_weight):
    positions = (block_order[:, :, None] * BLOCK + jnp.arange(BLOCK, dtype=jnp.int32)[None, None, :]).reshape(SEQS, LENGTH)
    weights = tuple((weight.astype(jnp.float32) for weight in (norm1_gain, q_weight, q_bias, k_weight, k_bias, v_weight, v_bias, o_weight, norm2_gain, gate_weight, up_weight, down_weight)))

    def forward(inputs_all, *params):

        def one_sequence(seq_pair):
            return one_layer(seq_pair[0], seq_pair[1], *params)
        return lax.map(one_sequence, (inputs_all, positions))
    result, pullback = jax.vjp(forward, tokens.astype(jnp.float32), *weights)
    gradients = pullback(out_grad.astype(jnp.float32))
    return (result.astype(jnp.bfloat16), gradients[0], gradients[1], gradients[2], gradients[3], gradients[4], gradients[5], gradients[6], gradients[7], gradients[8], gradients[9], gradients[10], gradients[11], gradients[12])
```

```python
import math

import jax
import jax.numpy as jnp
from jax import lax
from jax.sharding import PartitionSpec as P

HEADS = 14
KV_HEADS = 2
HEAD = 64
GROUP = HEADS // KV_HEADS
NORM_EPS = 1e-06
ROPE_BASE = 1000000.0
MASKED = -1e30
BF16 = jnp.bfloat16
F32 = jnp.float32


def rope_tables(positions, head_dim):
    half_dim = head_dim // 2
    inverse = jnp.exp(
        jnp.arange(half_dim, dtype=jnp.float32) * (-math.log(ROPE_BASE) * 2.0 / head_dim)
    )
    angles = positions.astype(jnp.float32)[:, None] * inverse[None, :]
    return (jnp.cos(angles)[:, None, :], jnp.sin(angles)[:, None, :])


def rotate(values, cosine_table, sine_table):
    half_dim = values.shape[-1] // 2
    front_half = values[..., :half_dim]
    back_half = values[..., half_dim:]
    return jnp.concatenate(
        [
            front_half * cosine_table - back_half * sine_table,
            back_half * cosine_table + front_half * sine_table,
        ],
        -1,
    )


def matmul(left_side, right_side):
    return jnp.dot(left_side, right_side, preferred_element_type=F32)


def contract_rows(left_side, right_side):
    return lax.dot_general(
        left_side, right_side, (((0,), (0,)), ((), ())), preferred_element_type=F32
    )


def times_transposed(left_side, right_side):
    return lax.dot_general(
        left_side, right_side, (((1,), (1,)), ((), ())), preferred_element_type=F32
    )


def rms_forward(values, gain_vec):
    inv_scale = lax.rsqrt(jnp.mean(values * values, -1, keepdims=True) + NORM_EPS)
    normed = values * inv_scale
    return (normed, inv_scale, (normed * gain_vec).astype(BF16))


def rms_backward(grad_out, normed, inv_scale, gain_vec):
    gain_grad = jnp.sum(grad_out * normed, 0)
    scaled = grad_out * gain_vec
    grad_in = inv_scale * (scaled - normed * jnp.mean(scaled * normed, -1, keepdims=True))
    return (grad_in, gain_grad)


def group_heads(values):
    tokens_here = values.shape[0]
    return (
        values.reshape(tokens_here, KV_HEADS, GROUP, HEAD)
        .transpose(1, 2, 0, 3)
        .reshape(KV_HEADS, GROUP * tokens_here, HEAD)
    )


def ungroup_heads(values, tokens_here):
    return (
        values.reshape(KV_HEADS, GROUP, tokens_here, HEAD)
        .transpose(2, 0, 1, 3)
        .reshape(tokens_here, KV_HEADS * GROUP * HEAD)
    )


def scores_of(queries, query_rows_pos, keys_block, key_pos_block, score_scale):
    raw_scores = jnp.einsum("gqd,kgd->gqk", queries, keys_block, preferred_element_type=F32)
    allowed = key_pos_block[None, None, :] <= query_rows_pos[None, :, None]
    return (jnp.where(allowed, raw_scores * score_scale, MASKED), allowed)


def attend_forward(queries, query_rows_pos, key_blocks, value_blocks, key_pos_blocks, score_scale):
    kv_heads, row_count, head_dim = queries.shape
    query_top = jnp.max(query_rows_pos)

    def step(carry, block_in):
        keys_block, values_block, key_pos_block = block_in

        def active(state):
            running_top, running_sum, running = state
            scores, allowed = scores_of(
                queries, query_rows_pos, keys_block, key_pos_block, score_scale
            )
            new_top = jnp.maximum(running_top, jnp.max(scores, -1))
            exp_scores = jnp.where(allowed, jnp.exp(scores - new_top[..., None]), 0.0)
            shrink = jnp.exp(running_top - new_top)
            running = running * shrink[..., None] + jnp.einsum(
                "gqk,kgd->gqd", exp_scores.astype(BF16), values_block, preferred_element_type=F32
            )
            return (new_top, running_sum * shrink + jnp.sum(exp_scores, -1), running)

        def passed(state):
            return state

        return (lax.cond(jnp.min(key_pos_block) <= query_top, active, passed, carry), None)

    start = (
        jnp.full((kv_heads, row_count), MASKED, F32),
        jnp.zeros((kv_heads, row_count), F32),
        jnp.zeros((kv_heads, row_count, head_dim), F32),
    )
    (final_top, final_sum, output), unused = lax.scan(
        step, start, (key_blocks, value_blocks, key_pos_blocks)
    )
    return (output / final_sum[..., None], final_top + jnp.log(final_sum))


def attend_backward(
    queries,
    query_rows_pos,
    key_blocks,
    value_blocks,
    key_pos_blocks,
    score_scale,
    log_total,
    grad_rows,
    row_delta,
):
    kv_heads, row_count, head_dim = queries.shape
    query_top = jnp.max(query_rows_pos)

    def back_step(carry, block_in):
        keys_block, values_block, key_pos_block = block_in
        block_rows = keys_block.shape[0]

        def back_active(running):
            scores, allowed = scores_of(
                queries, query_rows_pos, keys_block, key_pos_block, score_scale
            )
            prob_values = jnp.where(allowed, jnp.exp(scores - log_total[..., None]), 0.0)
            grad_values = jnp.einsum(
                "gqk,gqd->kgd", prob_values.astype(BF16), grad_rows, preferred_element_type=F32
            )
            grad_probs = jnp.einsum(
                "gqd,kgd->gqk", grad_rows, values_block, preferred_element_type=F32
            )
            grad_scores = (prob_values * (grad_probs - row_delta[..., None]) * score_scale).astype(
                BF16
            )
            running = running + jnp.einsum(
                "gqk,kgd->gqd", grad_scores, keys_block, preferred_element_type=F32
            )
            grad_keys = jnp.einsum(
                "gqk,gqd->kgd", grad_scores, queries, preferred_element_type=F32
            )
            stacked = jnp.concatenate(
                [
                    grad_keys.reshape(block_rows, kv_heads * head_dim),
                    grad_values.reshape(block_rows, kv_heads * head_dim),
                ],
                1,
            )
            return (running, stacked.astype(BF16))

        def back_passed(running):
            return (running, jnp.zeros((block_rows, 2 * kv_heads * head_dim), BF16))

        return lax.cond(jnp.min(key_pos_block) <= query_top, back_active, back_passed, carry)

    start_grad = jnp.zeros((kv_heads, row_count, head_dim), F32)
    return lax.scan(back_step, start_grad, (key_blocks, value_blocks, key_pos_blocks))


def local(
    tokens,
    out_grad,
    block_order,
    norm1_gain,
    q_weight,
    q_bias,
    k_weight,
    k_bias,
    v_weight,
    v_bias,
    o_weight,
    norm2_gain,
    gate_weight,
    up_weight,
    down_weight,
):
    n_ctx = lax.axis_size("ctx")
    n_z = lax.axis_size("fsdp")
    tp = 4 if n_ctx % 4 == 0 else (2 if n_ctx % 2 == 0 else 1)
    here = lax.axis_index("ctx")
    zed = lax.axis_index("fsdp")
    core = lax.axis_index("seq")
    n_part = 2 * tp
    part = lax.rem(here, tp) * 2 + core
    first_core = core == 0

    def swap(v):
        return lax.ppermute(v, "seq", [(0, 1), (1, 0)])

    def hop(v, k):
        if k == 0:
            return v
        return lax.ppermute(v, "ctx", [(i, i ^ k) for i in range(n_ctx)])

    def gather_z(v):
        return lax.all_gather(v, "fsdp", axis=0, tiled=True)

    def scatter_z(v):
        return lax.psum_scatter(v, "fsdp", scatter_dimension=0, tiled=True)

    tokens_here, width = tokens.shape[1:]
    ff = gate_weight.shape[1]
    rows_here = q_weight.shape[0]
    q_half = GROUP * HEAD
    key_width = KV_HEADS * HEAD
    score_scale = HEAD ** (-0.5)
    block_len = tokens_here * n_z

    vec_len = 3 * rows_here + 2 * k_bias.shape[0]
    vec = jnp.concatenate([norm1_gain, norm2_gain, q_bias, k_bias, v_bias])
    half_width = q_half + 2 * HEAD
    vec_rows = 16
    vec = jnp.pad(vec, (0, vec_rows * half_width - vec_len)).reshape(vec_rows, half_width)
    qkv_half = jnp.concatenate(
        [
            lax.dynamic_slice_in_dim(q_weight, core * q_half, q_half, 1),
            lax.dynamic_slice_in_dim(k_weight, core * HEAD, HEAD, 1),
            lax.dynamic_slice_in_dim(v_weight, core * HEAD, HEAD, 1),
        ],
        1,
    )
    got = gather_z(jnp.concatenate([qkv_half, vec], 0)).reshape(n_z, -1, half_width)
    w_qkv_own = got[:, :rows_here].reshape(width, half_width)
    w_qkv_oth = swap(w_qkv_own)
    vecs = got[:, rows_here:].reshape(n_z, -1)
    gain_one = vecs[:, :rows_here].reshape(-1)
    gain_two = vecs[:, rows_here : 2 * rows_here].reshape(-1)
    b_query = vecs[:, 2 * rows_here : 3 * rows_here].reshape(-1)
    kb = k_bias.shape[0]
    b_key = vecs[:, 3 * rows_here : 3 * rows_here + kb].reshape(-1)
    b_value = vecs[:, 3 * rows_here + kb : 3 * rows_here + 2 * kb].reshape(-1)

    ff_z = ff // n_z
    piece = ff_z // n_part
    piece_pad = -(-piece // 32) * 32
    ff_half = n_z * piece_pad

    def ff_columns(w):
        cuts = []
        for j in range(n_z):
            cut = lax.dynamic_slice_in_dim(w, j * ff_z + part * piece, piece, 1)
            cuts.append(jnp.pad(cut, ((0, 0), (0, piece_pad - piece))))
        return jnp.concatenate(cuts, 1)

    gu_own = gather_z(jnp.concatenate([ff_columns(gate_weight), ff_columns(up_weight)], 1))
    gu_oth = swap(gu_own)
    down_cut = lax.dynamic_slice_in_dim(down_weight, part * piece, piece, 0)
    down_own = gather_z(jnp.pad(down_cut, ((0, piece_pad - piece), (0, 0))))
    down_oth = swap(down_own)
    o_half = gather_z(lax.dynamic_slice_in_dim(o_weight, core * (width // 2), width // 2, 1))
    o_oth = swap(o_half)
    w_out = jnp.where(
        first_core,
        jnp.concatenate([o_half, o_oth], 1),
        jnp.concatenate([o_oth, o_half], 1),
    )
    og_here = out_grad[0]
    og_all = jnp.concatenate([hop(og_here, k) for k in range(tp)], 0)

    order_row = block_order[0]
    query_pos = (
        order_row[here] * block_len
        + zed * tokens_here
        + jnp.arange(tokens_here, dtype=jnp.int32)
    )
    if n_ctx == tp:
        block_at = jnp.stack([order_row[here ^ k] for k in range(n_ctx)])
    else:
        block_at = order_row
    key_pos_blocks = (
        block_at[:, None] * block_len + jnp.arange(block_len, dtype=jnp.int32)[None, :]
    )
    query_rows_pos = jnp.tile(query_pos, GROUP)
    cosine_table, sine_table = rope_tables(query_pos, HEAD)

    inputs = tokens[0].astype(F32)
    normed_one, scale_one, hidden_one = rms_forward(inputs, gain_one)
    pre_own = matmul(hidden_one, w_qkv_own)
    pre_oth = matmul(hidden_one, w_qkv_oth)
    pre_a = jnp.where(first_core, pre_own, pre_oth)
    pre_b = jnp.where(first_core, pre_oth, pre_own)
    query_pre = jnp.concatenate([pre_a[:, :q_half], pre_b[:, :q_half]], 1) + b_query
    key_pre = (
        jnp.concatenate([pre_a[:, q_half : q_half + HEAD], pre_b[:, q_half : q_half + HEAD]], 1)
        + b_key
    )
    value_pre = jnp.concatenate([pre_a[:, q_half + HEAD :], pre_b[:, q_half + HEAD :]], 1) + b_value
    query_rot = rotate(
        query_pre.reshape(tokens_here, HEADS, HEAD), cosine_table, sine_table
    ).astype(BF16)
    key_rot = rotate(key_pre.reshape(tokens_here, KV_HEADS, HEAD), cosine_table, sine_table).astype(
        BF16
    )
    kv_local = jnp.concatenate(
        [key_rot.reshape(tokens_here, key_width), value_pre.astype(BF16)], 1
    )
    kv_block = gather_z(kv_local)
    if n_ctx == tp:
        kv_whole = jnp.stack([hop(kv_block, k) for k in range(n_ctx)])
    else:
        kv_whole = lax.all_gather(kv_block, "ctx", axis=0, tiled=False)
    key_blocks = kv_whole[..., :key_width].reshape(n_ctx, block_len, KV_HEADS, HEAD)
    value_blocks = kv_whole[..., key_width:].reshape(n_ctx, block_len, KV_HEADS, HEAD)
    queries = group_heads(query_rot)
    output, log_total = attend_forward(
        queries, query_rows_pos, key_blocks, value_blocks, key_pos_blocks, score_scale
    )
    attended = ungroup_heads(output, tokens_here).astype(BF16)
    resid = inputs + matmul(attended, w_out)
    normed_two, scale_two, hidden_two = rms_forward(resid, gain_two)

    h2_all = jnp.concatenate([hop(hidden_two, k) for k in range(tp)], 0)

    def scatter_plane(v):
        parts = v.astype(BF16).reshape(tp, tokens_here, width)
        total = parts[0].astype(F32)
        for k in range(1, tp):
            total = total + hop(parts[k], k).astype(F32)
        return total

    def ff_half_pass(w_gu, w_d):
        gu = matmul(h2_all, w_gu)
        gate = gu[:, :ff_half]
        up = gu[:, ff_half:]
        sig = jax.nn.sigmoid(gate)
        silu = gate * sig
        act = (silu * up).astype(BF16)
        grad_act = times_transposed(og_all, w_d)
        grad_gate = (grad_act * up * sig * (1.0 + gate * (1.0 - sig))).astype(BF16)
        grad_up = (grad_act * silu).astype(BF16)
        return act, jnp.concatenate([grad_gate, grad_up], 1)

    act_own, ggu_own = ff_half_pass(gu_own, down_own)
    act_oth, ggu_oth = ff_half_pass(gu_oth, down_oth)
    grad_h2 = scatter_plane(times_transposed(ggu_own, gu_own) + times_transposed(ggu_oth, gu_oth))
    result = resid + scatter_plane(matmul(act_own, down_own) + matmul(act_oth, down_oth))
    layer_out = result.astype(BF16)[None]

    def ff_reduce(own, oth):
        total = (own + swap(oth.astype(BF16)).astype(F32)).astype(BF16)
        mine = scatter_z(total)
        if n_ctx != tp:
            groups = [[g * tp + c for g in range(n_ctx // tp)] for c in range(tp)]
            mine = lax.psum(mine, "ctx", axis_index_groups=groups)
        pieces = [hop(mine, k) for k in range(tp)]
        sibling = swap(jnp.stack(pieces))
        both = jnp.concatenate([jnp.stack(pieces), sibling], 0)
        idx = jnp.arange(n_part, dtype=jnp.int32)
        where_at = (idx // 2 ^ lax.rem(here, tp)) + jnp.where(idx % 2 == core, 0, tp)
        return jnp.take(both, where_at, axis=0)

    d_down = ff_reduce(contract_rows(act_own, og_all), contract_rows(act_oth, og_all))
    grad_w_down = d_down[:, :piece].reshape(ff_z, width).astype(F32)
    d_gu = ff_reduce(contract_rows(h2_all, ggu_own), contract_rows(h2_all, ggu_oth))
    d_gu = d_gu.reshape(n_part, rows_here, 2, n_z, piece_pad)[..., :piece]
    d_gu = d_gu.transpose(2, 1, 3, 0, 4).reshape(2, rows_here, ff).astype(F32)
    grad_w_gate = d_gu[0]
    grad_w_up = d_gu[1]

    grad_norm_two, grad_gain_two = rms_backward(grad_h2, normed_two, scale_two, gain_two)
    grad_resid = og_here.astype(F32) + grad_norm_two
    grad_proj = grad_resid.astype(BF16)
    grad_att = times_transposed(grad_proj, w_out).astype(BF16)
    grad_rows = group_heads(grad_att)
    row_delta = jnp.sum(grad_rows.astype(F32) * output, -1)
    grad_queries, grad_terms = attend_backward(
        queries,
        query_rows_pos,
        key_blocks,
        value_blocks,
        key_pos_blocks,
        score_scale,
        log_total,
        grad_rows,
        row_delta,
    )
    if n_ctx == tp:
        kv_sum = grad_terms[0].astype(F32)
        for k in range(1, n_ctx):
            kv_sum = kv_sum + hop(grad_terms[k], k).astype(F32)
        kv_sum = kv_sum.astype(BF16)
    else:
        kv_sum = lax.psum_scatter(grad_terms, "ctx", scatter_dimension=0, tiled=False)
    grad_kv = scatter_z(kv_sum).astype(F32)

    grad_q_pre = (
        rotate(
            ungroup_heads(grad_queries, tokens_here).reshape(tokens_here, HEADS, HEAD),
            cosine_table,
            -sine_table,
        )
        .reshape(tokens_here, HEADS * HEAD)
        .astype(BF16)
    )
    grad_k_pre = (
        rotate(
            grad_kv[:, :key_width].reshape(tokens_here, KV_HEADS, HEAD), cosine_table, -sine_table
        )
        .reshape(tokens_here, key_width)
        .astype(BF16)
    )
    grad_v_pre = grad_kv[:, key_width:].astype(BF16)

    def column_halves(q, k, v):
        return [
            jnp.concatenate(
                [
                    q[:, g * q_half : (g + 1) * q_half],
                    k[:, g * HEAD : (g + 1) * HEAD],
                    v[:, g * HEAD : (g + 1) * HEAD],
                ],
                1,
            )
            for g in range(2)
        ]

    halves = column_halves(grad_q_pre, grad_k_pre, grad_v_pre)
    g_own = jnp.where(first_core, halves[0], halves[1])
    g_oth = jnp.where(first_core, halves[1], halves[0])
    grad_hidden_one = times_transposed(g_own, w_qkv_own) + times_transposed(g_oth, w_qkv_oth)
    grad_norm_one, grad_gain_one = rms_backward(grad_hidden_one, normed_one, scale_one, gain_one)
    tokens_grad = (grad_resid + grad_norm_one)[None]

    def reduce_full(part_sum):
        cols = part_sum.shape[1]
        cut = part_sum.astype(BF16).reshape(n_z, 2, rows_here // 2, cols)
        own = lax.dynamic_index_in_dim(cut, core, 1, keepdims=False)
        oth = lax.dynamic_index_in_dim(cut, 1 - core, 1, keepdims=False)
        both = (own.astype(F32) + swap(oth).astype(F32)).astype(BF16)
        mine = scatter_z(both.reshape(-1, cols))
        if n_ctx == tp:
            k = 1
            while k < n_ctx:
                mine = lax.optimization_barrier(mine)
                mine = (mine.astype(F32) + hop(mine, k).astype(F32)).astype(BF16)
                k *= 2
            mine = lax.optimization_barrier(mine)
        else:
            mine = lax.psum(mine, "ctx")
        other = swap(mine)
        whole = jnp.where(
            first_core, jnp.concatenate([mine, other], 0), jnp.concatenate([other, mine], 0)
        )
        return whole.astype(F32)

    grad_w_out = reduce_full(contract_rows(attended, grad_proj))
    grad_w_query = reduce_full(contract_rows(hidden_one, grad_q_pre))
    grad_w_kv = reduce_full(
        contract_rows(hidden_one, jnp.concatenate([grad_k_pre, grad_v_pre], 1))
    )
    sums = lax.psum(
        jnp.concatenate(
            [
                grad_gain_one,
                grad_gain_two,
                jnp.sum(grad_q_pre.astype(F32), 0),
                jnp.sum(grad_k_pre.astype(F32), 0),
                jnp.sum(grad_v_pre.astype(F32), 0),
            ]
        ),
        ("seq", "ctx", "fsdp"),
    )

    def own_share(start, size):
        share = size // n_z
        return lax.dynamic_slice_in_dim(sums, start + zed * share, share, 0)

    return (
        layer_out,
        tokens_grad,
        own_share(0, width),
        grad_w_query,
        own_share(2 * width, width),
        grad_w_kv[:, :key_width],
        own_share(3 * width, key_width),
        grad_w_kv[:, key_width:],
        own_share(3 * width + key_width, key_width),
        grad_w_out,
        own_share(width, width),
        grad_w_gate,
        grad_w_up,
        grad_w_down,
    )


def solution(mesh):
    in_specs = (
        P("seq", ("ctx", "fsdp"), None),
        P("seq", ("ctx", "fsdp"), None),
        P("seq", None),
        P("fsdp"),
        P("fsdp", None),
        P("fsdp"),
        P("fsdp", None),
        P("fsdp"),
        P("fsdp", None),
        P("fsdp"),
        P("fsdp", None),
        P("fsdp"),
        P("fsdp", None),
        P("fsdp", None),
        P("fsdp", None),
    )
    out_specs = (
        P("seq", ("ctx", "fsdp"), None),
        P("seq", ("ctx", "fsdp"), None),
        P("fsdp"),
        P("fsdp", None),
        P("fsdp"),
        P("fsdp", None),
        P("fsdp"),
        P("fsdp", None),
        P("fsdp"),
        P("fsdp", None),
        P("fsdp"),
        P("fsdp", None),
        P("fsdp", None),
        P("fsdp", None),
    )
    return jax.shard_map(local, mesh=mesh, in_specs=in_specs, out_specs=out_specs, check_vma=False)
```

```python
import functools
import math

import jax
import jax.numpy as jnp
from jax import lax
from jax.experimental import pallas as pl
from jax.experimental.pallas import tpu as pltpu
from jax.sharding import PartitionSpec as P

HEADS = 14
KV_HEADS = 2
HEAD = 64
GROUP = HEADS // KV_HEADS
NORM_EPS = 1e-06
ROPE_BASE = 1000000.0
MASKED = -1e30
BF16 = jnp.bfloat16
F32 = jnp.float32


def rope_tables(positions, head_dim):
    half_dim = head_dim // 2
    inverse = jnp.exp(
        jnp.arange(half_dim, dtype=jnp.float32) * (-math.log(ROPE_BASE) * 2.0 / head_dim)
    )
    angles = positions.astype(jnp.float32)[:, None] * inverse[None, :]
    return (jnp.cos(angles)[:, None, :], jnp.sin(angles)[:, None, :])


def rotate(values, cosine_table, sine_table):
    half_dim = values.shape[-1] // 2
    front_half = values[..., :half_dim]
    back_half = values[..., half_dim:]
    return jnp.concatenate(
        [
            front_half * cosine_table - back_half * sine_table,
            back_half * cosine_table + front_half * sine_table,
        ],
        -1,
    )


def matmul(left_side, right_side):
    return jnp.dot(left_side, right_side, preferred_element_type=F32)


def contract_rows(left_side, right_side):
    return lax.dot_general(
        left_side, right_side, (((0,), (0,)), ((), ())), preferred_element_type=F32
    )


def times_transposed(left_side, right_side):
    return lax.dot_general(
        left_side, right_side, (((1,), (1,)), ((), ())), preferred_element_type=F32
    )


def rms_forward(values, gain_vec):
    inv_scale = lax.rsqrt(jnp.mean(values * values, -1, keepdims=True) + NORM_EPS)
    normed = values * inv_scale
    return (normed, inv_scale, (normed * gain_vec).astype(BF16))


def rms_backward(grad_out, normed, inv_scale, gain_vec):
    gain_grad = jnp.sum(grad_out * normed, 0)
    scaled = grad_out * gain_vec
    grad_in = inv_scale * (scaled - normed * jnp.mean(scaled * normed, -1, keepdims=True))
    return (grad_in, gain_grad)


def cut_heads(ref, head):
    tile = ref[:, (head // 2) * 128 : (head // 2 + 1) * 128].astype(F32)
    group = head // GROUP
    if head % 2 != group:
        tile = jnp.concatenate([tile[:, HEAD:], tile[:, :HEAD]], 1)
    lane = lax.broadcasted_iota(jnp.int32, tile.shape, 1)
    return jnp.where((lane >= HEAD) if group else (lane < HEAD), tile, 0.0)


def split_lanes(column, shape):
    high = column.astype(BF16).astype(F32)
    mid = (column - high).astype(BF16).astype(F32)
    low = column - high - mid
    lane = lax.broadcasted_iota(jnp.int32, shape, 1)
    return jnp.where(
        lane == 0, high, jnp.where(lane == 1, mid, jnp.where(lane == 2, low, 0.0))
    ).astype(BF16)


def piece_shift(at, zed, tokens_here, keys_here):
    pieces = keys_here // tokens_here
    shift = jnp.zeros(at.shape, jnp.int32)
    for k in range(pieces):
        here = (jnp.bitwise_xor(zed, k) - k - zed) * tokens_here
        shift = jnp.where(at >= k * tokens_here, here, shift)
    return shift


def forward_kernel(info_ref, q_ref, kv_ref, att_ref, qext_ref, top_ref, acc_ref):
    step = pl.program_id(0)
    last = pl.num_programs(0) - 1
    tokens_here = q_ref.shape[0]
    keys_here = kv_ref.shape[1]
    own = info_ref[0]
    zed = info_ref[1]
    block = info_ref[2 + step]

    @pl.when(step == 0)
    def _():
        for h in range(HEADS):
            qext_ref[h * tokens_here : (h + 1) * tokens_here, :128] = cut_heads(q_ref, h).astype(
                BF16
            )
        top_ref[...] = jnp.full(top_ref.shape, MASKED, F32)
        acc_ref[...] = jnp.zeros(acc_ref.shape, F32)

    def attend(masked):
        keys = kv_ref[0, :, :128]
        values = jnp.concatenate(
            [kv_ref[0, :, 128:], jnp.ones((keys_here, 128), BF16)], 1
        )
        if masked:
            row = lax.broadcasted_iota(jnp.int32, (tokens_here, keys_here), 0)
            col = lax.broadcasted_iota(jnp.int32, (tokens_here, keys_here), 1)
            allowed = col + piece_shift(col, zed, tokens_here, keys_here) <= row
        for h in range(HEADS):
            rows = slice(h * tokens_here, (h + 1) * tokens_here)
            scores = times_transposed(qext_ref[rows, :128], keys)
            if masked:
                scores = jnp.where(allowed, scores, MASKED)
            old = top_ref[rows, :]
            top = jnp.maximum(old, jnp.max(scores, -1, keepdims=True))
            probs = jnp.exp(scores - top[:, :1]).astype(BF16)
            shrink = jnp.exp(old - top)
            top_ref[rows, :] = top
            acc_ref[rows, :] = acc_ref[rows, :] * jnp.concatenate([shrink, shrink], 1) + matmul(
                probs, values
            )

    @pl.when(block == own)
    def _():
        attend(True)

    @pl.when(block < own)
    def _():
        attend(False)

    @pl.when(step == last)
    def _():
        lane = lax.broadcasted_iota(jnp.int32, (tokens_here, 128), 1)
        for pair in range(HEADS // 2):
            outs = []
            for h in (2 * pair, 2 * pair + 1):
                rows = slice(h * tokens_here, (h + 1) * tokens_here)
                total = acc_ref[rows, 128:]
                out = acc_ref[rows, :128] / total
                if h // GROUP != h % 2:
                    out = jnp.concatenate([out[:, HEAD:], out[:, :HEAD]], 1)
                outs.append(out)
                log_total = top_ref[rows, :] + jnp.log(total)
                qext_ref[rows, 128:] = split_lanes(-log_total, (tokens_here, 128))
            att_ref[:, pair * 128 : (pair + 1) * 128] = jnp.where(
                lane < HEAD, outs[0], outs[1]
            ).astype(BF16)


def backward_kernel(
    info_ref, qext_ref, do_ref, att_ref, kv_ref, dq_ref, dkv_ref, doext_ref, dqt_ref
):
    step = pl.program_id(0)
    last = pl.num_programs(0) - 1
    tokens_here = do_ref.shape[0]
    keys_here = kv_ref.shape[1]
    own = info_ref[0]
    zed = info_ref[1]
    block = info_ref[2 + step]
    span = 2 * tokens_here

    @pl.when(step == 0)
    def _():
        for h in range(HEADS):
            rows = slice(h * tokens_here, (h + 1) * tokens_here)
            grad = cut_heads(do_ref, h)
            delta = jnp.sum(grad * cut_heads(att_ref, h), -1, keepdims=True)
            doext_ref[rows, :128] = grad.astype(BF16)
            doext_ref[rows, 128:] = split_lanes(-delta, (tokens_here, 128))
        dqt_ref[...] = jnp.zeros(dqt_ref.shape, F32)

    def attend(masked):
        lane = lax.broadcasted_iota(jnp.int32, (keys_here, 128), 1)
        ones = jnp.where(lane < 3, 1.0, 0.0).astype(BF16)
        keys = kv_ref[0, :, :128]
        keys_ext = jnp.concatenate([keys, ones], 1)
        values_ext = jnp.concatenate([kv_ref[0, :, 128:], ones], 1)
        keys_t = keys.astype(F32).T.astype(BF16)
        if masked:
            row = lax.broadcasted_iota(jnp.int32, (keys_here, tokens_here), 0)
            col = lax.broadcasted_iota(jnp.int32, (keys_here, tokens_here), 1)
            allowed = row + piece_shift(row, zed, tokens_here, keys_here) <= col
            allowed = allowed.astype(F32)
            allowed = jnp.concatenate([allowed, allowed], 1) > 0.5
        dk = jnp.zeros((keys_here, 128), F32)
        dv = jnp.zeros((keys_here, 128), F32)
        for pair in range(HEADS // 2):
            rows = slice(pair * span, (pair + 1) * span)
            probs = jnp.exp(times_transposed(keys_ext, qext_ref[rows, :]))
            if masked:
                probs = jnp.where(allowed, probs, 0.0)
            slope = (probs * times_transposed(values_ext, doext_ref[rows, :])).astype(BF16)
            dv = dv + matmul(probs.astype(BF16), doext_ref[rows, :128])
            dk = dk + matmul(slope, qext_ref[rows, :128])
            dqt_ref[pair] = dqt_ref[pair] + matmul(keys_t, slope)
        dkv_ref[0] = jnp.concatenate([dk, dv], 1).astype(BF16)

    @pl.when(block == own)
    def _():
        attend(True)

    @pl.when(block < own)
    def _():
        attend(False)

    @pl.when(block > own)
    def _():
        dkv_ref[...] = jnp.zeros(dkv_ref.shape, BF16)

    @pl.when(step == last)
    def _():
        lane = lax.broadcasted_iota(jnp.int32, (tokens_here, 128), 1)
        for pair in range(HEADS // 2):
            turned = dqt_ref[pair].T
            outs = []
            for j in range(2):
                h = 2 * pair + j
                out = turned[j * tokens_here : (j + 1) * tokens_here]
                if h // GROUP != j:
                    out = jnp.concatenate([out[:, HEAD:], out[:, :HEAD]], 1)
                outs.append(out)
            dq_ref[:, pair * 128 : (pair + 1) * 128] = (
                jnp.where(lane < HEAD, outs[0], outs[1]) * HEAD ** (-0.5)
            )


def whole_spec(shape):
    return pl.BlockSpec(shape, lambda i, info: (0,) * len(shape))


def attend_forward(info, queries, kv):
    blocks, block_len, kv_width = kv.shape
    tokens_here, q_width = queries.shape
    rows = HEADS * tokens_here
    return pl.pallas_call(
        forward_kernel,
        grid_spec=pltpu.PrefetchScalarGridSpec(
            num_scalar_prefetch=1,
            grid=(blocks,),
            in_specs=[
                whole_spec((tokens_here, q_width)),
                pl.BlockSpec((1, block_len, kv_width), lambda i, info: (i, 0, 0)),
            ],
            out_specs=[whole_spec((tokens_here, q_width)), whole_spec((rows, 256))],
            scratch_shapes=[pltpu.VMEM((rows, 128), F32), pltpu.VMEM((rows, 256), F32)],
        ),
        out_shape=[
            jax.ShapeDtypeStruct((tokens_here, q_width), BF16),
            jax.ShapeDtypeStruct((rows, 256), BF16),
        ],
        compiler_params=pltpu.CompilerParams(
            dimension_semantics=("arbitrary",), vmem_limit_bytes=40 * 2**20
        ),
        cost_estimate=pl.CostEstimate(
            flops=4 * rows * blocks * block_len * 256,
            bytes_accessed=6 * 2**20,
            transcendentals=rows * blocks * block_len,
        ),
        name="attend_forward",
    )(info, queries, kv)


def attend_backward(info, queries_ext, grad_att, attended, kv):
    blocks, block_len, kv_width = kv.shape
    tokens_here, q_width = grad_att.shape
    rows = HEADS * tokens_here
    return pl.pallas_call(
        backward_kernel,
        grid_spec=pltpu.PrefetchScalarGridSpec(
            num_scalar_prefetch=1,
            grid=(blocks,),
            in_specs=[
                whole_spec((rows, 256)),
                whole_spec((tokens_here, q_width)),
                whole_spec((tokens_here, q_width)),
                pl.BlockSpec((1, block_len, kv_width), lambda i, info: (i, 0, 0)),
            ],
            out_specs=[
                whole_spec((tokens_here, q_width)),
                pl.BlockSpec((1, block_len, kv_width), lambda i, info: (i, 0, 0)),
            ],
            scratch_shapes=[
                pltpu.VMEM((rows, 256), BF16),
                pltpu.VMEM((HEADS // 2, 128, 2 * tokens_here), F32),
            ],
        ),
        out_shape=[
            jax.ShapeDtypeStruct((tokens_here, q_width), F32),
            jax.ShapeDtypeStruct(kv.shape, BF16),
        ],
        compiler_params=pltpu.CompilerParams(
            dimension_semantics=("arbitrary",), vmem_limit_bytes=40 * 2**20
        ),
        cost_estimate=pl.CostEstimate(
            flops=10 * rows * blocks * block_len * 256,
            bytes_accessed=8 * 2**20,
            transcendentals=rows * blocks * block_len,
        ),
        name="attend_backward",
    )(info, queries_ext, grad_att, attended, kv)


def spread_columns_kernel(n_z, where_ref, *refs):
    pieces, (gate_ref, up_ref, held) = refs[:-3], refs[-3:]
    n_part = len(pieces)
    for r in range(n_part):
        held[where_ref[r]] = pieces[r][...].astype(F32)
    half = held.shape[2] // 2
    pad = half // n_z
    piece = gate_ref.shape[1] // (n_z * n_part)
    for out, start in ((gate_ref, 0), (up_ref, half)):
        cuts = []
        for j in range(n_z):
            for e in range(n_part):
                cuts.append(held[e, :, start + j * pad : start + j * pad + piece])
        out[...] = jnp.concatenate(cuts, 1)


def spread_columns(where_at, pieces, n_z, ff):
    rows, cols = pieces[0].shape
    tile = 32
    n_part = len(pieces)
    return pl.pallas_call(
        functools.partial(spread_columns_kernel, n_z),
        grid_spec=pltpu.PrefetchScalarGridSpec(
            num_scalar_prefetch=1,
            grid=(rows // tile,),
            in_specs=[pl.BlockSpec((tile, cols), lambda i, w: (i, 0))] * n_part,
            out_specs=[pl.BlockSpec((tile, ff), lambda i, w: (i, 0))] * 2,
            scratch_shapes=[pltpu.VMEM((n_part, tile, cols), F32)],
        ),
        out_shape=[jax.ShapeDtypeStruct((rows, ff), F32)] * 2,
        compiler_params=pltpu.CompilerParams(
            dimension_semantics=("arbitrary",), vmem_limit_bytes=40 * 2**20
        ),
        cost_estimate=pl.CostEstimate(
            flops=0, bytes_accessed=rows * ff * 12, transcendentals=0
        ),
        name="spread_columns",
    )(where_at, *pieces)


def spread_rows_kernel(where_ref, *refs):
    pieces, out_ref = refs[:-1], refs[-1]
    piece = out_ref.shape[0] // len(pieces)
    for r in range(len(pieces)):
        start = pl.multiple_of(where_ref[r] * piece, 8)
        out_ref[pl.ds(start, piece), :] = pieces[r][...].astype(F32)[:piece]


def spread_rows(where_at, pieces, rows_out):
    rows, cols = pieces[0].shape
    tile = 128
    return pl.pallas_call(
        spread_rows_kernel,
        grid_spec=pltpu.PrefetchScalarGridSpec(
            num_scalar_prefetch=1,
            grid=(cols // tile,),
            in_specs=[pl.BlockSpec((rows, tile), lambda i, w: (0, i))] * len(pieces),
            out_specs=pl.BlockSpec((rows_out, tile), lambda i, w: (0, i)),
        ),
        out_shape=jax.ShapeDtypeStruct((rows_out, cols), F32),
        compiler_params=pltpu.CompilerParams(
            dimension_semantics=("arbitrary",), vmem_limit_bytes=40 * 2**20
        ),
        cost_estimate=pl.CostEstimate(
            flops=0, bytes_accessed=rows_out * cols * 6, transcendentals=0
        ),
        name="spread_rows",
    )(where_at, *pieces)


def local(
    tokens,
    out_grad,
    block_order,
    norm1_gain,
    q_weight,
    q_bias,
    k_weight,
    k_bias,
    v_weight,
    v_bias,
    o_weight,
    norm2_gain,
    gate_weight,
    up_weight,
    down_weight,
):
    n_ctx = lax.axis_size("ctx")
    n_z = lax.axis_size("fsdp")
    tp = 4 if n_ctx % 4 == 0 else (2 if n_ctx % 2 == 0 else 1)
    here = lax.axis_index("ctx")
    zed = lax.axis_index("fsdp")
    core = lax.axis_index("seq")
    n_part = 2 * tp
    part = lax.rem(here, tp) * 2 + core
    first_core = core == 0

    def swap(v):
        return lax.ppermute(v, "seq", [(0, 1), (1, 0)])

    def hop(v, k):
        if k == 0:
            return v
        return lax.ppermute(v, "ctx", [(i, i ^ k) for i in range(n_ctx)])

    def hop_z(v, k):
        if k == 0:
            return v
        return lax.ppermute(v, "fsdp", [(i, i ^ k) for i in range(n_z)])

    def gather_z(v):
        return lax.all_gather(v, "fsdp", axis=0, tiled=True)

    def scatter_z(v):
        return lax.psum_scatter(v, "fsdp", scatter_dimension=0, tiled=True)

    tokens_here, width = tokens.shape[1:]
    ff = gate_weight.shape[1]
    rows_here = q_weight.shape[0]
    q_half = GROUP * HEAD
    key_width = KV_HEADS * HEAD
    block_len = tokens_here * n_z

    vec_len = 3 * rows_here + 2 * k_bias.shape[0]
    vec = jnp.concatenate([norm1_gain, norm2_gain, q_bias, k_bias, v_bias])
    half_width = q_half + 2 * HEAD
    vec_rows = 16
    vec = jnp.pad(vec, (0, vec_rows * half_width - vec_len)).reshape(vec_rows, half_width)
    qkv_half = jnp.concatenate(
        [
            lax.dynamic_slice_in_dim(q_weight, core * q_half, q_half, 1),
            lax.dynamic_slice_in_dim(k_weight, core * HEAD, HEAD, 1),
            lax.dynamic_slice_in_dim(v_weight, core * HEAD, HEAD, 1),
        ],
        1,
    )
    got = gather_z(jnp.concatenate([qkv_half, vec], 0)).reshape(n_z, -1, half_width)
    w_qkv_own = got[:, :rows_here].reshape(width, half_width)
    w_qkv_oth = swap(w_qkv_own)
    vecs = got[:, rows_here:].reshape(n_z, -1)
    gain_one = vecs[:, :rows_here].reshape(-1)
    gain_two = vecs[:, rows_here : 2 * rows_here].reshape(-1)
    b_query = vecs[:, 2 * rows_here : 3 * rows_here].reshape(-1)
    kb = k_bias.shape[0]
    b_key = vecs[:, 3 * rows_here : 3 * rows_here + kb].reshape(-1)
    b_value = vecs[:, 3 * rows_here + kb : 3 * rows_here + 2 * kb].reshape(-1)

    ff_z = ff // n_z
    piece = ff_z // n_part
    piece_pad = -(-piece // 32) * 32
    ff_half = n_z * piece_pad

    def ff_columns(w):
        cuts = []
        for j in range(n_z):
            cut = lax.dynamic_slice_in_dim(w, j * ff_z + part * piece, piece, 1)
            cuts.append(jnp.pad(cut, ((0, 0), (0, piece_pad - piece))))
        return jnp.concatenate(cuts, 1)

    o_rows = rows_here // 2
    down_cut = lax.dynamic_slice_in_dim(down_weight, part * piece, piece, 0)
    do_cut = jnp.concatenate(
        [
            jnp.pad(down_cut, ((0, piece_pad - piece), (0, 0))),
            lax.dynamic_slice_in_dim(o_weight, core * o_rows, o_rows, 0),
        ],
        0,
    )
    gu_cut = jnp.concatenate([ff_columns(gate_weight), ff_columns(up_weight)], 1)
    w_qkv_own, do_cut, gu_cut = lax.optimization_barrier((w_qkv_own, do_cut, gu_cut))
    do_own = gather_z(do_cut)
    do_own, gu_cut = lax.optimization_barrier((do_own, gu_cut))
    gu_own = gather_z(gu_cut)
    gu_oth = swap(gu_own)
    do_oth = swap(do_own)
    do_own = do_own.reshape(n_z, -1, width)
    do_oth = do_oth.reshape(n_z, -1, width)
    down_own = do_own[:, :piece_pad].reshape(ff_half, width)
    down_oth = do_oth[:, :piece_pad].reshape(ff_half, width)
    o_own = do_own[:, piece_pad:]
    o_oth = do_oth[:, piece_pad:]
    w_out = jnp.where(
        first_core, jnp.stack([o_own, o_oth], 1), jnp.stack([o_oth, o_own], 1)
    ).reshape(width, width)
    og_here = out_grad[0]
    og_all = jnp.concatenate([hop(og_here, k) for k in range(tp)], 0)

    order_row = block_order[0]
    query_pos = (
        order_row[here] * block_len
        + zed * tokens_here
        + jnp.arange(tokens_here, dtype=jnp.int32)
    )
    if n_ctx == tp:
        block_at = jnp.stack([order_row[here ^ k] for k in range(n_ctx)])
    else:
        block_at = order_row
    info = jnp.concatenate([jnp.stack([order_row[here], zed]).astype(jnp.int32), block_at])
    cosine_table, sine_table = rope_tables(query_pos, HEAD)

    inputs = tokens[0].astype(F32)
    normed_one, scale_one, hidden_one = rms_forward(inputs, gain_one)
    pre_own = matmul(hidden_one, w_qkv_own)
    pre_oth = matmul(hidden_one, w_qkv_oth)
    pre_a = jnp.where(first_core, pre_own, pre_oth)
    pre_b = jnp.where(first_core, pre_oth, pre_own)
    query_pre = jnp.concatenate([pre_a[:, :q_half], pre_b[:, :q_half]], 1) + b_query
    key_pre = (
        jnp.concatenate([pre_a[:, q_half : q_half + HEAD], pre_b[:, q_half : q_half + HEAD]], 1)
        + b_key
    )
    value_pre = jnp.concatenate([pre_a[:, q_half + HEAD :], pre_b[:, q_half + HEAD :]], 1) + b_value
    queries = rotate(query_pre.reshape(tokens_here, HEADS, HEAD), cosine_table, sine_table)
    queries = queries.astype(BF16).reshape(tokens_here, HEADS * HEAD) * BF16(HEAD ** (-0.5))
    key_rot = rotate(key_pre.reshape(tokens_here, KV_HEADS, HEAD), cosine_table, sine_table)
    kv_local = jnp.concatenate(
        [key_rot.astype(BF16).reshape(tokens_here, key_width), value_pre.astype(BF16)], 1
    )
    kv_block = jnp.concatenate([hop_z(kv_local, k) for k in range(n_z)], 0)
    if n_ctx == tp:
        kv_whole = jnp.stack([hop(kv_block, k) for k in range(n_ctx)])
    else:
        kv_whole = lax.all_gather(kv_block, "ctx", axis=0, tiled=False)
    attended, queries_ext = attend_forward(info, queries, kv_whole)
    resid = inputs + matmul(attended, w_out)
    normed_two, scale_two, hidden_two = rms_forward(resid, gain_two)

    h2_all = jnp.concatenate([hop(hidden_two, k) for k in range(tp)], 0)

    def scatter_plane(v):
        parts = v.astype(BF16).reshape(tp, tokens_here, width)
        total = parts[0].astype(F32)
        for k in range(1, tp):
            total = total + hop(parts[k], k).astype(F32)
        return total

    def ff_half_pass(w_gu, w_d):
        gu = matmul(h2_all, w_gu)
        gate = gu[:, :ff_half]
        up = gu[:, ff_half:]
        sig = jax.nn.sigmoid(gate)
        silu = gate * sig
        act = (silu * up).astype(BF16)
        grad_act = times_transposed(og_all, w_d)
        grad_gate = (grad_act * up * sig * (1.0 + gate * (1.0 - sig))).astype(BF16)
        grad_up = (grad_act * silu).astype(BF16)
        return act, jnp.concatenate([grad_gate, grad_up], 1)

    act_own, ggu_own = ff_half_pass(gu_own, down_own)
    act_oth, ggu_oth = ff_half_pass(gu_oth, down_oth)
    grad_h2 = scatter_plane(times_transposed(ggu_own, gu_own) + times_transposed(ggu_oth, gu_oth))
    result = resid + scatter_plane(matmul(act_own, down_own) + matmul(act_oth, down_oth))
    layer_out = result.astype(BF16)[None]

    idx = jnp.arange(n_part, dtype=jnp.int32)
    where_at = ((idx // 2) ^ lax.rem(here, tp)) * 2 + ((idx % 2) ^ core)

    def reduce_start(part_sum):
        cols = part_sum.shape[1]
        cut = part_sum.astype(BF16).reshape(n_z, 2, rows_here // 2, cols)
        own = lax.dynamic_index_in_dim(cut, core, 1, keepdims=False)
        oth = lax.dynamic_index_in_dim(cut, 1 - core, 1, keepdims=False)
        return (own.astype(F32) + swap(oth).astype(F32)).astype(BF16).reshape(-1, cols)

    def scatter_hops(v):
        cut = v.reshape(n_z, -1, v.shape[1])
        total = lax.dynamic_index_in_dim(cut, zed, 0, keepdims=False).astype(F32)
        for k in range(1, n_z):
            out = lax.dynamic_index_in_dim(cut, zed ^ k, 0, keepdims=False)
            total = total + hop_z(out, k).astype(F32)
        return total.astype(BF16)

    def reduce_end(mine):
        if n_ctx == tp:
            k = 1
            while k < n_ctx:
                mine = lax.optimization_barrier(mine)
                mine = (mine.astype(F32) + hop(mine, k).astype(F32)).astype(BF16)
                k *= 2
            mine = lax.optimization_barrier(mine)
        else:
            mine = lax.psum(mine, "ctx")
        other = swap(mine)
        whole = jnp.where(
            first_core, jnp.concatenate([mine, other], 0), jnp.concatenate([other, mine], 0)
        )
        return whole.astype(F32)

    def core_sum(own, oth):
        return (own + swap(oth.astype(BF16)).astype(F32)).astype(BF16)

    def ff_pieces(mine):
        if n_ctx != tp:
            groups = [[g * tp + c for g in range(n_ctx // tp)] for c in range(tp)]
            mine = lax.psum(mine, "ctx", axis_index_groups=groups)
        pieces = []
        for k in range(tp):
            pieces.append(hop(mine, k))
            pieces.append(swap(pieces[-1]))
        return pieces

    d_gu = core_sum(contract_rows(h2_all, ggu_own), contract_rows(h2_all, ggu_oth))
    d_down = core_sum(contract_rows(act_own, og_all), contract_rows(act_oth, og_all))

    grad_norm_two, grad_gain_two = rms_backward(grad_h2, normed_two, scale_two, gain_two)
    grad_resid = og_here.astype(F32) + grad_norm_two
    grad_proj = grad_resid.astype(BF16)
    grad_att = times_transposed(grad_proj, w_out).astype(BF16)
    d_out = reduce_start(contract_rows(attended, grad_proj))
    grad_att, d_gu, d_down, d_out = lax.optimization_barrier((grad_att, d_gu, d_down, d_out))
    d_gu = scatter_z(d_gu)
    d_down = scatter_z(d_down)
    d_out = scatter_z(d_out)
    grad_queries, grad_terms = attend_backward(info, queries_ext, grad_att, attended, kv_whole)
    if n_ctx == tp:
        kv_sum = grad_terms[0].astype(F32)
        for k in range(1, n_ctx):
            kv_sum = kv_sum + hop(grad_terms[k], k).astype(F32)
        kv_sum = kv_sum.astype(BF16)
    else:
        kv_sum = lax.psum_scatter(grad_terms, "ctx", scatter_dimension=0, tiled=False)
    kv_sum = kv_sum.reshape(n_z, tokens_here, 2 * key_width)
    grad_kv = kv_sum[0].astype(F32)
    for k in range(1, n_z):
        grad_kv = grad_kv + hop_z(kv_sum[k], k).astype(F32)

    grad_q_pre = (
        rotate(grad_queries.reshape(tokens_here, HEADS, HEAD), cosine_table, -sine_table)
        .reshape(tokens_here, HEADS * HEAD)
        .astype(BF16)
    )
    grad_k_pre = (
        rotate(
            grad_kv[:, :key_width].reshape(tokens_here, KV_HEADS, HEAD), cosine_table, -sine_table
        )
        .reshape(tokens_here, key_width)
        .astype(BF16)
    )
    grad_v_pre = grad_kv[:, key_width:].astype(BF16)

    def column_halves(q, k, v):
        return [
            jnp.concatenate(
                [
                    q[:, g * q_half : (g + 1) * q_half],
                    k[:, g * HEAD : (g + 1) * HEAD],
                    v[:, g * HEAD : (g + 1) * HEAD],
                ],
                1,
            )
            for g in range(2)
        ]

    halves = column_halves(grad_q_pre, grad_k_pre, grad_v_pre)
    g_own = jnp.where(first_core, halves[0], halves[1])
    g_oth = jnp.where(first_core, halves[1], halves[0])
    grad_hidden_one = times_transposed(g_own, w_qkv_own) + times_transposed(g_oth, w_qkv_oth)
    grad_norm_one, grad_gain_one = rms_backward(grad_hidden_one, normed_one, scale_one, gain_one)
    tokens_grad = (grad_resid + grad_norm_one)[None]

    def by_rows(v):
        share = v.shape[0] // n_z
        return jnp.pad(v.reshape(n_z, share), ((0, 0), (0, rows_here - share))).reshape(width)

    columns = jnp.stack(
        [
            grad_gain_one,
            grad_gain_two,
            jnp.sum(grad_q_pre.astype(F32), 0),
            by_rows(jnp.sum(grad_k_pre.astype(F32), 0)),
            by_rows(jnp.sum(grad_v_pre.astype(F32), 0)),
        ],
        1,
    )
    grad_w_query = reduce_end(
        scatter_hops(reduce_start(contract_rows(hidden_one, grad_q_pre)))
    )
    grad_w_kv = jnp.concatenate(
        [
            contract_rows(hidden_one, jnp.concatenate([grad_k_pre, grad_v_pre], 1)),
            jnp.pad(columns, ((0, 0), (0, 128 - columns.shape[1]))),
        ],
        1,
    )
    grad_w_kv = reduce_end(scatter_hops(reduce_start(grad_w_kv)))
    sums = grad_w_kv[:, 2 * key_width :]
    grad_w_out = reduce_end(d_out)
    grad_w_gate, grad_w_up = spread_columns(where_at, ff_pieces(d_gu), n_z, ff)
    grad_w_down = spread_rows(where_at, ff_pieces(d_down), ff_z)

    return (
        layer_out,
        tokens_grad,
        sums[:, 0],
        grad_w_query,
        sums[:, 2],
        grad_w_kv[:, :key_width],
        sums[:kb, 3],
        grad_w_kv[:, key_width : 2 * key_width],
        sums[:kb, 4],
        grad_w_out,
        sums[:, 1],
        grad_w_gate,
        grad_w_up,
        grad_w_down,
    )


def solution(mesh):
    in_specs = (
        P("seq", ("ctx", "fsdp"), None),
        P("seq", ("ctx", "fsdp"), None),
        P("seq", None),
        P("fsdp"),
        P("fsdp", None),
        P("fsdp"),
        P("fsdp", None),
        P("fsdp"),
        P("fsdp", None),
        P("fsdp"),
        P("fsdp", None),
        P("fsdp"),
        P("fsdp", None),
        P("fsdp", None),
        P("fsdp", None),
    )
    out_specs = (
        P("seq", ("ctx", "fsdp"), None),
        P("seq", ("ctx", "fsdp"), None),
        P("fsdp"),
        P("fsdp", None),
        P("fsdp"),
        P("fsdp", None),
        P("fsdp"),
        P("fsdp", None),
        P("fsdp"),
        P("fsdp", None),
        P("fsdp"),
        P("fsdp", None),
        P("fsdp", None),
        P("fsdp", None),
    )
    return jax.shard_map(local, mesh=mesh, in_specs=in_specs, out_specs=out_specs, check_vma=False)
```

```python
import functools
import math

import jax
import jax.numpy as jnp
from jax import lax
from jax.experimental import pallas as pl
from jax.experimental.pallas import tpu as pltpu
from jax.sharding import PartitionSpec as P

HEADS = 14
KV_HEADS = 2
HEAD = 64
GROUP = HEADS // KV_HEADS
NORM_EPS = 1e-06
ROPE_BASE = 1000000.0
MASKED = -1e30
BF16 = jnp.bfloat16
F32 = jnp.float32


def rope_tables(positions, head_dim):
    half_dim = head_dim // 2
    inverse = jnp.exp(
        jnp.arange(half_dim, dtype=jnp.float32) * (-math.log(ROPE_BASE) * 2.0 / head_dim)
    )
    angles = positions.astype(jnp.float32)[:, None] * inverse[None, :]
    return (jnp.cos(angles)[:, None, :], jnp.sin(angles)[:, None, :])


def rotate(values, cosine_table, sine_table):
    half_dim = values.shape[-1] // 2
    front_half = values[..., :half_dim]
    back_half = values[..., half_dim:]
    return jnp.concatenate(
        [
            front_half * cosine_table - back_half * sine_table,
            back_half * cosine_table + front_half * sine_table,
        ],
        -1,
    )


def matmul(left_side, right_side):
    return jnp.dot(left_side, right_side, preferred_element_type=F32)


def contract_rows(left_side, right_side):
    return lax.dot_general(
        left_side, right_side, (((0,), (0,)), ((), ())), preferred_element_type=F32
    )


def times_transposed(left_side, right_side):
    return lax.dot_general(
        left_side, right_side, (((1,), (1,)), ((), ())), preferred_element_type=F32
    )


def rms_forward(values, gain_vec):
    inv_scale = lax.rsqrt(jnp.mean(values * values, -1, keepdims=True) + NORM_EPS)
    normed = values * inv_scale
    return (normed, inv_scale, (normed * gain_vec).astype(BF16))


def rms_backward(grad_out, normed, inv_scale, gain_vec):
    gain_grad = jnp.sum(grad_out * normed, 0)
    scaled = grad_out * gain_vec
    grad_in = inv_scale * (scaled - normed * jnp.mean(scaled * normed, -1, keepdims=True))
    return (grad_in, gain_grad)


def cut_heads(ref, head):
    tile = ref[:, (head // 2) * 128 : (head // 2 + 1) * 128].astype(F32)
    group = head // GROUP
    if head % 2 != group:
        tile = jnp.concatenate([tile[:, HEAD:], tile[:, :HEAD]], 1)
    lane = lax.broadcasted_iota(jnp.int32, tile.shape, 1)
    return jnp.where((lane >= HEAD) if group else (lane < HEAD), tile, 0.0)


def split_lanes(column, shape):
    high = column.astype(BF16).astype(F32)
    mid = (column - high).astype(BF16).astype(F32)
    low = column - high - mid
    lane = lax.broadcasted_iota(jnp.int32, shape, 1)
    return jnp.where(
        lane == 0, high, jnp.where(lane == 1, mid, jnp.where(lane == 2, low, 0.0))
    ).astype(BF16)


def piece_shift(at, zed, tokens_here, keys_here):
    pieces = keys_here // tokens_here
    shift = jnp.zeros(at.shape, jnp.int32)
    for k in range(pieces):
        here = (jnp.bitwise_xor(zed, k) - k - zed) * tokens_here
        shift = jnp.where(at >= k * tokens_here, here, shift)
    return shift


def forward_kernel(info_ref, q_ref, kv_ref, att_ref, qext_ref, top_ref, acc_ref):
    step = pl.program_id(0)
    last = pl.num_programs(0) - 1
    tokens_here = q_ref.shape[0]
    keys_here = kv_ref.shape[1]
    own = info_ref[0]
    zed = info_ref[1]
    block = info_ref[2 + step]

    @pl.when(step == 0)
    def _():
        for h in range(HEADS):
            qext_ref[h * tokens_here : (h + 1) * tokens_here, :128] = cut_heads(q_ref, h).astype(
                BF16
            )
        top_ref[...] = jnp.full(top_ref.shape, MASKED, F32)
        acc_ref[...] = jnp.zeros(acc_ref.shape, F32)

    def attend(masked):
        keys = kv_ref[0, :, :128]
        values = jnp.concatenate(
            [kv_ref[0, :, 128:], jnp.ones((keys_here, 128), BF16)], 1
        )
        if masked:
            row = lax.broadcasted_iota(jnp.int32, (tokens_here, keys_here), 0)
            col = lax.broadcasted_iota(jnp.int32, (tokens_here, keys_here), 1)
            allowed = col + piece_shift(col, zed, tokens_here, keys_here) <= row
        for h in range(HEADS):
            rows = slice(h * tokens_here, (h + 1) * tokens_here)
            scores = times_transposed(qext_ref[rows, :128], keys)
            if masked:
                scores = jnp.where(allowed, scores, MASKED)
            old = top_ref[rows, :]
            top = jnp.maximum(old, jnp.max(scores, -1, keepdims=True))
            probs = jnp.exp(scores - top[:, :1]).astype(BF16)
            shrink = jnp.exp(old - top)
            top_ref[rows, :] = top
            acc_ref[rows, :] = acc_ref[rows, :] * jnp.concatenate([shrink, shrink], 1) + matmul(
                probs, values
            )

    @pl.when(block == own)
    def _():
        attend(True)

    @pl.when(block < own)
    def _():
        attend(False)

    @pl.when(step == last)
    def _():
        lane = lax.broadcasted_iota(jnp.int32, (tokens_here, 128), 1)
        for pair in range(HEADS // 2):
            outs = []
            for h in (2 * pair, 2 * pair + 1):
                rows = slice(h * tokens_here, (h + 1) * tokens_here)
                total = acc_ref[rows, 128:]
                out = acc_ref[rows, :128] / total
                if h // GROUP != h % 2:
                    out = jnp.concatenate([out[:, HEAD:], out[:, :HEAD]], 1)
                outs.append(out)
                log_total = top_ref[rows, :] + jnp.log(total)
                qext_ref[rows, 128:] = split_lanes(-log_total, (tokens_here, 128))
            att_ref[:, pair * 128 : (pair + 1) * 128] = jnp.where(
                lane < HEAD, outs[0], outs[1]
            ).astype(BF16)


def backward_kernel(first, last, info_ref, qext_ref, do_ref, att_ref, kv_ref, *refs):
    if first:
        dkv_ref, doext_ref, dqt_ref = refs[-3:]
        prior_ref = None
    else:
        prior_ref, doext_ref = refs[:2]
        dkv_ref, dqt_ref = refs[-2:]
    if last:
        dq_ref = refs[0] if first else refs[2]
    step = pl.program_id(0)
    end = pl.num_programs(0) - 1
    tokens_here = do_ref.shape[0]
    keys_here = kv_ref.shape[1]
    own = info_ref[0]
    zed = info_ref[1]
    block = info_ref[2 + step]
    span = 2 * tokens_here

    @pl.when(step == 0)
    def _():
        if first:
            for h in range(HEADS):
                rows = slice(h * tokens_here, (h + 1) * tokens_here)
                grad = cut_heads(do_ref, h)
                delta = jnp.sum(grad * cut_heads(att_ref, h), -1, keepdims=True)
                doext_ref[rows, :128] = grad.astype(BF16)
                doext_ref[rows, 128:] = split_lanes(-delta, (tokens_here, 128))
            dqt_ref[...] = jnp.zeros(dqt_ref.shape, F32)
        else:
            dqt_ref[...] = prior_ref[...]

    def attend(masked):
        lane = lax.broadcasted_iota(jnp.int32, (keys_here, 128), 1)
        ones = jnp.where(lane < 3, 1.0, 0.0).astype(BF16)
        keys = kv_ref[0, :, :128]
        keys_ext = jnp.concatenate([keys, ones], 1)
        values_ext = jnp.concatenate([kv_ref[0, :, 128:], ones], 1)
        keys_t = keys.astype(F32).T.astype(BF16)
        if masked:
            row = lax.broadcasted_iota(jnp.int32, (keys_here, tokens_here), 0)
            col = lax.broadcasted_iota(jnp.int32, (keys_here, tokens_here), 1)
            allowed = row + piece_shift(row, zed, tokens_here, keys_here) <= col
            allowed = allowed.astype(F32)
            allowed = jnp.concatenate([allowed, allowed], 1) > 0.5
        dk = jnp.zeros((keys_here, 128), F32)
        dv = jnp.zeros((keys_here, 128), F32)
        for pair in range(HEADS // 2):
            rows = slice(pair * span, (pair + 1) * span)
            probs = jnp.exp(times_transposed(keys_ext, qext_ref[rows, :]))
            if masked:
                probs = jnp.where(allowed, probs, 0.0)
            slope = (probs * times_transposed(values_ext, doext_ref[rows, :])).astype(BF16)
            dv = dv + matmul(probs.astype(BF16), doext_ref[rows, :128])
            dk = dk + matmul(slope, qext_ref[rows, :128])
            dqt_ref[pair] = dqt_ref[pair] + matmul(keys_t, slope)
        dkv_ref[0] = jnp.concatenate([dk, dv], 1).astype(BF16)

    @pl.when(block == own)
    def _():
        attend(True)

    @pl.when(block < own)
    def _():
        attend(False)

    @pl.when(block > own)
    def _():
        dkv_ref[...] = jnp.zeros(dkv_ref.shape, BF16)

    if last:

        @pl.when(step == end)
        def _():
            lane = lax.broadcasted_iota(jnp.int32, (tokens_here, 128), 1)
            for pair in range(HEADS // 2):
                turned = dqt_ref[pair].T
                outs = []
                for j in range(2):
                    h = 2 * pair + j
                    out = turned[j * tokens_here : (j + 1) * tokens_here]
                    if h // GROUP != j:
                        out = jnp.concatenate([out[:, HEAD:], out[:, :HEAD]], 1)
                    outs.append(out)
                dq_ref[:, pair * 128 : (pair + 1) * 128] = (
                    jnp.where(lane < HEAD, outs[0], outs[1]) * HEAD ** (-0.5)
                )


def whole_spec(shape):
    return pl.BlockSpec(shape, lambda i, info: (0,) * len(shape))


def attend_forward(info, queries, kv):
    blocks, block_len, kv_width = kv.shape
    tokens_here, q_width = queries.shape
    rows = HEADS * tokens_here
    return pl.pallas_call(
        forward_kernel,
        grid_spec=pltpu.PrefetchScalarGridSpec(
            num_scalar_prefetch=1,
            grid=(blocks,),
            in_specs=[
                whole_spec((tokens_here, q_width)),
                pl.BlockSpec((1, block_len, kv_width), lambda i, info: (i, 0, 0)),
            ],
            out_specs=[whole_spec((tokens_here, q_width)), whole_spec((rows, 256))],
            scratch_shapes=[pltpu.VMEM((rows, 128), F32), pltpu.VMEM((rows, 256), F32)],
        ),
        out_shape=[
            jax.ShapeDtypeStruct((tokens_here, q_width), BF16),
            jax.ShapeDtypeStruct((rows, 256), BF16),
        ],
        compiler_params=pltpu.CompilerParams(
            dimension_semantics=("arbitrary",), vmem_limit_bytes=40 * 2**20
        ),
        cost_estimate=pl.CostEstimate(
            flops=4 * rows * blocks * block_len * 256,
            bytes_accessed=6 * 2**20,
            transcendentals=rows * blocks * block_len,
        ),
        name="attend_forward",
    )(info, queries, kv)


def attend_backward(info, queries_ext, grad_att, attended, kv, prior, last):
    blocks, block_len, kv_width = kv.shape
    tokens_here, q_width = grad_att.shape
    rows = HEADS * tokens_here
    first = prior is None
    turned = (HEADS // 2, 128, 2 * tokens_here)
    in_specs = [
        whole_spec((rows, 256)),
        whole_spec((tokens_here, q_width)),
        whole_spec((tokens_here, q_width)),
        pl.BlockSpec((1, block_len, kv_width), lambda i, info: (i, 0, 0)),
    ]
    out_specs = [pl.BlockSpec((1, block_len, kv_width), lambda i, info: (i, 0, 0))]
    out_shape = [jax.ShapeDtypeStruct(kv.shape, BF16)]
    scratch = []
    args = [info, queries_ext, grad_att, attended, kv]
    if first:
        if last:
            scratch.append(pltpu.VMEM((rows, 256), BF16))
        else:
            out_specs.append(whole_spec((rows, 256)))
            out_shape.append(jax.ShapeDtypeStruct((rows, 256), BF16))
    else:
        args += [prior[0], prior[1]]
        in_specs += [whole_spec(turned), whole_spec((rows, 256))]
    if last:
        out_specs.insert(0, whole_spec((tokens_here, q_width)))
        out_shape.insert(0, jax.ShapeDtypeStruct((tokens_here, q_width), F32))
        scratch.append(pltpu.VMEM(turned, F32))
    else:
        out_specs.append(whole_spec(turned))
        out_shape.append(jax.ShapeDtypeStruct(turned, F32))
    return pl.pallas_call(
        functools.partial(backward_kernel, first, last),
        grid_spec=pltpu.PrefetchScalarGridSpec(
            num_scalar_prefetch=1,
            grid=(blocks,),
            in_specs=in_specs,
            out_specs=out_specs,
            scratch_shapes=scratch,
        ),
        out_shape=out_shape,
        compiler_params=pltpu.CompilerParams(
            dimension_semantics=("arbitrary",), vmem_limit_bytes=40 * 2**20
        ),
        cost_estimate=pl.CostEstimate(
            flops=10 * rows * blocks * block_len * 256,
            bytes_accessed=8 * 2**20,
            transcendentals=rows * blocks * block_len,
        ),
        name="attend_backward",
    )(*args)


def spread_columns_kernel(n_z, where_ref, *refs):
    pieces, (out_ref, held) = refs[:-2], refs[-2:]
    n_part = len(pieces)
    for r in range(n_part):
        held[where_ref[r]] = pieces[r][...].astype(F32)
    pad = held.shape[2] // n_z
    piece = out_ref.shape[1] // (n_z * n_part)
    cuts = []
    for j in range(n_z):
        for e in range(n_part):
            cuts.append(held[e, :, j * pad : j * pad + piece])
    out_ref[...] = jnp.concatenate(cuts, 1)


def spread_columns(where_at, pieces, n_z, ff):
    rows, cols = pieces[0].shape
    tile = 32
    n_part = len(pieces)
    return pl.pallas_call(
        functools.partial(spread_columns_kernel, n_z),
        grid_spec=pltpu.PrefetchScalarGridSpec(
            num_scalar_prefetch=1,
            grid=(rows // tile,),
            in_specs=[pl.BlockSpec((tile, cols), lambda i, w: (i, 0))] * n_part,
            out_specs=pl.BlockSpec((tile, ff), lambda i, w: (i, 0)),
            scratch_shapes=[pltpu.VMEM((n_part, tile, cols), F32)],
        ),
        out_shape=jax.ShapeDtypeStruct((rows, ff), F32),
        compiler_params=pltpu.CompilerParams(
            dimension_semantics=("arbitrary",), vmem_limit_bytes=40 * 2**20
        ),
        cost_estimate=pl.CostEstimate(
            flops=0, bytes_accessed=rows * ff * 6, transcendentals=0
        ),
        name="spread_columns",
    )(where_at, *pieces)


def spread_rows_kernel(piece, where_ref, *refs):
    pieces, out_ref = refs[:-1], refs[-1]
    room = out_ref.shape[0] // piece
    for r in range(len(pieces)):

        @pl.when(where_ref[r] < room)
        def _():
            start = pl.multiple_of(where_ref[r] * piece, 8)
            out_ref[pl.ds(start, piece), :] = pieces[r][...].astype(F32)[:piece]


def spread_rows(where_at, pieces, piece, rows_out):
    rows, cols = pieces[0].shape
    tile = 128
    return pl.pallas_call(
        functools.partial(spread_rows_kernel, piece),
        grid_spec=pltpu.PrefetchScalarGridSpec(
            num_scalar_prefetch=1,
            grid=(cols // tile,),
            in_specs=[pl.BlockSpec((rows, tile), lambda i, w: (0, i))] * len(pieces),
            out_specs=pl.BlockSpec((rows_out, tile), lambda i, w: (0, i)),
        ),
        out_shape=jax.ShapeDtypeStruct((rows_out, cols), F32),
        compiler_params=pltpu.CompilerParams(
            dimension_semantics=("arbitrary",), vmem_limit_bytes=40 * 2**20
        ),
        cost_estimate=pl.CostEstimate(
            flops=0, bytes_accessed=rows_out * cols * 6, transcendentals=0
        ),
        name="spread_rows",
    )(where_at, *pieces)


def join_weight_kernel(where_ref, *refs):
    pieces, out_ref = refs[:-1], refs[-1]
    n_part = len(pieces)
    n_z, part_rows = pieces[0].shape[:2]
    room = out_ref.shape[1] // part_rows
    for r in range(n_part):

        @pl.when(where_ref[r] < room)
        def _():
            start = pl.multiple_of(where_ref[r] * part_rows, 16)
            for k in range(n_z):
                out_ref[where_ref[n_part + k], pl.ds(start, part_rows), :] = pieces[r][k]


def join_weight(where_at, pieces, rows_here):
    n_z, part_rows, cols = pieces[0].shape
    return pl.pallas_call(
        join_weight_kernel,
        grid_spec=pltpu.PrefetchScalarGridSpec(
            num_scalar_prefetch=1,
            grid=(1,),
            in_specs=[pl.BlockSpec(p.shape, lambda i, w: (0, 0, 0)) for p in pieces],
            out_specs=pl.BlockSpec((n_z, rows_here, cols), lambda i, w: (0, 0, 0)),
        ),
        out_shape=jax.ShapeDtypeStruct((n_z, rows_here, cols), BF16),
        compiler_params=pltpu.CompilerParams(
            dimension_semantics=("arbitrary",), vmem_limit_bytes=40 * 2**20
        ),
        cost_estimate=pl.CostEstimate(
            flops=0, bytes_accessed=4 * n_z * rows_here * cols, transcendentals=0
        ),
        name="join_weight",
    )(where_at, *pieces).reshape(n_z * rows_here, cols)


def local(
    tokens,
    out_grad,
    block_order,
    norm1_gain,
    q_weight,
    q_bias,
    k_weight,
    k_bias,
    v_weight,
    v_bias,
    o_weight,
    norm2_gain,
    gate_weight,
    up_weight,
    down_weight,
):
    n_ctx = lax.axis_size("ctx")
    n_z = lax.axis_size("fsdp")
    tp = 4 if n_ctx % 4 == 0 else (2 if n_ctx % 2 == 0 else 1)
    here = lax.axis_index("ctx")
    zed = lax.axis_index("fsdp")
    core = lax.axis_index("seq")
    n_part = 2 * tp
    part = lax.rem(here, tp) * 2 + core

    def swap(v):
        return lax.ppermute(v, "seq", [(0, 1), (1, 0)])

    def hop(v, k):
        if k == 0:
            return v
        return lax.ppermute(v, "ctx", [(i, i ^ k) for i in range(n_ctx)])

    def hop_z(v, k):
        if k == 0:
            return v
        return lax.ppermute(v, "fsdp", [(i, i ^ k) for i in range(n_z)])

    def gather_z(v):
        return lax.all_gather(v, "fsdp", axis=0, tiled=True)

    def scatter_z(v):
        return lax.psum_scatter(v, "fsdp", scatter_dimension=0, tiled=True)

    tokens_here, width = tokens.shape[1:]
    ff = gate_weight.shape[1]
    rows_here = q_weight.shape[0]
    key_width = KV_HEADS * HEAD
    block_len = tokens_here * n_z

    idx = jnp.arange(n_part, dtype=jnp.int32)
    where_at = ((idx // 2) ^ lax.rem(here, tp)) * 2 + ((idx % 2) ^ core)
    where_z = jnp.arange(n_z, dtype=jnp.int32) ^ zed
    part_rows = -(-rows_here // (n_part * 32)) * 32

    kb = k_bias.shape[0]
    vec = jnp.concatenate([norm1_gain, norm2_gain, q_bias, k_bias, v_bias])
    vec_rows = -(-vec.shape[0] // (16 * 2 * key_width)) * 16
    vec = jnp.pad(vec, (0, vec_rows * 2 * key_width - vec.shape[0])).reshape(vec_rows, -1)
    kv_pack = jnp.concatenate([jnp.concatenate([k_weight, v_weight], 1), vec], 0)
    kv_pack, q_weight, o_weight, gate_weight, up_weight, down_weight = lax.optimization_barrier(
        (kv_pack, q_weight, o_weight, gate_weight, up_weight, down_weight)
    )
    kv_got = jnp.stack([hop_z(kv_pack, k) for k in range(n_z)])
    kv_got = jnp.take(kv_got, where_z, axis=0)
    w_kv = kv_got[:, :rows_here].reshape(width, 2 * key_width)
    vecs = kv_got[:, rows_here:].reshape(n_z, -1)
    gain_one = vecs[:, :rows_here].reshape(-1)
    gain_two = vecs[:, rows_here : 2 * rows_here].reshape(-1)
    b_query = vecs[:, 2 * rows_here : 3 * rows_here].reshape(-1)
    b_key = vecs[:, 3 * rows_here : 3 * rows_here + kb].reshape(-1)
    b_value = vecs[:, 3 * rows_here + kb : 3 * rows_here + 2 * kb].reshape(-1)

    def gather_shared(w):
        mine = lax.dynamic_slice_in_dim(w, part * part_rows, part_rows, 0)
        mine = jnp.stack([hop_z(mine, k) for k in range(n_z)])
        pieces = []
        for k in range(tp):
            pieces.append(hop(mine, k))
            pieces.append(swap(pieces[-1]))
        return join_weight(jnp.concatenate([where_at, where_z]), pieces, rows_here)

    w_query = gather_shared(q_weight)
    w_out = gather_shared(o_weight)

    ff_z = ff // n_z
    piece = ff_z // n_part
    piece_pad = -(-piece // 32) * 32
    ff_half = n_z * piece_pad

    def ff_columns(w):
        cuts = []
        for j in range(n_z):
            cut = lax.dynamic_slice_in_dim(w, j * ff_z + part * piece, piece, 1)
            cuts.append(jnp.pad(cut, ((0, 0), (0, piece_pad - piece))))
        return jnp.concatenate(cuts, 1)

    gu_own = gather_z(jnp.concatenate([ff_columns(gate_weight), ff_columns(up_weight)], 1))
    gu_oth = swap(gu_own)
    down_cut = lax.dynamic_slice_in_dim(down_weight, part * piece, piece, 0)
    down_own = gather_z(jnp.pad(down_cut, ((0, piece_pad - piece), (0, 0))))
    down_oth = swap(down_own)
    og_here = out_grad[0]
    og_all = jnp.concatenate([hop(og_here, k) for k in range(tp)], 0)

    order_row = block_order[0]
    query_pos = (
        order_row[here] * block_len
        + zed * tokens_here
        + jnp.arange(tokens_here, dtype=jnp.int32)
    )
    if n_ctx == tp:
        block_at = jnp.stack([order_row[here ^ k] for k in range(n_ctx)])
    else:
        block_at = order_row
    info = jnp.concatenate([jnp.stack([order_row[here], zed]).astype(jnp.int32), block_at])
    cosine_table, sine_table = rope_tables(query_pos, HEAD)

    inputs = tokens[0].astype(F32)
    normed_one, scale_one, hidden_one = rms_forward(inputs, gain_one)
    key_value = matmul(hidden_one, w_kv)
    key_pre = key_value[:, :key_width] + b_key
    value_pre = key_value[:, key_width:] + b_value
    query_pre = matmul(hidden_one, w_query) + b_query
    queries = rotate(query_pre.reshape(tokens_here, HEADS, HEAD), cosine_table, sine_table)
    queries = queries.astype(BF16).reshape(tokens_here, HEADS * HEAD) * BF16(HEAD ** (-0.5))
    key_rot = rotate(key_pre.reshape(tokens_here, KV_HEADS, HEAD), cosine_table, sine_table)
    kv_local = jnp.concatenate(
        [key_rot.astype(BF16).reshape(tokens_here, key_width), value_pre.astype(BF16)], 1
    )
    kv_block = jnp.concatenate([hop_z(kv_local, k) for k in range(n_z)], 0)
    if n_ctx == tp:
        kv_blocks = [hop(kv_block, k) for k in range(n_ctx)]
        kv_whole = jnp.stack(kv_blocks)
    else:
        kv_whole = lax.all_gather(kv_block, "ctx", axis=0, tiled=False)
    attended, queries_ext = attend_forward(info, queries, kv_whole)
    resid = inputs + matmul(attended, w_out)
    normed_two, scale_two, hidden_two = rms_forward(resid, gain_two)

    h2_all = jnp.concatenate([hop(hidden_two, k) for k in range(tp)], 0)

    def scatter_plane(v):
        parts = v.astype(BF16).reshape(tp, tokens_here, width)
        return [hop(parts[k], k) for k in range(tp)]

    def ff_half_pass(w_gu, w_d):
        gu = matmul(h2_all, w_gu)
        gate = gu[:, :ff_half]
        up = gu[:, ff_half:]
        sig = jax.nn.sigmoid(gate)
        silu = gate * sig
        act = (silu * up).astype(BF16)
        grad_act = times_transposed(og_all, w_d)
        grad_gate = (grad_act * up * sig * (1.0 + gate * (1.0 - sig))).astype(BF16)
        grad_up = (grad_act * silu).astype(BF16)
        return act, grad_gate, grad_up

    act_own, gg_own, gup_own = ff_half_pass(gu_own, down_own)
    act_oth, gg_oth, gup_oth = ff_half_pass(gu_oth, down_oth)
    grad_h2_parts = scatter_plane(
        times_transposed(jnp.concatenate([gg_own, gup_own], 1), gu_own)
        + times_transposed(jnp.concatenate([gg_oth, gup_oth], 1), gu_oth)
    )
    ff_out = scatter_plane(matmul(act_own, down_own) + matmul(act_oth, down_oth))
    result = resid + sum(v.astype(F32) for v in ff_out)
    layer_out = result.astype(BF16)[None]

    def reduce_start(part_sum):
        cols = part_sum.shape[1]
        cut = part_sum.astype(BF16).reshape(n_z, rows_here, cols)
        cut = jnp.pad(cut, ((0, 0), (0, n_part * part_rows - rows_here), (0, 0)))
        cut = cut.reshape(n_z, tp, 2, part_rows, cols)
        own = lax.dynamic_index_in_dim(cut, core, 2, keepdims=False)
        oth = lax.dynamic_index_in_dim(cut, 1 - core, 2, keepdims=False)
        return (own.astype(F32) + swap(oth).astype(F32)).astype(BF16)

    def reduce_end(cut):
        cols = cut.shape[-1]
        total = 0.0
        for k in range(tp):
            at = lax.rem(here, tp) ^ k
            total = total + hop(lax.dynamic_index_in_dim(cut, at, 1, keepdims=False), k).astype(F32)
        cut = total.astype(BF16)
        total = 0.0
        for k in range(n_z):
            total = total + hop_z(
                lax.dynamic_index_in_dim(cut, zed ^ k, 0, keepdims=False), k
            ).astype(F32)
        total = ctx_groups_sum(total.astype(BF16))
        total = lax.optimization_barrier(total)
        pieces = []
        for k in range(tp):
            pieces.append(hop(total, k))
            pieces.append(swap(pieces[-1]))
        return spread_rows(where_at, pieces, part_rows, rows_here)

    def ctx_groups_sum(v):
        if n_ctx == tp:
            return v
        groups = [[g * tp + c for g in range(n_ctx // tp)] for c in range(tp)]
        return lax.psum(v, "ctx", axis_index_groups=groups)

    def core_sum(own, oth):
        return (own + swap(oth.astype(BF16)).astype(F32)).astype(BF16)

    def ff_pieces(mine):
        mine = ctx_groups_sum(mine)
        pieces = []
        for k in range(tp):
            pieces.append(hop(mine, k))
            pieces.append(swap(pieces[-1]))
        return pieces

    d_down = core_sum(contract_rows(act_own, og_all), contract_rows(act_oth, og_all))
    d_gate = core_sum(contract_rows(h2_all, gg_own), contract_rows(h2_all, gg_oth))
    d_up = core_sum(contract_rows(h2_all, gup_own), contract_rows(h2_all, gup_oth))
    grad_h2_parts, d_down, d_gate, d_up = lax.optimization_barrier(
        (grad_h2_parts, d_down, d_gate, d_up)
    )
    d_down = scatter_z(d_down)
    d_gate = scatter_z(d_gate)
    d_up = scatter_z(d_up)
    grad_h2 = sum(v.astype(F32) for v in grad_h2_parts)

    grad_norm_two, grad_gain_two = rms_backward(grad_h2, normed_two, scale_two, gain_two)
    grad_resid = og_here.astype(F32) + grad_norm_two
    grad_proj = grad_resid.astype(BF16)
    grad_att = times_transposed(grad_proj, w_out).astype(BF16)
    if n_ctx == tp:
        state = None
        sent = [None] * n_ctx
        for k in list(range(1, n_ctx)) + [0]:
            block_info = jnp.concatenate([info[:2], info[2 + k : 3 + k]])
            got = attend_backward(
                block_info, queries_ext, grad_att, attended, kv_blocks[k][None], state, k == 0
            )
            if k == 0:
                grad_queries, sent[0] = got
            elif state is None:
                sent[k], ext, turned = got
            else:
                sent[k], turned = got
            state = (turned, ext)
        kv_sum = sum(hop(sent[k][0], k).astype(F32) for k in range(n_ctx)).astype(BF16)
    else:
        grad_queries, grad_terms = attend_backward(
            info, queries_ext, grad_att, attended, kv_whole, None, True
        )
        kv_sum = lax.psum_scatter(grad_terms, "ctx", scatter_dimension=0, tiled=False)
    kv_sum = kv_sum.reshape(n_z, tokens_here, 2 * key_width)
    grad_kv = kv_sum[0].astype(F32)
    for k in range(1, n_z):
        grad_kv = grad_kv + hop_z(kv_sum[k], k).astype(F32)

    grad_q_pre = (
        rotate(grad_queries.reshape(tokens_here, HEADS, HEAD), cosine_table, -sine_table)
        .reshape(tokens_here, HEADS * HEAD)
        .astype(BF16)
    )
    grad_k_pre = (
        rotate(
            grad_kv[:, :key_width].reshape(tokens_here, KV_HEADS, HEAD), cosine_table, -sine_table
        )
        .reshape(tokens_here, key_width)
        .astype(BF16)
    )
    grad_v_pre = grad_kv[:, key_width:].astype(BF16)

    grad_kv_pre = jnp.concatenate([grad_k_pre, grad_v_pre], 1)
    grad_hidden_one = times_transposed(grad_q_pre, w_query) + times_transposed(grad_kv_pre, w_kv)
    grad_norm_one, grad_gain_one = rms_backward(grad_hidden_one, normed_one, scale_one, gain_one)
    tokens_grad = (grad_resid + grad_norm_one)[None]

    def by_rows(v):
        share = v.shape[0] // n_z
        return jnp.pad(v.reshape(n_z, share), ((0, 0), (0, rows_here - share))).reshape(width)

    columns = jnp.stack(
        [
            grad_gain_one,
            grad_gain_two,
            jnp.sum(grad_q_pre.astype(F32), 0),
            by_rows(jnp.sum(grad_k_pre.astype(F32), 0)),
            by_rows(jnp.sum(grad_v_pre.astype(F32), 0)),
        ],
        1,
    )
    grad_w_query = reduce_end(reduce_start(contract_rows(hidden_one, grad_q_pre)))
    grad_w_kv = jnp.concatenate(
        [
            contract_rows(hidden_one, grad_kv_pre),
            jnp.pad(columns, ((0, 0), (0, 128 - columns.shape[1]))),
        ],
        1,
    )
    grad_w_kv = reduce_end(reduce_start(grad_w_kv))
    sums = grad_w_kv[:, 2 * key_width :]
    grad_w_out = reduce_end(reduce_start(contract_rows(attended, grad_proj)))
    grad_w_down = spread_rows(where_at, ff_pieces(d_down), piece, ff_z)
    grad_w_gate = spread_columns(where_at, ff_pieces(d_gate), n_z, ff)
    grad_w_up = spread_columns(where_at, ff_pieces(d_up), n_z, ff)

    return (
        layer_out,
        tokens_grad,
        sums[:, 0],
        grad_w_query,
        sums[:, 2],
        grad_w_kv[:, :key_width],
        sums[:kb, 3],
        grad_w_kv[:, key_width : 2 * key_width],
        sums[:kb, 4],
        grad_w_out,
        sums[:, 1],
        grad_w_gate,
        grad_w_up,
        grad_w_down,
    )


def solution(mesh):
    in_specs = (
        P("seq", ("ctx", "fsdp"), None),
        P("seq", ("ctx", "fsdp"), None),
        P("seq", None),
        P("fsdp"),
        P("fsdp", None),
        P("fsdp"),
        P("fsdp", None),
        P("fsdp"),
        P("fsdp", None),
        P("fsdp"),
        P("fsdp", None),
        P("fsdp"),
        P("fsdp", None),
        P("fsdp", None),
        P("fsdp", None),
    )
    out_specs = (
        P("seq", ("ctx", "fsdp"), None),
        P("seq", ("ctx", "fsdp"), None),
        P("fsdp"),
        P("fsdp", None),
        P("fsdp"),
        P("fsdp", None),
        P("fsdp"),
        P("fsdp", None),
        P("fsdp"),
        P("fsdp", None),
        P("fsdp"),
        P("fsdp", None),
        P("fsdp", None),
        P("fsdp", None),
    )
    return jax.shard_map(local, mesh=mesh, in_specs=in_specs, out_specs=out_specs, check_vma=False)
```

```python
import functools
import math

import jax
import jax.numpy as jnp
from jax import lax
from jax.experimental import pallas as pl
from jax.experimental.pallas import tpu as pltpu
from jax.sharding import PartitionSpec as P

HEADS = 14
KV_HEADS = 2
HEAD = 64
GROUP = HEADS // KV_HEADS
NORM_EPS = 1e-06
ROPE_BASE = 1000000.0
MASKED = -1e30
BF16 = jnp.bfloat16
F32 = jnp.float32


def rope_tables(positions, head_dim):
    half_dim = head_dim // 2
    inverse = jnp.exp(
        jnp.arange(half_dim, dtype=jnp.float32) * (-math.log(ROPE_BASE) * 2.0 / head_dim)
    )
    angles = positions.astype(jnp.float32)[:, None] * inverse[None, :]
    return (jnp.cos(angles)[:, None, :], jnp.sin(angles)[:, None, :])


def rotate(values, cosine_table, sine_table):
    half_dim = values.shape[-1] // 2
    front_half = values[..., :half_dim]
    back_half = values[..., half_dim:]
    return jnp.concatenate(
        [
            front_half * cosine_table - back_half * sine_table,
            back_half * cosine_table + front_half * sine_table,
        ],
        -1,
    )


def matmul(left_side, right_side):
    return jnp.dot(left_side, right_side, preferred_element_type=F32)


def contract_rows(left_side, right_side):
    return lax.dot_general(
        left_side, right_side, (((0,), (0,)), ((), ())), preferred_element_type=F32
    )


def times_transposed(left_side, right_side):
    return lax.dot_general(
        left_side, right_side, (((1,), (1,)), ((), ())), preferred_element_type=F32
    )


def rms_forward(values, gain_vec):
    inv_scale = lax.rsqrt(jnp.mean(values * values, -1, keepdims=True) + NORM_EPS)
    normed = values * inv_scale
    return (normed, inv_scale, (normed * gain_vec).astype(BF16))


def rms_backward(grad_out, normed, inv_scale, gain_vec):
    scaled = grad_out * gain_vec
    grad_in = inv_scale * (scaled - normed * jnp.mean(scaled * normed, -1, keepdims=True))
    return (grad_in, grad_out * normed)


def cut_heads(ref, head):
    tile = ref[:, (head // 2) * 128 : (head // 2 + 1) * 128].astype(F32)
    group = head // GROUP
    if head % 2 != group:
        tile = jnp.concatenate([tile[:, HEAD:], tile[:, :HEAD]], 1)
    lane = lax.broadcasted_iota(jnp.int32, tile.shape, 1)
    return jnp.where((lane >= HEAD) if group else (lane < HEAD), tile, 0.0)


def split_lanes(column, shape):
    high = column.astype(BF16).astype(F32)
    mid = (column - high).astype(BF16).astype(F32)
    low = column - high - mid
    lane = lax.broadcasted_iota(jnp.int32, shape, 1)
    return jnp.where(
        lane == 0, high, jnp.where(lane == 1, mid, jnp.where(lane == 2, low, 0.0))
    ).astype(BF16)


def piece_shift(at, zed, tokens_here, keys_here):
    pieces = keys_here // tokens_here
    shift = jnp.zeros(at.shape, jnp.int32)
    for k in range(pieces):
        here = (jnp.bitwise_xor(zed, k) - k - zed) * tokens_here
        shift = jnp.where(at >= k * tokens_here, here, shift)
    return shift


def forward_kernel(by_xor, info_ref, q_ref, kv_ref, att_ref, qext_ref, top_ref, acc_ref):
    step = pl.program_id(0)
    last = pl.num_programs(0) - 1
    tokens_here = q_ref.shape[0]
    keys_here = kv_ref.shape[1]
    here = lax.axis_index("ctx")
    zed = lax.axis_index("fsdp")
    own = info_ref[here]
    block = info_ref[jnp.bitwise_xor(here, step) if by_xor else step]

    @pl.when(step == 0)
    def _():
        for h in range(HEADS):
            qext_ref[h * tokens_here : (h + 1) * tokens_here, :128] = cut_heads(q_ref, h).astype(
                BF16
            )
        top_ref[...] = jnp.full(top_ref.shape, MASKED, F32)
        acc_ref[...] = jnp.zeros(acc_ref.shape, F32)

    def attend(masked):
        keys = kv_ref[0, :, :128]
        values = jnp.concatenate(
            [kv_ref[0, :, 128:], jnp.ones((keys_here, 128), BF16)], 1
        )
        if masked:
            row = lax.broadcasted_iota(jnp.int32, (tokens_here, keys_here), 0)
            col = lax.broadcasted_iota(jnp.int32, (tokens_here, keys_here), 1)
            allowed = col + piece_shift(col, zed, tokens_here, keys_here) <= row
        for h in range(HEADS):
            rows = slice(h * tokens_here, (h + 1) * tokens_here)
            scores = times_transposed(qext_ref[rows, :128], keys)
            if masked:
                scores = jnp.where(allowed, scores, MASKED)
            old = top_ref[rows, :]
            top = jnp.maximum(old, jnp.max(scores, -1, keepdims=True))
            probs = jnp.exp(scores - top[:, :1]).astype(BF16)
            shrink = jnp.exp(old - top)
            top_ref[rows, :] = top
            acc_ref[rows, :] = acc_ref[rows, :] * jnp.concatenate([shrink, shrink], 1) + matmul(
                probs, values
            )

    @pl.when(block == own)
    def _():
        attend(True)

    @pl.when(block < own)
    def _():
        attend(False)

    @pl.when(step == last)
    def _():
        lane = lax.broadcasted_iota(jnp.int32, (tokens_here, 128), 1)
        for pair in range(HEADS // 2):
            outs = []
            for h in (2 * pair, 2 * pair + 1):
                rows = slice(h * tokens_here, (h + 1) * tokens_here)
                total = acc_ref[rows, 128:]
                out = acc_ref[rows, :128] / total
                if h // GROUP != h % 2:
                    out = jnp.concatenate([out[:, HEAD:], out[:, :HEAD]], 1)
                outs.append(out)
                log_total = top_ref[rows, :] + jnp.log(total)
                qext_ref[rows, 128:] = split_lanes(-log_total, (tokens_here, 128))
            att_ref[:, pair * 128 : (pair + 1) * 128] = jnp.where(
                lane < HEAD, outs[0], outs[1]
            ).astype(BF16)


def backward_kernel(
    by_xor, info_ref, qext_ref, do_ref, att_ref, kv_ref, dq_ref, dkv_ref, doext_ref, dqt_ref
):
    step = pl.program_id(0)
    last = pl.num_programs(0) - 1
    tokens_here = do_ref.shape[0]
    keys_here = kv_ref.shape[1]
    here = lax.axis_index("ctx")
    zed = lax.axis_index("fsdp")
    own = info_ref[here]
    block = info_ref[jnp.bitwise_xor(here, step) if by_xor else step]
    span = 2 * tokens_here

    @pl.when(step == 0)
    def _():
        for h in range(HEADS):
            rows = slice(h * tokens_here, (h + 1) * tokens_here)
            grad = cut_heads(do_ref, h)
            delta = jnp.sum(grad * cut_heads(att_ref, h), -1, keepdims=True)
            doext_ref[rows, :128] = grad.astype(BF16)
            doext_ref[rows, 128:] = split_lanes(-delta, (tokens_here, 128))
        dqt_ref[...] = jnp.zeros(dqt_ref.shape, F32)

    def attend(masked):
        lane = lax.broadcasted_iota(jnp.int32, (keys_here, 128), 1)
        ones = jnp.where(lane < 3, 1.0, 0.0).astype(BF16)
        keys = kv_ref[0, :, :128]
        keys_ext = jnp.concatenate([keys, ones], 1)
        values_ext = jnp.concatenate([kv_ref[0, :, 128:], ones], 1)
        keys_t = keys.astype(F32).T.astype(BF16)
        if masked:
            row = lax.broadcasted_iota(jnp.int32, (keys_here, tokens_here), 0)
            col = lax.broadcasted_iota(jnp.int32, (keys_here, tokens_here), 1)
            allowed = row + piece_shift(row, zed, tokens_here, keys_here) <= col
            allowed = allowed.astype(F32)
            allowed = jnp.concatenate([allowed, allowed], 1) > 0.5
        dk = jnp.zeros((keys_here, 128), F32)
        dv = jnp.zeros((keys_here, 128), F32)
        for pair in range(HEADS // 2):
            rows = slice(pair * span, (pair + 1) * span)
            probs = jnp.exp(times_transposed(keys_ext, qext_ref[rows, :]))
            if masked:
                probs = jnp.where(allowed, probs, 0.0)
            slope = (probs * times_transposed(values_ext, doext_ref[rows, :])).astype(BF16)
            dv = dv + matmul(probs.astype(BF16), doext_ref[rows, :128])
            dk = dk + matmul(slope, qext_ref[rows, :128])
            dqt_ref[pair] = dqt_ref[pair] + matmul(keys_t, slope)
        dkv_ref[0] = jnp.concatenate([dk, dv], 1).astype(BF16)

    @pl.when(block == own)
    def _():
        attend(True)

    @pl.when(block < own)
    def _():
        attend(False)

    @pl.when(block > own)
    def _():
        dkv_ref[...] = jnp.zeros(dkv_ref.shape, BF16)

    @pl.when(step == last)
    def _():
        lane = lax.broadcasted_iota(jnp.int32, (tokens_here, 128), 1)
        for pair in range(HEADS // 2):
            turned = dqt_ref[pair].T
            outs = []
            for j in range(2):
                h = 2 * pair + j
                out = turned[j * tokens_here : (j + 1) * tokens_here]
                if h // GROUP != j:
                    out = jnp.concatenate([out[:, HEAD:], out[:, :HEAD]], 1)
                outs.append(out)
            dq_ref[:, pair * 128 : (pair + 1) * 128] = (
                jnp.where(lane < HEAD, outs[0], outs[1]) * HEAD ** (-0.5)
            )


def whole_spec(shape):
    return pl.BlockSpec(shape, lambda i, info: (0,) * len(shape))


def attend_forward(info, by_xor, queries, kv):
    blocks, block_len, kv_width = kv.shape
    tokens_here, q_width = queries.shape
    rows = HEADS * tokens_here
    return pl.pallas_call(
        functools.partial(forward_kernel, by_xor),
        grid_spec=pltpu.PrefetchScalarGridSpec(
            num_scalar_prefetch=1,
            grid=(blocks,),
            in_specs=[
                whole_spec((tokens_here, q_width)),
                pl.BlockSpec((1, block_len, kv_width), lambda i, info: (i, 0, 0)),
            ],
            out_specs=[whole_spec((tokens_here, q_width)), whole_spec((rows, 256))],
            scratch_shapes=[pltpu.VMEM((rows, 128), F32), pltpu.VMEM((rows, 256), F32)],
        ),
        out_shape=[
            jax.ShapeDtypeStruct((tokens_here, q_width), BF16),
            jax.ShapeDtypeStruct((rows, 256), BF16),
        ],
        compiler_params=pltpu.CompilerParams(
            dimension_semantics=("arbitrary",), vmem_limit_bytes=40 * 2**20
        ),
        cost_estimate=pl.CostEstimate(
            flops=4 * rows * blocks * block_len * 256,
            bytes_accessed=6 * 2**20,
            transcendentals=rows * blocks * block_len,
        ),
        name="attend_forward",
    )(info, queries, kv)


def attend_backward(info, by_xor, queries_ext, grad_att, attended, kv):
    blocks, block_len, kv_width = kv.shape
    tokens_here, q_width = grad_att.shape
    rows = HEADS * tokens_here
    return pl.pallas_call(
        functools.partial(backward_kernel, by_xor),
        grid_spec=pltpu.PrefetchScalarGridSpec(
            num_scalar_prefetch=1,
            grid=(blocks,),
            in_specs=[
                whole_spec((rows, 256)),
                whole_spec((tokens_here, q_width)),
                whole_spec((tokens_here, q_width)),
                pl.BlockSpec((1, block_len, kv_width), lambda i, info: (i, 0, 0)),
            ],
            out_specs=[
                whole_spec((tokens_here, q_width)),
                pl.BlockSpec((1, block_len, kv_width), lambda i, info: (i, 0, 0)),
            ],
            scratch_shapes=[
                pltpu.VMEM((rows, 256), BF16),
                pltpu.VMEM((HEADS // 2, 128, 2 * tokens_here), F32),
            ],
        ),
        out_shape=[
            jax.ShapeDtypeStruct((tokens_here, q_width), F32),
            jax.ShapeDtypeStruct(kv.shape, BF16),
        ],
        compiler_params=pltpu.CompilerParams(
            dimension_semantics=("arbitrary",), vmem_limit_bytes=40 * 2**20
        ),
        cost_estimate=pl.CostEstimate(
            flops=10 * rows * blocks * block_len * 256,
            bytes_accessed=8 * 2**20,
            transcendentals=rows * blocks * block_len,
        ),
        name="attend_backward",
    )(info, queries_ext, grad_att, attended, kv)


def part_place(tp, j, k):
    at = jnp.bitwise_xor(lax.rem(lax.axis_index("ctx"), tp), k)
    return jnp.bitwise_xor(lax.axis_index("seq"), j) * tp + at


def spread_columns_kernel(n_z, *refs):
    pieces, outs, held = refs[:2], refs[2:-1], refs[-1]
    tp = pieces[0].shape[0]
    n_part = 2 * tp
    for j in range(2):
        for k in range(tp):
            held[part_place(tp, j, k)] = pieces[j][k].astype(F32)
    half = held.shape[2] // len(outs)
    pad = half // n_z
    for i, out in enumerate(outs):
        piece = out.shape[1] // (n_z * n_part)
        cuts = []
        for j in range(n_z):
            for e in range(n_part):
                start = i * half + j * pad
                cuts.append(held[e, :, start : start + piece])
        out[...] = jnp.concatenate(cuts, 1)


def spread_columns(pieces, n_z, ff, outs):
    tp, rows, cols = pieces[0].shape
    tile = 32
    return pl.pallas_call(
        functools.partial(spread_columns_kernel, n_z),
        grid=(rows // tile,),
        in_specs=[pl.BlockSpec((tp, tile, cols), lambda i: (0, i, 0))] * 2,
        out_specs=[pl.BlockSpec((tile, ff), lambda i: (i, 0))] * outs,
        scratch_shapes=[pltpu.VMEM((2 * tp, tile, cols), F32)],
        out_shape=[jax.ShapeDtypeStruct((rows, ff), F32)] * outs,
        compiler_params=pltpu.CompilerParams(
            dimension_semantics=("arbitrary",), vmem_limit_bytes=40 * 2**20
        ),
        cost_estimate=pl.CostEstimate(
            flops=0, bytes_accessed=rows * ff * 6 * outs, transcendentals=0
        ),
        name="spread_columns",
    )(*pieces)


def spread_rows_kernel(piece, *refs):
    pieces, out_ref = refs[:-1], refs[-1]
    room = out_ref.shape[0] // piece
    tp = pieces[0].shape[0]
    for j in range(2):
        for k in range(tp):
            place = part_place(tp, j, k)

            @pl.when(place < room)
            def _():
                start = pl.multiple_of(place * piece, 8)
                out_ref[pl.ds(start, piece), :] = pieces[j][k].astype(F32)[:piece]


def spread_rows(pieces, piece, rows_out):
    tp, rows, cols = pieces[0].shape
    tile = 128
    return pl.pallas_call(
        functools.partial(spread_rows_kernel, piece),
        grid=(cols // tile,),
        in_specs=[pl.BlockSpec((tp, rows, tile), lambda i: (0, 0, i))] * 2,
        out_specs=pl.BlockSpec((rows_out, tile), lambda i: (0, i)),
        out_shape=jax.ShapeDtypeStruct((rows_out, cols), F32),
        compiler_params=pltpu.CompilerParams(
            dimension_semantics=("arbitrary",), vmem_limit_bytes=40 * 2**20
        ),
        cost_estimate=pl.CostEstimate(
            flops=0, bytes_accessed=rows_out * cols * 6, transcendentals=0
        ),
        name="spread_rows",
    )(*pieces)


def join_weight_kernel(own_ref, sib_ref, out_ref):
    tp, n_z, part_rows = own_ref.shape[:3]
    room = out_ref.shape[1] // part_rows
    for j, ref in enumerate((own_ref, sib_ref)):
        for k in range(tp):
            place = part_place(tp, j, k)

            @pl.when(place < room)
            def _():
                start = pl.multiple_of(place * part_rows, 16)
                for z in range(n_z):
                    at = jnp.bitwise_xor(lax.axis_index("fsdp"), z)
                    out_ref[at, pl.ds(start, part_rows), :] = ref[k, z]


def join_weight(own, sib, rows_here):
    tp, n_z, part_rows, cols = own.shape
    return pl.pallas_call(
        join_weight_kernel,
        in_specs=[pl.BlockSpec(memory_space=pltpu.VMEM)] * 2,
        out_specs=pl.BlockSpec(memory_space=pltpu.VMEM),
        out_shape=jax.ShapeDtypeStruct((n_z, rows_here, cols), BF16),
        compiler_params=pltpu.CompilerParams(vmem_limit_bytes=40 * 2**20),
        cost_estimate=pl.CostEstimate(
            flops=0, bytes_accessed=4 * n_z * rows_here * cols, transcendentals=0
        ),
        name="join_weight",
    )(own, sib).reshape(n_z * rows_here, cols)


def join_kv_kernel(widths, *refs):
    pieces, (out_ref, vec_ref, held) = refs[:-3], refs[-3:]
    n_z, rows_here, cols = out_ref.shape
    for k in range(n_z):
        at = jnp.bitwise_xor(lax.axis_index("fsdp"), k)
        out_ref[at] = pieces[k][:rows_here]
        held[at] = pieces[k][rows_here:].astype(F32)
    vec_ref[...] = jnp.zeros(vec_ref.shape, F32)
    for i, size in enumerate(widths):
        row = jnp.concatenate([held[z, i : i + 1, :size] for z in range(n_z)], 1)
        vec_ref[i : i + 1, : n_z * size] = row


def join_kv(pieces, rows_here, widths):
    rows, cols = pieces[0].shape
    n_z = len(pieces)
    return pl.pallas_call(
        functools.partial(join_kv_kernel, widths),
        in_specs=[pl.BlockSpec(memory_space=pltpu.VMEM)] * n_z,
        out_specs=[pl.BlockSpec(memory_space=pltpu.VMEM)] * 2,
        out_shape=[
            jax.ShapeDtypeStruct((n_z, rows_here, cols), BF16),
            jax.ShapeDtypeStruct((8, n_z * rows_here), F32),
        ],
        scratch_shapes=[pltpu.VMEM((n_z, rows - rows_here, cols), F32)],
        compiler_params=pltpu.CompilerParams(vmem_limit_bytes=40 * 2**20),
        name="join_kv",
    )(*pieces)


def local(
    tokens,
    out_grad,
    block_order,
    norm1_gain,
    q_weight,
    q_bias,
    k_weight,
    k_bias,
    v_weight,
    v_bias,
    o_weight,
    norm2_gain,
    gate_weight,
    up_weight,
    down_weight,
):
    n_ctx = lax.axis_size("ctx")
    n_z = lax.axis_size("fsdp")
    tp = 4 if n_ctx % 4 == 0 else (2 if n_ctx % 2 == 0 else 1)
    here = lax.axis_index("ctx")
    zed = lax.axis_index("fsdp")
    core = lax.axis_index("seq")
    n_part = 2 * tp
    part = core * tp + lax.rem(here, tp)

    def swap(v):
        return lax.ppermute(v, "seq", [(0, 1), (1, 0)])

    def hop(v, k):
        if k == 0:
            return v
        return lax.ppermute(v, "ctx", [(i, i ^ k) for i in range(n_ctx)])

    def hop_z(v, k):
        if k == 0:
            return v
        return lax.ppermute(v, "fsdp", [(i, i ^ k) for i in range(n_z)])

    def gather_z(v):
        return lax.all_gather(v, "fsdp", axis=0, tiled=True)

    def scatter_z(v):
        return lax.psum_scatter(v, "fsdp", scatter_dimension=0, tiled=True)

    tokens_here, width = tokens.shape[1:]
    ff = gate_weight.shape[1]
    rows_here = q_weight.shape[0]
    key_width = KV_HEADS * HEAD
    block_len = tokens_here * n_z

    part_rows = -(-rows_here // (n_part * 32)) * 32

    kb = k_bias.shape[0]
    vectors = (norm1_gain, norm2_gain, q_bias, k_bias, v_bias)
    vec = sum(
        jnp.pad(v[None], ((i, 15 - i), (0, 2 * key_width - v.shape[0])))
        for i, v in enumerate(vectors)
    )
    kv_pack = jnp.concatenate([jnp.concatenate([k_weight, v_weight], 1), vec], 0)
    kv_got = [hop_z(kv_pack, k) for k in range(n_z)]
    w_kv, vecs = join_kv(kv_got, rows_here, tuple(v.shape[0] for v in vectors))
    w_kv = w_kv.reshape(width, 2 * key_width)
    gain_one = vecs[0:1, :width]
    gain_two = vecs[1:2, :width]
    b_query = vecs[2:3, :width]
    b_key = vecs[3:4, :key_width]
    b_value = vecs[4:5, :key_width]

    def share_pieces(mine):
        own = jnp.stack([hop(mine, k) for k in range(tp)])
        return own, swap(own)

    def gather_shared(w):
        mine = lax.dynamic_slice_in_dim(w, part * part_rows, part_rows, 0)
        mine = jnp.stack([hop_z(mine, k) for k in range(n_z)])
        own, sib = share_pieces(mine)
        return join_weight(own, sib, rows_here)

    w_query = gather_shared(q_weight)

    ff_z = ff // n_z
    piece = ff_z // n_part
    piece_pad = -(-piece // 32) * 32
    ff_half = n_z * piece_pad

    def ff_columns(w):
        cuts = []
        for j in range(n_z):
            cut = lax.dynamic_slice_in_dim(w, j * ff_z + part * piece, piece, 1)
            cuts.append(jnp.pad(cut, ((0, 0), (0, piece_pad - piece))))
        return jnp.concatenate(cuts, 1)

    gu_cut = jnp.concatenate([ff_columns(gate_weight), ff_columns(up_weight)], 1)
    down_cut = lax.dynamic_slice_in_dim(down_weight, part * piece, piece, 0)
    down_cut = jnp.pad(down_cut, ((0, piece_pad - piece), (0, 0)))
    w_kv, o_weight, gu_cut, down_cut = lax.optimization_barrier(
        (w_kv, o_weight, gu_cut, down_cut)
    )
    w_out = gather_shared(o_weight)
    gu_own = gather_z(gu_cut)
    gu_oth = swap(gu_own)
    down_own = gather_z(down_cut)
    down_oth = swap(down_own)
    og_here = out_grad[0]
    og_all = jnp.concatenate([hop(og_here, k) for k in range(tp)], 0)

    order_row = block_order[0]
    query_pos = (
        order_row[here] * block_len
        + zed * tokens_here
        + jnp.arange(tokens_here, dtype=jnp.int32)
    )
    cosine_table, sine_table = rope_tables(query_pos, HEAD)

    inputs = tokens[0].astype(F32)
    normed_one, scale_one, hidden_one = rms_forward(inputs, gain_one)
    key_value = matmul(hidden_one, w_kv)
    key_pre = key_value[:, :key_width] + b_key
    value_pre = key_value[:, key_width:] + b_value
    query_pre = matmul(hidden_one, w_query) + b_query
    queries = rotate(query_pre.reshape(tokens_here, HEADS, HEAD), cosine_table, sine_table)
    queries = queries.astype(BF16).reshape(tokens_here, HEADS * HEAD) * BF16(HEAD ** (-0.5))
    key_rot = rotate(key_pre.reshape(tokens_here, KV_HEADS, HEAD), cosine_table, sine_table)
    kv_local = jnp.concatenate(
        [key_rot.astype(BF16).reshape(tokens_here, key_width), value_pre.astype(BF16)], 1
    )
    kv_block = jnp.concatenate([hop_z(kv_local, k) for k in range(n_z)], 0)
    if n_ctx == tp:
        kv_blocks = [hop(kv_block, k) for k in range(n_ctx)]
        kv_whole = jnp.stack(kv_blocks)
    else:
        kv_whole = lax.all_gather(kv_block, "ctx", axis=0, tiled=False)
    attended, queries_ext = attend_forward(order_row, n_ctx == tp, queries, kv_whole)
    resid = inputs + matmul(attended, w_out)
    normed_two, scale_two, hidden_two = rms_forward(resid, gain_two)

    h2_all = jnp.concatenate([hop(hidden_two, k) for k in range(tp)], 0)

    def scatter_plane(v):
        parts = v.astype(BF16).reshape(tp, tokens_here, width)
        return [hop(parts[k], k) for k in range(tp)]

    def ff_half_pass(w_gu, w_d):
        gu = matmul(h2_all, w_gu)
        gate = gu[:, :ff_half]
        up = gu[:, ff_half:]
        sig = jax.nn.sigmoid(gate)
        silu = gate * sig
        act = (silu * up).astype(BF16)
        grad_act = times_transposed(og_all, w_d)
        grad_gate = (grad_act * up * sig * (1.0 + gate * (1.0 - sig))).astype(BF16)
        grad_up = (grad_act * silu).astype(BF16)
        return act, jnp.concatenate([grad_gate, grad_up], 1)

    act_own, ggu_own = ff_half_pass(gu_own, down_own)
    act_oth, ggu_oth = ff_half_pass(gu_oth, down_oth)
    grad_h2_parts = scatter_plane(
        times_transposed(ggu_own, gu_own) + times_transposed(ggu_oth, gu_oth)
    )

    def reduce_start(part_sum):
        cols = part_sum.shape[1]
        cut = part_sum.astype(BF16).reshape(n_z, rows_here, cols)
        cut = jnp.pad(cut, ((0, 0), (0, n_part * part_rows - rows_here), (0, 0)))
        own = lax.dynamic_slice_in_dim(cut, core * tp * part_rows, tp * part_rows, 1)
        oth = lax.dynamic_slice_in_dim(cut, (1 - core) * tp * part_rows, tp * part_rows, 1)
        both = (own.astype(F32) + swap(oth).astype(F32)).astype(BF16)
        return both.reshape(n_z, tp, part_rows, cols)

    def reduce_end(cut):
        cols = cut.shape[-1]
        total = 0.0
        for k in range(tp):
            at = lax.rem(here, tp) ^ k
            total = total + hop(lax.dynamic_index_in_dim(cut, at, 1, keepdims=False), k).astype(F32)
        cut = total.astype(BF16)
        total = 0.0
        for k in range(n_z):
            total = total + hop_z(
                lax.dynamic_index_in_dim(cut, zed ^ k, 0, keepdims=False), k
            ).astype(F32)
        total = ctx_groups_sum(total.astype(BF16))
        total = lax.optimization_barrier(total)
        own, sib = share_pieces(total)
        return spread_rows((own, sib), part_rows, rows_here)

    def ctx_groups_sum(v):
        if n_ctx == tp:
            return v
        groups = [[g * tp + c for g in range(n_ctx // tp)] for c in range(tp)]
        return lax.psum(v, "ctx", axis_index_groups=groups)

    def core_sum(own, oth):
        return (own + swap(oth.astype(BF16)).astype(F32)).astype(BF16)

    d_down = core_sum(contract_rows(act_own, og_all), contract_rows(act_oth, og_all))
    d_gu = core_sum(contract_rows(h2_all, ggu_own), contract_rows(h2_all, ggu_oth))
    grad_h2_parts, d_down, d_gu, act_own, act_oth = lax.optimization_barrier(
        (grad_h2_parts, d_down, d_gu, act_own, act_oth)
    )
    d_gu = scatter_z(d_gu)
    d_down = scatter_z(d_down)
    ff_out = scatter_plane(matmul(act_own, down_own) + matmul(act_oth, down_oth))
    result = resid + sum(v.astype(F32) for v in ff_out)
    layer_out = result.astype(BF16)[None]
    grad_h2 = sum(v.astype(F32) for v in grad_h2_parts)

    grad_norm_two, gain_two_terms = rms_backward(grad_h2, normed_two, scale_two, gain_two)
    grad_resid = og_here.astype(F32) + grad_norm_two
    grad_proj = grad_resid.astype(BF16)
    grad_att = times_transposed(grad_proj, w_out).astype(BF16)
    grad_queries, grad_terms = attend_backward(
        order_row, n_ctx == tp, queries_ext, grad_att, attended, kv_whole
    )
    if n_ctx == tp:
        kv_sum = sum(hop(grad_terms[k], k).astype(F32) for k in range(n_ctx)).astype(BF16)
    else:
        kv_sum = lax.psum_scatter(grad_terms, "ctx", scatter_dimension=0, tiled=False)
    kv_sum = kv_sum.reshape(n_z, tokens_here, 2 * key_width)
    grad_kv = kv_sum[0].astype(F32)
    for k in range(1, n_z):
        grad_kv = grad_kv + hop_z(kv_sum[k], k).astype(F32)

    grad_q_pre = (
        rotate(grad_queries.reshape(tokens_here, HEADS, HEAD), cosine_table, -sine_table)
        .reshape(tokens_here, HEADS * HEAD)
        .astype(BF16)
    )
    grad_k_pre = (
        rotate(
            grad_kv[:, :key_width].reshape(tokens_here, KV_HEADS, HEAD), cosine_table, -sine_table
        )
        .reshape(tokens_here, key_width)
        .astype(BF16)
    )
    grad_v_pre = grad_kv[:, key_width:].astype(BF16)

    grad_kv_pre = jnp.concatenate([grad_k_pre, grad_v_pre], 1)
    grad_hidden_one = times_transposed(grad_q_pre, w_query) + times_transposed(grad_kv_pre, w_kv)
    grad_norm_one, gain_one_terms = rms_backward(grad_hidden_one, normed_one, scale_one, gain_one)
    tokens_grad = (grad_resid + grad_norm_one)[None]

    def by_rows(v):
        share = v.shape[1] // n_z
        v = v.reshape(tokens_here, n_z, share)
        return jnp.pad(v, ((0, 0), (0, 0), (0, rows_here - share))).reshape(tokens_here, width)

    d_qo = jnp.concatenate(
        [contract_rows(hidden_one, grad_q_pre), contract_rows(attended, grad_proj)], 1
    )
    d_qo = reduce_end(reduce_start(d_qo))
    grad_w_query = d_qo[:, :width]
    grad_w_out = d_qo[:, width:]
    terms = (gain_one_terms, gain_two_terms, grad_q_pre, by_rows(grad_k_pre), by_rows(grad_v_pre))
    pick = jnp.arange(len(terms) * tokens_here)[:, None] // tokens_here == jnp.arange(128)[None]
    columns = contract_rows(
        jnp.concatenate([v.astype(BF16) for v in terms], 0), pick.astype(BF16)
    )
    grad_w_kv = jnp.concatenate([contract_rows(hidden_one, grad_kv_pre), columns], 1)
    grad_w_kv = reduce_end(reduce_start(grad_w_kv))
    sums = grad_w_kv[:, 2 * key_width :]
    grad_w_down = spread_rows(share_pieces(ctx_groups_sum(d_down)), piece, ff_z)
    grad_w_gate, grad_w_up = spread_columns(share_pieces(ctx_groups_sum(d_gu)), n_z, ff, 2)

    return (
        layer_out,
        tokens_grad,
        sums[:, 0],
        grad_w_query,
        sums[:, 2],
        grad_w_kv[:, :key_width],
        sums[:kb, 3],
        grad_w_kv[:, key_width : 2 * key_width],
        sums[:kb, 4],
        grad_w_out,
        sums[:, 1],
        grad_w_gate,
        grad_w_up,
        grad_w_down,
    )


def solution(mesh):
    in_specs = (
        P("seq", ("ctx", "fsdp"), None),
        P("seq", ("ctx", "fsdp"), None),
        P("seq", None),
        P("fsdp"),
        P("fsdp", None),
        P("fsdp"),
        P("fsdp", None),
        P("fsdp"),
        P("fsdp", None),
        P("fsdp"),
        P("fsdp", None),
        P("fsdp"),
        P("fsdp", None),
        P("fsdp", None),
        P("fsdp", None),
    )
    out_specs = (
        P("seq", ("ctx", "fsdp"), None),
        P("seq", ("ctx", "fsdp"), None),
        P("fsdp"),
        P("fsdp", None),
        P("fsdp"),
        P("fsdp", None),
        P("fsdp"),
        P("fsdp", None),
        P("fsdp"),
        P("fsdp", None),
        P("fsdp"),
        P("fsdp", None),
        P("fsdp", None),
        P("fsdp", None),
    )
    return jax.shard_map(local, mesh=mesh, in_specs=in_specs, out_specs=out_specs, check_vma=False)
```

```python
import functools
import math

import jax
import jax.numpy as jnp
from jax import lax
from jax.experimental import pallas as pl
from jax.experimental.pallas import tpu as pltpu
from jax.sharding import PartitionSpec as P

HEADS = 14
KV_HEADS = 2
HEAD = 64
GROUP = HEADS // KV_HEADS
NORM_EPS = 1e-06
ROPE_BASE = 1000000.0
MASKED = -1e30
BF16 = jnp.bfloat16
F32 = jnp.float32


def rope_tables(positions, head_dim):
    half_dim = head_dim // 2
    inverse = jnp.exp(
        jnp.arange(half_dim, dtype=jnp.float32) * (-math.log(ROPE_BASE) * 2.0 / head_dim)
    )
    angles = positions.astype(jnp.float32)[:, None] * inverse[None, :]
    return (jnp.cos(angles)[:, None, :], jnp.sin(angles)[:, None, :])


def rotate(values, cosine_table, sine_table):
    half_dim = values.shape[-1] // 2
    front_half = values[..., :half_dim]
    back_half = values[..., half_dim:]
    return jnp.concatenate(
        [
            front_half * cosine_table - back_half * sine_table,
            back_half * cosine_table + front_half * sine_table,
        ],
        -1,
    )


def matmul(left_side, right_side):
    return jnp.dot(left_side, right_side, preferred_element_type=F32)


def contract_rows(left_side, right_side):
    return lax.dot_general(
        left_side, right_side, (((0,), (0,)), ((), ())), preferred_element_type=F32
    )


def times_transposed(left_side, right_side):
    return lax.dot_general(
        left_side, right_side, (((1,), (1,)), ((), ())), preferred_element_type=F32
    )


def rms_forward(values, gain_vec):
    inv_scale = lax.rsqrt(jnp.mean(values * values, -1, keepdims=True) + NORM_EPS)
    normed = values * inv_scale
    return (normed, inv_scale, (normed * gain_vec).astype(BF16))


def rms_backward(grad_out, normed, inv_scale, gain_vec):
    scaled = grad_out * gain_vec
    grad_in = inv_scale * (scaled - normed * jnp.mean(scaled * normed, -1, keepdims=True))
    return (grad_in, grad_out * normed)


def cut_heads(ref, head):
    tile = ref[:, (head // 2) * 128 : (head // 2 + 1) * 128].astype(F32)
    group = head // GROUP
    if head % 2 != group:
        tile = jnp.concatenate([tile[:, HEAD:], tile[:, :HEAD]], 1)
    lane = lax.broadcasted_iota(jnp.int32, tile.shape, 1)
    return jnp.where((lane >= HEAD) if group else (lane < HEAD), tile, 0.0)


def split_lanes(column, shape):
    high = column.astype(BF16).astype(F32)
    mid = (column - high).astype(BF16).astype(F32)
    low = column - high - mid
    lane = lax.broadcasted_iota(jnp.int32, shape, 1)
    return jnp.where(
        lane == 0, high, jnp.where(lane == 1, mid, jnp.where(lane == 2, low, 0.0))
    ).astype(BF16)


def piece_shift(at, zed, tokens_here, keys_here):
    pieces = keys_here // tokens_here
    shift = jnp.zeros(at.shape, jnp.int32)
    for k in range(pieces):
        here = (jnp.bitwise_xor(zed, k) - k - zed) * tokens_here
        shift = jnp.where(at >= k * tokens_here, here, shift)
    return shift


def forward_kernel(by_xor, info_ref, q_ref, kv_ref, att_ref, qext_ref, top_ref, acc_ref):
    step = pl.program_id(0)
    last = pl.num_programs(0) - 1
    tokens_here = q_ref.shape[0]
    keys_here = kv_ref.shape[1]
    here = lax.axis_index("ctx")
    zed = lax.axis_index("fsdp")
    own = info_ref[here]
    block = info_ref[jnp.bitwise_xor(here, step) if by_xor else step]

    @pl.when(step == 0)
    def _():
        for h in range(HEADS):
            qext_ref[h * tokens_here : (h + 1) * tokens_here, :128] = cut_heads(q_ref, h).astype(
                BF16
            )
        top_ref[...] = jnp.full(top_ref.shape, MASKED, F32)
        acc_ref[...] = jnp.zeros(acc_ref.shape, F32)

    def attend(masked):
        keys = kv_ref[0, :, :128]
        values = jnp.concatenate(
            [kv_ref[0, :, 128:], jnp.ones((keys_here, 128), BF16)], 1
        )
        if masked:
            row = lax.broadcasted_iota(jnp.int32, (tokens_here, keys_here), 0)
            col = lax.broadcasted_iota(jnp.int32, (tokens_here, keys_here), 1)
            allowed = col + piece_shift(col, zed, tokens_here, keys_here) <= row
        for h in range(HEADS):
            rows = slice(h * tokens_here, (h + 1) * tokens_here)
            scores = times_transposed(qext_ref[rows, :128], keys)
            if masked:
                scores = jnp.where(allowed, scores, MASKED)
            old = top_ref[rows, :]
            top = jnp.maximum(old, jnp.max(scores, -1, keepdims=True))
            probs = jnp.exp(scores - top[:, :1]).astype(BF16)
            shrink = jnp.exp(old - top)
            top_ref[rows, :] = top
            acc_ref[rows, :] = acc_ref[rows, :] * jnp.concatenate([shrink, shrink], 1) + matmul(
                probs, values
            )

    @pl.when(block == own)
    def _():
        attend(True)

    @pl.when(block < own)
    def _():
        attend(False)

    @pl.when(step == last)
    def _():
        lane = lax.broadcasted_iota(jnp.int32, (tokens_here, 128), 1)
        for pair in range(HEADS // 2):
            outs = []
            for h in (2 * pair, 2 * pair + 1):
                rows = slice(h * tokens_here, (h + 1) * tokens_here)
                total = acc_ref[rows, 128:]
                out = acc_ref[rows, :128] / total
                if h // GROUP != h % 2:
                    out = jnp.concatenate([out[:, HEAD:], out[:, :HEAD]], 1)
                outs.append(out)
                log_total = top_ref[rows, :] + jnp.log(total)
                qext_ref[rows, 128:] = split_lanes(-log_total, (tokens_here, 128))
            att_ref[:, pair * 128 : (pair + 1) * 128] = jnp.where(
                lane < HEAD, outs[0], outs[1]
            ).astype(BF16)


def backward_kernel(
    by_xor, info_ref, qext_ref, do_ref, att_ref, kv_ref, dq_ref, dkv_ref, doext_ref, dqt_ref
):
    step = pl.program_id(0)
    last = pl.num_programs(0) - 1
    tokens_here = do_ref.shape[0]
    keys_here = kv_ref.shape[1]
    here = lax.axis_index("ctx")
    zed = lax.axis_index("fsdp")
    own = info_ref[here]
    block = info_ref[jnp.bitwise_xor(here, step) if by_xor else step]
    span = 2 * tokens_here

    @pl.when(step == 0)
    def _():
        for h in range(HEADS):
            rows = slice(h * tokens_here, (h + 1) * tokens_here)
            grad = cut_heads(do_ref, h)
            delta = jnp.sum(grad * cut_heads(att_ref, h), -1, keepdims=True)
            doext_ref[rows, :128] = grad.astype(BF16)
            doext_ref[rows, 128:] = split_lanes(-delta, (tokens_here, 128))
        dqt_ref[...] = jnp.zeros(dqt_ref.shape, F32)

    def attend(masked):
        lane = lax.broadcasted_iota(jnp.int32, (keys_here, 128), 1)
        ones = jnp.where(lane < 3, 1.0, 0.0).astype(BF16)
        keys = kv_ref[0, :, :128]
        keys_ext = jnp.concatenate([keys, ones], 1)
        values_ext = jnp.concatenate([kv_ref[0, :, 128:], ones], 1)
        keys_t = keys.astype(F32).T.astype(BF16)
        if masked:
            row = lax.broadcasted_iota(jnp.int32, (keys_here, tokens_here), 0)
            col = lax.broadcasted_iota(jnp.int32, (keys_here, tokens_here), 1)
            allowed = row + piece_shift(row, zed, tokens_here, keys_here) <= col
            allowed = allowed.astype(F32)
            allowed = jnp.concatenate([allowed, allowed], 1) > 0.5
        dk = jnp.zeros((keys_here, 128), F32)
        dv = jnp.zeros((keys_here, 128), F32)
        for pair in range(HEADS // 2):
            rows = slice(pair * span, (pair + 1) * span)
            probs = jnp.exp(times_transposed(keys_ext, qext_ref[rows, :]))
            if masked:
                probs = jnp.where(allowed, probs, 0.0)
            slope = (probs * times_transposed(values_ext, doext_ref[rows, :])).astype(BF16)
            dv = dv + matmul(probs.astype(BF16), doext_ref[rows, :128])
            dk = dk + matmul(slope, qext_ref[rows, :128])
            dqt_ref[pair] = dqt_ref[pair] + matmul(keys_t, slope)
        dkv_ref[0] = jnp.concatenate([dk, dv], 1).astype(BF16)

    @pl.when(block == own)
    def _():
        attend(True)

    @pl.when(block < own)
    def _():
        attend(False)

    @pl.when(block > own)
    def _():
        dkv_ref[...] = jnp.zeros(dkv_ref.shape, BF16)

    @pl.when(step == last)
    def _():
        lane = lax.broadcasted_iota(jnp.int32, (tokens_here, 128), 1)
        for pair in range(HEADS // 2):
            turned = dqt_ref[pair].T
            outs = []
            for j in range(2):
                h = 2 * pair + j
                out = turned[j * tokens_here : (j + 1) * tokens_here]
                if h // GROUP != j:
                    out = jnp.concatenate([out[:, HEAD:], out[:, :HEAD]], 1)
                outs.append(out)
            dq_ref[:, pair * 128 : (pair + 1) * 128] = (
                jnp.where(lane < HEAD, outs[0], outs[1]) * HEAD ** (-0.5)
            )


def whole_spec(shape):
    return pl.BlockSpec(shape, lambda i, info: (0,) * len(shape))


def attend_forward(info, by_xor, queries, kv):
    blocks, block_len, kv_width = kv.shape
    tokens_here, q_width = queries.shape
    rows = HEADS * tokens_here
    return pl.pallas_call(
        functools.partial(forward_kernel, by_xor),
        grid_spec=pltpu.PrefetchScalarGridSpec(
            num_scalar_prefetch=1,
            grid=(blocks,),
            in_specs=[
                whole_spec((tokens_here, q_width)),
                pl.BlockSpec((1, block_len, kv_width), lambda i, info: (i, 0, 0)),
            ],
            out_specs=[whole_spec((tokens_here, q_width)), whole_spec((rows, 256))],
            scratch_shapes=[pltpu.VMEM((rows, 128), F32), pltpu.VMEM((rows, 256), F32)],
        ),
        out_shape=[
            jax.ShapeDtypeStruct((tokens_here, q_width), BF16),
            jax.ShapeDtypeStruct((rows, 256), BF16),
        ],
        compiler_params=pltpu.CompilerParams(
            dimension_semantics=("arbitrary",), vmem_limit_bytes=40 * 2**20
        ),
        cost_estimate=pl.CostEstimate(
            flops=4 * rows * blocks * block_len * 256,
            bytes_accessed=6 * 2**20,
            transcendentals=rows * blocks * block_len,
        ),
        name="attend_forward",
    )(info, queries, kv)


def attend_backward(info, by_xor, queries_ext, grad_att, attended, kv):
    blocks, block_len, kv_width = kv.shape
    tokens_here, q_width = grad_att.shape
    rows = HEADS * tokens_here
    return pl.pallas_call(
        functools.partial(backward_kernel, by_xor),
        grid_spec=pltpu.PrefetchScalarGridSpec(
            num_scalar_prefetch=1,
            grid=(blocks,),
            in_specs=[
                whole_spec((rows, 256)),
                whole_spec((tokens_here, q_width)),
                whole_spec((tokens_here, q_width)),
                pl.BlockSpec((1, block_len, kv_width), lambda i, info: (i, 0, 0)),
            ],
            out_specs=[
                whole_spec((tokens_here, q_width)),
                pl.BlockSpec((1, block_len, kv_width), lambda i, info: (i, 0, 0)),
            ],
            scratch_shapes=[
                pltpu.VMEM((rows, 256), BF16),
                pltpu.VMEM((HEADS // 2, 128, 2 * tokens_here), F32),
            ],
        ),
        out_shape=[
            jax.ShapeDtypeStruct((tokens_here, q_width), F32),
            jax.ShapeDtypeStruct(kv.shape, BF16),
        ],
        compiler_params=pltpu.CompilerParams(
            dimension_semantics=("arbitrary",), vmem_limit_bytes=40 * 2**20
        ),
        cost_estimate=pl.CostEstimate(
            flops=10 * rows * blocks * block_len * 256,
            bytes_accessed=8 * 2**20,
            transcendentals=rows * blocks * block_len,
        ),
        name="attend_backward",
    )(info, queries_ext, grad_att, attended, kv)


def part_place(tp, j, k):
    at = jnp.bitwise_xor(lax.rem(lax.axis_index("ctx"), tp), k)
    return jnp.bitwise_xor(lax.axis_index("seq"), j) * tp + at


def spread_columns_kernel(n_z, *refs):
    pieces, outs, held = refs[:2], refs[2:-1], refs[-1]
    tp = pieces[0].shape[0]
    n_part = 2 * tp
    for j in range(2):
        for k in range(tp):
            held[part_place(tp, j, k)] = pieces[j][k].astype(F32)
    half = held.shape[2] // len(outs)
    pad = half // n_z
    for i, out in enumerate(outs):
        piece = out.shape[1] // (n_z * n_part)
        cuts = []
        for j in range(n_z):
            for e in range(n_part):
                start = i * half + j * pad
                cuts.append(held[e, :, start : start + piece])
        out[...] = jnp.concatenate(cuts, 1)


def spread_columns(pieces, n_z, ff, outs):
    tp, rows, cols = pieces[0].shape
    tile = 32
    return pl.pallas_call(
        functools.partial(spread_columns_kernel, n_z),
        grid=(rows // tile,),
        in_specs=[pl.BlockSpec((tp, tile, cols), lambda i: (0, i, 0))] * 2,
        out_specs=[pl.BlockSpec((tile, ff), lambda i: (i, 0))] * outs,
        scratch_shapes=[pltpu.VMEM((2 * tp, tile, cols), F32)],
        out_shape=[jax.ShapeDtypeStruct((rows, ff), F32)] * outs,
        compiler_params=pltpu.CompilerParams(
            dimension_semantics=("arbitrary",), vmem_limit_bytes=40 * 2**20
        ),
        cost_estimate=pl.CostEstimate(
            flops=0, bytes_accessed=rows * ff * 6 * outs, transcendentals=0
        ),
        name="spread_columns",
    )(*pieces)


def spread_rows_kernel(piece, *refs):
    pieces, out_ref = refs[:-1], refs[-1]
    room = out_ref.shape[0] // piece
    tp = pieces[0].shape[0]
    for j in range(2):
        for k in range(tp):
            place = part_place(tp, j, k)

            @pl.when(place < room)
            def _():
                start = pl.multiple_of(place * piece, 8)
                out_ref[pl.ds(start, piece), :] = pieces[j][k].astype(F32)[:piece]


def spread_rows(pieces, piece, rows_out):
    tp, rows, cols = pieces[0].shape
    tile = 128
    return pl.pallas_call(
        functools.partial(spread_rows_kernel, piece),
        grid=(cols // tile,),
        in_specs=[pl.BlockSpec((tp, rows, tile), lambda i: (0, 0, i))] * 2,
        out_specs=pl.BlockSpec((rows_out, tile), lambda i: (0, i)),
        out_shape=jax.ShapeDtypeStruct((rows_out, cols), F32),
        compiler_params=pltpu.CompilerParams(
            dimension_semantics=("arbitrary",), vmem_limit_bytes=40 * 2**20
        ),
        cost_estimate=pl.CostEstimate(
            flops=0, bytes_accessed=rows_out * cols * 6, transcendentals=0
        ),
        name="spread_rows",
    )(*pieces)


def join_weight_kernel(own_ref, sib_ref, out_ref):
    tp, n_z, part_rows = own_ref.shape[:3]
    room = out_ref.shape[1] // part_rows
    for j, ref in enumerate((own_ref, sib_ref)):
        for k in range(tp):
            place = part_place(tp, j, k)

            @pl.when(place < room)
            def _():
                start = pl.multiple_of(place * part_rows, 16)
                for z in range(n_z):
                    at = jnp.bitwise_xor(lax.axis_index("fsdp"), z)
                    out_ref[at, pl.ds(start, part_rows), :] = ref[k, z]


def join_weight(own, sib, rows_here):
    tp, n_z, part_rows, cols = own.shape
    return pl.pallas_call(
        join_weight_kernel,
        in_specs=[pl.BlockSpec(memory_space=pltpu.VMEM)] * 2,
        out_specs=pl.BlockSpec(memory_space=pltpu.VMEM),
        out_shape=jax.ShapeDtypeStruct((n_z, rows_here, cols), BF16),
        compiler_params=pltpu.CompilerParams(vmem_limit_bytes=40 * 2**20),
        cost_estimate=pl.CostEstimate(
            flops=0, bytes_accessed=4 * n_z * rows_here * cols, transcendentals=0
        ),
        name="join_weight",
    )(own, sib).reshape(n_z * rows_here, cols)


def join_kv_kernel(widths, *refs):
    pieces, (out_ref, vec_ref, held) = refs[:-3], refs[-3:]
    n_z, rows_here, cols = out_ref.shape
    for k in range(n_z):
        at = jnp.bitwise_xor(lax.axis_index("fsdp"), k)
        out_ref[at] = pieces[k][:rows_here]
        held[at] = pieces[k][rows_here:].astype(F32)
    vec_ref[...] = jnp.zeros(vec_ref.shape, F32)
    for i, size in enumerate(widths):
        row = jnp.concatenate([held[z, i : i + 1, :size] for z in range(n_z)], 1)
        vec_ref[i : i + 1, : n_z * size] = row


def join_kv(pieces, rows_here, widths):
    rows, cols = pieces[0].shape
    n_z = len(pieces)
    return pl.pallas_call(
        functools.partial(join_kv_kernel, widths),
        in_specs=[pl.BlockSpec(memory_space=pltpu.VMEM)] * n_z,
        out_specs=[pl.BlockSpec(memory_space=pltpu.VMEM)] * 2,
        out_shape=[
            jax.ShapeDtypeStruct((n_z, rows_here, cols), BF16),
            jax.ShapeDtypeStruct((8, n_z * rows_here), F32),
        ],
        scratch_shapes=[pltpu.VMEM((n_z, rows - rows_here, cols), F32)],
        compiler_params=pltpu.CompilerParams(vmem_limit_bytes=40 * 2**20),
        name="join_kv",
    )(*pieces)


def ff_kernel(tp, *refs):
    hidden, grads, weights = refs[:tp], refs[tp : 2 * tp], refs[2 * tp : 2 * tp + 4]
    act_refs, back_refs = refs[2 * tp + 4 : 2 * tp + 6], refs[2 * tp + 6 : 2 * tp + 8]
    outs = refs[2 * tp + 8 : 3 * tp + 8]
    gu_buf, down_buf, acc, sems = refs[3 * tp + 8 :]
    copies = [
        pltpu.make_async_copy(weights[i], (gu_buf if i < 2 else down_buf).at[i % 2], sems.at[i])
        for i in range(4)
    ]
    for i in (0, 2, 1, 3):
        copies[i].start()
    tokens_here = hidden[0].shape[0]
    half = down_buf.shape[1]
    step = 2 if tp % 2 == 0 else 1
    for i in range(2):
        copies[i].wait()
        for t in range(0, tp, step):
            rows = slice(t * tokens_here, (t + step) * tokens_here)
            here = jnp.concatenate([hidden[t + n][...] for n in range(step)], 0)
            grad = jnp.concatenate([grads[t + n][...] for n in range(step)], 0)
            gate = matmul(here, gu_buf[i, :, :half])
            up = matmul(here, gu_buf[i, :, half:])
            if t == 0:
                copies[2 + i].wait()
            grad_act = times_transposed(grad, down_buf[i])
            sig = 1.0 / (1.0 + jnp.exp(-gate))
            silu = gate * sig
            act_refs[i][rows, :] = (silu * up).astype(BF16)
            grad_gate = (grad_act * up * (sig + silu * (1.0 - sig))).astype(BF16)
            grad_up = (grad_act * silu).astype(BF16)
            back_refs[i][rows, :half] = grad_gate
            back_refs[i][rows, half:] = grad_up
            part = times_transposed(grad_gate, gu_buf[i, :, :half]) + times_transposed(
                grad_up, gu_buf[i, :, half:]
            )
            if i == 0:
                acc[rows, :] = part
            else:
                part = (part + acc[rows, :]).astype(BF16)
                for n in range(step):
                    outs[t + n][...] = part[n * tokens_here : (n + 1) * tokens_here]


def ff_pass(hidden, grads, gu, down):
    tp = len(hidden)
    tokens_here, width = hidden[0].shape
    half = down[0].shape[0]
    rows = tp * tokens_here
    vmem = pl.BlockSpec(memory_space=pltpu.VMEM)
    got = pl.pallas_call(
        functools.partial(ff_kernel, tp),
        in_specs=[vmem] * (2 * tp) + [pl.BlockSpec(memory_space=pl.ANY)] * 4,
        out_specs=[vmem] * (tp + 4),
        out_shape=[jax.ShapeDtypeStruct((rows, half), BF16)] * 2
        + [jax.ShapeDtypeStruct((rows, 2 * half), BF16)] * 2
        + [jax.ShapeDtypeStruct((tokens_here, width), BF16)] * tp,
        scratch_shapes=[
            pltpu.VMEM((2, width, 2 * half), BF16),
            pltpu.VMEM((2, half, width), BF16),
            pltpu.VMEM((rows, width), F32),
            pltpu.SemaphoreType.DMA((4,)),
        ],
        compiler_params=pltpu.CompilerParams(vmem_limit_bytes=56 * 2**20),
        cost_estimate=pl.CostEstimate(
            flops=20 * rows * width * half,
            bytes_accessed=20 * 2**20,
            transcendentals=2 * rows * half,
        ),
        name="ff_pass",
    )(*hidden, *grads, *gu, *down)
    return got[:2], got[2:4], got[4:]


def local(
    tokens,
    out_grad,
    block_order,
    norm1_gain,
    q_weight,
    q_bias,
    k_weight,
    k_bias,
    v_weight,
    v_bias,
    o_weight,
    norm2_gain,
    gate_weight,
    up_weight,
    down_weight,
):
    n_ctx = lax.axis_size("ctx")
    n_z = lax.axis_size("fsdp")
    tp = 4 if n_ctx % 4 == 0 else (2 if n_ctx % 2 == 0 else 1)
    here = lax.axis_index("ctx")
    zed = lax.axis_index("fsdp")
    core = lax.axis_index("seq")
    n_part = 2 * tp
    part = core * tp + lax.rem(here, tp)

    def swap(v):
        return lax.ppermute(v, "seq", [(0, 1), (1, 0)])

    def hop(v, k):
        if k == 0:
            return v
        return lax.ppermute(v, "ctx", [(i, i ^ k) for i in range(n_ctx)])

    def hop_z(v, k):
        if k == 0:
            return v
        return lax.ppermute(v, "fsdp", [(i, i ^ k) for i in range(n_z)])

    def gather_z(v):
        return lax.all_gather(v, "fsdp", axis=0, tiled=True)

    def scatter_z(v):
        return lax.psum_scatter(v, "fsdp", scatter_dimension=0, tiled=True)

    tokens_here, width = tokens.shape[1:]
    ff = gate_weight.shape[1]
    rows_here = q_weight.shape[0]
    key_width = KV_HEADS * HEAD
    block_len = tokens_here * n_z

    part_rows = -(-rows_here // (n_part * 32)) * 32

    kb = k_bias.shape[0]
    vectors = (norm1_gain, norm2_gain, q_bias, k_bias, v_bias)
    vec = sum(
        jnp.pad(v[None], ((i, 15 - i), (0, 2 * key_width - v.shape[0])))
        for i, v in enumerate(vectors)
    )
    kv_pack = jnp.concatenate([jnp.concatenate([k_weight, v_weight], 1), vec], 0)
    og_here = out_grad[0]

    def own_part(w):
        return lax.dynamic_slice_in_dim(w, part * part_rows, part_rows, 0)

    kv_pack, q_part, o_part, gate_weight, up_weight, down_weight = lax.optimization_barrier(
        (kv_pack, own_part(q_weight), own_part(o_weight), gate_weight, up_weight, down_weight)
    )
    kv_got = [hop_z(kv_pack, k) for k in range(n_z)]
    q_got = [hop_z(q_part, k) for k in range(n_z)]
    og_parts = [hop(og_here, k) for k in range(tp)]
    kv_got, q_got, og_parts, o_part = lax.optimization_barrier((kv_got, q_got, og_parts, o_part))
    w_kv, vecs = join_kv(kv_got, rows_here, tuple(v.shape[0] for v in vectors))
    w_kv = w_kv.reshape(width, 2 * key_width)
    gain_one = vecs[0:1, :width]
    gain_two = vecs[1:2, :width]
    b_query = vecs[2:3, :width]
    b_key = vecs[3:4, :key_width]
    b_value = vecs[4:5, :key_width]

    def share_pieces(mine):
        own = jnp.stack([hop(mine, k) for k in range(tp)])
        return own, swap(own)

    q_own = [hop(jnp.stack(q_got), k) for k in range(tp)]

    ff_z = ff // n_z
    piece = ff_z // n_part
    piece_pad = -(-piece // 32) * 32
    ff_half = n_z * piece_pad

    def ff_columns(w):
        cuts = []
        for j in range(n_z):
            cut = lax.dynamic_slice_in_dim(w, j * ff_z + part * piece, piece, 1)
            cuts.append(jnp.pad(cut, ((0, 0), (0, piece_pad - piece))))
        return jnp.concatenate(cuts, 1)

    gu_cut = jnp.concatenate([ff_columns(gate_weight), ff_columns(up_weight)], 1)
    down_cut = lax.dynamic_slice_in_dim(down_weight, part * piece, piece, 0)
    down_cut = jnp.pad(down_cut, ((0, piece_pad - piece), (0, 0)))
    order_row = block_order[0]
    query_pos = (
        order_row[here] * block_len
        + zed * tokens_here
        + jnp.arange(tokens_here, dtype=jnp.int32)
    )
    cosine_table, sine_table = rope_tables(query_pos, HEAD)

    inputs = tokens[0].astype(F32)
    normed_one, scale_one, hidden_one = rms_forward(inputs, gain_one)
    key_value = matmul(hidden_one, w_kv)
    key_pre = key_value[:, :key_width] + b_key
    value_pre = key_value[:, key_width:] + b_value
    key_rot = rotate(key_pre.reshape(tokens_here, KV_HEADS, HEAD), cosine_table, sine_table)
    kv_local = jnp.concatenate(
        [key_rot.astype(BF16).reshape(tokens_here, key_width), value_pre.astype(BF16)], 1
    )
    kv_local, o_part = lax.optimization_barrier((kv_local, o_part))
    kv_z = [hop_z(kv_local, k) for k in range(n_z)]
    o_got = [hop_z(o_part, k) for k in range(n_z)]
    kv_z, o_got, q_own, gu_cut, down_cut = lax.optimization_barrier(
        (kv_z, o_got, q_own, gu_cut, down_cut)
    )
    kv_block = jnp.concatenate(kv_z, 0)
    gu_own = gather_z(gu_cut)
    gu_oth = swap(gu_own)
    down_own = gather_z(down_cut)
    down_oth = swap(down_own)
    if n_ctx == tp:
        kv_blocks = [hop(kv_block, k) for k in range(n_ctx)]
    else:
        kv_blocks = lax.all_gather(kv_block, "ctx", axis=0, tiled=False)
    q_own = jnp.stack(q_own)
    w_query = join_weight(q_own, swap(q_own), rows_here)
    query_pre = matmul(hidden_one, w_query) + b_query
    queries = rotate(query_pre.reshape(tokens_here, HEADS, HEAD), cosine_table, sine_table)
    queries = queries.astype(BF16).reshape(tokens_here, HEADS * HEAD) * BF16(HEAD ** (-0.5))
    kv_blocks, o_got = lax.optimization_barrier((kv_blocks, o_got))
    o_own = [hop(jnp.stack(o_got), k) for k in range(tp)]
    kv_whole = jnp.stack(kv_blocks) if n_ctx == tp else kv_blocks
    attended, queries_ext = attend_forward(order_row, n_ctx == tp, queries, kv_whole)
    attended, o_own = lax.optimization_barrier((attended, o_own))
    o_own = jnp.stack(o_own)
    w_out = join_weight(o_own, swap(o_own), rows_here)
    resid = inputs + matmul(attended, w_out)
    normed_two, scale_two, hidden_two = rms_forward(resid, gain_two)

    h2_parts = [hop(hidden_two, k) for k in range(tp)]

    def scatter_plane(v):
        parts = v.astype(BF16).reshape(tp, tokens_here, width)
        return [hop(parts[k], k) for k in range(tp)]

    acts, ggus, dh2 = ff_pass(h2_parts, og_parts, (gu_own, gu_oth), (down_own, down_oth))
    grad_h2_parts = [hop(dh2[k], k) for k in range(tp)]
    h2_all = jnp.concatenate(h2_parts, 0)
    og_all = jnp.concatenate(og_parts, 0)

    def reduce_start(part_sum):
        cols = part_sum.shape[1]
        cut = part_sum.astype(BF16).reshape(n_z, rows_here, cols)
        cut = jnp.pad(cut, ((0, 0), (0, n_part * part_rows - rows_here), (0, 0)))
        own = lax.dynamic_slice_in_dim(cut, core * tp * part_rows, tp * part_rows, 1)
        oth = lax.dynamic_slice_in_dim(cut, (1 - core) * tp * part_rows, tp * part_rows, 1)
        both = (own.astype(F32) + swap(oth).astype(F32)).astype(BF16)
        return both.reshape(n_z, tp, part_rows, cols)

    def reduce_end(cut, z_first):
        cols = cut.shape[-1]
        total = 0.0
        if z_first:
            for k in range(n_z):
                out = lax.dynamic_index_in_dim(cut, zed ^ k, 0, keepdims=False)
                total = total + hop_z(out, k).astype(F32)
            cut = total.astype(BF16)
            total = 0.0
        for k in range(tp):
            at = lax.rem(here, tp) ^ k
            out = lax.dynamic_index_in_dim(cut, at, cut.ndim - 3, keepdims=False)
            total = total + hop(out, k).astype(F32)
        if not z_first:
            cut = total.astype(BF16)
            total = 0.0
            for k in range(n_z):
                out = lax.dynamic_index_in_dim(cut, zed ^ k, 0, keepdims=False)
                total = total + hop_z(out, k).astype(F32)
        total = ctx_groups_sum(total.astype(BF16))
        total = lax.optimization_barrier(total)
        own, sib = share_pieces(total)
        return spread_rows((own, sib), part_rows, rows_here)

    def ctx_groups_sum(v):
        if n_ctx == tp:
            return v
        groups = [[g * tp + c for g in range(n_ctx // tp)] for c in range(tp)]
        return lax.psum(v, "ctx", axis_index_groups=groups)

    def core_sum(own, oth):
        return (own + swap(oth.astype(BF16)).astype(F32)).astype(BF16)

    d_gu = core_sum(contract_rows(h2_all, ggus[0]), contract_rows(h2_all, ggus[1]))
    d_down = core_sum(contract_rows(acts[0], og_all), contract_rows(acts[1], og_all))
    ff_out = (matmul(acts[0], down_own) + matmul(acts[1], down_oth)).astype(BF16)
    grad_h2_parts, d_down, d_gu, ff_out = lax.optimization_barrier(
        (grad_h2_parts, d_down, d_gu, ff_out)
    )
    d_gu = scatter_z(d_gu)
    ff_out = scatter_plane(ff_out)
    grad_h2 = sum(v.astype(F32) for v in grad_h2_parts)

    grad_norm_two, gain_two_terms = rms_backward(grad_h2, normed_two, scale_two, gain_two)
    grad_resid = og_here.astype(F32) + grad_norm_two
    grad_proj = grad_resid.astype(BF16)
    grad_att = times_transposed(grad_proj, w_out).astype(BF16)
    grad_queries, grad_terms = attend_backward(
        order_row, n_ctx == tp, queries_ext, grad_att, attended, kv_whole
    )
    grad_terms, d_gu, ff_out, d_down = lax.optimization_barrier((grad_terms, d_gu, ff_out, d_down))
    d_down = scatter_z(d_down)
    result = resid + sum(v.astype(F32) for v in ff_out)
    layer_out = result.astype(BF16)[None]
    if n_ctx == tp:
        kv_terms = [hop(grad_terms[k], k) for k in range(n_ctx)]
        kv_terms, d_gu = lax.optimization_barrier((kv_terms, d_gu))
        kv_sum = sum(v.astype(F32) for v in kv_terms).astype(BF16)
    else:
        kv_sum = lax.psum_scatter(grad_terms, "ctx", scatter_dimension=0, tiled=False)
    d_gu = share_pieces(ctx_groups_sum(d_gu))
    kv_sum = kv_sum.reshape(n_z, tokens_here, 2 * key_width)
    grad_kv = kv_sum[0].astype(F32)
    for k in range(1, n_z):
        grad_kv = grad_kv + hop_z(kv_sum[k], k).astype(F32)

    grad_q_pre = (
        rotate(grad_queries.reshape(tokens_here, HEADS, HEAD), cosine_table, -sine_table)
        .reshape(tokens_here, HEADS * HEAD)
        .astype(BF16)
    )
    grad_k_pre = (
        rotate(
            grad_kv[:, :key_width].reshape(tokens_here, KV_HEADS, HEAD), cosine_table, -sine_table
        )
        .reshape(tokens_here, key_width)
        .astype(BF16)
    )
    grad_v_pre = grad_kv[:, key_width:].astype(BF16)

    grad_kv_pre = jnp.concatenate([grad_k_pre, grad_v_pre], 1)
    grad_hidden_one = times_transposed(grad_q_pre, w_query) + times_transposed(grad_kv_pre, w_kv)
    grad_norm_one, gain_one_terms = rms_backward(grad_hidden_one, normed_one, scale_one, gain_one)
    tokens_grad = (grad_resid + grad_norm_one)[None]

    def by_rows(v):
        share = v.shape[1] // n_z
        v = v.reshape(tokens_here, n_z, share)
        return jnp.pad(v, ((0, 0), (0, 0), (0, rows_here - share))).reshape(tokens_here, width)

    d_qo = jnp.concatenate(
        [contract_rows(hidden_one, grad_q_pre), contract_rows(attended, grad_proj)], 1
    )
    d_qo = reduce_end(reduce_start(d_qo), True)
    grad_w_query = d_qo[:, :width]
    grad_w_out = d_qo[:, width:]
    terms = (gain_one_terms, gain_two_terms, grad_q_pre, by_rows(grad_k_pre), by_rows(grad_v_pre))
    pick = jnp.arange(len(terms) * tokens_here)[:, None] // tokens_here == jnp.arange(128)[None]
    columns = contract_rows(
        jnp.concatenate([v.astype(BF16) for v in terms], 0), pick.astype(BF16)
    )
    grad_w_kv = jnp.concatenate([contract_rows(hidden_one, grad_kv_pre), columns], 1)
    grad_w_kv = reduce_end(reduce_start(grad_w_kv), False)
    sums = grad_w_kv[:, 2 * key_width :]
    grad_w_down = spread_rows(share_pieces(ctx_groups_sum(d_down)), piece, ff_z)
    grad_w_gate, grad_w_up = spread_columns(d_gu, n_z, ff, 2)

    return (
        layer_out,
        tokens_grad,
        sums[:, 0],
        grad_w_query,
        sums[:, 2],
        grad_w_kv[:, :key_width],
        sums[:kb, 3],
        grad_w_kv[:, key_width : 2 * key_width],
        sums[:kb, 4],
        grad_w_out,
        sums[:, 1],
        grad_w_gate,
        grad_w_up,
        grad_w_down,
    )


def solution(mesh):
    in_specs = (
        P("seq", ("ctx", "fsdp"), None),
        P("seq", ("ctx", "fsdp"), None),
        P("seq", None),
        P("fsdp"),
        P("fsdp", None),
        P("fsdp"),
        P("fsdp", None),
        P("fsdp"),
        P("fsdp", None),
        P("fsdp"),
        P("fsdp", None),
        P("fsdp"),
        P("fsdp", None),
        P("fsdp", None),
        P("fsdp", None),
    )
    out_specs = (
        P("seq", ("ctx", "fsdp"), None),
        P("seq", ("ctx", "fsdp"), None),
        P("fsdp"),
        P("fsdp", None),
        P("fsdp"),
        P("fsdp", None),
        P("fsdp"),
        P("fsdp", None),
        P("fsdp"),
        P("fsdp", None),
        P("fsdp"),
        P("fsdp", None),
        P("fsdp", None),
        P("fsdp", None),
    )
    return jax.shard_map(local, mesh=mesh, in_specs=in_specs, out_specs=out_specs, check_vma=False)
```

```python
import functools
import math

import jax
import jax.numpy as jnp
from jax import lax
from jax.experimental import pallas as pl
from jax.experimental.pallas import tpu as pltpu
from jax.sharding import PartitionSpec as P

HEADS = 14
KV_HEADS = 2
HEAD = 64
GROUP = HEADS // KV_HEADS
NORM_EPS = 1e-06
ROPE_BASE = 1000000.0
MASKED = -1e30
BF16 = jnp.bfloat16
F32 = jnp.float32
NO_COST = pl.CostEstimate(flops=0, bytes_accessed=0, transcendentals=0)


def rope_tables(positions, head_dim):
    half_dim = head_dim // 2
    inverse = jnp.exp(
        jnp.arange(half_dim, dtype=jnp.float32) * (-math.log(ROPE_BASE) * 2.0 / head_dim)
    )
    angles = positions.astype(jnp.float32)[:, None] * inverse[None, :]
    return (jnp.cos(angles)[:, None, :], jnp.sin(angles)[:, None, :])


def rotate(values, cosine_table, sine_table):
    half_dim = values.shape[-1] // 2
    front_half = values[..., :half_dim]
    back_half = values[..., half_dim:]
    return jnp.concatenate(
        [
            front_half * cosine_table - back_half * sine_table,
            back_half * cosine_table + front_half * sine_table,
        ],
        -1,
    )


def matmul(left_side, right_side):
    return jnp.dot(left_side, right_side, preferred_element_type=F32)


def contract_rows(left_side, right_side):
    return lax.dot_general(
        left_side, right_side, (((0,), (0,)), ((), ())), preferred_element_type=F32
    )


def times_transposed(left_side, right_side):
    return lax.dot_general(
        left_side, right_side, (((1,), (1,)), ((), ())), preferred_element_type=F32
    )


def rms_backward(grad_out, normed, inv_scale, gain_vec):
    scaled = grad_out * gain_vec
    grad_in = inv_scale * (scaled - normed * jnp.mean(scaled * normed, -1, keepdims=True))
    return (grad_in, grad_out * normed)


def cut_heads(ref, head):
    tile = ref[:, (head // 2) * 128 : (head // 2 + 1) * 128].astype(F32)
    group = head // GROUP
    if head % 2 != group:
        tile = jnp.concatenate([tile[:, HEAD:], tile[:, :HEAD]], 1)
    lane = lax.broadcasted_iota(jnp.int32, tile.shape, 1)
    return jnp.where((lane >= HEAD) if group else (lane < HEAD), tile, 0.0)


def split_lanes(column, shape):
    high = column.astype(BF16).astype(F32)
    mid = (column - high).astype(BF16).astype(F32)
    low = column - high - mid
    lane = lax.broadcasted_iota(jnp.int32, shape, 1)
    return jnp.where(
        lane == 0, high, jnp.where(lane == 1, mid, jnp.where(lane == 2, low, 0.0))
    ).astype(BF16)


def piece_shift(at, zed, tokens_here, keys_here):
    pieces = keys_here // tokens_here
    shift = jnp.zeros(at.shape, jnp.int32)
    for k in range(pieces):
        here = (jnp.bitwise_xor(zed, k) - k - zed) * tokens_here
        shift = jnp.where(at >= k * tokens_here, here, shift)
    return shift


def forward_kernel(by_xor, info_ref, q_ref, kv_ref, att_ref, qext_ref, top_ref, acc_ref):
    step = pl.program_id(0)
    last = pl.num_programs(0) - 1
    tokens_here = q_ref.shape[0]
    keys_here = kv_ref.shape[1]
    here = lax.axis_index("ctx")
    zed = lax.axis_index("fsdp")
    own = info_ref[here]
    block = info_ref[jnp.bitwise_xor(here, step) if by_xor else step]

    @pl.when(step == 0)
    def _():
        for h in range(HEADS):
            qext_ref[h * tokens_here : (h + 1) * tokens_here, :128] = cut_heads(q_ref, h).astype(
                BF16
            )
        top_ref[...] = jnp.full(top_ref.shape, MASKED, F32)
        acc_ref[...] = jnp.zeros(acc_ref.shape, F32)

    def attend(masked):
        keys = kv_ref[0, :, :128]
        values = jnp.concatenate(
            [kv_ref[0, :, 128:], jnp.ones((keys_here, 128), BF16)], 1
        )
        if masked:
            row = lax.broadcasted_iota(jnp.int32, (tokens_here, keys_here), 0)
            col = lax.broadcasted_iota(jnp.int32, (tokens_here, keys_here), 1)
            allowed = col + piece_shift(col, zed, tokens_here, keys_here) <= row
        for h in range(HEADS):
            rows = slice(h * tokens_here, (h + 1) * tokens_here)
            scores = times_transposed(qext_ref[rows, :128], keys)
            if masked:
                scores = jnp.where(allowed, scores, MASKED)
            old = top_ref[rows, :]
            top = jnp.maximum(old, jnp.max(scores, -1, keepdims=True))
            probs = jnp.exp(scores - top[:, :1]).astype(BF16)
            shrink = jnp.exp(old - top)
            top_ref[rows, :] = top
            acc_ref[rows, :] = acc_ref[rows, :] * jnp.concatenate([shrink, shrink], 1) + matmul(
                probs, values
            )

    @pl.when(block == own)
    def _():
        attend(True)

    @pl.when(block < own)
    def _():
        attend(False)

    @pl.when(step == last)
    def _():
        lane = lax.broadcasted_iota(jnp.int32, (tokens_here, 128), 1)
        for pair in range(HEADS // 2):
            outs = []
            for h in (2 * pair, 2 * pair + 1):
                rows = slice(h * tokens_here, (h + 1) * tokens_here)
                total = acc_ref[rows, 128:]
                out = acc_ref[rows, :128] / total
                if h // GROUP != h % 2:
                    out = jnp.concatenate([out[:, HEAD:], out[:, :HEAD]], 1)
                outs.append(out)
                log_total = top_ref[rows, :] + jnp.log(total)
                qext_ref[rows, 128:] = split_lanes(-log_total, (tokens_here, 128))
            att_ref[:, pair * 128 : (pair + 1) * 128] = jnp.where(
                lane < HEAD, outs[0], outs[1]
            ).astype(BF16)


def backward_kernel(
    by_xor, info_ref, qext_ref, do_ref, att_ref, kv_ref, dq_ref, dkv_ref, doext_ref, dqt_ref
):
    step = pl.program_id(0)
    last = pl.num_programs(0) - 1
    tokens_here = do_ref.shape[0]
    keys_here = kv_ref.shape[1]
    here = lax.axis_index("ctx")
    zed = lax.axis_index("fsdp")
    own = info_ref[here]
    block = info_ref[jnp.bitwise_xor(here, step) if by_xor else step]
    span = 2 * tokens_here

    @pl.when(step == 0)
    def _():
        for h in range(HEADS):
            rows = slice(h * tokens_here, (h + 1) * tokens_here)
            grad = cut_heads(do_ref, h)
            delta = jnp.sum(grad * cut_heads(att_ref, h), -1, keepdims=True)
            doext_ref[rows, :128] = grad.astype(BF16)
            doext_ref[rows, 128:] = split_lanes(-delta, (tokens_here, 128))
        dqt_ref[...] = jnp.zeros(dqt_ref.shape, F32)

    def attend(masked):
        lane = lax.broadcasted_iota(jnp.int32, (keys_here, 128), 1)
        ones = jnp.where(lane < 3, 1.0, 0.0).astype(BF16)
        keys = kv_ref[0, :, :128]
        keys_ext = jnp.concatenate([keys, ones], 1)
        values_ext = jnp.concatenate([kv_ref[0, :, 128:], ones], 1)
        keys_t = keys.astype(F32).T.astype(BF16)
        if masked:
            row = lax.broadcasted_iota(jnp.int32, (keys_here, tokens_here), 0)
            col = lax.broadcasted_iota(jnp.int32, (keys_here, tokens_here), 1)
            allowed = row + piece_shift(row, zed, tokens_here, keys_here) <= col
            allowed = allowed.astype(F32)
            allowed = jnp.concatenate([allowed, allowed], 1) > 0.5
        dk = jnp.zeros((keys_here, 128), F32)
        dv = jnp.zeros((keys_here, 128), F32)
        for pair in range(HEADS // 2):
            rows = slice(pair * span, (pair + 1) * span)
            probs = jnp.exp(times_transposed(keys_ext, qext_ref[rows, :]))
            if masked:
                probs = jnp.where(allowed, probs, 0.0)
            slope = (probs * times_transposed(values_ext, doext_ref[rows, :])).astype(BF16)
            dv = dv + matmul(probs.astype(BF16), doext_ref[rows, :128])
            dk = dk + matmul(slope, qext_ref[rows, :128])
            dqt_ref[pair] = dqt_ref[pair] + matmul(keys_t, slope)
        dkv_ref[0] = jnp.concatenate([dk, dv], 1).astype(BF16)

    @pl.when(block == own)
    def _():
        attend(True)

    @pl.when(block < own)
    def _():
        attend(False)

    @pl.when(block > own)
    def _():
        dkv_ref[...] = jnp.zeros(dkv_ref.shape, BF16)

    @pl.when(step == last)
    def _():
        lane = lax.broadcasted_iota(jnp.int32, (tokens_here, 128), 1)
        for pair in range(HEADS // 2):
            turned = dqt_ref[pair].T
            outs = []
            for j in range(2):
                h = 2 * pair + j
                out = turned[j * tokens_here : (j + 1) * tokens_here]
                if h // GROUP != j:
                    out = jnp.concatenate([out[:, HEAD:], out[:, :HEAD]], 1)
                outs.append(out)
            dq_ref[:, pair * 128 : (pair + 1) * 128] = (
                jnp.where(lane < HEAD, outs[0], outs[1]) * HEAD ** (-0.5)
            )


def whole_spec(shape):
    return pl.BlockSpec(shape, lambda i, info: (0,) * len(shape))


def attend_forward(info, by_xor, queries, kv):
    blocks, block_len, kv_width = kv.shape
    tokens_here, q_width = queries.shape
    rows = HEADS * tokens_here
    return pl.pallas_call(
        functools.partial(forward_kernel, by_xor),
        grid_spec=pltpu.PrefetchScalarGridSpec(
            num_scalar_prefetch=1,
            grid=(blocks,),
            in_specs=[
                whole_spec((tokens_here, q_width)),
                pl.BlockSpec((1, block_len, kv_width), lambda i, info: (i, 0, 0)),
            ],
            out_specs=[whole_spec((tokens_here, q_width)), whole_spec((rows, 256))],
            scratch_shapes=[pltpu.VMEM((rows, 128), F32), pltpu.VMEM((rows, 256), F32)],
        ),
        out_shape=[
            jax.ShapeDtypeStruct((tokens_here, q_width), BF16),
            jax.ShapeDtypeStruct((rows, 256), BF16),
        ],
        compiler_params=pltpu.CompilerParams(
            dimension_semantics=("arbitrary",), vmem_limit_bytes=40 * 2**20
        ),
        cost_estimate=NO_COST,
        name="attend_forward",
    )(info, queries, kv)


def attend_backward(info, by_xor, queries_ext, grad_att, attended, kv):
    blocks, block_len, kv_width = kv.shape
    tokens_here, q_width = grad_att.shape
    rows = HEADS * tokens_here
    return pl.pallas_call(
        functools.partial(backward_kernel, by_xor),
        grid_spec=pltpu.PrefetchScalarGridSpec(
            num_scalar_prefetch=1,
            grid=(blocks,),
            in_specs=[
                whole_spec((rows, 256)),
                whole_spec((tokens_here, q_width)),
                whole_spec((tokens_here, q_width)),
                pl.BlockSpec((1, block_len, kv_width), lambda i, info: (i, 0, 0)),
            ],
            out_specs=[
                whole_spec((tokens_here, q_width)),
                pl.BlockSpec((1, block_len, kv_width), lambda i, info: (i, 0, 0)),
            ],
            scratch_shapes=[
                pltpu.VMEM((rows, 256), BF16),
                pltpu.VMEM((HEADS // 2, 128, 2 * tokens_here), F32),
            ],
        ),
        out_shape=[
            jax.ShapeDtypeStruct((tokens_here, q_width), F32),
            jax.ShapeDtypeStruct(kv.shape, BF16),
        ],
        compiler_params=pltpu.CompilerParams(
            dimension_semantics=("arbitrary",), vmem_limit_bytes=40 * 2**20
        ),
        cost_estimate=NO_COST,
        name="attend_backward",
    )(info, queries_ext, grad_att, attended, kv)


def part_place(tp, j, k):
    at = jnp.bitwise_xor(lax.rem(lax.axis_index("ctx"), tp), k)
    return jnp.bitwise_xor(lax.axis_index("seq"), j) * tp + at


def spread_columns_kernel(n_z, *refs):
    pieces, outs, held = refs[:2], refs[2:-1], refs[-1]
    tp = pieces[0].shape[0]
    n_part = 2 * tp
    for j in range(2):
        for k in range(tp):
            held[part_place(tp, j, k)] = pieces[j][k].astype(F32)
    half = held.shape[2] // len(outs)
    pad = half // n_z
    for i, out in enumerate(outs):
        piece = out.shape[1] // (n_z * n_part)
        cuts = []
        for j in range(n_z):
            for e in range(n_part):
                start = i * half + j * pad
                cuts.append(held[e, :, start : start + piece])
        out[...] = jnp.concatenate(cuts, 1)


def spread_columns(pieces, n_z, ff, outs):
    tp, rows, cols = pieces[0].shape
    tile = 32
    return pl.pallas_call(
        functools.partial(spread_columns_kernel, n_z),
        grid=(rows // tile,),
        in_specs=[pl.BlockSpec((tp, tile, cols), lambda i: (0, i, 0))] * 2,
        out_specs=[pl.BlockSpec((tile, ff), lambda i: (i, 0))] * outs,
        scratch_shapes=[pltpu.VMEM((2 * tp, tile, cols), F32)],
        out_shape=[jax.ShapeDtypeStruct((rows, ff), F32)] * outs,
        compiler_params=pltpu.CompilerParams(
            dimension_semantics=("arbitrary",), vmem_limit_bytes=40 * 2**20
        ),
        cost_estimate=NO_COST,
        name="spread_columns",
    )(*pieces)


def spread_rows_kernel(piece, *refs):
    pieces, out_ref = refs[:-1], refs[-1]
    room = out_ref.shape[0] // piece
    tp = pieces[0].shape[0]
    for j in range(2):
        for k in range(tp):
            place = part_place(tp, j, k)

            @pl.when(place < room)
            def _():
                start = pl.multiple_of(place * piece, 8)
                out_ref[pl.ds(start, piece), :] = pieces[j][k].astype(F32)[:piece]


def spread_rows(pieces, piece, rows_out):
    tp, rows, cols = pieces[0].shape
    tile = 128
    return pl.pallas_call(
        functools.partial(spread_rows_kernel, piece),
        grid=(cols // tile,),
        in_specs=[pl.BlockSpec((tp, rows, tile), lambda i: (0, 0, i))] * 2,
        out_specs=pl.BlockSpec((rows_out, tile), lambda i: (0, i)),
        out_shape=jax.ShapeDtypeStruct((rows_out, cols), F32),
        compiler_params=pltpu.CompilerParams(
            dimension_semantics=("arbitrary",), vmem_limit_bytes=40 * 2**20
        ),
        cost_estimate=NO_COST,
        name="spread_rows",
    )(*pieces)


def join_weight(own_ref, sib_ref, out_ref):
    tp, n_z, part_rows = own_ref.shape[:3]
    room = out_ref.shape[1] // part_rows
    for j, ref in enumerate((own_ref, sib_ref)):
        for k in range(tp):
            place = part_place(tp, j, k)

            @pl.when(place < room)
            def _():
                start = pl.multiple_of(place * part_rows, 16)
                for z in range(n_z):
                    at = jnp.bitwise_xor(lax.axis_index("fsdp"), z)
                    out_ref[at, pl.ds(start, part_rows), :] = ref[k, z]


def whole_weight(ref):
    return jnp.concatenate([ref[z] for z in range(ref.shape[0])], 0)


def turn_tile(tile, cos, sin):
    h = HEAD // 2
    cuts = [tile[:, h : 2 * h], tile[:, :h], tile[:, 3 * h :], tile[:, 2 * h : 3 * h]]
    return tile * cos + jnp.concatenate(cuts, 1) * sin


def normed_rows(values, gain):
    inv = lax.rsqrt(jnp.mean(values * values, -1, keepdims=True) + NORM_EPS)
    return (values * inv * gain).astype(BF16)


def kv_kernel(widths, *refs):
    x_ref, cos_ref, sin_ref = refs[-8:-5]
    pieces, (out_ref, vec_ref, kv_ref, hid_ref, held) = refs[:-8], refs[-5:]
    n_z, rows_here, cols = out_ref.shape
    for k in range(n_z):
        at = jnp.bitwise_xor(lax.axis_index("fsdp"), k)
        out_ref[at] = pieces[k][:rows_here]
        held[at] = pieces[k][rows_here:].astype(F32)
    vec_ref[...] = jnp.zeros(vec_ref.shape, F32)
    for i, size in enumerate(widths):
        row = jnp.concatenate([held[z, i : i + 1, :size] for z in range(n_z)], 1)
        vec_ref[i : i + 1, : n_z * size] = row
    hidden = normed_rows(x_ref[...].astype(F32), vec_ref[0:1, :])
    hid_ref[...] = hidden
    half = cols // 2
    both = matmul(hidden, whole_weight(out_ref))
    keys = both[:, :half] + vec_ref[3:4, :half]
    kv_ref[:, :half] = turn_tile(keys, cos_ref[...], sin_ref[...]).astype(BF16)
    kv_ref[:, half:] = (both[:, half:] + vec_ref[4:5, :half]).astype(BF16)


def project_kv(pieces, tokens, cos, sin, rows_here, widths):
    rows, cols = pieces[0].shape
    n_z = len(pieces)
    vmem = pl.BlockSpec(memory_space=pltpu.VMEM)
    return pl.pallas_call(
        functools.partial(kv_kernel, widths),
        in_specs=[vmem] * (n_z + 3),
        out_specs=[vmem] * 4,
        out_shape=[
            jax.ShapeDtypeStruct((n_z, rows_here, cols), BF16),
            jax.ShapeDtypeStruct((8, n_z * rows_here), F32),
            jax.ShapeDtypeStruct((tokens.shape[0], cols), BF16),
            jax.ShapeDtypeStruct(tokens.shape, BF16),
        ],
        scratch_shapes=[pltpu.VMEM((n_z, rows - rows_here, cols), F32)],
        compiler_params=pltpu.CompilerParams(vmem_limit_bytes=40 * 2**20),
        cost_estimate=NO_COST,
        name="project_kv",
    )(*pieces, tokens, cos, sin)


def query_kernel(own_ref, sib_ref, hid_ref, vec_ref, cos_ref, sin_ref, out_ref, q_ref):
    join_weight(own_ref, sib_ref, out_ref)
    whole = matmul(hid_ref[...], whole_weight(out_ref)) + vec_ref[2:3, :]
    for pair in range(HEADS // 2):
        lanes = slice(pair * 128, (pair + 1) * 128)
        tile = turn_tile(whole[:, lanes], cos_ref[...], sin_ref[...]).astype(BF16)
        q_ref[:, lanes] = (tile.astype(F32) * HEAD ** (-0.5)).astype(BF16)


def project_query(own, sib, hidden, vecs, cos, sin, rows_here):
    n_z, cols = own.shape[1], own.shape[3]
    vmem = pl.BlockSpec(memory_space=pltpu.VMEM)
    return pl.pallas_call(
        query_kernel,
        in_specs=[vmem] * 6,
        out_specs=[vmem] * 2,
        out_shape=[
            jax.ShapeDtypeStruct((n_z, rows_here, cols), BF16),
            jax.ShapeDtypeStruct((hidden.shape[0], cols), BF16),
        ],
        compiler_params=pltpu.CompilerParams(vmem_limit_bytes=40 * 2**20),
        cost_estimate=NO_COST,
        name="project_query",
    )(own, sib, hidden, vecs, cos, sin)


def out_kernel(own_ref, sib_ref, att_ref, x_ref, vec_ref, out_ref, resid_ref, hid_ref):
    join_weight(own_ref, sib_ref, out_ref)
    resid = x_ref[...].astype(F32) + matmul(att_ref[...], whole_weight(out_ref))
    resid_ref[...] = resid
    hid_ref[...] = normed_rows(resid, vec_ref[1:2, :])


def project_out(own, sib, attended, tokens, vecs, rows_here):
    n_z, cols = own.shape[1], own.shape[3]
    vmem = pl.BlockSpec(memory_space=pltpu.VMEM)
    return pl.pallas_call(
        out_kernel,
        in_specs=[vmem] * 5,
        out_specs=[vmem] * 3,
        out_shape=[
            jax.ShapeDtypeStruct((n_z, rows_here, cols), BF16),
            jax.ShapeDtypeStruct(tokens.shape, F32),
            jax.ShapeDtypeStruct(tokens.shape, BF16),
        ],
        compiler_params=pltpu.CompilerParams(vmem_limit_bytes=40 * 2**20),
        cost_estimate=NO_COST,
        name="project_out",
    )(own, sib, attended, tokens, vecs)


def grad_weight_kernel(left_ref, right_ref, *refs):
    total = matmul(left_ref[...], right_ref[...])
    if len(refs) == 2:
        total = total + refs[0][...].astype(F32)
    refs[-1][...] = total.astype(BF16)


def grad_weight(left, right, other=None):
    rows, depth = left.shape
    cols = right.shape[1]
    tile = 128
    by_rows = lambda width: pl.BlockSpec((tile, width), lambda i: (i, 0))
    in_specs = [by_rows(depth), pl.BlockSpec((depth, cols), lambda i: (0, 0))]
    args = [left, right]
    if other is not None:
        in_specs.append(by_rows(cols))
        args.append(other)
    return pl.pallas_call(
        grad_weight_kernel,
        grid=(rows // tile,),
        in_specs=in_specs,
        out_specs=by_rows(cols),
        out_shape=jax.ShapeDtypeStruct((rows, cols), BF16),
        compiler_params=pltpu.CompilerParams(
            dimension_semantics=("arbitrary",), vmem_limit_bytes=40 * 2**20
        ),
        cost_estimate=NO_COST,
        name="grad_weight",
    )(*args)


def ff_kernel(tp, n_z, *refs):
    hidden, grads, weights = refs[:tp], refs[tp : 2 * tp], refs[2 * tp : 2 * tp + 4]
    rest = refs[2 * tp + 4 :]
    act_refs, back_refs, (hid_t, grad_all) = rest[:2], rest[2:4], rest[4:6]
    dh_outs, outs = rest[6 : 6 + tp], rest[6 + tp : 6 + 2 * tp]
    gu_buf, down_buf, acc, acc_out, sems = rest[6 + 2 * tp :]
    part_rows = weights[2].shape[1]
    gu_copies = [
        pltpu.make_async_copy(weights[i], gu_buf.at[i], sems.at[i]) for i in range(2)
    ]
    down_copies = []
    for i in range(2):
        for z in range(n_z):
            at = jnp.bitwise_xor(lax.axis_index("fsdp"), z) * part_rows
            to = down_buf.at[i, pl.ds(pl.multiple_of(at, 16), part_rows)]
            sem = sems.at[2 + i * n_z + z]
            down_copies.append(pltpu.make_async_copy(weights[2 + i].at[z], to, sem))
    gu_copies[0].start()
    for c in down_copies[:n_z]:
        c.start()
    gu_copies[1].start()
    for c in down_copies[n_z:]:
        c.start()
    tokens_here = hidden[0].shape[0]
    half = down_buf.shape[1]
    step = 2 if tp % 2 == 0 else 1
    for i in range(2):
        gu_copies[i].wait()
        for t in range(0, tp, step):
            rows = slice(t * tokens_here, (t + step) * tokens_here)
            here = jnp.concatenate([hidden[t + n][...] for n in range(step)], 0)
            grad = jnp.concatenate([grads[t + n][...] for n in range(step)], 0)
            if i == 0:
                hid_t[:, rows] = here.astype(F32).T.astype(BF16)
                grad_all[rows, :] = grad
            gate = matmul(here, gu_buf[i, :, :half])
            up = matmul(here, gu_buf[i, :, half:])
            if t == 0:
                for c in down_copies[i * n_z : (i + 1) * n_z]:
                    c.wait()
            grad_act = times_transposed(grad, down_buf[i])
            sig = 1.0 / (1.0 + jnp.exp(-gate))
            silu = gate * sig
            act = silu * up
            act_refs[i][:, rows] = act.T.astype(BF16)
            grad_gate = (grad_act * up * (sig + silu * (1.0 - sig))).astype(BF16)
            grad_up = (grad_act * silu).astype(BF16)
            back_refs[i][rows, :half] = grad_gate
            back_refs[i][rows, half:] = grad_up
            part = times_transposed(grad_gate, gu_buf[i, :, :half]) + times_transposed(
                grad_up, gu_buf[i, :, half:]
            )
            out = matmul(act.astype(BF16), down_buf[i])
            if i == 0:
                acc[rows, :] = part
                acc_out[rows, :] = out
            else:
                part = (part + acc[rows, :]).astype(BF16)
                out = (out + acc_out[rows, :]).astype(BF16)
                for n in range(step):
                    mine = slice(n * tokens_here, (n + 1) * tokens_here)
                    dh_outs[t + n][...] = part[mine]
                    outs[t + n][...] = out[mine]


def ff_pass(hidden, grads, gu, down):
    tp = len(hidden)
    n_z, part_rows = down[0].shape[:2]
    tokens_here, width = hidden[0].shape
    half = n_z * part_rows
    rows = tp * tokens_here
    vmem = pl.BlockSpec(memory_space=pltpu.VMEM)
    got = pl.pallas_call(
        functools.partial(ff_kernel, tp, n_z),
        in_specs=[vmem] * (2 * tp) + [pl.BlockSpec(memory_space=pl.ANY)] * 4,
        out_specs=[vmem] * (2 * tp + 6),
        out_shape=[jax.ShapeDtypeStruct((half, rows), BF16)] * 2
        + [jax.ShapeDtypeStruct((rows, 2 * half), BF16)] * 2
        + [jax.ShapeDtypeStruct((width, rows), BF16), jax.ShapeDtypeStruct((rows, width), BF16)]
        + [jax.ShapeDtypeStruct((tokens_here, width), BF16)] * (2 * tp),
        scratch_shapes=[
            pltpu.VMEM((2, width, 2 * half), BF16),
            pltpu.VMEM((2, half, width), BF16),
            pltpu.VMEM((rows, width), F32),
            pltpu.VMEM((rows, width), F32),
            pltpu.SemaphoreType.DMA((2 + 2 * n_z,)),
        ],
        compiler_params=pltpu.CompilerParams(vmem_limit_bytes=58 * 2**20),
        cost_estimate=NO_COST,
        name="ff_pass",
    )(*hidden, *grads, *gu, *down)
    return got[:2], got[2:4], got[4], got[5], got[6 : 6 + tp], got[6 + tp :]


def local(
    tokens,
    out_grad,
    block_order,
    norm1_gain,
    q_weight,
    q_bias,
    k_weight,
    k_bias,
    v_weight,
    v_bias,
    o_weight,
    norm2_gain,
    gate_weight,
    up_weight,
    down_weight,
):
    n_ctx = lax.axis_size("ctx")
    n_z = lax.axis_size("fsdp")
    tp = 4 if n_ctx % 4 == 0 else (2 if n_ctx % 2 == 0 else 1)
    here = lax.axis_index("ctx")
    zed = lax.axis_index("fsdp")
    core = lax.axis_index("seq")
    n_part = 2 * tp
    part = core * tp + lax.rem(here, tp)

    def swap(v):
        return lax.ppermute(v, "seq", [(0, 1), (1, 0)])

    def hop(v, k):
        if k == 0:
            return v
        return lax.ppermute(v, "ctx", [(i, i ^ k) for i in range(n_ctx)])

    def hop_z(v, k):
        if k == 0:
            return v
        return lax.ppermute(v, "fsdp", [(i, i ^ k) for i in range(n_z)])

    def gather_z(v):
        return lax.all_gather(v, "fsdp", axis=0, tiled=True)

    def scatter_z(v):
        return lax.psum_scatter(v, "fsdp", scatter_dimension=0, tiled=True)

    tokens_here, width = tokens.shape[1:]
    ff = gate_weight.shape[1]
    rows_here = q_weight.shape[0]
    key_width = KV_HEADS * HEAD
    block_len = tokens_here * n_z

    part_rows = -(-rows_here // (n_part * 32)) * 32

    kb = k_bias.shape[0]
    vectors = (norm1_gain, norm2_gain, q_bias, k_bias, v_bias)
    vec = sum(
        jnp.pad(v[None], ((i, 15 - i), (0, 2 * key_width - v.shape[0])))
        for i, v in enumerate(vectors)
    )
    kv_pack = jnp.concatenate([jnp.concatenate([k_weight, v_weight], 1), vec], 0)
    og_here = out_grad[0]

    def own_part(w):
        return lax.dynamic_slice_in_dim(w, part * part_rows, part_rows, 0)

    ff_z = ff // n_z
    piece = ff_z // n_part
    piece_pad = -(-piece // 32) * 32

    def ff_columns(w):
        cuts = []
        for j in range(n_z):
            cut = lax.dynamic_slice_in_dim(w, j * ff_z + part * piece, piece, 1)
            cuts.append(jnp.pad(cut, ((0, 0), (0, piece_pad - piece))))
        return jnp.concatenate(cuts, 1)

    order_row = block_order[0]
    x_here = tokens[0]
    kv_pack, q_part, o_part, gate_weight, up_weight, down_weight, query_at = (
        lax.optimization_barrier(
            (
                kv_pack,
                own_part(q_weight),
                own_part(o_weight),
                gate_weight,
                up_weight,
                down_weight,
                order_row[here] * block_len + zed * tokens_here,
            )
        )
    )
    kv_got = [hop_z(kv_pack, k) for k in range(n_z)]
    q_got = [hop_z(q_part, k) for k in range(n_z)]
    gu_cut = jnp.concatenate([ff_columns(gate_weight), ff_columns(up_weight)], 1)
    down_cut = lax.dynamic_slice_in_dim(down_weight, part * piece, piece, 0)
    down_cut = jnp.pad(down_cut, ((0, piece_pad - piece), (0, 0)))
    query_pos = query_at + jnp.arange(tokens_here, dtype=jnp.int32)
    cosine_table, sine_table = rope_tables(query_pos, HEAD)
    cos_wide = jnp.tile(cosine_table[:, 0], (1, 4))
    sin_wide = jnp.tile(jnp.concatenate([-sine_table[:, 0], sine_table[:, 0]], 1), (1, 2))
    kv_got, q_got, cos_wide, sin_wide, gu_cut, down_cut, o_part, og_here = (
        lax.optimization_barrier(
            (kv_got, q_got, cos_wide, sin_wide, gu_cut, down_cut, o_part, og_here)
        )
    )

    q_own = [hop(jnp.stack(q_got), k) for k in range(tp)]
    og_parts = [hop(og_here, k) for k in range(tp)]
    widths = tuple(v.shape[0] for v in vectors)
    w_kv, vecs, kv_local, hidden_one = project_kv(
        kv_got, x_here, cos_wide, sin_wide, rows_here, widths
    )
    w_kv = w_kv.reshape(width, 2 * key_width)
    gain_one = vecs[0:1, :width]
    gain_two = vecs[1:2, :width]
    kv_z = [hop_z(kv_local, k) for k in range(n_z)]
    o_got = [hop_z(o_part, k) for k in range(n_z)]
    kv_z, o_got, q_own, og_parts, gu_cut, down_cut = lax.optimization_barrier(
        (kv_z, o_got, q_own, og_parts, gu_cut, down_cut)
    )

    kv_block = jnp.concatenate(kv_z, 0)
    if n_ctx == tp:
        kv_blocks = [hop(kv_block, k) for k in range(n_ctx)]
    else:
        kv_blocks = lax.all_gather(kv_block, "ctx", axis=0, tiled=False)
    gu_own = gather_z(gu_cut)
    down_own = [hop_z(down_cut, k) for k in range(n_z)]
    q_own = jnp.stack(q_own)
    w_query, queries = project_query(
        q_own, swap(q_own), hidden_one, vecs, cos_wide, sin_wide, rows_here
    )
    w_query = w_query.reshape(width, width)
    kv_blocks, queries, o_got = lax.optimization_barrier((kv_blocks, queries, o_got))

    o_own = [hop(jnp.stack(o_got), k) for k in range(tp)]
    kv_whole = jnp.stack(kv_blocks) if n_ctx == tp else kv_blocks
    attended, queries_ext = attend_forward(order_row, n_ctx == tp, queries, kv_whole)
    attended, o_own, queries_ext = lax.optimization_barrier((attended, o_own, queries_ext))
    o_own = jnp.stack(o_own)
    w_out, resid, hidden_two = project_out(
        o_own, swap(o_own), attended, x_here, vecs, rows_here
    )
    w_out = w_out.reshape(width, width)
    h2_parts = [hop(hidden_two, k) for k in range(tp)]
    h2_parts, gu_own, down_own = lax.optimization_barrier((h2_parts, gu_own, down_own))
    gu_oth = swap(gu_own)
    down_own = jnp.stack(down_own)
    down_oth = swap(down_own)

    acts, ggus, h2_turned, og_all, dh2, ff_out = ff_pass(
        h2_parts, og_parts, (gu_own, gu_oth), (down_own, down_oth)
    )
    grad_h2_parts = [hop(dh2[k], k) for k in range(tp)]

    def share_pieces(mine):
        own = jnp.stack([hop(mine, k) for k in range(tp)])
        return own, swap(own)

    def reduce_start(part_sum):
        cols = part_sum.shape[1]
        cut = part_sum.astype(BF16).reshape(n_z, rows_here, cols)
        cut = jnp.pad(cut, ((0, 0), (0, n_part * part_rows - rows_here), (0, 0)))
        own = lax.dynamic_slice_in_dim(cut, core * tp * part_rows, tp * part_rows, 1)
        oth = lax.dynamic_slice_in_dim(cut, (1 - core) * tp * part_rows, tp * part_rows, 1)
        both = (own.astype(F32) + swap(oth).astype(F32)).astype(BF16)
        return both.reshape(n_z, tp, part_rows, cols)

    def reduce_end(cut, z_first):
        cols = cut.shape[-1]
        total = 0.0
        if z_first:
            for k in range(n_z):
                out = lax.dynamic_index_in_dim(cut, zed ^ k, 0, keepdims=False)
                total = total + hop_z(out, k).astype(F32)
            cut = total.astype(BF16)
            total = 0.0
        for k in range(tp):
            at = lax.rem(here, tp) ^ k
            out = lax.dynamic_index_in_dim(cut, at, cut.ndim - 3, keepdims=False)
            total = total + hop(out, k).astype(F32)
        if not z_first:
            cut = total.astype(BF16)
            total = 0.0
            for k in range(n_z):
                out = lax.dynamic_index_in_dim(cut, zed ^ k, 0, keepdims=False)
                total = total + hop_z(out, k).astype(F32)
        total = ctx_groups_sum(total.astype(BF16))
        total = lax.optimization_barrier(total)
        own, sib = share_pieces(total)
        return spread_rows((own, sib), part_rows, rows_here)

    def ctx_groups_sum(v):
        if n_ctx == tp:
            return v
        groups = [[g * tp + c for g in range(n_ctx // tp)] for c in range(tp)]
        return lax.psum(v, "ctx", axis_index_groups=groups)

    d_gu = grad_weight(h2_turned, ggus[0], swap(grad_weight(h2_turned, ggus[1])))
    d_down = grad_weight(acts[0], og_all, swap(grad_weight(acts[1], og_all)))
    grad_h2_parts, d_gu, d_down, ff_out = lax.optimization_barrier(
        (grad_h2_parts, d_gu, d_down, ff_out)
    )
    d_gu = scatter_z(d_gu)
    ff_out = [hop(ff_out[k], k) for k in range(tp)]
    d_down = d_down.reshape(n_z, piece_pad, width)
    d_down = [
        hop_z(lax.dynamic_index_in_dim(d_down, zed ^ k, 0, keepdims=False), k) for k in range(n_z)
    ]
    grad_h2 = sum(v.astype(F32) for v in grad_h2_parts)
    scale_two = lax.rsqrt(jnp.mean(resid * resid, -1, keepdims=True) + NORM_EPS)
    normed_two = resid * scale_two

    grad_norm_two, gain_two_terms = rms_backward(grad_h2, normed_two, scale_two, gain_two)
    grad_resid = og_here.astype(F32) + grad_norm_two
    grad_proj = grad_resid.astype(BF16)
    grad_att = times_transposed(grad_proj, w_out).astype(BF16)
    grad_queries, grad_terms = attend_backward(
        order_row, n_ctx == tp, queries_ext, grad_att, attended, kv_whole
    )
    grad_queries, grad_terms, ff_out, grad_proj = lax.optimization_barrier(
        (grad_queries, grad_terms, ff_out, grad_proj)
    )

    grad_q_pre = (
        rotate(grad_queries.reshape(tokens_here, HEADS, HEAD), cosine_table, -sine_table)
        .reshape(tokens_here, HEADS * HEAD)
        .astype(BF16)
    )
    d_qo = jnp.concatenate(
        [contract_rows(hidden_one, grad_q_pre), contract_rows(attended, grad_proj)], 1
    )
    d_qo = reduce_start(d_qo)
    if n_ctx == tp:
        kv_terms = [hop(grad_terms[k], k) for k in range(n_ctx)]
        kv_terms, d_gu, d_down, d_qo, ff_out = lax.optimization_barrier(
            (kv_terms, d_gu, d_down, d_qo, ff_out)
        )
        kv_sum = sum(v.astype(F32) for v in kv_terms).astype(BF16)
    else:
        kv_sum = lax.psum_scatter(grad_terms, "ctx", scatter_dimension=0, tiled=False)
    result = resid + sum(v.astype(F32) for v in ff_out)
    layer_out = result.astype(BF16)[None]
    d_gu = share_pieces(ctx_groups_sum(d_gu))
    d_down = ctx_groups_sum(sum(v.astype(F32) for v in d_down).astype(BF16))
    d_down = lax.optimization_barrier(d_down)
    kv_sum = kv_sum.reshape(n_z, tokens_here, 2 * key_width)
    kv_terms = [hop_z(kv_sum[k], k) for k in range(n_z)]
    kv_terms, d_qo, d_down = lax.optimization_barrier((kv_terms, d_qo, d_down))
    grad_kv = sum(v.astype(F32) for v in kv_terms)

    grad_k_pre = (
        rotate(
            grad_kv[:, :key_width].reshape(tokens_here, KV_HEADS, HEAD), cosine_table, -sine_table
        )
        .reshape(tokens_here, key_width)
        .astype(BF16)
    )
    grad_v_pre = grad_kv[:, key_width:].astype(BF16)

    grad_kv_pre = jnp.concatenate([grad_k_pre, grad_v_pre], 1)
    grad_hidden_one = times_transposed(grad_q_pre, w_query) + times_transposed(grad_kv_pre, w_kv)
    inputs = x_here.astype(F32)
    scale_one = lax.rsqrt(jnp.mean(inputs * inputs, -1, keepdims=True) + NORM_EPS)
    normed_one = inputs * scale_one
    grad_norm_one, gain_one_terms = rms_backward(grad_hidden_one, normed_one, scale_one, gain_one)
    tokens_grad = (grad_resid + grad_norm_one)[None]

    def by_rows(v):
        share = v.shape[1] // n_z
        v = v.reshape(tokens_here, n_z, share)
        return jnp.pad(v, ((0, 0), (0, 0), (0, rows_here - share))).reshape(tokens_here, width)

    d_qo = reduce_end(d_qo, True)
    grad_w_query = d_qo[:, :width]
    grad_w_out = d_qo[:, width:]
    terms = (gain_one_terms, gain_two_terms, grad_q_pre, by_rows(grad_k_pre), by_rows(grad_v_pre))
    pick = jnp.arange(len(terms) * tokens_here)[:, None] // tokens_here == jnp.arange(128)[None]
    columns = contract_rows(
        jnp.concatenate([v.astype(BF16) for v in terms], 0), pick.astype(BF16)
    )
    grad_w_kv = jnp.concatenate([contract_rows(hidden_one, grad_kv_pre), columns], 1)
    grad_w_kv = reduce_end(reduce_start(grad_w_kv), False)
    sums = grad_w_kv[:, 2 * key_width :]
    grad_w_down = spread_rows(share_pieces(d_down), piece, ff_z)
    grad_w_gate, grad_w_up = spread_columns(d_gu, n_z, ff, 2)

    return (
        layer_out,
        tokens_grad,
        sums[:, 0],
        grad_w_query,
        sums[:, 2],
        grad_w_kv[:, :key_width],
        sums[:kb, 3],
        grad_w_kv[:, key_width : 2 * key_width],
        sums[:kb, 4],
        grad_w_out,
        sums[:, 1],
        grad_w_gate,
        grad_w_up,
        grad_w_down,
    )


def solution(mesh):
    in_specs = (
        P("seq", ("ctx", "fsdp"), None),
        P("seq", ("ctx", "fsdp"), None),
        P("seq", None),
        P("fsdp"),
        P("fsdp", None),
        P("fsdp"),
        P("fsdp", None),
        P("fsdp"),
        P("fsdp", None),
        P("fsdp"),
        P("fsdp", None),
        P("fsdp"),
        P("fsdp", None),
        P("fsdp", None),
        P("fsdp", None),
    )
    out_specs = (
        P("seq", ("ctx", "fsdp"), None),
        P("seq", ("ctx", "fsdp"), None),
        P("fsdp"),
        P("fsdp", None),
        P("fsdp"),
        P("fsdp", None),
        P("fsdp"),
        P("fsdp", None),
        P("fsdp"),
        P("fsdp", None),
        P("fsdp"),
        P("fsdp", None),
        P("fsdp", None),
        P("fsdp", None),
    )
    return jax.shard_map(local, mesh=mesh, in_specs=in_specs, out_specs=out_specs, check_vma=False)
```

```python
import functools
import math

import jax
import jax.numpy as jnp
from jax import lax
from jax.experimental import pallas as pl
from jax.experimental.pallas import tpu as pltpu
from jax.sharding import PartitionSpec as P

HEADS = 14
KV_HEADS = 2
HEAD = 64
GROUP = HEADS // KV_HEADS
NORM_EPS = 1e-06
ROPE_BASE = 1000000.0
MASKED = -1e30
BF16 = jnp.bfloat16
F32 = jnp.float32
NO_COST = pl.CostEstimate(flops=0, bytes_accessed=0, transcendentals=0)


def rope_tables(positions, head_dim):
    half_dim = head_dim // 2
    inverse = jnp.exp(
        jnp.arange(half_dim, dtype=jnp.float32) * (-math.log(ROPE_BASE) * 2.0 / head_dim)
    )
    angles = positions.astype(jnp.float32)[:, None] * inverse[None, :]
    return (jnp.cos(angles)[:, None, :], jnp.sin(angles)[:, None, :])


def rotate(values, cosine_table, sine_table):
    half_dim = values.shape[-1] // 2
    front_half = values[..., :half_dim]
    back_half = values[..., half_dim:]
    return jnp.concatenate(
        [
            front_half * cosine_table - back_half * sine_table,
            back_half * cosine_table + front_half * sine_table,
        ],
        -1,
    )


def matmul(left_side, right_side):
    return jnp.dot(left_side, right_side, preferred_element_type=F32)


def contract_rows(left_side, right_side):
    return lax.dot_general(
        left_side, right_side, (((0,), (0,)), ((), ())), preferred_element_type=F32
    )


def times_transposed(left_side, right_side):
    return lax.dot_general(
        left_side, right_side, (((1,), (1,)), ((), ())), preferred_element_type=F32
    )


def rms_backward(grad_out, normed, inv_scale, gain_vec):
    scaled = grad_out * gain_vec
    grad_in = inv_scale * (scaled - normed * jnp.mean(scaled * normed, -1, keepdims=True))
    return (grad_in, grad_out * normed)


def cut_heads(ref, head):
    tile = ref[:, (head // 2) * 128 : (head // 2 + 1) * 128].astype(F32)
    group = head // GROUP
    if head % 2 != group:
        tile = jnp.concatenate([tile[:, HEAD:], tile[:, :HEAD]], 1)
    lane = lax.broadcasted_iota(jnp.int32, tile.shape, 1)
    return jnp.where((lane >= HEAD) if group else (lane < HEAD), tile, 0.0)


def split_lanes(column, shape):
    high = column.astype(BF16).astype(F32)
    mid = (column - high).astype(BF16).astype(F32)
    low = column - high - mid
    lane = lax.broadcasted_iota(jnp.int32, shape, 1)
    return jnp.where(
        lane == 0, high, jnp.where(lane == 1, mid, jnp.where(lane == 2, low, 0.0))
    ).astype(BF16)


def piece_shift(at, zed, tokens_here, keys_here):
    pieces = keys_here // tokens_here
    shift = jnp.zeros(at.shape, jnp.int32)
    for k in range(pieces):
        here = (jnp.bitwise_xor(zed, k) - k - zed) * tokens_here
        shift = jnp.where(at >= k * tokens_here, here, shift)
    return shift


def forward_kernel(by_xor, info_ref, q_ref, kv_ref, att_ref, qext_ref, top_ref, acc_ref):
    step = pl.program_id(0)
    last = pl.num_programs(0) - 1
    tokens_here = q_ref.shape[0]
    keys_here = kv_ref.shape[1]
    here = lax.axis_index("ctx")
    zed = lax.axis_index("fsdp")
    own = info_ref[here]
    block = info_ref[jnp.bitwise_xor(here, step) if by_xor else step]

    @pl.when(step == 0)
    def _():
        for h in range(HEADS):
            qext_ref[h * tokens_here : (h + 1) * tokens_here, :128] = cut_heads(q_ref, h).astype(
                BF16
            )
        top_ref[...] = jnp.full(top_ref.shape, MASKED, F32)
        acc_ref[...] = jnp.zeros(acc_ref.shape, F32)

    def attend(masked):
        keys = kv_ref[0, :, :128]
        values = jnp.concatenate(
            [kv_ref[0, :, 128:], jnp.ones((keys_here, 128), BF16)], 1
        )
        if masked:
            row = lax.broadcasted_iota(jnp.int32, (tokens_here, keys_here), 0)
            col = lax.broadcasted_iota(jnp.int32, (tokens_here, keys_here), 1)
            allowed = col + piece_shift(col, zed, tokens_here, keys_here) <= row
        for h in range(HEADS):
            rows = slice(h * tokens_here, (h + 1) * tokens_here)
            scores = times_transposed(qext_ref[rows, :128], keys)
            if masked:
                scores = jnp.where(allowed, scores, MASKED)
            old = top_ref[rows, :]
            top = jnp.maximum(old, jnp.max(scores, -1, keepdims=True))
            probs = jnp.exp(scores - top[:, :1]).astype(BF16)
            shrink = jnp.exp(old - top)
            top_ref[rows, :] = top
            acc_ref[rows, :] = acc_ref[rows, :] * jnp.concatenate([shrink, shrink], 1) + matmul(
                probs, values
            )

    @pl.when(block == own)
    def _():
        attend(True)

    @pl.when(block < own)
    def _():
        attend(False)

    @pl.when(step == last)
    def _():
        lane = lax.broadcasted_iota(jnp.int32, (tokens_here, 128), 1)
        for pair in range(HEADS // 2):
            outs = []
            for h in (2 * pair, 2 * pair + 1):
                rows = slice(h * tokens_here, (h + 1) * tokens_here)
                total = acc_ref[rows, 128:]
                out = acc_ref[rows, :128] / total
                if h // GROUP != h % 2:
                    out = jnp.concatenate([out[:, HEAD:], out[:, :HEAD]], 1)
                outs.append(out)
                log_total = top_ref[rows, :] + jnp.log(total)
                qext_ref[rows, 128:] = split_lanes(-log_total, (tokens_here, 128))
            att_ref[:, pair * 128 : (pair + 1) * 128] = jnp.where(
                lane < HEAD, outs[0], outs[1]
            ).astype(BF16)


def backward_kernel(
    by_xor, info_ref, qext_ref, do_ref, att_ref, kv_ref, dq_ref, dkv_ref, doext_ref, dqt_ref
):
    step = pl.program_id(0)
    last = pl.num_programs(0) - 1
    tokens_here = do_ref.shape[0]
    keys_here = kv_ref.shape[1]
    here = lax.axis_index("ctx")
    zed = lax.axis_index("fsdp")
    own = info_ref[here]
    block = info_ref[jnp.bitwise_xor(here, step) if by_xor else step]
    span = 2 * tokens_here

    @pl.when(step == 0)
    def _():
        for h in range(HEADS):
            rows = slice(h * tokens_here, (h + 1) * tokens_here)
            grad = cut_heads(do_ref, h)
            delta = jnp.sum(grad * cut_heads(att_ref, h), -1, keepdims=True)
            doext_ref[rows, :128] = grad.astype(BF16)
            doext_ref[rows, 128:] = split_lanes(-delta, (tokens_here, 128))
        dqt_ref[...] = jnp.zeros(dqt_ref.shape, F32)

    def attend(masked):
        lane = lax.broadcasted_iota(jnp.int32, (keys_here, 128), 1)
        ones = jnp.where(lane < 3, 1.0, 0.0).astype(BF16)
        keys = kv_ref[0, :, :128]
        keys_ext = jnp.concatenate([keys, ones], 1)
        values_ext = jnp.concatenate([kv_ref[0, :, 128:], ones], 1)
        keys_t = keys.astype(F32).T.astype(BF16)
        if masked:
            row = lax.broadcasted_iota(jnp.int32, (keys_here, tokens_here), 0)
            col = lax.broadcasted_iota(jnp.int32, (keys_here, tokens_here), 1)
            allowed = row + piece_shift(row, zed, tokens_here, keys_here) <= col
            allowed = allowed.astype(F32)
            allowed = jnp.concatenate([allowed, allowed], 1) > 0.5
        dk = jnp.zeros((keys_here, 128), F32)
        dv = jnp.zeros((keys_here, 128), F32)
        for pair in range(HEADS // 2):
            rows = slice(pair * span, (pair + 1) * span)
            probs = jnp.exp(times_transposed(keys_ext, qext_ref[rows, :]))
            if masked:
                probs = jnp.where(allowed, probs, 0.0)
            slope = (probs * times_transposed(values_ext, doext_ref[rows, :])).astype(BF16)
            dv = dv + matmul(probs.astype(BF16), doext_ref[rows, :128])
            dk = dk + matmul(slope, qext_ref[rows, :128])
            dqt_ref[pair] = dqt_ref[pair] + matmul(keys_t, slope)
        dkv_ref[0] = jnp.concatenate([dk, dv], 1).astype(BF16)

    @pl.when(block == own)
    def _():
        attend(True)

    @pl.when(block < own)
    def _():
        attend(False)

    @pl.when(block > own)
    def _():
        dkv_ref[...] = jnp.zeros(dkv_ref.shape, BF16)

    @pl.when(step == last)
    def _():
        lane = lax.broadcasted_iota(jnp.int32, (tokens_here, 128), 1)
        for pair in range(HEADS // 2):
            turned = dqt_ref[pair].T
            outs = []
            for j in range(2):
                h = 2 * pair + j
                out = turned[j * tokens_here : (j + 1) * tokens_here]
                if h // GROUP != j:
                    out = jnp.concatenate([out[:, HEAD:], out[:, :HEAD]], 1)
                outs.append(out)
            dq_ref[:, pair * 128 : (pair + 1) * 128] = (
                jnp.where(lane < HEAD, outs[0], outs[1]) * HEAD ** (-0.5)
            )


def whole_spec(shape):
    return pl.BlockSpec(shape, lambda i, info: (0,) * len(shape))


def attend_forward(info, by_xor, queries, kv):
    blocks, block_len, kv_width = kv.shape
    tokens_here, q_width = queries.shape
    rows = HEADS * tokens_here
    return pl.pallas_call(
        functools.partial(forward_kernel, by_xor),
        grid_spec=pltpu.PrefetchScalarGridSpec(
            num_scalar_prefetch=1,
            grid=(blocks,),
            in_specs=[
                whole_spec((tokens_here, q_width)),
                pl.BlockSpec((1, block_len, kv_width), lambda i, info: (i, 0, 0)),
            ],
            out_specs=[whole_spec((tokens_here, q_width)), whole_spec((rows, 256))],
            scratch_shapes=[pltpu.VMEM((rows, 128), F32), pltpu.VMEM((rows, 256), F32)],
        ),
        out_shape=[
            jax.ShapeDtypeStruct((tokens_here, q_width), BF16),
            jax.ShapeDtypeStruct((rows, 256), BF16),
        ],
        compiler_params=pltpu.CompilerParams(
            dimension_semantics=("arbitrary",), vmem_limit_bytes=40 * 2**20
        ),
        cost_estimate=NO_COST,
        name="attend_forward",
    )(info, queries, kv)


def attend_backward(info, by_xor, queries_ext, grad_att, attended, kv):
    blocks, block_len, kv_width = kv.shape
    tokens_here, q_width = grad_att.shape
    rows = HEADS * tokens_here
    return pl.pallas_call(
        functools.partial(backward_kernel, by_xor),
        grid_spec=pltpu.PrefetchScalarGridSpec(
            num_scalar_prefetch=1,
            grid=(blocks,),
            in_specs=[
                whole_spec((rows, 256)),
                whole_spec((tokens_here, q_width)),
                whole_spec((tokens_here, q_width)),
                pl.BlockSpec((1, block_len, kv_width), lambda i, info: (i, 0, 0)),
            ],
            out_specs=[
                whole_spec((tokens_here, q_width)),
                pl.BlockSpec((1, block_len, kv_width), lambda i, info: (i, 0, 0)),
            ],
            scratch_shapes=[
                pltpu.VMEM((rows, 256), BF16),
                pltpu.VMEM((HEADS // 2, 128, 2 * tokens_here), F32),
            ],
        ),
        out_shape=[
            jax.ShapeDtypeStruct((tokens_here, q_width), F32),
            jax.ShapeDtypeStruct(kv.shape, BF16),
        ],
        compiler_params=pltpu.CompilerParams(
            dimension_semantics=("arbitrary",), vmem_limit_bytes=40 * 2**20
        ),
        cost_estimate=NO_COST,
        name="attend_backward",
    )(info, queries_ext, grad_att, attended, kv)


def part_place(tp, j, k):
    at = jnp.bitwise_xor(lax.rem(lax.axis_index("ctx"), tp), k)
    return jnp.bitwise_xor(lax.axis_index("seq"), j) * tp + at


def spread_columns_kernel(n_z, *refs):
    pieces, outs, held = refs[:2], refs[2:-1], refs[-1]
    tp = pieces[0].shape[0]
    n_part = 2 * tp
    for j in range(2):
        for k in range(tp):
            held[part_place(tp, j, k)] = pieces[j][k].astype(F32)
    half = held.shape[2] // len(outs)
    pad = half // n_z
    for i, out in enumerate(outs):
        piece = out.shape[1] // (n_z * n_part)
        cuts = []
        for j in range(n_z):
            for e in range(n_part):
                start = i * half + j * pad
                cuts.append(held[e, :, start : start + piece])
        out[...] = jnp.concatenate(cuts, 1)


def spread_columns(pieces, n_z, ff, outs):
    tp, rows, cols = pieces[0].shape
    tile = 32
    return pl.pallas_call(
        functools.partial(spread_columns_kernel, n_z),
        grid=(rows // tile,),
        in_specs=[pl.BlockSpec((tp, tile, cols), lambda i: (0, i, 0))] * 2,
        out_specs=[pl.BlockSpec((tile, ff), lambda i: (i, 0))] * outs,
        scratch_shapes=[pltpu.VMEM((2 * tp, tile, cols), F32)],
        out_shape=[jax.ShapeDtypeStruct((rows, ff), F32)] * outs,
        compiler_params=pltpu.CompilerParams(
            dimension_semantics=("arbitrary",), vmem_limit_bytes=40 * 2**20
        ),
        cost_estimate=NO_COST,
        name="spread_columns",
    )(*pieces)


def spread_rows_kernel(piece, *refs):
    pieces, out_ref = refs[:-1], refs[-1]
    room = out_ref.shape[0] // piece
    tp = pieces[0].shape[0]
    for j in range(2):
        for k in range(tp):
            place = part_place(tp, j, k)

            @pl.when(place < room)
            def _():
                start = pl.multiple_of(place * piece, 8)
                out_ref[pl.ds(start, piece), :] = pieces[j][k].astype(F32)[:piece]


def spread_rows(pieces, piece, rows_out):
    tp, rows, cols = pieces[0].shape
    tile = 128
    return pl.pallas_call(
        functools.partial(spread_rows_kernel, piece),
        grid=(cols // tile,),
        in_specs=[pl.BlockSpec((tp, rows, tile), lambda i: (0, 0, i))] * 2,
        out_specs=pl.BlockSpec((rows_out, tile), lambda i: (0, i)),
        out_shape=jax.ShapeDtypeStruct((rows_out, cols), F32),
        compiler_params=pltpu.CompilerParams(
            dimension_semantics=("arbitrary",), vmem_limit_bytes=40 * 2**20
        ),
        cost_estimate=NO_COST,
        name="spread_rows",
    )(*pieces)


def join_weight(own_ref, sib_ref, out_ref):
    tp, n_z, part_rows = own_ref.shape[:3]
    room = out_ref.shape[1] // part_rows
    for j, ref in enumerate((own_ref, sib_ref)):
        for k in range(tp):
            place = part_place(tp, j, k)

            @pl.when(place < room)
            def _():
                start = pl.multiple_of(place * part_rows, 16)
                for z in range(n_z):
                    at = jnp.bitwise_xor(lax.axis_index("fsdp"), z)
                    out_ref[at, pl.ds(start, part_rows), :] = ref[k, z]


def whole_weight(ref):
    return jnp.concatenate([ref[z] for z in range(ref.shape[0])], 0)


def turn_tile(tile, cos, sin):
    h = HEAD // 2
    cuts = [tile[:, h : 2 * h], tile[:, :h], tile[:, 3 * h :], tile[:, 2 * h : 3 * h]]
    return tile * cos + jnp.concatenate(cuts, 1) * sin


def normed_rows(values, gain):
    inv = lax.rsqrt(jnp.mean(values * values, -1, keepdims=True) + NORM_EPS)
    return (values * inv * gain).astype(BF16)


def kv_kernel(widths, *refs):
    x_ref, cos_ref, sin_ref = refs[-8:-5]
    pieces, (out_ref, vec_ref, kv_ref, hid_ref, held) = refs[:-8], refs[-5:]
    n_z, rows_here, cols = out_ref.shape
    for k in range(n_z):
        at = jnp.bitwise_xor(lax.axis_index("fsdp"), k)
        out_ref[at] = pieces[k][:rows_here]
        held[at] = pieces[k][rows_here:].astype(F32)
    vec_ref[...] = jnp.zeros(vec_ref.shape, F32)
    for i, size in enumerate(widths):
        row = jnp.concatenate([held[z, i : i + 1, :size] for z in range(n_z)], 1)
        vec_ref[i : i + 1, : n_z * size] = row
    hidden = normed_rows(x_ref[...].astype(F32), vec_ref[0:1, :])
    hid_ref[...] = hidden
    half = cols // 2
    both = matmul(hidden, whole_weight(out_ref))
    keys = both[:, :half] + vec_ref[3:4, :half]
    kv_ref[:, :half] = turn_tile(keys, cos_ref[...], sin_ref[...]).astype(BF16)
    kv_ref[:, half:] = (both[:, half:] + vec_ref[4:5, :half]).astype(BF16)


def project_kv(pieces, tokens, cos, sin, rows_here, widths):
    rows, cols = pieces[0].shape
    n_z = len(pieces)
    vmem = pl.BlockSpec(memory_space=pltpu.VMEM)
    return pl.pallas_call(
        functools.partial(kv_kernel, widths),
        in_specs=[vmem] * (n_z + 3),
        out_specs=[vmem] * 4,
        out_shape=[
            jax.ShapeDtypeStruct((n_z, rows_here, cols), BF16),
            jax.ShapeDtypeStruct((8, n_z * rows_here), F32),
            jax.ShapeDtypeStruct((tokens.shape[0], cols), BF16),
            jax.ShapeDtypeStruct(tokens.shape, BF16),
        ],
        scratch_shapes=[pltpu.VMEM((n_z, rows - rows_here, cols), F32)],
        compiler_params=pltpu.CompilerParams(vmem_limit_bytes=40 * 2**20),
        cost_estimate=NO_COST,
        name="project_kv",
    )(*pieces, tokens, cos, sin)


def query_kernel(own_ref, sib_ref, hid_ref, vec_ref, cos_ref, sin_ref, out_ref, q_ref):
    join_weight(own_ref, sib_ref, out_ref)
    whole = matmul(hid_ref[...], whole_weight(out_ref)) + vec_ref[2:3, :]
    for pair in range(HEADS // 2):
        lanes = slice(pair * 128, (pair + 1) * 128)
        tile = turn_tile(whole[:, lanes], cos_ref[...], sin_ref[...]).astype(BF16)
        q_ref[:, lanes] = (tile.astype(F32) * HEAD ** (-0.5)).astype(BF16)


def project_query(own, sib, hidden, vecs, cos, sin, rows_here):
    n_z, cols = own.shape[1], own.shape[3]
    vmem = pl.BlockSpec(memory_space=pltpu.VMEM)
    return pl.pallas_call(
        query_kernel,
        in_specs=[vmem] * 6,
        out_specs=[vmem] * 2,
        out_shape=[
            jax.ShapeDtypeStruct((n_z, rows_here, cols), BF16),
            jax.ShapeDtypeStruct((hidden.shape[0], cols), BF16),
        ],
        compiler_params=pltpu.CompilerParams(vmem_limit_bytes=40 * 2**20),
        cost_estimate=NO_COST,
        name="project_query",
    )(own, sib, hidden, vecs, cos, sin)


def out_kernel(own_ref, sib_ref, att_ref, x_ref, vec_ref, out_ref, resid_ref, hid_ref):
    join_weight(own_ref, sib_ref, out_ref)
    resid = x_ref[...].astype(F32) + matmul(att_ref[...], whole_weight(out_ref))
    resid_ref[...] = resid
    hid_ref[...] = normed_rows(resid, vec_ref[1:2, :])


def project_out(own, sib, attended, tokens, vecs, rows_here):
    n_z, cols = own.shape[1], own.shape[3]
    vmem = pl.BlockSpec(memory_space=pltpu.VMEM)
    return pl.pallas_call(
        out_kernel,
        in_specs=[vmem] * 5,
        out_specs=[vmem] * 3,
        out_shape=[
            jax.ShapeDtypeStruct((n_z, rows_here, cols), BF16),
            jax.ShapeDtypeStruct(tokens.shape, F32),
            jax.ShapeDtypeStruct(tokens.shape, BF16),
        ],
        compiler_params=pltpu.CompilerParams(vmem_limit_bytes=40 * 2**20),
        cost_estimate=NO_COST,
        name="project_out",
    )(own, sib, attended, tokens, vecs)


def grad_weight_kernel(left_ref, right_ref, *refs):
    total = matmul(left_ref[...], right_ref[...])
    if len(refs) == 2:
        total = total + refs[0][...].astype(F32)
    refs[-1][...] = total.astype(BF16)


def grad_weight(left, right, other=None):
    rows, depth = left.shape
    cols = right.shape[1]
    tile = rows // 2 if rows % 32 == 0 else rows
    by_rows = lambda width: pl.BlockSpec((tile, width), lambda i: (i, 0))
    in_specs = [by_rows(depth), pl.BlockSpec((depth, cols), lambda i: (0, 0))]
    args = [left, right]
    if other is not None:
        in_specs.append(by_rows(cols))
        args.append(other)
    return pl.pallas_call(
        grad_weight_kernel,
        grid=(rows // tile,),
        in_specs=in_specs,
        out_specs=by_rows(cols),
        out_shape=jax.ShapeDtypeStruct((rows, cols), BF16),
        compiler_params=pltpu.CompilerParams(
            dimension_semantics=("arbitrary",), vmem_limit_bytes=40 * 2**20
        ),
        cost_estimate=NO_COST,
        name="grad_weight",
    )(*args)


def ff_kernel(tp, n_z, *refs):
    hidden, grads, weights = refs[:tp], refs[tp : 2 * tp], refs[2 * tp : 2 * tp + 4]
    rest = refs[2 * tp + 4 :]
    act_refs, back_refs, (hid_t, grad_all) = rest[:2], rest[2:4], rest[4:6]
    dh_outs, outs = rest[6 : 6 + tp], rest[6 + tp : 6 + 2 * tp]
    gu_buf, down_buf, acc, acc_out, sems = rest[6 + 2 * tp :]
    part_rows = weights[2].shape[1]
    gu_copies = [
        pltpu.make_async_copy(weights[i], gu_buf.at[i], sems.at[i]) for i in range(2)
    ]
    down_copies = []
    for i in range(2):
        for z in range(n_z):
            at = jnp.bitwise_xor(lax.axis_index("fsdp"), z) * part_rows
            to = down_buf.at[i, pl.ds(pl.multiple_of(at, 16), part_rows)]
            sem = sems.at[2 + i * n_z + z]
            down_copies.append(pltpu.make_async_copy(weights[2 + i].at[z], to, sem))
    gu_copies[0].start()
    for c in down_copies[:n_z]:
        c.start()
    gu_copies[1].start()
    for c in down_copies[n_z:]:
        c.start()
    tokens_here = hidden[0].shape[0]
    half = down_buf.shape[1]
    step = 2 if tp % 2 == 0 else 1
    for i in range(2):
        gu_copies[i].wait()
        for t in range(0, tp, step):
            rows = slice(t * tokens_here, (t + step) * tokens_here)
            here = jnp.concatenate([hidden[t + n][...] for n in range(step)], 0)
            grad = jnp.concatenate([grads[t + n][...] for n in range(step)], 0)
            if i == 0:
                hid_t[:, rows] = here.astype(F32).T.astype(BF16)
                grad_all[rows, :] = grad
            gate = matmul(here, gu_buf[i, :, :half])
            up = matmul(here, gu_buf[i, :, half:])
            if t == 0:
                for c in down_copies[i * n_z : (i + 1) * n_z]:
                    c.wait()
            grad_act = times_transposed(grad, down_buf[i])
            sig = 1.0 / (1.0 + jnp.exp(-gate))
            silu = gate * sig
            act = silu * up
            act_refs[i][:, rows] = act.T.astype(BF16)
            grad_gate = (grad_act * up * (sig + silu * (1.0 - sig))).astype(BF16)
            grad_up = (grad_act * silu).astype(BF16)
            back_refs[i][rows, :half] = grad_gate
            back_refs[i][rows, half:] = grad_up
            part = times_transposed(grad_gate, gu_buf[i, :, :half]) + times_transposed(
                grad_up, gu_buf[i, :, half:]
            )
            out = matmul(act.astype(BF16), down_buf[i])
            if i == 0:
                acc[rows, :] = part
                acc_out[rows, :] = out
            else:
                part = (part + acc[rows, :]).astype(BF16)
                out = (out + acc_out[rows, :]).astype(BF16)
                for n in range(step):
                    mine = slice(n * tokens_here, (n + 1) * tokens_here)
                    dh_outs[t + n][...] = part[mine]
                    outs[t + n][...] = out[mine]


def ff_pass(hidden, grads, gu, down):
    tp = len(hidden)
    n_z, part_rows = down[0].shape[:2]
    tokens_here, width = hidden[0].shape
    half = n_z * part_rows
    rows = tp * tokens_here
    vmem = pl.BlockSpec(memory_space=pltpu.VMEM)
    got = pl.pallas_call(
        functools.partial(ff_kernel, tp, n_z),
        in_specs=[vmem] * (2 * tp) + [pl.BlockSpec(memory_space=pl.ANY)] * 4,
        out_specs=[vmem] * (2 * tp + 6),
        out_shape=[jax.ShapeDtypeStruct((half, rows), BF16)] * 2
        + [jax.ShapeDtypeStruct((rows, 2 * half), BF16)] * 2
        + [jax.ShapeDtypeStruct((width, rows), BF16), jax.ShapeDtypeStruct((rows, width), BF16)]
        + [jax.ShapeDtypeStruct((tokens_here, width), BF16)] * (2 * tp),
        scratch_shapes=[
            pltpu.VMEM((2, width, 2 * half), BF16),
            pltpu.VMEM((2, half, width), BF16),
            pltpu.VMEM((rows, width), F32),
            pltpu.VMEM((rows, width), F32),
            pltpu.SemaphoreType.DMA((2 + 2 * n_z,)),
        ],
        compiler_params=pltpu.CompilerParams(vmem_limit_bytes=58 * 2**20),
        cost_estimate=NO_COST,
        name="ff_pass",
    )(*hidden, *grads, *gu, *down)
    return got[:2], got[2:4], got[4], got[5], got[6 : 6 + tp], got[6 + tp :]


def local(
    tokens,
    out_grad,
    block_order,
    norm1_gain,
    q_weight,
    q_bias,
    k_weight,
    k_bias,
    v_weight,
    v_bias,
    o_weight,
    norm2_gain,
    gate_weight,
    up_weight,
    down_weight,
):
    n_ctx = lax.axis_size("ctx")
    n_z = lax.axis_size("fsdp")
    tp = 4 if n_ctx % 4 == 0 else (2 if n_ctx % 2 == 0 else 1)
    here = lax.axis_index("ctx")
    zed = lax.axis_index("fsdp")
    core = lax.axis_index("seq")
    n_part = 2 * tp
    part = core * tp + lax.rem(here, tp)

    def swap(v):
        return lax.ppermute(v, "seq", [(0, 1), (1, 0)])

    def hop(v, k):
        if k == 0:
            return v
        return lax.ppermute(v, "ctx", [(i, i ^ k) for i in range(n_ctx)])

    def hop_z(v, k):
        if k == 0:
            return v
        return lax.ppermute(v, "fsdp", [(i, i ^ k) for i in range(n_z)])

    def gather_z(v):
        return lax.all_gather(v, "fsdp", axis=0, tiled=True)

    def scatter_z(v):
        return lax.psum_scatter(v, "fsdp", scatter_dimension=0, tiled=True)

    tokens_here, width = tokens.shape[1:]
    ff = gate_weight.shape[1]
    rows_here = q_weight.shape[0]
    key_width = KV_HEADS * HEAD
    block_len = tokens_here * n_z

    part_rows = -(-rows_here // (n_part * 32)) * 32

    kb = k_bias.shape[0]
    vectors = (norm1_gain, norm2_gain, q_bias, k_bias, v_bias)
    vec = sum(
        jnp.pad(v[None], ((i, 15 - i), (0, 2 * key_width - v.shape[0])))
        for i, v in enumerate(vectors)
    )
    kv_pack = jnp.concatenate([jnp.concatenate([k_weight, v_weight], 1), vec], 0)
    og_here = out_grad[0]

    def own_part(w):
        return lax.dynamic_slice_in_dim(w, part * part_rows, part_rows, 0)

    ff_z = ff // n_z
    piece = ff_z // n_part
    piece_pad = -(-piece // 32) * 32

    def ff_columns(w):
        cuts = []
        for j in range(n_z):
            cut = lax.dynamic_slice_in_dim(w, j * ff_z + part * piece, piece, 1)
            cuts.append(jnp.pad(cut, ((0, 0), (0, piece_pad - piece))))
        return jnp.concatenate(cuts, 1)

    order_row = block_order[0]
    x_here = tokens[0]
    kv_pack, q_part, o_part, gate_weight, up_weight, down_weight, query_at = (
        lax.optimization_barrier(
            (
                kv_pack,
                own_part(q_weight),
                own_part(o_weight),
                gate_weight,
                up_weight,
                down_weight,
                order_row[here] * block_len + zed * tokens_here,
            )
        )
    )
    kv_got = [hop_z(kv_pack, k) for k in range(n_z)]
    q_got = [hop_z(q_part, k) for k in range(n_z)]
    gu_cut = jnp.concatenate([ff_columns(gate_weight), ff_columns(up_weight)], 1)
    down_cut = lax.dynamic_slice_in_dim(down_weight, part * piece, piece, 0)
    down_cut = jnp.pad(down_cut, ((0, piece_pad - piece), (0, 0)))
    query_pos = query_at + jnp.arange(tokens_here, dtype=jnp.int32)
    cosine_table, sine_table = rope_tables(query_pos, HEAD)
    cos_wide = jnp.tile(cosine_table[:, 0], (1, 4))
    sin_wide = jnp.tile(jnp.concatenate([-sine_table[:, 0], sine_table[:, 0]], 1), (1, 2))
    kv_got, q_got, cos_wide, sin_wide, gu_cut, down_cut, o_part, og_here = (
        lax.optimization_barrier(
            (kv_got, q_got, cos_wide, sin_wide, gu_cut, down_cut, o_part, og_here)
        )
    )

    q_own = [hop(jnp.stack(q_got), k) for k in range(tp)]
    widths = tuple(v.shape[0] for v in vectors)
    w_kv, vecs, kv_local, hidden_one = project_kv(
        kv_got, x_here, cos_wide, sin_wide, rows_here, widths
    )
    w_kv = w_kv.reshape(width, 2 * key_width)
    gain_one = vecs[0:1, :width]
    gain_two = vecs[1:2, :width]
    kv_z = [hop_z(kv_local, k) for k in range(n_z)]
    kv_z, gu_cut, down_cut, o_part = lax.optimization_barrier((kv_z, gu_cut, down_cut, o_part))

    kv_block = jnp.concatenate(kv_z, 0)
    if n_ctx == tp:
        kv_blocks = [hop(kv_block, k) for k in range(n_ctx)]
    else:
        kv_blocks = lax.all_gather(kv_block, "ctx", axis=0, tiled=False)
    gu_own = gather_z(gu_cut)
    down_own = [hop_z(down_cut, k) for k in range(n_z)]
    o_got = [hop_z(o_part, k) for k in range(n_z)]
    q_own = jnp.stack(q_own)
    w_query, queries = project_query(
        q_own, swap(q_own), hidden_one, vecs, cos_wide, sin_wide, rows_here
    )
    w_query = w_query.reshape(width, width)
    kv_blocks, queries, o_got, og_here = lax.optimization_barrier(
        (kv_blocks, queries, o_got, og_here)
    )

    o_own = [hop(jnp.stack(o_got), k) for k in range(tp)]
    og_parts = [hop(og_here, k) for k in range(tp)]
    kv_whole = jnp.stack(kv_blocks) if n_ctx == tp else kv_blocks
    attended, queries_ext = attend_forward(order_row, n_ctx == tp, queries, kv_whole)
    attended, o_own, queries_ext, og_parts, down_own = lax.optimization_barrier(
        (attended, o_own, queries_ext, og_parts, down_own)
    )
    o_own = jnp.stack(o_own)
    w_out, resid, hidden_two = project_out(
        o_own, swap(o_own), attended, x_here, vecs, rows_here
    )
    w_out = w_out.reshape(width, width)
    h2_parts = [hop(hidden_two, k) for k in range(tp)]
    gu_oth = swap(gu_own)
    down_own = jnp.stack(down_own)
    down_oth = swap(down_own)

    acts, ggus, h2_turned, og_all, dh2, ff_out = ff_pass(
        h2_parts, og_parts, (gu_own, gu_oth), (down_own, down_oth)
    )
    grad_h2_parts = [hop(dh2[k], k) for k in range(tp)]

    def share_pieces(mine):
        own = jnp.stack([hop(mine, k) for k in range(tp)])
        return own, swap(own)

    def core_halves(part_sum):
        cols = part_sum.shape[1]
        cut = part_sum.astype(BF16).reshape(n_z, rows_here, cols)
        cut = jnp.pad(cut, ((0, 0), (0, n_part * part_rows - rows_here), (0, 0)))
        own = lax.dynamic_slice_in_dim(cut, core * tp * part_rows, tp * part_rows, 1)
        oth = lax.dynamic_slice_in_dim(cut, (1 - core) * tp * part_rows, tp * part_rows, 1)
        return own, oth

    def core_total(own, sib):
        return (own.astype(F32) + sib.astype(F32)).astype(BF16)

    def scatter_hops(cut):
        return [
            hop_z(lax.dynamic_index_in_dim(cut, zed ^ k, 0, keepdims=False), k)
            for k in range(n_z)
        ]

    def ctx_groups_sum(v):
        if n_ctx == tp:
            return v
        groups = [[g * tp + c for g in range(n_ctx // tp)] for c in range(tp)]
        return lax.psum(v, "ctx", axis_index_groups=groups)

    d_gu = grad_weight(h2_turned, ggus[0], swap(grad_weight(h2_turned, ggus[1])))
    d_down = grad_weight(acts[0], og_all, swap(grad_weight(acts[1], og_all)))
    grad_h2_parts, d_gu, d_down, ff_out = lax.optimization_barrier(
        (grad_h2_parts, d_gu, d_down, ff_out)
    )
    d_gu = scatter_z(d_gu)
    ff_out = [hop(ff_out[k], k) for k in range(tp)]
    d_down = d_down.reshape(n_z, piece_pad, width)
    d_down = [
        hop_z(lax.dynamic_index_in_dim(d_down, zed ^ k, 0, keepdims=False), k) for k in range(n_z)
    ]
    grad_h2 = sum(v.astype(F32) for v in grad_h2_parts)
    scale_two = lax.rsqrt(jnp.mean(resid * resid, -1, keepdims=True) + NORM_EPS)
    normed_two = resid * scale_two

    grad_norm_two, gain_two_terms = rms_backward(grad_h2, normed_two, scale_two, gain_two)
    grad_resid = og_here.astype(F32) + grad_norm_two
    grad_proj = grad_resid.astype(BF16)
    grad_att = times_transposed(grad_proj, w_out).astype(BF16)
    grad_queries, grad_terms = attend_backward(
        order_row, n_ctx == tp, queries_ext, grad_att, attended, kv_whole
    )
    grad_queries, grad_terms, ff_out, grad_proj = lax.optimization_barrier(
        (grad_queries, grad_terms, ff_out, grad_proj)
    )

    grad_q_pre = (
        rotate(grad_queries.reshape(tokens_here, HEADS, HEAD), cosine_table, -sine_table)
        .reshape(tokens_here, HEADS * HEAD)
        .astype(BF16)
    )
    qo_own, qo_oth = core_halves(
        jnp.concatenate(
            [contract_rows(hidden_one, grad_q_pre), contract_rows(attended, grad_proj)], 1
        )
    )
    if n_ctx == tp:
        kv_terms = [hop(grad_terms[k], k) for k in range(n_ctx)]
    else:
        kv_terms = [lax.psum_scatter(grad_terms, "ctx", scatter_dimension=0, tiled=False)]
    kv_terms, d_gu, d_down, qo_own, qo_oth, ff_out = lax.optimization_barrier(
        (kv_terms, d_gu, d_down, qo_own, qo_oth, ff_out)
    )

    kv_sum = sum(v.astype(F32) for v in kv_terms).astype(BF16)
    kv_sum = kv_sum.reshape(n_z, tokens_here, 2 * key_width)
    kv_terms = [hop_z(kv_sum[k], k) for k in range(n_z)]
    d_gu = ctx_groups_sum(d_gu)
    gu_pieces = [hop(d_gu, k) for k in range(tp)]
    qo_sib = swap(qo_oth)
    result = resid + sum(v.astype(F32) for v in ff_out)
    layer_out = result.astype(BF16)[None]
    kv_terms, qo_own, qo_sib, d_down = lax.optimization_barrier(
        (kv_terms, qo_own, qo_sib, d_down)
    )

    qo_cut = core_total(qo_own, qo_sib)
    qo_terms = scatter_hops(qo_cut)
    grad_kv = sum(v.astype(F32) for v in kv_terms)
    grad_k_pre = (
        rotate(
            grad_kv[:, :key_width].reshape(tokens_here, KV_HEADS, HEAD), cosine_table, -sine_table
        )
        .reshape(tokens_here, key_width)
        .astype(BF16)
    )
    grad_v_pre = grad_kv[:, key_width:].astype(BF16)
    grad_kv_pre = jnp.concatenate([grad_k_pre, grad_v_pre], 1)
    grad_hidden_one = times_transposed(grad_q_pre, w_query) + times_transposed(grad_kv_pre, w_kv)
    inputs = x_here.astype(F32)
    scale_one = lax.rsqrt(jnp.mean(inputs * inputs, -1, keepdims=True) + NORM_EPS)
    normed_one = inputs * scale_one
    grad_norm_one, gain_one_terms = rms_backward(grad_hidden_one, normed_one, scale_one, gain_one)
    tokens_grad = (grad_resid + grad_norm_one)[None]

    def by_rows(v):
        share = v.shape[1] // n_z
        v = v.reshape(tokens_here, n_z, share)
        return jnp.pad(v, ((0, 0), (0, 0), (0, rows_here - share))).reshape(tokens_here, width)

    terms = (gain_one_terms, gain_two_terms, grad_q_pre, by_rows(grad_k_pre), by_rows(grad_v_pre))
    pick = jnp.arange(len(terms) * tokens_here)[:, None] // tokens_here == jnp.arange(128)[None]
    columns = contract_rows(
        jnp.concatenate([v.astype(BF16) for v in terms], 0), pick.astype(BF16)
    )
    kv_own, kv_oth = core_halves(
        jnp.concatenate([contract_rows(hidden_one, grad_kv_pre), columns], 1)
    )
    kv_sib = swap(kv_oth)
    kv_own, kv_sib, gu_pieces, d_down = lax.optimization_barrier(
        (kv_own, kv_sib, gu_pieces, d_down)
    )

    kv_terms = scatter_hops(core_total(kv_own, kv_sib))
    d_down = ctx_groups_sum(sum(v.astype(F32) for v in d_down).astype(BF16))
    d_down = lax.optimization_barrier(d_down)
    down_pieces = [hop(d_down, k) for k in range(tp)]
    gu_pieces = jnp.stack(gu_pieces)
    gu_sib = swap(gu_pieces)
    qo_terms, kv_terms, down_pieces, gu_sib, gu_pieces = lax.optimization_barrier(
        (qo_terms, kv_terms, down_pieces, gu_sib, gu_pieces)
    )

    last = jnp.concatenate(
        [sum(v.astype(F32) for v in qo_terms), sum(v.astype(F32) for v in kv_terms)], 1
    ).astype(BF16)
    last = last.reshape(tp, part_rows, -1)
    at = lax.rem(here, tp)
    last = [hop(lax.dynamic_index_in_dim(last, at ^ k, 0, keepdims=False), k) for k in range(tp)]
    down_pieces = jnp.stack(down_pieces)
    down_sib = swap(down_pieces)
    grad_w_gate, grad_w_up = spread_columns((gu_pieces, gu_sib), n_z, ff, 2)
    last, down_sib, down_pieces, grad_w_gate, grad_w_up = lax.optimization_barrier(
        (last, down_sib, down_pieces, grad_w_gate, grad_w_up)
    )

    last = ctx_groups_sum(sum(v.astype(F32) for v in last).astype(BF16))
    last = lax.optimization_barrier(last)
    grad_w_down = spread_rows((down_pieces, down_sib), piece, ff_z)
    last = spread_rows(share_pieces(last), part_rows, rows_here)
    grad_w_query = last[:, :width]
    grad_w_out = last[:, width : 2 * width]
    grad_w_kv = last[:, 2 * width :]
    sums = grad_w_kv[:, 2 * key_width :]

    return (
        layer_out,
        tokens_grad,
        sums[:, 0],
        grad_w_query,
        sums[:, 2],
        grad_w_kv[:, :key_width],
        sums[:kb, 3],
        grad_w_kv[:, key_width : 2 * key_width],
        sums[:kb, 4],
        grad_w_out,
        sums[:, 1],
        grad_w_gate,
        grad_w_up,
        grad_w_down,
    )


def solution(mesh):
    in_specs = (
        P("seq", ("ctx", "fsdp"), None),
        P("seq", ("ctx", "fsdp"), None),
        P("seq", None),
        P("fsdp"),
        P("fsdp", None),
        P("fsdp"),
        P("fsdp", None),
        P("fsdp"),
        P("fsdp", None),
        P("fsdp"),
        P("fsdp", None),
        P("fsdp"),
        P("fsdp", None),
        P("fsdp", None),
        P("fsdp", None),
    )
    out_specs = (
        P("seq", ("ctx", "fsdp"), None),
        P("seq", ("ctx", "fsdp"), None),
        P("fsdp"),
        P("fsdp", None),
        P("fsdp"),
        P("fsdp", None),
        P("fsdp"),
        P("fsdp", None),
        P("fsdp"),
        P("fsdp", None),
        P("fsdp"),
        P("fsdp", None),
        P("fsdp", None),
        P("fsdp", None),
    )
    return jax.shard_map(local, mesh=mesh, in_specs=in_specs, out_specs=out_specs, check_vma=False)
```

```python
import functools
import math

import jax
import jax.numpy as jnp
from jax import lax
from jax.experimental import pallas as pl
from jax.experimental.pallas import tpu as pltpu
from jax.sharding import PartitionSpec as P

HEADS = 14
KV_HEADS = 2
HEAD = 64
GROUP = HEADS // KV_HEADS
NORM_EPS = 1e-06
ROPE_BASE = 1000000.0
MASKED = -1e30
BF16 = jnp.bfloat16
F32 = jnp.float32
NO_COST = pl.CostEstimate(flops=0, bytes_accessed=0, transcendentals=0)


def rope_tables(positions, head_dim):
    half_dim = head_dim // 2
    inverse = jnp.exp(
        jnp.arange(half_dim, dtype=jnp.float32) * (-math.log(ROPE_BASE) * 2.0 / head_dim)
    )
    angles = positions.astype(jnp.float32)[:, None] * inverse[None, :]
    return (jnp.cos(angles)[:, None, :], jnp.sin(angles)[:, None, :])


def rotate(values, cosine_table, sine_table):
    half_dim = values.shape[-1] // 2
    front_half = values[..., :half_dim]
    back_half = values[..., half_dim:]
    return jnp.concatenate(
        [
            front_half * cosine_table - back_half * sine_table,
            back_half * cosine_table + front_half * sine_table,
        ],
        -1,
    )


def matmul(left_side, right_side):
    return jnp.dot(left_side, right_side, preferred_element_type=F32)


def contract_rows(left_side, right_side):
    return lax.dot_general(
        left_side, right_side, (((0,), (0,)), ((), ())), preferred_element_type=F32
    )


def times_transposed(left_side, right_side):
    return lax.dot_general(
        left_side, right_side, (((1,), (1,)), ((), ())), preferred_element_type=F32
    )


def rms_backward(grad_out, normed, inv_scale, gain_vec):
    scaled = grad_out * gain_vec
    grad_in = inv_scale * (scaled - normed * jnp.mean(scaled * normed, -1, keepdims=True))
    return (grad_in, grad_out * normed)


def cut_heads(ref, head):
    tile = ref[:, (head // 2) * 128 : (head // 2 + 1) * 128].astype(F32)
    group = head // GROUP
    if head % 2 != group:
        tile = jnp.concatenate([tile[:, HEAD:], tile[:, :HEAD]], 1)
    lane = lax.broadcasted_iota(jnp.int32, tile.shape, 1)
    return jnp.where((lane >= HEAD) if group else (lane < HEAD), tile, 0.0)


def split_lanes(column, shape):
    high = column.astype(BF16).astype(F32)
    mid = (column - high).astype(BF16).astype(F32)
    low = column - high - mid
    lane = lax.broadcasted_iota(jnp.int32, shape, 1)
    return jnp.where(
        lane == 0, high, jnp.where(lane == 1, mid, jnp.where(lane == 2, low, 0.0))
    ).astype(BF16)


def piece_shift(at, zed, tokens_here, keys_here):
    pieces = keys_here // tokens_here
    shift = jnp.zeros(at.shape, jnp.int32)
    for k in range(pieces):
        here = (jnp.bitwise_xor(zed, k) - k - zed) * tokens_here
        shift = jnp.where(at >= k * tokens_here, here, shift)
    return shift


def forward_kernel(by_xor, info_ref, q_ref, kv_ref, att_ref, qext_ref, top_ref, acc_ref):
    step = pl.program_id(0)
    last = pl.num_programs(0) - 1
    tokens_here = q_ref.shape[0]
    keys_here = kv_ref.shape[1]
    here = lax.axis_index("ctx")
    zed = lax.axis_index("fsdp")
    own = info_ref[here]
    block = info_ref[jnp.bitwise_xor(here, step) if by_xor else step]

    @pl.when(step == 0)
    def _():
        for h in range(HEADS):
            qext_ref[h * tokens_here : (h + 1) * tokens_here, :128] = cut_heads(q_ref, h).astype(
                BF16
            )
        top_ref[...] = jnp.full(top_ref.shape, MASKED, F32)
        acc_ref[...] = jnp.zeros(acc_ref.shape, F32)

    def attend(masked):
        keys = kv_ref[0, :, :128]
        values = jnp.concatenate(
            [kv_ref[0, :, 128:], jnp.ones((keys_here, 128), BF16)], 1
        )
        if masked:
            row = lax.broadcasted_iota(jnp.int32, (tokens_here, keys_here), 0)
            col = lax.broadcasted_iota(jnp.int32, (tokens_here, keys_here), 1)
            allowed = col + piece_shift(col, zed, tokens_here, keys_here) <= row
        for h in range(HEADS):
            rows = slice(h * tokens_here, (h + 1) * tokens_here)
            scores = times_transposed(qext_ref[rows, :128], keys)
            if masked:
                scores = jnp.where(allowed, scores, MASKED)
            old = top_ref[rows, :]
            top = jnp.maximum(old, jnp.max(scores, -1, keepdims=True))
            probs = jnp.exp(scores - top[:, :1]).astype(BF16)
            shrink = jnp.exp(old - top)
            top_ref[rows, :] = top
            acc_ref[rows, :] = acc_ref[rows, :] * jnp.concatenate([shrink, shrink], 1) + matmul(
                probs, values
            )

    @pl.when(block == own)
    def _():
        attend(True)

    @pl.when(block < own)
    def _():
        attend(False)

    @pl.when(step == last)
    def _():
        lane = lax.broadcasted_iota(jnp.int32, (tokens_here, 128), 1)
        for pair in range(HEADS // 2):
            outs = []
            for h in (2 * pair, 2 * pair + 1):
                rows = slice(h * tokens_here, (h + 1) * tokens_here)
                total = acc_ref[rows, 128:]
                out = acc_ref[rows, :128] / total
                if h // GROUP != h % 2:
                    out = jnp.concatenate([out[:, HEAD:], out[:, :HEAD]], 1)
                outs.append(out)
                log_total = top_ref[rows, :] + jnp.log(total)
                qext_ref[rows, 128:] = split_lanes(-log_total, (tokens_here, 128))
            att_ref[:, pair * 128 : (pair + 1) * 128] = jnp.where(
                lane < HEAD, outs[0], outs[1]
            ).astype(BF16)


def backward_kernel(
    by_xor, info_ref, qext_ref, do_ref, att_ref, kv_ref, dq_ref, dkv_ref, doext_ref, dqt_ref
):
    step = pl.program_id(0)
    last = pl.num_programs(0) - 1
    tokens_here = do_ref.shape[0]
    keys_here = kv_ref.shape[1]
    here = lax.axis_index("ctx")
    zed = lax.axis_index("fsdp")
    own = info_ref[here]
    block = info_ref[jnp.bitwise_xor(here, step) if by_xor else step]
    span = 2 * tokens_here

    @pl.when(step == 0)
    def _():
        for h in range(HEADS):
            rows = slice(h * tokens_here, (h + 1) * tokens_here)
            grad = cut_heads(do_ref, h)
            delta = jnp.sum(grad * cut_heads(att_ref, h), -1, keepdims=True)
            doext_ref[rows, :128] = grad.astype(BF16)
            doext_ref[rows, 128:] = split_lanes(-delta, (tokens_here, 128))
        dqt_ref[...] = jnp.zeros(dqt_ref.shape, F32)

    def attend(masked):
        lane = lax.broadcasted_iota(jnp.int32, (keys_here, 128), 1)
        ones = jnp.where(lane < 3, 1.0, 0.0).astype(BF16)
        keys = kv_ref[0, :, :128]
        keys_ext = jnp.concatenate([keys, ones], 1)
        values_ext = jnp.concatenate([kv_ref[0, :, 128:], ones], 1)
        keys_t = keys.astype(F32).T.astype(BF16)
        if masked:
            row = lax.broadcasted_iota(jnp.int32, (keys_here, tokens_here), 0)
            col = lax.broadcasted_iota(jnp.int32, (keys_here, tokens_here), 1)
            allowed = row + piece_shift(row, zed, tokens_here, keys_here) <= col
            allowed = allowed.astype(F32)
            allowed = jnp.concatenate([allowed, allowed], 1) > 0.5
        dk = jnp.zeros((keys_here, 128), F32)
        dv = jnp.zeros((keys_here, 128), F32)
        for pair in range(HEADS // 2):
            rows = slice(pair * span, (pair + 1) * span)
            probs = jnp.exp(times_transposed(keys_ext, qext_ref[rows, :]))
            if masked:
                probs = jnp.where(allowed, probs, 0.0)
            slope = (probs * times_transposed(values_ext, doext_ref[rows, :])).astype(BF16)
            dv = dv + matmul(probs.astype(BF16), doext_ref[rows, :128])
            dk = dk + matmul(slope, qext_ref[rows, :128])
            dqt_ref[pair] = dqt_ref[pair] + matmul(keys_t, slope)
        dkv_ref[0] = jnp.concatenate([dk, dv], 1).astype(BF16)

    @pl.when(block == own)
    def _():
        attend(True)

    @pl.when(block < own)
    def _():
        attend(False)

    @pl.when(block > own)
    def _():
        dkv_ref[...] = jnp.zeros(dkv_ref.shape, BF16)

    @pl.when(step == last)
    def _():
        lane = lax.broadcasted_iota(jnp.int32, (tokens_here, 128), 1)
        for pair in range(HEADS // 2):
            turned = dqt_ref[pair].T
            outs = []
            for j in range(2):
                h = 2 * pair + j
                out = turned[j * tokens_here : (j + 1) * tokens_here]
                if h // GROUP != j:
                    out = jnp.concatenate([out[:, HEAD:], out[:, :HEAD]], 1)
                outs.append(out)
            dq_ref[:, pair * 128 : (pair + 1) * 128] = (
                jnp.where(lane < HEAD, outs[0], outs[1]) * HEAD ** (-0.5)
            )


def whole_spec(shape):
    return pl.BlockSpec(shape, lambda i, info: (0,) * len(shape))


def attend_forward(info, by_xor, queries, kv):
    blocks, block_len, kv_width = kv.shape
    tokens_here, q_width = queries.shape
    rows = HEADS * tokens_here
    return pl.pallas_call(
        functools.partial(forward_kernel, by_xor),
        grid_spec=pltpu.PrefetchScalarGridSpec(
            num_scalar_prefetch=1,
            grid=(blocks,),
            in_specs=[
                whole_spec((tokens_here, q_width)),
                pl.BlockSpec((1, block_len, kv_width), lambda i, info: (i, 0, 0)),
            ],
            out_specs=[whole_spec((tokens_here, q_width)), whole_spec((rows, 256))],
            scratch_shapes=[pltpu.VMEM((rows, 128), F32), pltpu.VMEM((rows, 256), F32)],
        ),
        out_shape=[
            jax.ShapeDtypeStruct((tokens_here, q_width), BF16),
            jax.ShapeDtypeStruct((rows, 256), BF16),
        ],
        compiler_params=pltpu.CompilerParams(
            dimension_semantics=("arbitrary",), vmem_limit_bytes=40 * 2**20
        ),
        cost_estimate=pl.CostEstimate(
            flops=3 * 10**10, bytes_accessed=2**23, transcendentals=0
        ),
        name="attend_forward",
    )(info, queries, kv)


def attend_backward(info, by_xor, queries_ext, grad_att, attended, kv):
    blocks, block_len, kv_width = kv.shape
    tokens_here, q_width = grad_att.shape
    rows = HEADS * tokens_here
    return pl.pallas_call(
        functools.partial(backward_kernel, by_xor),
        grid_spec=pltpu.PrefetchScalarGridSpec(
            num_scalar_prefetch=1,
            grid=(blocks,),
            in_specs=[
                whole_spec((rows, 256)),
                whole_spec((tokens_here, q_width)),
                whole_spec((tokens_here, q_width)),
                pl.BlockSpec((1, block_len, kv_width), lambda i, info: (i, 0, 0)),
            ],
            out_specs=[
                whole_spec((tokens_here, q_width)),
                pl.BlockSpec((1, block_len, kv_width), lambda i, info: (i, 0, 0)),
            ],
            scratch_shapes=[
                pltpu.VMEM((rows, 256), BF16),
                pltpu.VMEM((HEADS // 2, 128, 2 * tokens_here), F32),
            ],
        ),
        out_shape=[
            jax.ShapeDtypeStruct((tokens_here, q_width), F32),
            jax.ShapeDtypeStruct(kv.shape, BF16),
        ],
        compiler_params=pltpu.CompilerParams(
            dimension_semantics=("arbitrary",), vmem_limit_bytes=40 * 2**20
        ),
        cost_estimate=pl.CostEstimate(
            flops=5 * 10**10, bytes_accessed=2**23, transcendentals=0
        ),
        name="attend_backward",
    )(info, queries_ext, grad_att, attended, kv)


def part_place(tp, j, k):
    at = jnp.bitwise_xor(lax.rem(lax.axis_index("ctx"), tp), k)
    return jnp.bitwise_xor(lax.axis_index("seq"), j) * tp + at


def spread_columns_kernel(n_z, *refs):
    pieces, outs, held = refs[:2], refs[2:-1], refs[-1]
    tp = pieces[0].shape[0]
    n_part = 2 * tp
    for j in range(2):
        for k in range(tp):
            held[part_place(tp, j, k)] = pieces[j][k].astype(F32)
    half = held.shape[2] // len(outs)
    pad = half // n_z
    for i, out in enumerate(outs):
        piece = out.shape[1] // (n_z * n_part)
        cuts = []
        for j in range(n_z):
            for e in range(n_part):
                start = i * half + j * pad
                cuts.append(held[e, :, start : start + piece])
        out[...] = jnp.concatenate(cuts, 1)


def spread_columns(pieces, n_z, ff, outs):
    tp, rows, cols = pieces[0].shape
    tile = 32
    return pl.pallas_call(
        functools.partial(spread_columns_kernel, n_z),
        grid=(rows // tile,),
        in_specs=[pl.BlockSpec((tp, tile, cols), lambda i: (0, i, 0))] * 2,
        out_specs=[pl.BlockSpec((tile, ff), lambda i: (i, 0))] * outs,
        scratch_shapes=[pltpu.VMEM((2 * tp, tile, cols), F32)],
        out_shape=[jax.ShapeDtypeStruct((rows, ff), F32)] * outs,
        compiler_params=pltpu.CompilerParams(
            dimension_semantics=("arbitrary",), vmem_limit_bytes=40 * 2**20
        ),
        cost_estimate=NO_COST,
        name="spread_columns",
    )(*pieces)


def spread_rows_kernel(piece, *refs):
    pieces, out_ref = refs[:-1], refs[-1]
    room = out_ref.shape[0] // piece
    tp = pieces[0].shape[0]
    for j in range(2):
        for k in range(tp):
            place = part_place(tp, j, k)

            @pl.when(place < room)
            def _():
                start = pl.multiple_of(place * piece, 8)
                out_ref[pl.ds(start, piece), :] = pieces[j][k].astype(F32)[:piece]


def spread_rows(pieces, piece, rows_out):
    tp, rows, cols = pieces[0].shape
    tile = 128
    return pl.pallas_call(
        functools.partial(spread_rows_kernel, piece),
        grid=(cols // tile,),
        in_specs=[pl.BlockSpec((tp, rows, tile), lambda i: (0, 0, i))] * 2,
        out_specs=pl.BlockSpec((rows_out, tile), lambda i: (0, i)),
        out_shape=jax.ShapeDtypeStruct((rows_out, cols), F32),
        compiler_params=pltpu.CompilerParams(
            dimension_semantics=("arbitrary",), vmem_limit_bytes=40 * 2**20
        ),
        cost_estimate=NO_COST,
        name="spread_rows",
    )(*pieces)


def join_weight(own_ref, sib_ref, out_ref):
    tp, n_z, part_rows = own_ref.shape[:3]
    room = out_ref.shape[1] // part_rows
    for j, ref in enumerate((own_ref, sib_ref)):
        for k in range(tp):
            place = part_place(tp, j, k)

            @pl.when(place < room)
            def _():
                start = pl.multiple_of(place * part_rows, 16)
                for z in range(n_z):
                    at = jnp.bitwise_xor(lax.axis_index("fsdp"), z)
                    out_ref[at, pl.ds(start, part_rows), :] = ref[k, z]


def whole_weight(ref):
    return jnp.concatenate([ref[z] for z in range(ref.shape[0])], 0)


def turn_tile(tile, cos, sin):
    h = HEAD // 2
    cuts = [tile[:, h : 2 * h], tile[:, :h], tile[:, 3 * h :], tile[:, 2 * h : 3 * h]]
    return tile * cos + jnp.concatenate(cuts, 1) * sin


def normed_rows(values, gain):
    inv = lax.rsqrt(jnp.mean(values * values, -1, keepdims=True) + NORM_EPS)
    return (values * inv * gain).astype(BF16)


def kv_kernel(widths, *refs):
    x_ref, cos_ref, sin_ref = refs[-8:-5]
    pieces, (out_ref, vec_ref, kv_ref, hid_ref, held) = refs[:-8], refs[-5:]
    n_z, rows_here, cols = out_ref.shape
    for k in range(n_z):
        at = jnp.bitwise_xor(lax.axis_index("fsdp"), k)
        out_ref[at] = pieces[k][:rows_here]
        held[at] = pieces[k][rows_here:].astype(F32)
    vec_ref[...] = jnp.zeros(vec_ref.shape, F32)
    for i, size in enumerate(widths):
        row = jnp.concatenate([held[z, i : i + 1, :size] for z in range(n_z)], 1)
        vec_ref[i : i + 1, : n_z * size] = row
    hidden = normed_rows(x_ref[...].astype(F32), vec_ref[0:1, :])
    hid_ref[...] = hidden
    half = cols // 2
    both = matmul(hidden, whole_weight(out_ref))
    keys = both[:, :half] + vec_ref[3:4, :half]
    kv_ref[:, :half] = turn_tile(keys, cos_ref[...], sin_ref[...]).astype(BF16)
    kv_ref[:, half:] = (both[:, half:] + vec_ref[4:5, :half]).astype(BF16)


def project_kv(pieces, tokens, cos, sin, rows_here, widths):
    rows, cols = pieces[0].shape
    n_z = len(pieces)
    vmem = pl.BlockSpec(memory_space=pltpu.VMEM)
    return pl.pallas_call(
        functools.partial(kv_kernel, widths),
        in_specs=[vmem] * (n_z + 3),
        out_specs=[vmem] * 4,
        out_shape=[
            jax.ShapeDtypeStruct((n_z, rows_here, cols), BF16),
            jax.ShapeDtypeStruct((8, n_z * rows_here), F32),
            jax.ShapeDtypeStruct((tokens.shape[0], cols), BF16),
            jax.ShapeDtypeStruct(tokens.shape, BF16),
        ],
        scratch_shapes=[pltpu.VMEM((n_z, rows - rows_here, cols), F32)],
        compiler_params=pltpu.CompilerParams(vmem_limit_bytes=40 * 2**20),
        cost_estimate=NO_COST,
        name="project_kv",
    )(*pieces, tokens, cos, sin)


def query_kernel(own_ref, sib_ref, hid_ref, vec_ref, cos_ref, sin_ref, out_ref, q_ref):
    join_weight(own_ref, sib_ref, out_ref)
    whole = matmul(hid_ref[...], whole_weight(out_ref)) + vec_ref[2:3, :]
    for pair in range(HEADS // 2):
        lanes = slice(pair * 128, (pair + 1) * 128)
        tile = turn_tile(whole[:, lanes], cos_ref[...], sin_ref[...]).astype(BF16)
        q_ref[:, lanes] = (tile.astype(F32) * HEAD ** (-0.5)).astype(BF16)


def project_query(own, sib, hidden, vecs, cos, sin, rows_here):
    n_z, cols = own.shape[1], own.shape[3]
    vmem = pl.BlockSpec(memory_space=pltpu.VMEM)
    return pl.pallas_call(
        query_kernel,
        in_specs=[vmem] * 6,
        out_specs=[vmem] * 2,
        out_shape=[
            jax.ShapeDtypeStruct((n_z, rows_here, cols), BF16),
            jax.ShapeDtypeStruct((hidden.shape[0], cols), BF16),
        ],
        compiler_params=pltpu.CompilerParams(vmem_limit_bytes=40 * 2**20),
        cost_estimate=NO_COST,
        name="project_query",
    )(own, sib, hidden, vecs, cos, sin)


def out_kernel(own_ref, sib_ref, att_ref, x_ref, vec_ref, out_ref, resid_ref, hid_ref):
    join_weight(own_ref, sib_ref, out_ref)
    resid = x_ref[...].astype(F32) + matmul(att_ref[...], whole_weight(out_ref))
    resid_ref[...] = resid
    hid_ref[...] = normed_rows(resid, vec_ref[1:2, :])


def project_out(own, sib, attended, tokens, vecs, rows_here):
    n_z, cols = own.shape[1], own.shape[3]
    vmem = pl.BlockSpec(memory_space=pltpu.VMEM)
    return pl.pallas_call(
        out_kernel,
        in_specs=[vmem] * 5,
        out_specs=[vmem] * 3,
        out_shape=[
            jax.ShapeDtypeStruct((n_z, rows_here, cols), BF16),
            jax.ShapeDtypeStruct(tokens.shape, F32),
            jax.ShapeDtypeStruct(tokens.shape, BF16),
        ],
        compiler_params=pltpu.CompilerParams(vmem_limit_bytes=40 * 2**20),
        cost_estimate=NO_COST,
        name="project_out",
    )(own, sib, attended, tokens, vecs)


def grad_weight_kernel(left_ref, right_ref, *refs):
    total = matmul(left_ref[...], right_ref[...])
    if len(refs) == 2:
        total = total + refs[0][...].astype(F32)
    refs[-1][...] = total.astype(BF16)


def grad_weight(left, right, other=None):
    rows, depth = left.shape
    cols = right.shape[1]
    tile = rows // 2 if rows % 32 == 0 else rows
    by_rows = lambda width: pl.BlockSpec((tile, width), lambda i: (i, 0))
    in_specs = [by_rows(depth), pl.BlockSpec((depth, cols), lambda i: (0, 0))]
    args = [left, right]
    if other is not None:
        in_specs.append(by_rows(cols))
        args.append(other)
    return pl.pallas_call(
        grad_weight_kernel,
        grid=(rows // tile,),
        in_specs=in_specs,
        out_specs=by_rows(cols),
        out_shape=jax.ShapeDtypeStruct((rows, cols), BF16),
        compiler_params=pltpu.CompilerParams(
            dimension_semantics=("arbitrary",), vmem_limit_bytes=40 * 2**20
        ),
        cost_estimate=NO_COST,
        name="grad_weight",
    )(*args)


def ff_kernel(tp, n_z, *refs):
    hidden, grads, weights = refs[:tp], refs[tp : 2 * tp], refs[2 * tp : 2 * tp + 4]
    rest = refs[2 * tp + 4 :]
    act_refs, back_refs, (hid_t, grad_all) = rest[:2], rest[2:4], rest[4:6]
    dh_outs, outs = rest[6 : 6 + tp], rest[6 + tp : 6 + 2 * tp]
    gu_buf, down_buf, acc, acc_out, sems = rest[6 + 2 * tp :]
    part_rows = weights[2].shape[1]
    gu_copies = [
        pltpu.make_async_copy(weights[i], gu_buf.at[i], sems.at[i]) for i in range(2)
    ]
    down_copies = []
    for i in range(2):
        for z in range(n_z):
            at = jnp.bitwise_xor(lax.axis_index("fsdp"), z) * part_rows
            to = down_buf.at[i, pl.ds(pl.multiple_of(at, 16), part_rows)]
            sem = sems.at[2 + i * n_z + z]
            down_copies.append(pltpu.make_async_copy(weights[2 + i].at[z], to, sem))
    gu_copies[0].start()
    for c in down_copies[:n_z]:
        c.start()
    gu_copies[1].start()
    for c in down_copies[n_z:]:
        c.start()
    tokens_here = hidden[0].shape[0]
    half = down_buf.shape[1]
    step = 2 if tp % 2 == 0 else 1
    for i in range(2):
        gu_copies[i].wait()
        for t in range(0, tp, step):
            rows = slice(t * tokens_here, (t + step) * tokens_here)
            here = jnp.concatenate([hidden[t + n][...] for n in range(step)], 0)
            grad = jnp.concatenate([grads[t + n][...] for n in range(step)], 0)
            if i == 0:
                hid_t[:, rows] = here.astype(F32).T.astype(BF16)
                grad_all[rows, :] = grad
            gate = matmul(here, gu_buf[i, :, :half])
            up = matmul(here, gu_buf[i, :, half:])
            if t == 0:
                for c in down_copies[i * n_z : (i + 1) * n_z]:
                    c.wait()
            grad_act = times_transposed(grad, down_buf[i])
            sig = 1.0 / (1.0 + jnp.exp(-gate))
            silu = gate * sig
            act = silu * up
            act_refs[i][:, rows] = act.T.astype(BF16)
            grad_gate = (grad_act * up * (sig + silu * (1.0 - sig))).astype(BF16)
            grad_up = (grad_act * silu).astype(BF16)
            back_refs[i][rows, :half] = grad_gate
            back_refs[i][rows, half:] = grad_up
            part = times_transposed(grad_gate, gu_buf[i, :, :half]) + times_transposed(
                grad_up, gu_buf[i, :, half:]
            )
            out = matmul(act.astype(BF16), down_buf[i])
            if i == 0:
                acc[rows, :] = part
                acc_out[rows, :] = out
            else:
                part = (part + acc[rows, :]).astype(BF16)
                out = (out + acc_out[rows, :]).astype(BF16)
                for n in range(step):
                    mine = slice(n * tokens_here, (n + 1) * tokens_here)
                    dh_outs[t + n][...] = part[mine]
                    outs[t + n][...] = out[mine]


def ff_pass(hidden, grads, gu, down):
    tp = len(hidden)
    n_z, part_rows = down[0].shape[:2]
    tokens_here, width = hidden[0].shape
    half = n_z * part_rows
    rows = tp * tokens_here
    vmem = pl.BlockSpec(memory_space=pltpu.VMEM)
    got = pl.pallas_call(
        functools.partial(ff_kernel, tp, n_z),
        in_specs=[vmem] * (2 * tp) + [pl.BlockSpec(memory_space=pl.ANY)] * 4,
        out_specs=[vmem] * (2 * tp + 6),
        out_shape=[jax.ShapeDtypeStruct((half, rows), BF16)] * 2
        + [jax.ShapeDtypeStruct((rows, 2 * half), BF16)] * 2
        + [jax.ShapeDtypeStruct((width, rows), BF16), jax.ShapeDtypeStruct((rows, width), BF16)]
        + [jax.ShapeDtypeStruct((tokens_here, width), BF16)] * (2 * tp),
        scratch_shapes=[
            pltpu.VMEM((2, width, 2 * half), BF16),
            pltpu.VMEM((2, half, width), BF16),
            pltpu.VMEM((rows, width), F32),
            pltpu.VMEM((rows, width), F32),
            pltpu.SemaphoreType.DMA((2 + 2 * n_z,)),
        ],
        compiler_params=pltpu.CompilerParams(vmem_limit_bytes=58 * 2**20),
        cost_estimate=NO_COST,
        name="ff_pass",
    )(*hidden, *grads, *gu, *down)
    return got[:2], got[2:4], got[4], got[5], got[6 : 6 + tp], got[6 + tp :]


def local(
    tokens,
    out_grad,
    block_order,
    norm1_gain,
    q_weight,
    q_bias,
    k_weight,
    k_bias,
    v_weight,
    v_bias,
    o_weight,
    norm2_gain,
    gate_weight,
    up_weight,
    down_weight,
):
    n_ctx = lax.axis_size("ctx")
    n_z = lax.axis_size("fsdp")
    tp = 4 if n_ctx % 4 == 0 else (2 if n_ctx % 2 == 0 else 1)
    here = lax.axis_index("ctx")
    zed = lax.axis_index("fsdp")
    core = lax.axis_index("seq")
    n_part = 2 * tp
    part = core * tp + lax.rem(here, tp)

    def swap(v):
        return lax.ppermute(v, "seq", [(0, 1), (1, 0)])

    def hop(v, k):
        if k == 0:
            return v
        return lax.ppermute(v, "ctx", [(i, i ^ k) for i in range(n_ctx)])

    def hop_z(v, k):
        if k == 0:
            return v
        return lax.ppermute(v, "fsdp", [(i, i ^ k) for i in range(n_z)])

    def gather_z(v):
        return lax.all_gather(v, "fsdp", axis=0, tiled=True)

    def scatter_z(v):
        return lax.psum_scatter(v, "fsdp", scatter_dimension=0, tiled=True)

    tokens_here, width = tokens.shape[1:]
    ff = gate_weight.shape[1]
    rows_here = q_weight.shape[0]
    key_width = KV_HEADS * HEAD
    block_len = tokens_here * n_z

    part_rows = -(-rows_here // (n_part * 32)) * 32

    kb = k_bias.shape[0]
    vectors = (norm1_gain, norm2_gain, q_bias, k_bias, v_bias)
    vec = sum(
        jnp.pad(v[None], ((i, 15 - i), (0, 2 * key_width - v.shape[0])))
        for i, v in enumerate(vectors)
    )
    kv_pack = jnp.concatenate([jnp.concatenate([k_weight, v_weight], 1), vec], 0)
    og_here = out_grad[0]

    def own_part(w):
        return lax.dynamic_slice_in_dim(w, part * part_rows, part_rows, 0)

    ff_z = ff // n_z
    piece = ff_z // n_part
    piece_pad = -(-piece // 32) * 32

    def ff_columns(w):
        cuts = []
        for j in range(n_z):
            cut = lax.dynamic_slice_in_dim(w, j * ff_z + part * piece, piece, 1)
            cuts.append(jnp.pad(cut, ((0, 0), (0, piece_pad - piece))))
        return jnp.concatenate(cuts, 1)

    order_row = block_order[0]
    x_here = tokens[0]
    kv_pack, q_part, o_part, gate_weight, up_weight, down_weight, query_at = (
        lax.optimization_barrier(
            (
                kv_pack,
                own_part(q_weight),
                own_part(o_weight),
                gate_weight,
                up_weight,
                down_weight,
                order_row[here] * block_len + zed * tokens_here,
            )
        )
    )
    kv_got = [hop_z(kv_pack, k) for k in range(n_z)]
    q_got = [hop_z(q_part, k) for k in range(n_z)]
    o_got = [hop_z(o_part, k) for k in range(n_z)]
    gu_cut = jnp.concatenate([ff_columns(gate_weight), ff_columns(up_weight)], 1)
    down_cut = lax.dynamic_slice_in_dim(down_weight, part * piece, piece, 0)
    down_cut = jnp.pad(down_cut, ((0, piece_pad - piece), (0, 0)))
    query_pos = query_at + jnp.arange(tokens_here, dtype=jnp.int32)
    cosine_table, sine_table = rope_tables(query_pos, HEAD)
    cos_wide = jnp.tile(cosine_table[:, 0], (1, 4))
    sin_wide = jnp.tile(jnp.concatenate([-sine_table[:, 0], sine_table[:, 0]], 1), (1, 2))
    kv_got, q_got, cos_wide, sin_wide, gu_cut, down_cut, o_got, og_here = (
        lax.optimization_barrier(
            (kv_got, q_got, cos_wide, sin_wide, gu_cut, down_cut, o_got, og_here)
        )
    )

    q_own = [hop(jnp.stack(q_got), k) for k in range(tp)]
    widths = tuple(v.shape[0] for v in vectors)
    w_kv, vecs, kv_local, hidden_one = project_kv(
        kv_got, x_here, cos_wide, sin_wide, rows_here, widths
    )
    w_kv = w_kv.reshape(width, 2 * key_width)
    gain_one = vecs[0:1, :width]
    gain_two = vecs[1:2, :width]
    kv_z = [hop_z(kv_local, k) for k in range(n_z)]
    kv_z, q_own, gu_cut, down_cut = lax.optimization_barrier((kv_z, q_own, gu_cut, down_cut))

    kv_block = jnp.concatenate(kv_z, 0)
    if n_ctx == tp:
        kv_blocks = [hop(kv_block, k) for k in range(n_ctx)]
    else:
        kv_blocks = lax.all_gather(kv_block, "ctx", axis=0, tiled=False)
    gu_own = gather_z(gu_cut)
    q_own = jnp.stack(q_own)
    w_query, queries = project_query(
        q_own, swap(q_own), hidden_one, vecs, cos_wide, sin_wide, rows_here
    )
    w_query = w_query.reshape(width, width)
    kv_blocks, queries, o_got, og_here, down_cut = lax.optimization_barrier(
        (kv_blocks, queries, o_got, og_here, down_cut)
    )

    o_own = [hop(jnp.stack(o_got), k) for k in range(tp)]
    og_parts = [hop(og_here, k) for k in range(tp)]
    down_own = [hop_z(down_cut, k) for k in range(n_z)]
    kv_whole = jnp.stack(kv_blocks) if n_ctx == tp else kv_blocks
    attended, queries_ext = attend_forward(order_row, n_ctx == tp, queries, kv_whole)
    attended, o_own, queries_ext, og_parts, down_own = lax.optimization_barrier(
        (attended, o_own, queries_ext, og_parts, down_own)
    )
    o_own = jnp.stack(o_own)
    w_out, resid, hidden_two = project_out(
        o_own, swap(o_own), attended, x_here, vecs, rows_here
    )
    w_out = w_out.reshape(width, width)
    h2_parts = [hop(hidden_two, k) for k in range(tp)]
    gu_oth = swap(gu_own)
    down_own = jnp.stack(down_own)
    down_oth = swap(down_own)

    acts, ggus, h2_turned, og_all, dh2, ff_out = ff_pass(
        h2_parts, og_parts, (gu_own, gu_oth), (down_own, down_oth)
    )
    grad_h2_parts = [hop(dh2[k], k) for k in range(tp)]

    def share_pieces(mine):
        own = jnp.stack([hop(mine, k) for k in range(tp)])
        return own, swap(own)

    def core_halves(part_sum):
        cols = part_sum.shape[1]
        cut = part_sum.astype(BF16).reshape(n_z, rows_here, cols)
        cut = jnp.pad(cut, ((0, 0), (0, n_part * part_rows - rows_here), (0, 0)))
        own = lax.dynamic_slice_in_dim(cut, core * tp * part_rows, tp * part_rows, 1)
        oth = lax.dynamic_slice_in_dim(cut, (1 - core) * tp * part_rows, tp * part_rows, 1)
        return own, oth

    def core_total(own, sib):
        return (own.astype(F32) + sib.astype(F32)).astype(BF16)

    def scatter_parts(cut):
        cut = cut.reshape(n_z, tp, part_rows, -1)
        at = lax.rem(here, tp)
        return [
            hop(lax.dynamic_index_in_dim(cut, at ^ k, 1, keepdims=False), k) for k in range(tp)
        ]

    def ctx_groups_sum(v):
        if n_ctx == tp:
            return v
        groups = [[g * tp + c for g in range(n_ctx // tp)] for c in range(tp)]
        return lax.psum(v, "ctx", axis_index_groups=groups)

    d_gu = grad_weight(h2_turned, ggus[0], swap(grad_weight(h2_turned, ggus[1])))
    d_down = grad_weight(acts[0], og_all, swap(grad_weight(acts[1], og_all)))
    grad_h2_parts, d_gu, d_down, ff_out = lax.optimization_barrier(
        (grad_h2_parts, d_gu, d_down, ff_out)
    )
    d_gu = scatter_z(d_gu)
    d_down = d_down.reshape(n_z, piece_pad, width)
    grad_h2 = sum(v.astype(F32) for v in grad_h2_parts)
    scale_two = lax.rsqrt(jnp.mean(resid * resid, -1, keepdims=True) + NORM_EPS)
    normed_two = resid * scale_two

    grad_norm_two, gain_two_terms = rms_backward(grad_h2, normed_two, scale_two, gain_two)
    grad_resid = og_here.astype(F32) + grad_norm_two
    grad_proj = grad_resid.astype(BF16)
    grad_att = times_transposed(grad_proj, w_out).astype(BF16)
    o_own, o_oth = core_halves(contract_rows(attended, grad_proj))
    o_own, o_sib, grad_att, ff_out = lax.optimization_barrier(
        (o_own, swap(o_oth), grad_att, ff_out)
    )
    ff_out = [hop(ff_out[k], k) for k in range(tp)]
    o_terms = scatter_parts(core_total(o_own, o_sib))
    grad_queries, grad_terms = attend_backward(
        order_row, n_ctx == tp, queries_ext, grad_att, attended, kv_whole
    )
    grad_queries, grad_terms, ff_out, o_terms, d_down = lax.optimization_barrier(
        (grad_queries, grad_terms, ff_out, o_terms, d_down)
    )

    grad_q_pre = (
        rotate(grad_queries.reshape(tokens_here, HEADS, HEAD), cosine_table, -sine_table)
        .reshape(tokens_here, HEADS * HEAD)
        .astype(BF16)
    )
    q_own, q_oth = core_halves(contract_rows(hidden_one, grad_q_pre))
    if n_ctx == tp:
        kv_terms = [hop(grad_terms[k], k) for k in range(n_ctx)]
    else:
        kv_terms = [lax.psum_scatter(grad_terms, "ctx", scatter_dimension=0, tiled=False)]
    kv_terms, d_gu, d_down, q_own, q_oth, ff_out, o_terms = lax.optimization_barrier(
        (kv_terms, d_gu, d_down, q_own, q_oth, ff_out, o_terms)
    )

    kv_sum = sum(v.astype(F32) for v in kv_terms).astype(BF16)
    kv_sum = kv_sum.reshape(n_z, tokens_here, 2 * key_width)
    kv_terms = [hop_z(kv_sum[k], k) for k in range(n_z)]
    d_gu = ctx_groups_sum(d_gu)
    gu_pieces = [hop(d_gu, k) for k in range(tp)]
    q_sib = swap(q_oth)
    result = resid + sum(v.astype(F32) for v in ff_out)
    layer_out = result.astype(BF16)[None]
    kv_terms, q_own, q_sib, d_down = lax.optimization_barrier((kv_terms, q_own, q_sib, d_down))

    q_terms = scatter_parts(core_total(q_own, q_sib))
    d_down = [
        hop_z(lax.dynamic_index_in_dim(d_down, zed ^ k, 0, keepdims=False), k) for k in range(n_z)
    ]
    grad_kv = sum(v.astype(F32) for v in kv_terms)
    grad_k_pre = (
        rotate(
            grad_kv[:, :key_width].reshape(tokens_here, KV_HEADS, HEAD), cosine_table, -sine_table
        )
        .reshape(tokens_here, key_width)
        .astype(BF16)
    )
    grad_v_pre = grad_kv[:, key_width:].astype(BF16)
    grad_kv_pre = jnp.concatenate([grad_k_pre, grad_v_pre], 1)
    grad_hidden_one = times_transposed(grad_q_pre, w_query) + times_transposed(grad_kv_pre, w_kv)
    inputs = x_here.astype(F32)
    scale_one = lax.rsqrt(jnp.mean(inputs * inputs, -1, keepdims=True) + NORM_EPS)
    normed_one = inputs * scale_one
    grad_norm_one, gain_one_terms = rms_backward(grad_hidden_one, normed_one, scale_one, gain_one)
    tokens_grad = (grad_resid + grad_norm_one)[None]

    def by_rows(v):
        share = v.shape[1] // n_z
        v = v.reshape(tokens_here, n_z, share)
        return jnp.pad(v, ((0, 0), (0, 0), (0, rows_here - share))).reshape(tokens_here, width)

    terms = (gain_one_terms, gain_two_terms, grad_q_pre, by_rows(grad_k_pre), by_rows(grad_v_pre))
    pick = jnp.arange(len(terms) * tokens_here)[:, None] // tokens_here == jnp.arange(128)[None]
    columns = contract_rows(
        jnp.concatenate([v.astype(BF16) for v in terms], 0), pick.astype(BF16)
    )
    kv_own, kv_oth = core_halves(
        jnp.concatenate([contract_rows(hidden_one, grad_kv_pre), columns], 1)
    )
    kv_sib = swap(kv_oth)
    kv_own, kv_sib, gu_pieces, q_terms = lax.optimization_barrier(
        (kv_own, kv_sib, gu_pieces, q_terms)
    )

    kv_terms = scatter_parts(core_total(kv_own, kv_sib))
    gu_pieces = jnp.stack(gu_pieces)
    gu_sib = swap(gu_pieces)
    kv_terms, d_down = lax.optimization_barrier((kv_terms, d_down))

    last = jnp.concatenate(
        [sum(v.astype(F32) for v in t).astype(BF16) for t in (q_terms, o_terms, kv_terms)], 2
    )
    last = [
        hop_z(lax.dynamic_index_in_dim(last, zed ^ k, 0, keepdims=False), k) for k in range(n_z)
    ]
    d_down = ctx_groups_sum(sum(v.astype(F32) for v in d_down).astype(BF16))
    d_down = lax.optimization_barrier(d_down)
    down_pieces = [hop(d_down, k) for k in range(tp)]
    grad_w_gate, grad_w_up = spread_columns((gu_pieces, gu_sib), n_z, ff, 2)
    last, down_pieces, grad_w_gate, grad_w_up = lax.optimization_barrier(
        (last, down_pieces, grad_w_gate, grad_w_up)
    )

    last = ctx_groups_sum(sum(v.astype(F32) for v in last).astype(BF16))
    last = lax.optimization_barrier(last)
    last = [hop(last, k) for k in range(tp)]
    down_pieces = jnp.stack(down_pieces)
    down_sib = swap(down_pieces)
    last, down_pieces, down_sib = lax.optimization_barrier((last, down_pieces, down_sib))
    last = jnp.stack(last)
    grad_w_down = spread_rows((down_pieces, down_sib), piece, ff_z)
    last = spread_rows((last, swap(last)), part_rows, rows_here)
    grad_w_query = last[:, :width]
    grad_w_out = last[:, width : 2 * width]
    grad_w_kv = last[:, 2 * width :]
    sums = grad_w_kv[:, 2 * key_width :]

    return (
        layer_out,
        tokens_grad,
        sums[:, 0],
        grad_w_query,
        sums[:, 2],
        grad_w_kv[:, :key_width],
        sums[:kb, 3],
        grad_w_kv[:, key_width : 2 * key_width],
        sums[:kb, 4],
        grad_w_out,
        sums[:, 1],
        grad_w_gate,
        grad_w_up,
        grad_w_down,
    )


def solution(mesh):
    in_specs = (
        P("seq", ("ctx", "fsdp"), None),
        P("seq", ("ctx", "fsdp"), None),
        P("seq", None),
        P("fsdp"),
        P("fsdp", None),
        P("fsdp"),
        P("fsdp", None),
        P("fsdp"),
        P("fsdp", None),
        P("fsdp"),
        P("fsdp", None),
        P("fsdp"),
        P("fsdp", None),
        P("fsdp", None),
        P("fsdp", None),
    )
    out_specs = (
        P("seq", ("ctx", "fsdp"), None),
        P("seq", ("ctx", "fsdp"), None),
        P("fsdp"),
        P("fsdp", None),
        P("fsdp"),
        P("fsdp", None),
        P("fsdp"),
        P("fsdp", None),
        P("fsdp"),
        P("fsdp", None),
        P("fsdp"),
        P("fsdp", None),
        P("fsdp", None),
        P("fsdp", None),
    )
    return jax.shard_map(local, mesh=mesh, in_specs=in_specs, out_specs=out_specs, check_vma=False)
```

```python
import functools
import math

import jax
import jax.numpy as jnp
from jax import lax
from jax.experimental import pallas as pl
from jax.experimental.pallas import tpu as pltpu
from jax.sharding import PartitionSpec as P

HEADS = 14
KV_HEADS = 2
HEAD = 64
GROUP = HEADS // KV_HEADS
NORM_EPS = 1e-06
ROPE_BASE = 1000000.0
MASKED = -1e30
BF16 = jnp.bfloat16
F32 = jnp.float32
NO_COST = pl.CostEstimate(flops=0, bytes_accessed=0, transcendentals=0)


def rope_tables(positions, head_dim):
    half_dim = head_dim // 2
    inverse = jnp.exp(
        jnp.arange(half_dim, dtype=jnp.float32) * (-math.log(ROPE_BASE) * 2.0 / head_dim)
    )
    angles = positions.astype(jnp.float32)[:, None] * inverse[None, :]
    return (jnp.cos(angles)[:, None, :], jnp.sin(angles)[:, None, :])


def matmul(left_side, right_side):
    return jnp.dot(left_side, right_side, preferred_element_type=F32)


def contract_rows(left_side, right_side):
    return lax.dot_general(
        left_side, right_side, (((0,), (0,)), ((), ())), preferred_element_type=F32
    )


def times_transposed(left_side, right_side):
    return lax.dot_general(
        left_side, right_side, (((1,), (1,)), ((), ())), preferred_element_type=F32
    )


def rms_backward(grad_out, normed, inv_scale, gain_vec):
    scaled = grad_out * gain_vec
    grad_in = inv_scale * (scaled - normed * jnp.mean(scaled * normed, -1, keepdims=True))
    return (grad_in, grad_out * normed)


def cut_heads(ref, head):
    tile = ref[:, (head // 2) * 128 : (head // 2 + 1) * 128].astype(F32)
    group = head // GROUP
    if head % 2 != group:
        tile = jnp.concatenate([tile[:, HEAD:], tile[:, :HEAD]], 1)
    lane = lax.broadcasted_iota(jnp.int32, tile.shape, 1)
    return jnp.where((lane >= HEAD) if group else (lane < HEAD), tile, 0.0)


def split_lanes(column, shape):
    high = column.astype(BF16).astype(F32)
    mid = (column - high).astype(BF16).astype(F32)
    low = column - high - mid
    lane = lax.broadcasted_iota(jnp.int32, shape, 1)
    return jnp.where(
        lane == 0, high, jnp.where(lane == 1, mid, jnp.where(lane == 2, low, 0.0))
    ).astype(BF16)


def piece_shift(at, zed, tokens_here, keys_here):
    pieces = keys_here // tokens_here
    shift = jnp.zeros(at.shape, jnp.int32)
    for k in range(pieces):
        here = (jnp.bitwise_xor(zed, k) - k - zed) * tokens_here
        shift = jnp.where(at >= k * tokens_here, here, shift)
    return shift


def forward_kernel(by_xor, info_ref, q_ref, kv_ref, att_ref, qext_ref, top_ref, acc_ref):
    step = pl.program_id(0)
    last = pl.num_programs(0) - 1
    tokens_here = q_ref.shape[0]
    keys_here = kv_ref.shape[1]
    here = lax.axis_index("ctx")
    zed = lax.axis_index("fsdp")
    own = info_ref[here]
    block = info_ref[jnp.bitwise_xor(here, step) if by_xor else step]

    @pl.when(step == 0)
    def _():
        for h in range(HEADS):
            qext_ref[h * tokens_here : (h + 1) * tokens_here, :128] = cut_heads(q_ref, h).astype(
                BF16
            )
        top_ref[...] = jnp.full(top_ref.shape, MASKED, F32)
        acc_ref[...] = jnp.zeros(acc_ref.shape, F32)

    def attend(masked):
        keys = kv_ref[0, :, :128]
        values = jnp.concatenate(
            [kv_ref[0, :, 128:], jnp.ones((keys_here, 128), BF16)], 1
        )
        if masked:
            row = lax.broadcasted_iota(jnp.int32, (tokens_here, keys_here), 0)
            col = lax.broadcasted_iota(jnp.int32, (tokens_here, keys_here), 1)
            allowed = col + piece_shift(col, zed, tokens_here, keys_here) <= row
        for h in range(HEADS):
            rows = slice(h * tokens_here, (h + 1) * tokens_here)
            scores = times_transposed(qext_ref[rows, :128], keys)
            if masked:
                scores = jnp.where(allowed, scores, MASKED)
            old = top_ref[rows, :]
            top = jnp.maximum(old, jnp.max(scores, -1, keepdims=True))
            probs = jnp.exp(scores - top[:, :1]).astype(BF16)
            shrink = jnp.exp(old - top)
            top_ref[rows, :] = top
            acc_ref[rows, :] = acc_ref[rows, :] * jnp.concatenate([shrink, shrink], 1) + matmul(
                probs, values
            )

    @pl.when(block == own)
    def _():
        attend(True)

    @pl.when(block < own)
    def _():
        attend(False)

    @pl.when(step == last)
    def _():
        lane = lax.broadcasted_iota(jnp.int32, (tokens_here, 128), 1)
        for pair in range(HEADS // 2):
            outs = []
            for h in (2 * pair, 2 * pair + 1):
                rows = slice(h * tokens_here, (h + 1) * tokens_here)
                total = acc_ref[rows, 128:]
                out = acc_ref[rows, :128] / total
                if h // GROUP != h % 2:
                    out = jnp.concatenate([out[:, HEAD:], out[:, :HEAD]], 1)
                outs.append(out)
                log_total = top_ref[rows, :] + jnp.log(total)
                qext_ref[rows, 128:] = split_lanes(-log_total, (tokens_here, 128))
            att_ref[:, pair * 128 : (pair + 1) * 128] = jnp.where(
                lane < HEAD, outs[0], outs[1]
            ).astype(BF16)


def backward_kernel(
    by_xor, info_ref, qext_ref, do_ref, att_ref, cos_ref, sin_ref, kv_ref, dq_ref, dkv_ref,
    doext_ref, dqt_ref
):
    step = pl.program_id(0)
    last = pl.num_programs(0) - 1
    tokens_here = do_ref.shape[0]
    keys_here = kv_ref.shape[1]
    here = lax.axis_index("ctx")
    zed = lax.axis_index("fsdp")
    own = info_ref[here]
    block = info_ref[jnp.bitwise_xor(here, step) if by_xor else step]
    span = 2 * tokens_here

    @pl.when(step == 0)
    def _():
        for h in range(HEADS):
            rows = slice(h * tokens_here, (h + 1) * tokens_here)
            grad = cut_heads(do_ref, h)
            delta = jnp.sum(grad * cut_heads(att_ref, h), -1, keepdims=True)
            doext_ref[rows, :128] = grad.astype(BF16)
            doext_ref[rows, 128:] = split_lanes(-delta, (tokens_here, 128))
        dqt_ref[...] = jnp.zeros(dqt_ref.shape, F32)

    def attend(masked):
        lane = lax.broadcasted_iota(jnp.int32, (keys_here, 128), 1)
        ones = jnp.where(lane < 3, 1.0, 0.0).astype(BF16)
        keys = kv_ref[0, :, :128]
        keys_ext = jnp.concatenate([keys, ones], 1)
        values_ext = jnp.concatenate([kv_ref[0, :, 128:], ones], 1)
        keys_t = keys.astype(F32).T.astype(BF16)
        if masked:
            row = lax.broadcasted_iota(jnp.int32, (keys_here, tokens_here), 0)
            col = lax.broadcasted_iota(jnp.int32, (keys_here, tokens_here), 1)
            allowed = row + piece_shift(row, zed, tokens_here, keys_here) <= col
            allowed = allowed.astype(F32)
            allowed = jnp.concatenate([allowed, allowed], 1) > 0.5
        dk = jnp.zeros((keys_here, 128), F32)
        dv = jnp.zeros((keys_here, 128), F32)
        for pair in range(HEADS // 2):
            rows = slice(pair * span, (pair + 1) * span)
            probs = jnp.exp(times_transposed(keys_ext, qext_ref[rows, :]))
            if masked:
                probs = jnp.where(allowed, probs, 0.0)
            slope = (probs * times_transposed(values_ext, doext_ref[rows, :])).astype(BF16)
            dv = dv + matmul(probs.astype(BF16), doext_ref[rows, :128])
            dk = dk + matmul(slope, qext_ref[rows, :128])
            dqt_ref[pair] = dqt_ref[pair] + matmul(keys_t, slope)
        dkv_ref[0] = jnp.concatenate([dk, dv], 1).astype(BF16)

    @pl.when(block == own)
    def _():
        attend(True)

    @pl.when(block < own)
    def _():
        attend(False)

    @pl.when(block > own)
    def _():
        dkv_ref[...] = jnp.zeros(dkv_ref.shape, BF16)

    @pl.when(step == last)
    def _():
        lane = lax.broadcasted_iota(jnp.int32, (tokens_here, 128), 1)
        for pair in range(HEADS // 2):
            turned = dqt_ref[pair].T
            outs = []
            for j in range(2):
                h = 2 * pair + j
                out = turned[j * tokens_here : (j + 1) * tokens_here]
                if h // GROUP != j:
                    out = jnp.concatenate([out[:, HEAD:], out[:, :HEAD]], 1)
                outs.append(out)
            out = jnp.where(lane < HEAD, outs[0], outs[1]) * HEAD ** (-0.5)
            dq_ref[:, pair * 128 : (pair + 1) * 128] = turn_tile(
                out, cos_ref[...], -sin_ref[...]
            ).astype(BF16)


def whole_spec(shape):
    return pl.BlockSpec(shape, lambda i, info: (0,) * len(shape))


def attend_forward(info, by_xor, queries, kv):
    blocks, block_len, kv_width = kv.shape
    tokens_here, q_width = queries.shape
    rows = HEADS * tokens_here
    return pl.pallas_call(
        functools.partial(forward_kernel, by_xor),
        grid_spec=pltpu.PrefetchScalarGridSpec(
            num_scalar_prefetch=1,
            grid=(blocks,),
            in_specs=[
                whole_spec((tokens_here, q_width)),
                pl.BlockSpec((1, block_len, kv_width), lambda i, info: (i, 0, 0)),
            ],
            out_specs=[whole_spec((tokens_here, q_width)), whole_spec((rows, 256))],
            scratch_shapes=[pltpu.VMEM((rows, 128), F32), pltpu.VMEM((rows, 256), F32)],
        ),
        out_shape=[
            jax.ShapeDtypeStruct((tokens_here, q_width), BF16),
            jax.ShapeDtypeStruct((rows, 256), BF16),
        ],
        compiler_params=pltpu.CompilerParams(
            dimension_semantics=("arbitrary",), vmem_limit_bytes=40 * 2**20
        ),
        cost_estimate=pl.CostEstimate(
            flops=3 * 10**10, bytes_accessed=2**23, transcendentals=0
        ),
        name="attend_forward",
    )(info, queries, kv)


def attend_backward(info, by_xor, queries_ext, grad_att, attended, cos, sin, kv):
    blocks, block_len, kv_width = kv.shape
    tokens_here, q_width = grad_att.shape
    rows = HEADS * tokens_here
    return pl.pallas_call(
        functools.partial(backward_kernel, by_xor),
        grid_spec=pltpu.PrefetchScalarGridSpec(
            num_scalar_prefetch=1,
            grid=(blocks,),
            in_specs=[
                whole_spec((rows, 256)),
                whole_spec((tokens_here, q_width)),
                whole_spec((tokens_here, q_width)),
                whole_spec(cos.shape),
                whole_spec(sin.shape),
                pl.BlockSpec((1, block_len, kv_width), lambda i, info: (i, 0, 0)),
            ],
            out_specs=[
                whole_spec((tokens_here, q_width)),
                pl.BlockSpec((1, block_len, kv_width), lambda i, info: (i, 0, 0)),
            ],
            scratch_shapes=[
                pltpu.VMEM((rows, 256), BF16),
                pltpu.VMEM((HEADS // 2, 128, 2 * tokens_here), F32),
            ],
        ),
        out_shape=[
            jax.ShapeDtypeStruct((tokens_here, q_width), BF16),
            jax.ShapeDtypeStruct(kv.shape, BF16),
        ],
        compiler_params=pltpu.CompilerParams(
            dimension_semantics=("arbitrary",), vmem_limit_bytes=40 * 2**20
        ),
        cost_estimate=pl.CostEstimate(
            flops=5 * 10**10, bytes_accessed=2**23, transcendentals=0
        ),
        name="attend_backward",
    )(info, queries_ext, grad_att, attended, cos, sin, kv)


def part_place(tp, j, k):
    at = jnp.bitwise_xor(lax.rem(lax.axis_index("ctx"), tp), k)
    return jnp.bitwise_xor(lax.axis_index("seq"), j) * tp + at


def spread_columns_kernel(n_z, *refs):
    pieces, outs, held = refs[:2], refs[2:-1], refs[-1]
    tp = pieces[0].shape[0]
    n_part = 2 * tp
    for j in range(2):
        for k in range(tp):
            held[part_place(tp, j, k)] = pieces[j][k].astype(F32)
    half = held.shape[2] // len(outs)
    pad = half // n_z
    for i, out in enumerate(outs):
        piece = out.shape[1] // (n_z * n_part)
        cuts = []
        for j in range(n_z):
            for e in range(n_part):
                start = i * half + j * pad
                cuts.append(held[e, :, start : start + piece])
        out[...] = jnp.concatenate(cuts, 1)


def spread_columns(pieces, n_z, ff, outs):
    tp, rows, cols = pieces[0].shape
    tile = 32
    return pl.pallas_call(
        functools.partial(spread_columns_kernel, n_z),
        grid=(rows // tile,),
        in_specs=[pl.BlockSpec((tp, tile, cols), lambda i: (0, i, 0))] * 2,
        out_specs=[pl.BlockSpec((tile, ff), lambda i: (i, 0))] * outs,
        scratch_shapes=[pltpu.VMEM((2 * tp, tile, cols), F32)],
        out_shape=[jax.ShapeDtypeStruct((rows, ff), F32)] * outs,
        compiler_params=pltpu.CompilerParams(
            dimension_semantics=("arbitrary",), vmem_limit_bytes=40 * 2**20
        ),
        cost_estimate=NO_COST,
        name="spread_columns",
    )(*pieces)


def spread_rows_kernel(piece, *refs):
    pieces, out_ref = refs[:-1], refs[-1]
    room = out_ref.shape[0] // piece
    tp = pieces[0].shape[0]
    for j in range(2):
        for k in range(tp):
            place = part_place(tp, j, k)

            @pl.when(place < room)
            def _():
                start = pl.multiple_of(place * piece, 8)
                out_ref[pl.ds(start, piece), :] = pieces[j][k].astype(F32)[:piece]


def spread_rows(pieces, piece, rows_out):
    tp, rows, cols = pieces[0].shape
    tile = 128
    return pl.pallas_call(
        functools.partial(spread_rows_kernel, piece),
        grid=(cols // tile,),
        in_specs=[pl.BlockSpec((tp, rows, tile), lambda i: (0, 0, i))] * 2,
        out_specs=pl.BlockSpec((rows_out, tile), lambda i: (0, i)),
        out_shape=jax.ShapeDtypeStruct((rows_out, cols), F32),
        compiler_params=pltpu.CompilerParams(
            dimension_semantics=("arbitrary",), vmem_limit_bytes=40 * 2**20
        ),
        cost_estimate=NO_COST,
        name="spread_rows",
    )(*pieces)


def join_weight(own_ref, sib_ref, first, part_rows, out_ref):
    tp, n_z = own_ref.shape[:2]
    room = out_ref.shape[1] // part_rows
    for j, ref in enumerate((own_ref, sib_ref)):
        for k in range(tp):
            place = part_place(tp, j, k)

            @pl.when(place < room)
            def _():
                start = pl.multiple_of(place * part_rows, 16)
                for z in range(n_z):
                    at = jnp.bitwise_xor(lax.axis_index("fsdp"), z)
                    out_ref[at, pl.ds(start, part_rows), :] = ref[k, z, first : first + part_rows]


def whole_weight(ref):
    return jnp.concatenate([ref[z] for z in range(ref.shape[0])], 0)


def turn_tile(tile, cos, sin):
    h = HEAD // 2
    cuts = [tile[:, h : 2 * h], tile[:, :h], tile[:, 3 * h :], tile[:, 2 * h : 3 * h]]
    return tile * cos + jnp.concatenate(cuts, 1) * sin


def normed_rows(values, gain):
    inv = lax.rsqrt(jnp.mean(values * values, -1, keepdims=True) + NORM_EPS)
    return (values * inv * gain).astype(BF16)


def kv_kernel(widths, *refs):
    x_ref, cos_ref, sin_ref = refs[-8:-5]
    pieces, (out_ref, vec_ref, kv_ref, hid_ref, held) = refs[:-8], refs[-5:]
    n_z, rows_here, cols = out_ref.shape
    for k in range(n_z):
        at = jnp.bitwise_xor(lax.axis_index("fsdp"), k)
        out_ref[at] = pieces[k][:rows_here]
        held[at] = pieces[k][rows_here:].astype(F32)
    vec_ref[...] = jnp.zeros(vec_ref.shape, F32)
    for i, size in enumerate(widths):
        row = jnp.concatenate([held[z, i : i + 1, :size] for z in range(n_z)], 1)
        vec_ref[i : i + 1, : n_z * size] = row
    hidden = normed_rows(x_ref[...].astype(F32), vec_ref[0:1, :])
    hid_ref[...] = hidden
    half = cols // 2
    both = matmul(hidden, whole_weight(out_ref))
    keys = both[:, :half] + vec_ref[3:4, :half]
    kv_ref[:, :half] = turn_tile(keys, cos_ref[...], sin_ref[...]).astype(BF16)
    kv_ref[:, half:] = (both[:, half:] + vec_ref[4:5, :half]).astype(BF16)


def project_kv(pieces, tokens, cos, sin, rows_here, widths):
    rows, cols = pieces[0].shape
    n_z = len(pieces)
    vmem = pl.BlockSpec(memory_space=pltpu.VMEM)
    return pl.pallas_call(
        functools.partial(kv_kernel, widths),
        in_specs=[vmem] * (n_z + 3),
        out_specs=[vmem] * 4,
        out_shape=[
            jax.ShapeDtypeStruct((n_z, rows_here, cols), BF16),
            jax.ShapeDtypeStruct((8, n_z * rows_here), F32),
            jax.ShapeDtypeStruct((tokens.shape[0], cols), BF16),
            jax.ShapeDtypeStruct(tokens.shape, BF16),
        ],
        scratch_shapes=[pltpu.VMEM((n_z, rows - rows_here, cols), F32)],
        compiler_params=pltpu.CompilerParams(vmem_limit_bytes=40 * 2**20),
        cost_estimate=NO_COST,
        name="project_kv",
    )(*pieces, tokens, cos, sin)


def query_kernel(own_ref, sib_ref, hid_ref, vec_ref, cos_ref, sin_ref, out_ref, q_ref):
    part_rows = own_ref.shape[2] // 2
    join_weight(own_ref, sib_ref, 0, part_rows, out_ref)
    whole = matmul(hid_ref[...], whole_weight(out_ref)) + vec_ref[2:3, :]
    for pair in range(HEADS // 2):
        lanes = slice(pair * 128, (pair + 1) * 128)
        tile = turn_tile(whole[:, lanes], cos_ref[...], sin_ref[...]).astype(BF16)
        q_ref[:, lanes] = (tile.astype(F32) * HEAD ** (-0.5)).astype(BF16)


def project_query(own, sib, hidden, vecs, cos, sin, rows_here):
    n_z, cols = own.shape[1], own.shape[3]
    vmem = pl.BlockSpec(memory_space=pltpu.VMEM)
    return pl.pallas_call(
        query_kernel,
        in_specs=[vmem] * 6,
        out_specs=[vmem] * 2,
        out_shape=[
            jax.ShapeDtypeStruct((n_z, rows_here, cols), BF16),
            jax.ShapeDtypeStruct((hidden.shape[0], cols), BF16),
        ],
        compiler_params=pltpu.CompilerParams(vmem_limit_bytes=40 * 2**20),
        cost_estimate=NO_COST,
        name="project_query",
    )(own, sib, hidden, vecs, cos, sin)


def out_kernel(own_ref, sib_ref, att_ref, x_ref, vec_ref, out_ref, resid_ref, hid_ref):
    part_rows = own_ref.shape[2] // 2
    join_weight(own_ref, sib_ref, part_rows, part_rows, out_ref)
    resid = x_ref[...].astype(F32) + matmul(att_ref[...], whole_weight(out_ref))
    resid_ref[...] = resid
    hid_ref[...] = normed_rows(resid, vec_ref[1:2, :])


def project_out(own, sib, attended, tokens, vecs, rows_here):
    n_z, cols = own.shape[1], own.shape[3]
    vmem = pl.BlockSpec(memory_space=pltpu.VMEM)
    return pl.pallas_call(
        out_kernel,
        in_specs=[vmem] * 5,
        out_specs=[vmem] * 3,
        out_shape=[
            jax.ShapeDtypeStruct((n_z, rows_here, cols), BF16),
            jax.ShapeDtypeStruct(tokens.shape, F32),
            jax.ShapeDtypeStruct(tokens.shape, BF16),
        ],
        compiler_params=pltpu.CompilerParams(vmem_limit_bytes=40 * 2**20),
        cost_estimate=NO_COST,
        name="project_out",
    )(own, sib, attended, tokens, vecs)


def kv_back_kernel(n_z, *refs):
    terms, rest = refs[:n_z], refs[n_z:]
    cos_ref, sin_ref, gq_ref, hid_ref, wq_ref, wkv_ref, x_ref, res_ref, vec_ref, two_ref = rest[:10]
    tokens_ref, part_ref = rest[10:]
    rows_here, width = x_ref.shape
    total = sum(t[...].astype(F32) for t in terms)
    half = total.shape[1] // 2
    keys = turn_tile(total[:, :half], cos_ref[...], -sin_ref[...]).astype(BF16)
    both = jnp.concatenate([keys, total[:, half:].astype(BF16)], 1)
    grad = times_transposed(gq_ref[...], wq_ref[...]) + times_transposed(both, wkv_ref[...])
    x = x_ref[...].astype(F32)
    inv = lax.rsqrt(jnp.mean(x * x, -1, keepdims=True) + NORM_EPS)
    normed = x * inv
    scaled = grad * vec_ref[0:1, :]
    tokens_ref[...] = res_ref[...] + inv * (
        scaled - normed * jnp.mean(scaled * normed, -1, keepdims=True)
    )
    sums = jnp.sum(both.astype(F32), 0, keepdims=True)
    share = half // n_z
    gap = jnp.zeros((1, width // n_z - share), F32)
    spread = []
    for i in range(2):
        cuts = []
        for z in range(n_z):
            at = i * half + z * share
            cuts += [sums[:, at : at + share], gap]
        spread.append(jnp.concatenate(cuts, 1))
    columns = [
        jnp.sum(grad * normed, 0, keepdims=True),
        two_ref[...],
        jnp.sum(gq_ref[...].astype(F32), 0, keepdims=True),
    ] + spread
    row = lax.broadcasted_iota(jnp.int32, (128, width), 0)
    table = jnp.zeros((128, width), F32)
    for i, v in enumerate(columns):
        table = jnp.where(row == i, v, table)
    part_ref[:, 2 * half :] = table.T.astype(BF16)
    pad = -rows_here % 128
    left = jnp.concatenate([hid_ref[...].astype(F32), jnp.zeros((pad, width), F32)], 0)
    right = jnp.concatenate([both, jnp.zeros((pad, 2 * half), BF16)], 0)
    part_ref[:, : 2 * half] = matmul(left.T.astype(BF16), right).astype(BF16)


def kv_back(terms, cos, sin, gq, hidden, wq, wkv, tokens, resid_grad, vecs, two_sum):
    vmem = pl.BlockSpec(memory_space=pltpu.VMEM)
    width = tokens.shape[1]
    return pl.pallas_call(
        functools.partial(kv_back_kernel, len(terms)),
        in_specs=[vmem] * (len(terms) + 10),
        out_specs=[vmem] * 2,
        out_shape=[
            jax.ShapeDtypeStruct(tokens.shape, F32),
            jax.ShapeDtypeStruct((width, wkv.shape[1] + 128), BF16),
        ],
        compiler_params=pltpu.CompilerParams(vmem_limit_bytes=40 * 2**20),
        cost_estimate=NO_COST,
        name="kv_back",
    )(*terms, cos, sin, gq, hidden, wq, wkv, tokens, resid_grad, vecs, two_sum)


def grad_weight_kernel(left_ref, right_ref, *refs):
    total = matmul(left_ref[...], right_ref[...])
    if len(refs) == 2:
        total = total + refs[0][...].astype(F32)
    refs[-1][...] = total.astype(BF16)


def grad_weight(left, right, other=None):
    rows, depth = left.shape
    cols = right.shape[1]
    tile = rows // 2 if rows % 32 == 0 else rows
    by_rows = lambda width: pl.BlockSpec((tile, width), lambda i: (i, 0))
    in_specs = [by_rows(depth), pl.BlockSpec((depth, cols), lambda i: (0, 0))]
    args = [left, right]
    if other is not None:
        in_specs.append(by_rows(cols))
        args.append(other)
    return pl.pallas_call(
        grad_weight_kernel,
        grid=(rows // tile,),
        in_specs=in_specs,
        out_specs=by_rows(cols),
        out_shape=jax.ShapeDtypeStruct((rows, cols), BF16),
        compiler_params=pltpu.CompilerParams(
            dimension_semantics=("arbitrary",), vmem_limit_bytes=40 * 2**20
        ),
        cost_estimate=NO_COST,
        name="grad_weight",
    )(*args)


def ff_kernel(tp, n_z, *refs):
    hidden, grads, weights = refs[:tp], refs[tp : 2 * tp], refs[2 * tp : 2 * tp + 4]
    rest = refs[2 * tp + 4 :]
    act_refs, back_refs, (hid_t, grad_all) = rest[:2], rest[2:4], rest[4:6]
    dh_outs, outs = rest[6 : 6 + tp], rest[6 + tp : 6 + 2 * tp]
    gu_buf, down_buf, acc, acc_out, sems = rest[6 + 2 * tp :]
    part_rows = weights[2].shape[1]
    gu_copies = [
        pltpu.make_async_copy(weights[i], gu_buf.at[i], sems.at[i]) for i in range(2)
    ]
    down_copies = []
    for i in range(2):
        for z in range(n_z):
            at = jnp.bitwise_xor(lax.axis_index("fsdp"), z) * part_rows
            to = down_buf.at[i, pl.ds(pl.multiple_of(at, 16), part_rows)]
            sem = sems.at[2 + i * n_z + z]
            down_copies.append(pltpu.make_async_copy(weights[2 + i].at[z], to, sem))
    gu_copies[0].start()
    for c in down_copies[:n_z]:
        c.start()
    gu_copies[1].start()
    for c in down_copies[n_z:]:
        c.start()
    tokens_here = hidden[0].shape[0]
    half = down_buf.shape[1]
    step = 2 if tp % 2 == 0 else 1
    for i in range(2):
        gu_copies[i].wait()
        for t in range(0, tp, step):
            rows = slice(t * tokens_here, (t + step) * tokens_here)
            here = jnp.concatenate([hidden[t + n][...] for n in range(step)], 0)
            grad = jnp.concatenate([grads[t + n][...] for n in range(step)], 0)
            if i == 0:
                hid_t[:, rows] = here.astype(F32).T.astype(BF16)
                grad_all[rows, :] = grad
            gate = matmul(here, gu_buf[i, :, :half])
            up = matmul(here, gu_buf[i, :, half:])
            if t == 0:
                for c in down_copies[i * n_z : (i + 1) * n_z]:
                    c.wait()
            grad_act = times_transposed(grad, down_buf[i])
            sig = 1.0 / (1.0 + jnp.exp(-gate))
            silu = gate * sig
            act = silu * up
            act_refs[i][:, rows] = act.T.astype(BF16)
            grad_gate = (grad_act * up * (sig + silu * (1.0 - sig))).astype(BF16)
            grad_up = (grad_act * silu).astype(BF16)
            back_refs[i][rows, :half] = grad_gate
            back_refs[i][rows, half:] = grad_up
            part = times_transposed(grad_gate, gu_buf[i, :, :half]) + times_transposed(
                grad_up, gu_buf[i, :, half:]
            )
            out = matmul(act.astype(BF16), down_buf[i])
            if i == 0:
                acc[rows, :] = part
                acc_out[rows, :] = out
            else:
                part = (part + acc[rows, :]).astype(BF16)
                out = (out + acc_out[rows, :]).astype(BF16)
                for n in range(step):
                    mine = slice(n * tokens_here, (n + 1) * tokens_here)
                    dh_outs[t + n][...] = part[mine]
                    outs[t + n][...] = out[mine]


def ff_pass(hidden, grads, gu, down):
    tp = len(hidden)
    n_z, part_rows = down[0].shape[:2]
    tokens_here, width = hidden[0].shape
    half = n_z * part_rows
    rows = tp * tokens_here
    vmem = pl.BlockSpec(memory_space=pltpu.VMEM)
    got = pl.pallas_call(
        functools.partial(ff_kernel, tp, n_z),
        in_specs=[vmem] * (2 * tp) + [pl.BlockSpec(memory_space=pl.ANY)] * 4,
        out_specs=[vmem] * (2 * tp + 6),
        out_shape=[jax.ShapeDtypeStruct((half, rows), BF16)] * 2
        + [jax.ShapeDtypeStruct((rows, 2 * half), BF16)] * 2
        + [jax.ShapeDtypeStruct((width, rows), BF16), jax.ShapeDtypeStruct((rows, width), BF16)]
        + [jax.ShapeDtypeStruct((tokens_here, width), BF16)] * (2 * tp),
        scratch_shapes=[
            pltpu.VMEM((2, width, 2 * half), BF16),
            pltpu.VMEM((2, half, width), BF16),
            pltpu.VMEM((rows, width), F32),
            pltpu.VMEM((rows, width), F32),
            pltpu.SemaphoreType.DMA((2 + 2 * n_z,)),
        ],
        compiler_params=pltpu.CompilerParams(vmem_limit_bytes=58 * 2**20),
        cost_estimate=NO_COST,
        name="ff_pass",
    )(*hidden, *grads, *gu, *down)
    return got[:2], got[2:4], got[4], got[5], got[6 : 6 + tp], got[6 + tp :]


def local(
    tokens,
    out_grad,
    block_order,
    norm1_gain,
    q_weight,
    q_bias,
    k_weight,
    k_bias,
    v_weight,
    v_bias,
    o_weight,
    norm2_gain,
    gate_weight,
    up_weight,
    down_weight,
):
    n_ctx = lax.axis_size("ctx")
    n_z = lax.axis_size("fsdp")
    tp = 4 if n_ctx % 4 == 0 else (2 if n_ctx % 2 == 0 else 1)
    here = lax.axis_index("ctx")
    zed = lax.axis_index("fsdp")
    core = lax.axis_index("seq")
    n_part = 2 * tp
    part = core * tp + lax.rem(here, tp)

    def swap(v):
        return lax.ppermute(v, "seq", [(0, 1), (1, 0)])

    def hop(v, k):
        if k == 0:
            return v
        return lax.ppermute(v, "ctx", [(i, i ^ k) for i in range(n_ctx)])

    def hop_z(v, k):
        if k == 0:
            return v
        return lax.ppermute(v, "fsdp", [(i, i ^ k) for i in range(n_z)])

    def gather_z(v):
        return lax.all_gather(v, "fsdp", axis=0, tiled=True)

    def scatter_z(v):
        return lax.psum_scatter(v, "fsdp", scatter_dimension=0, tiled=True)

    tokens_here, width = tokens.shape[1:]
    ff = gate_weight.shape[1]
    rows_here = q_weight.shape[0]
    key_width = KV_HEADS * HEAD
    block_len = tokens_here * n_z

    part_rows = -(-rows_here // (n_part * 32)) * 32

    kb = k_bias.shape[0]
    vectors = (norm1_gain, norm2_gain, q_bias, k_bias, v_bias)
    vec = sum(
        jnp.pad(v[None], ((i, 15 - i), (0, 2 * key_width - v.shape[0])))
        for i, v in enumerate(vectors)
    )
    kv_pack = jnp.concatenate([jnp.concatenate([k_weight, v_weight], 1), vec], 0)
    og_here = out_grad[0]

    def own_part(w):
        return lax.dynamic_slice_in_dim(w, part * part_rows, part_rows, 0)

    ff_z = ff // n_z
    piece = ff_z // n_part
    piece_pad = -(-piece // 32) * 32

    def ff_columns(w):
        cuts = []
        for j in range(n_z):
            cut = lax.dynamic_slice_in_dim(w, j * ff_z + part * piece, piece, 1)
            cuts.append(jnp.pad(cut, ((0, 0), (0, piece_pad - piece))))
        return jnp.concatenate(cuts, 1)

    order_row = block_order[0]
    x_here = tokens[0]
    kv_pack, q_part, o_part, gate_weight, up_weight, down_weight, query_at = (
        lax.optimization_barrier(
            (
                kv_pack,
                own_part(q_weight),
                own_part(o_weight),
                gate_weight,
                up_weight,
                down_weight,
                order_row[here] * block_len + zed * tokens_here,
            )
        )
    )
    pack_rows = kv_pack.shape[0]
    qo_part = jnp.concatenate([q_part, o_part], 0)
    pack = jnp.concatenate([kv_pack, qo_part.reshape(-1, 2 * key_width)], 0)
    got = [hop_z(pack, k) for k in range(n_z)]
    gu_cut = jnp.concatenate([ff_columns(gate_weight), ff_columns(up_weight)], 1)
    down_cut = lax.dynamic_slice_in_dim(down_weight, part * piece, piece, 0)
    down_cut = jnp.pad(down_cut, ((0, piece_pad - piece), (0, 0)))
    query_pos = query_at + jnp.arange(tokens_here, dtype=jnp.int32)
    cosine_table, sine_table = rope_tables(query_pos, HEAD)
    cos_wide = jnp.tile(cosine_table[:, 0], (1, 4))
    sin_wide = jnp.tile(jnp.concatenate([-sine_table[:, 0], sine_table[:, 0]], 1), (1, 2))
    got, cos_wide, sin_wide, gu_cut, down_cut, og_here = lax.optimization_barrier(
        (got, cos_wide, sin_wide, gu_cut, down_cut, og_here)
    )
    kv_got = [v[:pack_rows] for v in got]

    qo_got = jnp.stack([v[pack_rows:].reshape(2 * part_rows, width) for v in got])
    qo_own = [hop(qo_got, k) for k in range(tp)]
    widths = tuple(v.shape[0] for v in vectors)
    w_kv, vecs, kv_local, hidden_one = project_kv(
        kv_got, x_here, cos_wide, sin_wide, rows_here, widths
    )
    w_kv = w_kv.reshape(width, 2 * key_width)
    gain_one = vecs[0:1, :width]
    gain_two = vecs[1:2, :width]
    kv_z = [hop_z(kv_local, k) for k in range(n_z)]
    kv_z, qo_own, gu_cut, down_cut = lax.optimization_barrier((kv_z, qo_own, gu_cut, down_cut))

    kv_block = jnp.concatenate(kv_z, 0)
    if n_ctx == tp:
        kv_blocks = [hop(kv_block, k) for k in range(n_ctx)]
    else:
        kv_blocks = lax.all_gather(kv_block, "ctx", axis=0, tiled=False)
    gu_own = gather_z(gu_cut)
    qo_own = jnp.stack(qo_own)
    qo_sib = swap(qo_own)
    w_query, queries = project_query(
        qo_own, qo_sib, hidden_one, vecs, cos_wide, sin_wide, rows_here
    )
    w_query = w_query.reshape(width, width)
    kv_blocks, queries, og_here, down_cut = lax.optimization_barrier(
        (kv_blocks, queries, og_here, down_cut)
    )

    og_parts = [hop(og_here, k) for k in range(tp)]
    down_own = [hop_z(down_cut, k) for k in range(n_z)]
    kv_whole = jnp.stack(kv_blocks) if n_ctx == tp else kv_blocks
    attended, queries_ext = attend_forward(order_row, n_ctx == tp, queries, kv_whole)
    attended, queries_ext, og_parts, down_own, gu_own = lax.optimization_barrier(
        (attended, queries_ext, og_parts, down_own, gu_own)
    )
    w_out, resid, hidden_two = project_out(
        qo_own, qo_sib, attended, x_here, vecs, rows_here
    )
    w_out = w_out.reshape(width, width)
    h2_parts = [hop(hidden_two, k) for k in range(tp)]
    gu_oth = swap(gu_own)
    down_own = jnp.stack(down_own)
    down_oth = swap(down_own)

    acts, ggus, h2_turned, og_all, dh2, ff_out = ff_pass(
        h2_parts, og_parts, (gu_own, gu_oth), (down_own, down_oth)
    )
    grad_h2_parts = [hop(dh2[k], k) for k in range(tp)]

    def share_pieces(mine):
        own = jnp.stack([hop(mine, k) for k in range(tp)])
        return own, swap(own)

    def core_halves(part_sum):
        cols = part_sum.shape[1]
        cut = part_sum.astype(BF16).reshape(n_z, rows_here, cols)
        cut = jnp.pad(cut, ((0, 0), (0, n_part * part_rows - rows_here), (0, 0)))
        own = lax.dynamic_slice_in_dim(cut, core * tp * part_rows, tp * part_rows, 1)
        oth = lax.dynamic_slice_in_dim(cut, (1 - core) * tp * part_rows, tp * part_rows, 1)
        return own, oth

    def core_total(own, sib):
        return (own.astype(F32) + sib.astype(F32)).astype(BF16)

    def scatter_parts(cut):
        cut = cut.reshape(n_z, tp, part_rows, -1)
        at = lax.rem(here, tp)
        return [
            hop(lax.dynamic_index_in_dim(cut, at ^ k, 1, keepdims=False), k) for k in range(tp)
        ]

    def ctx_groups_sum(v):
        if n_ctx == tp:
            return v
        groups = [[g * tp + c for g in range(n_ctx // tp)] for c in range(tp)]
        return lax.psum(v, "ctx", axis_index_groups=groups)

    d_gu = grad_weight(h2_turned, ggus[0], swap(grad_weight(h2_turned, ggus[1])))
    d_down = grad_weight(acts[0], og_all, swap(grad_weight(acts[1], og_all)))
    d_down = d_down.reshape(n_z, piece_pad, width)
    grad_h2 = sum(v.astype(F32) for v in grad_h2_parts)
    scale_two = lax.rsqrt(jnp.mean(resid * resid, -1, keepdims=True) + NORM_EPS)
    normed_two = resid * scale_two

    grad_norm_two, gain_two_terms = rms_backward(grad_h2, normed_two, scale_two, gain_two)
    grad_resid = og_here.astype(F32) + grad_norm_two
    grad_proj = grad_resid.astype(BF16)
    grad_att = times_transposed(grad_proj, w_out).astype(BF16)
    grad_att, d_gu, ff_out = lax.optimization_barrier((grad_att, d_gu, ff_out))
    d_gu = scatter_z(d_gu)
    ff_out = [hop(ff_out[k], k) for k in range(tp)]
    grad_q_pre, grad_terms = attend_backward(
        order_row, n_ctx == tp, queries_ext, grad_att, attended, cos_wide, sin_wide, kv_whole
    )
    grad_q_pre, grad_terms, ff_out, d_down, grad_proj = lax.optimization_barrier(
        (grad_q_pre, grad_terms, ff_out, d_down, grad_proj)
    )

    qo_own, qo_oth = core_halves(
        jnp.concatenate(
            [contract_rows(hidden_one, grad_q_pre), contract_rows(attended, grad_proj)], 1
        )
    )
    if n_ctx == tp:
        kv_terms = [hop(grad_terms[k], k) for k in range(n_ctx)]
    else:
        kv_terms = [lax.psum_scatter(grad_terms, "ctx", scatter_dimension=0, tiled=False)]
    kv_terms, d_gu, d_down, qo_own, qo_oth, ff_out = lax.optimization_barrier(
        (kv_terms, d_gu, d_down, qo_own, qo_oth, ff_out)
    )

    kv_sum = sum(v.astype(F32) for v in kv_terms).astype(BF16)
    kv_sum = kv_sum.reshape(n_z, tokens_here, 2 * key_width)
    kv_terms = [hop_z(kv_sum[k], k) for k in range(n_z)]
    d_gu = ctx_groups_sum(d_gu)
    gu_pieces = [hop(d_gu, k) for k in range(tp)]
    qo_sib = swap(qo_oth)
    result = resid + sum(v.astype(F32) for v in ff_out)
    layer_out = result.astype(BF16)[None]
    kv_terms, qo_own, qo_sib, d_down = lax.optimization_barrier(
        (kv_terms, qo_own, qo_sib, d_down)
    )

    tokens_grad, kv_part = kv_back(
        kv_terms,
        cos_wide,
        sin_wide,
        grad_q_pre,
        hidden_one,
        w_query,
        w_kv,
        x_here,
        grad_resid,
        vecs,
        jnp.sum(gain_two_terms, 0, keepdims=True),
    )
    tokens_grad = tokens_grad[None]
    kv_own, kv_oth = core_halves(kv_part)
    last = core_total(qo_own, qo_sib)
    kv_own, kv_sib, gu_pieces, d_down, last = lax.optimization_barrier(
        (kv_own, swap(kv_oth), gu_pieces, d_down, last)
    )

    last = scatter_parts(jnp.concatenate([last, core_total(kv_own, kv_sib)], 2))
    d_down = [
        hop_z(lax.dynamic_index_in_dim(d_down, zed ^ k, 0, keepdims=False), k) for k in range(n_z)
    ]
    gu_pieces = jnp.stack(gu_pieces)
    gu_sib = swap(gu_pieces)
    last, d_down, gu_pieces, gu_sib = lax.optimization_barrier((last, d_down, gu_pieces, gu_sib))

    last = sum(v.astype(F32) for v in last).astype(BF16)
    last = [
        hop_z(lax.dynamic_index_in_dim(last, zed ^ k, 0, keepdims=False), k) for k in range(n_z)
    ]
    d_down = ctx_groups_sum(sum(v.astype(F32) for v in d_down).astype(BF16))
    d_down = lax.optimization_barrier(d_down)
    down_pieces = [hop(d_down, k) for k in range(tp)]
    grad_w_gate, grad_w_up = spread_columns((gu_pieces, gu_sib), n_z, ff, 2)
    last, down_pieces, grad_w_gate, grad_w_up = lax.optimization_barrier(
        (last, down_pieces, grad_w_gate, grad_w_up)
    )

    last = ctx_groups_sum(sum(v.astype(F32) for v in last).astype(BF16))
    last = lax.optimization_barrier(last)
    last = [hop(last, k) for k in range(tp)]
    down_pieces = jnp.stack(down_pieces)
    down_sib = swap(down_pieces)
    last, down_pieces, down_sib = lax.optimization_barrier((last, down_pieces, down_sib))
    last = jnp.stack(last)
    grad_w_down = spread_rows((down_pieces, down_sib), piece, ff_z)
    last = spread_rows((last, swap(last)), part_rows, rows_here)
    grad_w_query = last[:, :width]
    grad_w_out = last[:, width : 2 * width]
    grad_w_kv = last[:, 2 * width :]
    sums = grad_w_kv[:, 2 * key_width :]

    return (
        layer_out,
        tokens_grad,
        sums[:, 0],
        grad_w_query,
        sums[:, 2],
        grad_w_kv[:, :key_width],
        sums[:kb, 3],
        grad_w_kv[:, key_width : 2 * key_width],
        sums[:kb, 4],
        grad_w_out,
        sums[:, 1],
        grad_w_gate,
        grad_w_up,
        grad_w_down,
    )


def solution(mesh):
    in_specs = (
        P("seq", ("ctx", "fsdp"), None),
        P("seq", ("ctx", "fsdp"), None),
        P("seq", None),
        P("fsdp"),
        P("fsdp", None),
        P("fsdp"),
        P("fsdp", None),
        P("fsdp"),
        P("fsdp", None),
        P("fsdp"),
        P("fsdp", None),
        P("fsdp"),
        P("fsdp", None),
        P("fsdp", None),
        P("fsdp", None),
    )
    out_specs = (
        P("seq", ("ctx", "fsdp"), None),
        P("seq", ("ctx", "fsdp"), None),
        P("fsdp"),
        P("fsdp", None),
        P("fsdp"),
        P("fsdp", None),
        P("fsdp"),
        P("fsdp", None),
        P("fsdp"),
        P("fsdp", None),
        P("fsdp"),
        P("fsdp", None),
        P("fsdp", None),
        P("fsdp", None),
    )
    return jax.shard_map(local, mesh=mesh, in_specs=in_specs, out_specs=out_specs, check_vma=False)
```

```python
import functools
import math

import jax
import jax.numpy as jnp
from jax import lax
from jax.experimental import pallas as pl
from jax.experimental.pallas import tpu as pltpu
from jax.sharding import PartitionSpec as P

HEADS = 14
KV_HEADS = 2
HEAD = 64
GROUP = HEADS // KV_HEADS
NORM_EPS = 1e-06
ROPE_BASE = 1000000.0
MASKED = -1e30
BF16 = jnp.bfloat16
F32 = jnp.float32
NO_COST = pl.CostEstimate(flops=0, bytes_accessed=0, transcendentals=0)


def rope_tables(positions, head_dim):
    half_dim = head_dim // 2
    inverse = jnp.exp(
        jnp.arange(half_dim, dtype=jnp.float32) * (-math.log(ROPE_BASE) * 2.0 / head_dim)
    )
    angles = positions.astype(jnp.float32)[:, None] * inverse[None, :]
    return (jnp.cos(angles)[:, None, :], jnp.sin(angles)[:, None, :])


def matmul(left_side, right_side):
    return jnp.dot(left_side, right_side, preferred_element_type=F32)


def contract_rows(left_side, right_side):
    return lax.dot_general(
        left_side, right_side, (((0,), (0,)), ((), ())), preferred_element_type=F32
    )


def times_transposed(left_side, right_side):
    return lax.dot_general(
        left_side, right_side, (((1,), (1,)), ((), ())), preferred_element_type=F32
    )


def rms_backward(grad_out, normed, inv_scale, gain_vec):
    scaled = grad_out * gain_vec
    grad_in = inv_scale * (scaled - normed * jnp.mean(scaled * normed, -1, keepdims=True))
    return (grad_in, grad_out * normed)


def cut_heads(ref, head):
    tile = ref[:, (head // 2) * 128 : (head // 2 + 1) * 128].astype(F32)
    group = head // GROUP
    if head % 2 != group:
        tile = jnp.concatenate([tile[:, HEAD:], tile[:, :HEAD]], 1)
    lane = lax.broadcasted_iota(jnp.int32, tile.shape, 1)
    return jnp.where((lane >= HEAD) if group else (lane < HEAD), tile, 0.0)


def split_lanes(column, shape):
    high = column.astype(BF16).astype(F32)
    mid = (column - high).astype(BF16).astype(F32)
    low = column - high - mid
    lane = lax.broadcasted_iota(jnp.int32, shape, 1)
    return jnp.where(
        lane == 0, high, jnp.where(lane == 1, mid, jnp.where(lane == 2, low, 0.0))
    ).astype(BF16)


def piece_shift(at, zed, tokens_here, keys_here):
    pieces = keys_here // tokens_here
    shift = jnp.zeros(at.shape, jnp.int32)
    for k in range(pieces):
        here = (jnp.bitwise_xor(zed, k) - k - zed) * tokens_here
        shift = jnp.where(at >= k * tokens_here, here, shift)
    return shift


def forward_kernel(by_xor, info_ref, q_ref, kv_ref, att_ref, qext_ref, top_ref, acc_ref):
    step = pl.program_id(0)
    last = pl.num_programs(0) - 1
    tokens_here = q_ref.shape[0]
    keys_here = kv_ref.shape[1]
    here = lax.axis_index("ctx")
    zed = lax.axis_index("fsdp")
    own = info_ref[here]
    block = info_ref[jnp.bitwise_xor(here, step) if by_xor else step]

    @pl.when(step == 0)
    def _():
        for h in range(HEADS):
            qext_ref[h * tokens_here : (h + 1) * tokens_here, :128] = cut_heads(q_ref, h).astype(
                BF16
            )
        top_ref[...] = jnp.full(top_ref.shape, MASKED, F32)
        acc_ref[...] = jnp.zeros(acc_ref.shape, F32)

    def attend(masked):
        keys = kv_ref[0, :, :128]
        values = jnp.concatenate(
            [kv_ref[0, :, 128:], jnp.ones((keys_here, 128), BF16)], 1
        )
        if masked:
            row = lax.broadcasted_iota(jnp.int32, (tokens_here, keys_here), 0)
            col = lax.broadcasted_iota(jnp.int32, (tokens_here, keys_here), 1)
            allowed = col + piece_shift(col, zed, tokens_here, keys_here) <= row
        for h in range(HEADS):
            rows = slice(h * tokens_here, (h + 1) * tokens_here)
            scores = times_transposed(qext_ref[rows, :128], keys)
            if masked:
                scores = jnp.where(allowed, scores, MASKED)
            old = top_ref[rows, :]
            top = jnp.maximum(old, jnp.max(scores, -1, keepdims=True))
            probs = jnp.exp(scores - top[:, :1]).astype(BF16)
            shrink = jnp.exp(old - top)
            top_ref[rows, :] = top
            acc_ref[rows, :] = acc_ref[rows, :] * jnp.concatenate([shrink, shrink], 1) + matmul(
                probs, values
            )

    @pl.when(block == own)
    def _():
        attend(True)

    @pl.when(block < own)
    def _():
        attend(False)

    @pl.when(step == last)
    def _():
        lane = lax.broadcasted_iota(jnp.int32, (tokens_here, 128), 1)
        for pair in range(HEADS // 2):
            outs = []
            for h in (2 * pair, 2 * pair + 1):
                rows = slice(h * tokens_here, (h + 1) * tokens_here)
                total = acc_ref[rows, 128:]
                out = acc_ref[rows, :128] / total
                if h // GROUP != h % 2:
                    out = jnp.concatenate([out[:, HEAD:], out[:, :HEAD]], 1)
                outs.append(out)
                log_total = top_ref[rows, :] + jnp.log(total)
                qext_ref[rows, 128:] = split_lanes(-log_total, (tokens_here, 128))
            att_ref[:, pair * 128 : (pair + 1) * 128] = jnp.where(
                lane < HEAD, outs[0], outs[1]
            ).astype(BF16)


def backward_kernel(
    by_xor, info_ref, qext_ref, do_ref, att_ref, cos_ref, sin_ref, kv_ref, dq_ref, dkv_ref,
    doext_ref, dqt_ref
):
    step = pl.program_id(0)
    last = pl.num_programs(0) - 1
    tokens_here = do_ref.shape[0]
    keys_here = kv_ref.shape[1]
    here = lax.axis_index("ctx")
    zed = lax.axis_index("fsdp")
    own = info_ref[here]
    block = info_ref[jnp.bitwise_xor(here, step) if by_xor else step]
    span = 2 * tokens_here

    @pl.when(step == 0)
    def _():
        for h in range(HEADS):
            rows = slice(h * tokens_here, (h + 1) * tokens_here)
            grad = cut_heads(do_ref, h)
            delta = jnp.sum(grad * cut_heads(att_ref, h), -1, keepdims=True)
            doext_ref[rows, :128] = grad.astype(BF16)
            doext_ref[rows, 128:] = split_lanes(-delta, (tokens_here, 128))
        dqt_ref[...] = jnp.zeros(dqt_ref.shape, F32)

    def attend(masked):
        lane = lax.broadcasted_iota(jnp.int32, (keys_here, 128), 1)
        ones = jnp.where(lane < 3, 1.0, 0.0).astype(BF16)
        keys = kv_ref[0, :, :128]
        keys_ext = jnp.concatenate([keys, ones], 1)
        values_ext = jnp.concatenate([kv_ref[0, :, 128:], ones], 1)
        keys_t = keys.astype(F32).T.astype(BF16)
        if masked:
            row = lax.broadcasted_iota(jnp.int32, (keys_here, tokens_here), 0)
            col = lax.broadcasted_iota(jnp.int32, (keys_here, tokens_here), 1)
            allowed = row + piece_shift(row, zed, tokens_here, keys_here) <= col
            allowed = allowed.astype(F32)
            allowed = jnp.concatenate([allowed, allowed], 1) > 0.5
        dk = jnp.zeros((keys_here, 128), F32)
        dv = jnp.zeros((keys_here, 128), F32)
        for pair in range(HEADS // 2):
            rows = slice(pair * span, (pair + 1) * span)
            probs = jnp.exp(times_transposed(keys_ext, qext_ref[rows, :]))
            if masked:
                probs = jnp.where(allowed, probs, 0.0)
            slope = (probs * times_transposed(values_ext, doext_ref[rows, :])).astype(BF16)
            dv = dv + matmul(probs.astype(BF16), doext_ref[rows, :128])
            dk = dk + matmul(slope, qext_ref[rows, :128])
            dqt_ref[pair] = dqt_ref[pair] + matmul(keys_t, slope)
        dkv_ref[0] = jnp.concatenate([dk, dv], 1).astype(BF16)

    @pl.when(block == own)
    def _():
        attend(True)

    @pl.when(block < own)
    def _():
        attend(False)

    @pl.when(block > own)
    def _():
        dkv_ref[...] = jnp.zeros(dkv_ref.shape, BF16)

    @pl.when(step == last)
    def _():
        lane = lax.broadcasted_iota(jnp.int32, (tokens_here, 128), 1)
        for pair in range(HEADS // 2):
            turned = dqt_ref[pair].T
            outs = []
            for j in range(2):
                h = 2 * pair + j
                out = turned[j * tokens_here : (j + 1) * tokens_here]
                if h // GROUP != j:
                    out = jnp.concatenate([out[:, HEAD:], out[:, :HEAD]], 1)
                outs.append(out)
            out = jnp.where(lane < HEAD, outs[0], outs[1]) * HEAD ** (-0.5)
            dq_ref[:, pair * 128 : (pair + 1) * 128] = turn_tile(
                out, cos_ref[...], -sin_ref[...]
            ).astype(BF16)


def whole_spec(shape):
    return pl.BlockSpec(shape, lambda i, info: (0,) * len(shape))


def attend_forward(info, by_xor, queries, kv):
    blocks, block_len, kv_width = kv.shape
    tokens_here, q_width = queries.shape
    rows = HEADS * tokens_here
    return pl.pallas_call(
        functools.partial(forward_kernel, by_xor),
        grid_spec=pltpu.PrefetchScalarGridSpec(
            num_scalar_prefetch=1,
            grid=(blocks,),
            in_specs=[
                whole_spec((tokens_here, q_width)),
                pl.BlockSpec((1, block_len, kv_width), lambda i, info: (i, 0, 0)),
            ],
            out_specs=[whole_spec((tokens_here, q_width)), whole_spec((rows, 256))],
            scratch_shapes=[pltpu.VMEM((rows, 128), F32), pltpu.VMEM((rows, 256), F32)],
        ),
        out_shape=[
            jax.ShapeDtypeStruct((tokens_here, q_width), BF16),
            jax.ShapeDtypeStruct((rows, 256), BF16),
        ],
        compiler_params=pltpu.CompilerParams(
            dimension_semantics=("arbitrary",), vmem_limit_bytes=40 * 2**20
        ),
        cost_estimate=pl.CostEstimate(
            flops=3 * 10**10, bytes_accessed=2**23, transcendentals=0
        ),
        name="attend_forward",
    )(info, queries, kv)


def attend_backward(info, by_xor, queries_ext, grad_att, attended, cos, sin, kv):
    blocks, block_len, kv_width = kv.shape
    tokens_here, q_width = grad_att.shape
    rows = HEADS * tokens_here
    return pl.pallas_call(
        functools.partial(backward_kernel, by_xor),
        grid_spec=pltpu.PrefetchScalarGridSpec(
            num_scalar_prefetch=1,
            grid=(blocks,),
            in_specs=[
                whole_spec((rows, 256)),
                whole_spec((tokens_here, q_width)),
                whole_spec((tokens_here, q_width)),
                whole_spec(cos.shape),
                whole_spec(sin.shape),
                pl.BlockSpec((1, block_len, kv_width), lambda i, info: (i, 0, 0)),
            ],
            out_specs=[
                whole_spec((tokens_here, q_width)),
                pl.BlockSpec((1, block_len, kv_width), lambda i, info: (i, 0, 0)),
            ],
            scratch_shapes=[
                pltpu.VMEM((rows, 256), BF16),
                pltpu.VMEM((HEADS // 2, 128, 2 * tokens_here), F32),
            ],
        ),
        out_shape=[
            jax.ShapeDtypeStruct((tokens_here, q_width), BF16),
            jax.ShapeDtypeStruct(kv.shape, BF16),
        ],
        compiler_params=pltpu.CompilerParams(
            dimension_semantics=("arbitrary",), vmem_limit_bytes=40 * 2**20
        ),
        cost_estimate=pl.CostEstimate(
            flops=5 * 10**10, bytes_accessed=2**23, transcendentals=0
        ),
        name="attend_backward",
    )(info, queries_ext, grad_att, attended, cos, sin, kv)


def part_place(tp, j, k):
    at = jnp.bitwise_xor(lax.rem(lax.axis_index("ctx"), tp), k)
    return jnp.bitwise_xor(lax.axis_index("seq"), j) * tp + at


def spread_columns_kernel(n_z, *refs):
    pieces, outs, held = refs[:2], refs[2:-1], refs[-1]
    tp = pieces[0].shape[0]
    n_part = 2 * tp
    for j in range(2):
        for k in range(tp):
            held[part_place(tp, j, k)] = pieces[j][k].astype(F32)
    half = held.shape[2] // len(outs)
    pad = half // n_z
    for i, out in enumerate(outs):
        piece = out.shape[1] // (n_z * n_part)
        cuts = []
        for j in range(n_z):
            for e in range(n_part):
                start = i * half + j * pad
                cuts.append(held[e, :, start : start + piece])
        out[...] = jnp.concatenate(cuts, 1)


def spread_columns(pieces, n_z, ff, outs):
    tp, rows, cols = pieces[0].shape
    tile = 32
    return pl.pallas_call(
        functools.partial(spread_columns_kernel, n_z),
        grid=(rows // tile,),
        in_specs=[pl.BlockSpec((tp, tile, cols), lambda i: (0, i, 0))] * 2,
        out_specs=[pl.BlockSpec((tile, ff), lambda i: (i, 0))] * outs,
        scratch_shapes=[pltpu.VMEM((2 * tp, tile, cols), F32)],
        out_shape=[jax.ShapeDtypeStruct((rows, ff), F32)] * outs,
        compiler_params=pltpu.CompilerParams(
            dimension_semantics=("arbitrary",), vmem_limit_bytes=40 * 2**20
        ),
        cost_estimate=NO_COST,
        name="spread_columns",
    )(*pieces)


def spread_rows_kernel(piece, *refs):
    pieces, out_ref = refs[:-1], refs[-1]
    room = out_ref.shape[0] // piece
    tp = pieces[0].shape[0]
    for j in range(2):
        for k in range(tp):
            place = part_place(tp, j, k)

            @pl.when(place < room)
            def _():
                start = pl.multiple_of(place * piece, 8)
                out_ref[pl.ds(start, piece), :] = pieces[j][k].astype(F32)[:piece]


def spread_rows(pieces, piece, rows_out):
    tp, rows, cols = pieces[0].shape
    tile = 128
    return pl.pallas_call(
        functools.partial(spread_rows_kernel, piece),
        grid=(cols // tile,),
        in_specs=[pl.BlockSpec((tp, rows, tile), lambda i: (0, 0, i))] * 2,
        out_specs=pl.BlockSpec((rows_out, tile), lambda i: (0, i)),
        out_shape=jax.ShapeDtypeStruct((rows_out, cols), F32),
        compiler_params=pltpu.CompilerParams(
            dimension_semantics=("arbitrary",), vmem_limit_bytes=40 * 2**20
        ),
        cost_estimate=NO_COST,
        name="spread_rows",
    )(*pieces)


def join_weight(own_ref, sib_ref, first, part_rows, out_ref):
    tp, n_z = own_ref.shape[:2]
    room = out_ref.shape[1] // part_rows
    for j, ref in enumerate((own_ref, sib_ref)):
        for k in range(tp):
            place = part_place(tp, j, k)

            @pl.when(place < room)
            def _():
                start = pl.multiple_of(place * part_rows, 16)
                for z in range(n_z):
                    at = jnp.bitwise_xor(lax.axis_index("fsdp"), z)
                    out_ref[at, pl.ds(start, part_rows), :] = ref[k, z, first : first + part_rows]


def whole_weight(ref):
    return jnp.concatenate([ref[z] for z in range(ref.shape[0])], 0)


def turn_tile(tile, cos, sin):
    h = HEAD // 2
    cuts = [tile[:, h : 2 * h], tile[:, :h], tile[:, 3 * h :], tile[:, 2 * h : 3 * h]]
    return tile * cos + jnp.concatenate(cuts, 1) * sin


def normed_rows(values, gain):
    inv = lax.rsqrt(jnp.mean(values * values, -1, keepdims=True) + NORM_EPS)
    return (values * inv * gain).astype(BF16)


def kv_kernel(widths, *refs):
    x_ref, cos_ref, sin_ref = refs[-8:-5]
    pieces, (out_ref, vec_ref, kv_ref, hid_ref, held) = refs[:-8], refs[-5:]
    n_z, rows_here, cols = out_ref.shape
    for k in range(n_z):
        at = jnp.bitwise_xor(lax.axis_index("fsdp"), k)
        out_ref[at] = pieces[k][:rows_here]
        held[at] = pieces[k][rows_here:].astype(F32)
    vec_ref[...] = jnp.zeros(vec_ref.shape, F32)
    for i, size in enumerate(widths):
        row = jnp.concatenate([held[z, i : i + 1, :size] for z in range(n_z)], 1)
        vec_ref[i : i + 1, : n_z * size] = row
    hidden = normed_rows(x_ref[...].astype(F32), vec_ref[0:1, :])
    hid_ref[...] = hidden
    half = cols // 2
    both = matmul(hidden, whole_weight(out_ref))
    keys = both[:, :half] + vec_ref[3:4, :half]
    kv_ref[:, :half] = turn_tile(keys, cos_ref[...], sin_ref[...]).astype(BF16)
    kv_ref[:, half:] = (both[:, half:] + vec_ref[4:5, :half]).astype(BF16)


def project_kv(pieces, tokens, cos, sin, rows_here, widths):
    rows, cols = pieces[0].shape
    n_z = len(pieces)
    vmem = pl.BlockSpec(memory_space=pltpu.VMEM)
    return pl.pallas_call(
        functools.partial(kv_kernel, widths),
        in_specs=[vmem] * (n_z + 3),
        out_specs=[vmem] * 4,
        out_shape=[
            jax.ShapeDtypeStruct((n_z, rows_here, cols), BF16),
            jax.ShapeDtypeStruct((8, n_z * rows_here), F32),
            jax.ShapeDtypeStruct((tokens.shape[0], cols), BF16),
            jax.ShapeDtypeStruct(tokens.shape, BF16),
        ],
        scratch_shapes=[pltpu.VMEM((n_z, rows - rows_here, cols), F32)],
        compiler_params=pltpu.CompilerParams(vmem_limit_bytes=40 * 2**20),
        cost_estimate=NO_COST,
        name="project_kv",
    )(*pieces, tokens, cos, sin)


def query_kernel(own_ref, sib_ref, hid_ref, vec_ref, cos_ref, sin_ref, out_ref, q_ref):
    part_rows = own_ref.shape[2] // 2
    join_weight(own_ref, sib_ref, 0, part_rows, out_ref)
    whole = matmul(hid_ref[...], whole_weight(out_ref)) + vec_ref[2:3, :]
    for pair in range(HEADS // 2):
        lanes = slice(pair * 128, (pair + 1) * 128)
        tile = turn_tile(whole[:, lanes], cos_ref[...], sin_ref[...]).astype(BF16)
        q_ref[:, lanes] = (tile.astype(F32) * HEAD ** (-0.5)).astype(BF16)


def project_query(own, sib, hidden, vecs, cos, sin, rows_here):
    n_z, cols = own.shape[1], own.shape[3]
    vmem = pl.BlockSpec(memory_space=pltpu.VMEM)
    return pl.pallas_call(
        query_kernel,
        in_specs=[vmem] * 6,
        out_specs=[vmem] * 2,
        out_shape=[
            jax.ShapeDtypeStruct((n_z, rows_here, cols), BF16),
            jax.ShapeDtypeStruct((hidden.shape[0], cols), BF16),
        ],
        compiler_params=pltpu.CompilerParams(vmem_limit_bytes=40 * 2**20),
        cost_estimate=NO_COST,
        name="project_query",
    )(own, sib, hidden, vecs, cos, sin)


def out_kernel(own_ref, sib_ref, att_ref, x_ref, vec_ref, out_ref, resid_ref, hid_ref):
    part_rows = own_ref.shape[2] // 2
    join_weight(own_ref, sib_ref, part_rows, part_rows, out_ref)
    resid = x_ref[...].astype(F32) + matmul(att_ref[...], whole_weight(out_ref))
    resid_ref[...] = resid
    hid_ref[...] = normed_rows(resid, vec_ref[1:2, :])


def project_out(own, sib, attended, tokens, vecs, rows_here):
    n_z, cols = own.shape[1], own.shape[3]
    vmem = pl.BlockSpec(memory_space=pltpu.VMEM)
    return pl.pallas_call(
        out_kernel,
        in_specs=[vmem] * 5,
        out_specs=[vmem] * 3,
        out_shape=[
            jax.ShapeDtypeStruct((n_z, rows_here, cols), BF16),
            jax.ShapeDtypeStruct(tokens.shape, F32),
            jax.ShapeDtypeStruct(tokens.shape, BF16),
        ],
        compiler_params=pltpu.CompilerParams(vmem_limit_bytes=40 * 2**20),
        cost_estimate=NO_COST,
        name="project_out",
    )(own, sib, attended, tokens, vecs)


def kv_back_kernel(n_z, *refs):
    terms, rest = refs[:n_z], refs[n_z:]
    cos_ref, sin_ref, gq_ref, hid_ref, wq_ref, wkv_ref, x_ref, res_ref, vec_ref, two_ref = rest[:10]
    tokens_ref, part_ref = rest[10:]
    rows_here, width = x_ref.shape
    total = sum(t[...].astype(F32) for t in terms)
    half = total.shape[1] // 2
    keys = turn_tile(total[:, :half], cos_ref[...], -sin_ref[...]).astype(BF16)
    both = jnp.concatenate([keys, total[:, half:].astype(BF16)], 1)
    grad = times_transposed(gq_ref[...], wq_ref[...]) + times_transposed(both, wkv_ref[...])
    x = x_ref[...].astype(F32)
    inv = lax.rsqrt(jnp.mean(x * x, -1, keepdims=True) + NORM_EPS)
    normed = x * inv
    scaled = grad * vec_ref[0:1, :]
    tokens_ref[...] = res_ref[...] + inv * (
        scaled - normed * jnp.mean(scaled * normed, -1, keepdims=True)
    )
    sums = jnp.sum(both.astype(F32), 0, keepdims=True)
    share = half // n_z
    gap = jnp.zeros((1, width // n_z - share), F32)
    spread = []
    for i in range(2):
        cuts = []
        for z in range(n_z):
            at = i * half + z * share
            cuts += [sums[:, at : at + share], gap]
        spread.append(jnp.concatenate(cuts, 1))
    columns = [
        jnp.sum(grad * normed, 0, keepdims=True),
        two_ref[...],
        jnp.sum(gq_ref[...].astype(F32), 0, keepdims=True),
    ] + spread
    row = lax.broadcasted_iota(jnp.int32, (128, width), 0)
    table = jnp.zeros((128, width), F32)
    for i, v in enumerate(columns):
        table = jnp.where(row == i, v, table)
    part_ref[:, 2 * half :] = table.T.astype(BF16)
    pad = -rows_here % 128
    left = jnp.concatenate([hid_ref[...].astype(F32), jnp.zeros((pad, width), F32)], 0)
    right = jnp.concatenate([both, jnp.zeros((pad, 2 * half), BF16)], 0)
    part_ref[:, : 2 * half] = matmul(left.T.astype(BF16), right).astype(BF16)


def kv_back(terms, cos, sin, gq, hidden, wq, wkv, tokens, resid_grad, vecs, two_sum):
    vmem = pl.BlockSpec(memory_space=pltpu.VMEM)
    width = tokens.shape[1]
    return pl.pallas_call(
        functools.partial(kv_back_kernel, len(terms)),
        in_specs=[vmem] * (len(terms) + 10),
        out_specs=[vmem] * 2,
        out_shape=[
            jax.ShapeDtypeStruct(tokens.shape, F32),
            jax.ShapeDtypeStruct((width, wkv.shape[1] + 128), BF16),
        ],
        compiler_params=pltpu.CompilerParams(vmem_limit_bytes=40 * 2**20),
        cost_estimate=NO_COST,
        name="kv_back",
    )(*terms, cos, sin, gq, hidden, wq, wkv, tokens, resid_grad, vecs, two_sum)


def grad_weight_kernel(left_ref, right_ref, *refs):
    total = matmul(left_ref[...], right_ref[...])
    if len(refs) == 2:
        total = total + refs[0][...].astype(F32)
    refs[-1][...] = total.astype(BF16)


def grad_weight(left, right, other=None):
    rows, depth = left.shape
    cols = right.shape[1]
    tile = rows // 2 if rows % 32 == 0 else rows
    by_rows = lambda width: pl.BlockSpec((tile, width), lambda i: (i, 0))
    in_specs = [by_rows(depth), pl.BlockSpec((depth, cols), lambda i: (0, 0))]
    args = [left, right]
    if other is not None:
        in_specs.append(by_rows(cols))
        args.append(other)
    return pl.pallas_call(
        grad_weight_kernel,
        grid=(rows // tile,),
        in_specs=in_specs,
        out_specs=by_rows(cols),
        out_shape=jax.ShapeDtypeStruct((rows, cols), BF16),
        compiler_params=pltpu.CompilerParams(
            dimension_semantics=("arbitrary",), vmem_limit_bytes=40 * 2**20
        ),
        cost_estimate=NO_COST,
        name="grad_weight",
    )(*args)


def ff_kernel(tp, n_z, *refs):
    hidden, grads, weights = refs[:tp], refs[tp : 2 * tp], refs[2 * tp : 2 * tp + 4]
    rest = refs[2 * tp + 4 :]
    act_refs, back_refs, (hid_t, grad_all) = rest[:2], rest[2:4], rest[4:6]
    dh_outs, outs = rest[6 : 6 + tp], rest[6 + tp : 6 + 2 * tp]
    gu_buf, down_buf, acc, acc_out, sems = rest[6 + 2 * tp :]
    part_rows = weights[2].shape[1]
    gu_copies = [
        pltpu.make_async_copy(weights[i], gu_buf.at[i], sems.at[i]) for i in range(2)
    ]
    down_copies = []
    for i in range(2):
        for z in range(n_z):
            to = down_buf.at[i, pl.ds(z * part_rows, part_rows)]
            sem = sems.at[2 + i * n_z + z]
            down_copies.append(pltpu.make_async_copy(weights[2 + i].at[z], to, sem))
    gu_copies[0].start()
    for c in down_copies[:n_z]:
        c.start()
    gu_copies[1].start()
    for c in down_copies[n_z:]:
        c.start()
    tokens_here = hidden[0].shape[0]
    half = down_buf.shape[1]
    step = 2 if tp % 2 == 0 else 1
    for i in range(2):
        gu_copies[i].wait()
        for t in range(0, tp, step):
            rows = slice(t * tokens_here, (t + step) * tokens_here)
            here = jnp.concatenate([hidden[t + n][...] for n in range(step)], 0)
            grad = jnp.concatenate([grads[t + n][...] for n in range(step)], 0)
            if i == 0:
                hid_t[:, rows] = here.astype(F32).T.astype(BF16)
                grad_all[rows, :] = grad
            gate = matmul(here, gu_buf[i, :, :half])
            up = matmul(here, gu_buf[i, :, half:])
            if t == 0:
                for c in down_copies[i * n_z : (i + 1) * n_z]:
                    c.wait()
            grad_act = times_transposed(grad, down_buf[i])
            sig = 1.0 / (1.0 + jnp.exp(-gate))
            silu = gate * sig
            act = silu * up
            act_refs[i][:, rows] = act.T.astype(BF16)
            grad_gate = (grad_act * up * (sig + silu * (1.0 - sig))).astype(BF16)
            grad_up = (grad_act * silu).astype(BF16)
            back_refs[i][rows, :half] = grad_gate
            back_refs[i][rows, half:] = grad_up
            part = times_transposed(grad_gate, gu_buf[i, :, :half]) + times_transposed(
                grad_up, gu_buf[i, :, half:]
            )
            out = matmul(act.astype(BF16), down_buf[i])
            if i == 0:
                acc[rows, :] = part
                acc_out[rows, :] = out
            else:
                part = (part + acc[rows, :]).astype(BF16)
                out = (out + acc_out[rows, :]).astype(BF16)
                for n in range(step):
                    mine = slice(n * tokens_here, (n + 1) * tokens_here)
                    dh_outs[t + n][...] = part[mine]
                    outs[t + n][...] = out[mine]


def ff_pass(hidden, grads, gu, down):
    tp = len(hidden)
    n_z, part_rows = down[0].shape[:2]
    tokens_here, width = hidden[0].shape
    half = n_z * part_rows
    rows = tp * tokens_here
    vmem = pl.BlockSpec(memory_space=pltpu.VMEM)
    got = pl.pallas_call(
        functools.partial(ff_kernel, tp, n_z),
        in_specs=[vmem] * (2 * tp) + [pl.BlockSpec(memory_space=pl.ANY)] * 4,
        out_specs=[vmem] * (2 * tp + 6),
        out_shape=[jax.ShapeDtypeStruct((half, rows), BF16)] * 2
        + [jax.ShapeDtypeStruct((rows, 2 * half), BF16)] * 2
        + [jax.ShapeDtypeStruct((width, rows), BF16), jax.ShapeDtypeStruct((rows, width), BF16)]
        + [jax.ShapeDtypeStruct((tokens_here, width), BF16)] * (2 * tp),
        scratch_shapes=[
            pltpu.VMEM((2, width, 2 * half), BF16),
            pltpu.VMEM((2, half, width), BF16),
            pltpu.VMEM((rows, width), F32),
            pltpu.VMEM((rows, width), F32),
            pltpu.SemaphoreType.DMA((2 + 2 * n_z,)),
        ],
        compiler_params=pltpu.CompilerParams(vmem_limit_bytes=58 * 2**20),
        cost_estimate=NO_COST,
        name="ff_pass",
    )(*hidden, *grads, *gu, *down)
    return got[:2], got[2:4], got[4], got[5], got[6 : 6 + tp], got[6 + tp :]


def local(
    tokens,
    out_grad,
    block_order,
    norm1_gain,
    q_weight,
    q_bias,
    k_weight,
    k_bias,
    v_weight,
    v_bias,
    o_weight,
    norm2_gain,
    gate_weight,
    up_weight,
    down_weight,
):
    n_ctx = lax.axis_size("ctx")
    n_z = lax.axis_size("fsdp")
    tp = 4 if n_ctx % 4 == 0 else (2 if n_ctx % 2 == 0 else 1)
    here = lax.axis_index("ctx")
    zed = lax.axis_index("fsdp")
    core = lax.axis_index("seq")
    n_part = 2 * tp
    part = core * tp + lax.rem(here, tp)

    def swap(v):
        return lax.ppermute(v, "seq", [(0, 1), (1, 0)])

    def hop(v, k):
        if k == 0:
            return v
        return lax.ppermute(v, "ctx", [(i, i ^ k) for i in range(n_ctx)])

    def hop_z(v, k):
        if k == 0:
            return v
        return lax.ppermute(v, "fsdp", [(i, i ^ k) for i in range(n_z)])

    def gather_z(v):
        return lax.all_gather(v, "fsdp", axis=0, tiled=True)

    def scatter_z(v):
        return lax.psum_scatter(v, "fsdp", scatter_dimension=0, tiled=True)

    tokens_here, width = tokens.shape[1:]
    ff = gate_weight.shape[1]
    rows_here = q_weight.shape[0]
    key_width = KV_HEADS * HEAD
    block_len = tokens_here * n_z

    part_rows = -(-rows_here // (n_part * 32)) * 32

    kb = k_bias.shape[0]
    vectors = (norm1_gain, norm2_gain, q_bias, k_bias, v_bias)
    vec = sum(
        jnp.pad(v[None], ((i, 15 - i), (0, 2 * key_width - v.shape[0])))
        for i, v in enumerate(vectors)
    )
    kv_pack = jnp.concatenate([jnp.concatenate([k_weight, v_weight], 1), vec], 0)
    og_here = out_grad[0]

    def own_part(w):
        return lax.dynamic_slice_in_dim(w, part * part_rows, part_rows, 0)

    ff_z = ff // n_z
    piece = ff_z // n_part
    piece_pad = -(-piece // 32) * 32

    def ff_columns(w):
        cuts = []
        for j in range(n_z):
            cut = lax.dynamic_slice_in_dim(w, j * ff_z + part * piece, piece, 1)
            cuts.append(jnp.pad(cut, ((0, 0), (0, piece_pad - piece))))
        return jnp.concatenate(cuts, 1)

    order_row = block_order[0]
    x_here = tokens[0]
    kv_pack, q_part, o_part, gate_weight, up_weight, down_weight, query_at = (
        lax.optimization_barrier(
            (
                kv_pack,
                own_part(q_weight),
                own_part(o_weight),
                gate_weight,
                up_weight,
                down_weight,
                order_row[here] * block_len + zed * tokens_here,
            )
        )
    )
    pack_rows = kv_pack.shape[0]
    qo_part = jnp.concatenate([q_part, o_part], 0)
    pack = jnp.concatenate([kv_pack, qo_part.reshape(-1, 2 * key_width)], 0)
    got = [hop_z(pack, k) for k in range(n_z)]
    gu_cut = jnp.concatenate([ff_columns(gate_weight), ff_columns(up_weight)], 1)
    down_cut = lax.dynamic_slice_in_dim(down_weight, part * piece, piece, 0)
    down_cut = jnp.pad(down_cut, ((0, piece_pad - piece), (0, 0)))
    query_pos = query_at + jnp.arange(tokens_here, dtype=jnp.int32)
    cosine_table, sine_table = rope_tables(query_pos, HEAD)
    cos_wide = jnp.tile(cosine_table[:, 0], (1, 4))
    sin_wide = jnp.tile(jnp.concatenate([-sine_table[:, 0], sine_table[:, 0]], 1), (1, 2))
    got, cos_wide, sin_wide, gu_cut, down_cut, og_here = lax.optimization_barrier(
        (got, cos_wide, sin_wide, gu_cut, down_cut, og_here)
    )
    kv_got = [v[:pack_rows] for v in got]

    qo_got = jnp.stack([v[pack_rows:].reshape(2 * part_rows, width) for v in got])
    qo_own = [hop(qo_got, k) for k in range(tp)]
    widths = tuple(v.shape[0] for v in vectors)
    w_kv, vecs, kv_local, hidden_one = project_kv(
        kv_got, x_here, cos_wide, sin_wide, rows_here, widths
    )
    w_kv = w_kv.reshape(width, 2 * key_width)
    gain_one = vecs[0:1, :width]
    gain_two = vecs[1:2, :width]
    kv_z = [hop_z(kv_local, k) for k in range(n_z)]
    kv_z, qo_own, gu_cut, down_cut = lax.optimization_barrier((kv_z, qo_own, gu_cut, down_cut))

    kv_block = jnp.concatenate(kv_z, 0)
    if n_ctx == tp:
        kv_blocks = [hop(kv_block, k) for k in range(n_ctx)]
    else:
        kv_blocks = lax.all_gather(kv_block, "ctx", axis=0, tiled=False)
    gu_own = gather_z(gu_cut)
    qo_own = jnp.stack(qo_own)
    qo_sib = swap(qo_own)
    w_query, queries = project_query(
        qo_own, qo_sib, hidden_one, vecs, cos_wide, sin_wide, rows_here
    )
    w_query = w_query.reshape(width, width)
    kv_blocks, queries, og_here, down_cut = lax.optimization_barrier(
        (kv_blocks, queries, og_here, down_cut)
    )

    og_parts = [hop(og_here, k) for k in range(tp)]
    kv_whole = jnp.stack(kv_blocks) if n_ctx == tp else kv_blocks
    attended, queries_ext = attend_forward(order_row, n_ctx == tp, queries, kv_whole)
    attended, queries_ext, og_parts, down_cut, gu_own = lax.optimization_barrier(
        (attended, queries_ext, og_parts, down_cut, gu_own)
    )
    w_out, resid, hidden_two = project_out(
        qo_own, qo_sib, attended, x_here, vecs, rows_here
    )
    w_out = w_out.reshape(width, width)
    h2_parts = [hop(hidden_two, k) for k in range(tp)]
    gu_oth = swap(gu_own)
    down_own = gather_z(down_cut).reshape(n_z, piece_pad, width)
    down_oth = swap(down_own)

    acts, ggus, h2_turned, og_all, dh2, ff_out = ff_pass(
        h2_parts, og_parts, (gu_own, gu_oth), (down_own, down_oth)
    )
    grad_h2_parts = [hop(dh2[k], k) for k in range(tp)]

    def share_pieces(mine):
        own = jnp.stack([hop(mine, k) for k in range(tp)])
        return own, swap(own)

    def core_halves(part_sum):
        cols = part_sum.shape[1]
        cut = part_sum.astype(BF16).reshape(n_z, rows_here, cols)
        cut = jnp.pad(cut, ((0, 0), (0, n_part * part_rows - rows_here), (0, 0)))
        own = lax.dynamic_slice_in_dim(cut, core * tp * part_rows, tp * part_rows, 1)
        oth = lax.dynamic_slice_in_dim(cut, (1 - core) * tp * part_rows, tp * part_rows, 1)
        return own, oth

    def core_total(own, sib):
        return (own.astype(F32) + sib.astype(F32)).astype(BF16)

    def scatter_parts(cut):
        cut = cut.reshape(n_z, tp, part_rows, -1)
        at = lax.rem(here, tp)
        return [
            hop(lax.dynamic_index_in_dim(cut, at ^ k, 1, keepdims=False), k) for k in range(tp)
        ]

    def ctx_groups_sum(v):
        if n_ctx == tp:
            return v
        groups = [[g * tp + c for g in range(n_ctx // tp)] for c in range(tp)]
        return lax.psum(v, "ctx", axis_index_groups=groups)

    if tp > 1:
        grad_h2_parts[1], h2_turned, ggus = lax.optimization_barrier(
            (grad_h2_parts[1], h2_turned, ggus)
        )
    d_gu = grad_weight(h2_turned, ggus[0], swap(grad_weight(h2_turned, ggus[1])))
    grad_h2 = sum(v.astype(F32) for v in grad_h2_parts)
    scale_two = lax.rsqrt(jnp.mean(resid * resid, -1, keepdims=True) + NORM_EPS)
    normed_two = resid * scale_two

    grad_norm_two, gain_two_terms = rms_backward(grad_h2, normed_two, scale_two, gain_two)
    grad_resid = og_here.astype(F32) + grad_norm_two
    grad_proj = grad_resid.astype(BF16)
    grad_att = times_transposed(grad_proj, w_out).astype(BF16)
    grad_att, d_gu, ff_out = lax.optimization_barrier((grad_att, d_gu, ff_out))
    d_gu = scatter_z(d_gu)
    ff_out = [hop(ff_out[k], k) for k in range(tp)]
    grad_q_pre, grad_terms = attend_backward(
        order_row, n_ctx == tp, queries_ext, grad_att, attended, cos_wide, sin_wide, kv_whole
    )
    grad_q_pre, grad_terms, ff_out, acts, grad_proj = lax.optimization_barrier(
        (grad_q_pre, grad_terms, ff_out, acts, grad_proj)
    )
    d_down = grad_weight(acts[0], og_all, swap(grad_weight(acts[1], og_all)))

    qo_own, qo_oth = core_halves(
        jnp.concatenate(
            [contract_rows(hidden_one, grad_q_pre), contract_rows(attended, grad_proj)], 1
        )
    )
    if n_ctx == tp:
        kv_terms = [hop(grad_terms[k], k) for k in range(n_ctx)]
    else:
        kv_terms = [lax.psum_scatter(grad_terms, "ctx", scatter_dimension=0, tiled=False)]
    kv_terms, d_gu, d_down, qo_own, qo_oth, ff_out = lax.optimization_barrier(
        (kv_terms, d_gu, d_down, qo_own, qo_oth, ff_out)
    )

    kv_sum = sum(v.astype(F32) for v in kv_terms).astype(BF16)
    kv_sum = kv_sum.reshape(n_z, tokens_here, 2 * key_width)
    kv_terms = [hop_z(kv_sum[k], k) for k in range(n_z)]
    d_gu = ctx_groups_sum(d_gu)
    gu_pieces = [hop(d_gu, k) for k in range(tp)]
    qo_sib = swap(qo_oth)
    result = resid + sum(v.astype(F32) for v in ff_out)
    layer_out = result.astype(BF16)[None]
    d_down = scatter_z(d_down)
    kv_terms, qo_own, qo_sib = lax.optimization_barrier((kv_terms, qo_own, qo_sib))

    tokens_grad, kv_part = kv_back(
        kv_terms,
        cos_wide,
        sin_wide,
        grad_q_pre,
        hidden_one,
        w_query,
        w_kv,
        x_here,
        grad_resid,
        vecs,
        jnp.sum(gain_two_terms, 0, keepdims=True),
    )
    tokens_grad = tokens_grad[None]
    kv_own, kv_oth = core_halves(kv_part)
    last = core_total(qo_own, qo_sib)
    kv_own, kv_sib, last = lax.optimization_barrier((kv_own, swap(kv_oth), last))

    last = scatter_parts(jnp.concatenate([last, core_total(kv_own, kv_sib)], 2))
    last, d_down, gu_pieces = lax.optimization_barrier((last, d_down, gu_pieces))

    last = sum(v.astype(F32) for v in last).astype(BF16)
    last = [
        hop_z(lax.dynamic_index_in_dim(last, zed ^ k, 0, keepdims=False), k) for k in range(n_z)
    ]
    d_down = ctx_groups_sum(d_down)
    gu_pieces = jnp.stack(gu_pieces)
    gu_sib = swap(gu_pieces)
    down_pieces = [hop(d_down, k) for k in range(tp)]
    last, down_pieces, gu_pieces, gu_sib = lax.optimization_barrier(
        (last, down_pieces, gu_pieces, gu_sib)
    )

    last = ctx_groups_sum(sum(v.astype(F32) for v in last).astype(BF16))
    last = lax.optimization_barrier(last)
    last = [hop(last, k) for k in range(tp)]
    down_pieces = jnp.stack(down_pieces)
    down_sib = swap(down_pieces)
    grad_w_gate, grad_w_up = spread_columns((gu_pieces, gu_sib), n_z, ff, 2)
    last, down_pieces, down_sib, grad_w_gate, grad_w_up = lax.optimization_barrier(
        (last, down_pieces, down_sib, grad_w_gate, grad_w_up)
    )
    last = jnp.stack(last)
    grad_w_down = spread_rows((down_pieces, down_sib), piece, ff_z)
    last = spread_rows((last, swap(last)), part_rows, rows_here)
    grad_w_query = last[:, :width]
    grad_w_out = last[:, width : 2 * width]
    grad_w_kv = last[:, 2 * width :]
    sums = grad_w_kv[:, 2 * key_width :]

    return (
        layer_out,
        tokens_grad,
        sums[:, 0],
        grad_w_query,
        sums[:, 2],
        grad_w_kv[:, :key_width],
        sums[:kb, 3],
        grad_w_kv[:, key_width : 2 * key_width],
        sums[:kb, 4],
        grad_w_out,
        sums[:, 1],
        grad_w_gate,
        grad_w_up,
        grad_w_down,
    )


def solution(mesh):
    in_specs = (
        P("seq", ("ctx", "fsdp"), None),
        P("seq", ("ctx", "fsdp"), None),
        P("seq", None),
        P("fsdp"),
        P("fsdp", None),
        P("fsdp"),
        P("fsdp", None),
        P("fsdp"),
        P("fsdp", None),
        P("fsdp"),
        P("fsdp", None),
        P("fsdp"),
        P("fsdp", None),
        P("fsdp", None),
        P("fsdp", None),
    )
    out_specs = (
        P("seq", ("ctx", "fsdp"), None),
        P("seq", ("ctx", "fsdp"), None),
        P("fsdp"),
        P("fsdp", None),
        P("fsdp"),
        P("fsdp", None),
        P("fsdp"),
        P("fsdp", None),
        P("fsdp"),
        P("fsdp", None),
        P("fsdp"),
        P("fsdp", None),
        P("fsdp", None),
        P("fsdp", None),
    )
    return jax.shard_map(local, mesh=mesh, in_specs=in_specs, out_specs=out_specs, check_vma=False)
```

```python
import functools
import math

import jax
import jax.numpy as jnp
from jax import lax
from jax.experimental import pallas as pl
from jax.experimental.pallas import tpu as pltpu
from jax.sharding import PartitionSpec as P

HEADS = 14
KV_HEADS = 2
HEAD = 64
GROUP = HEADS // KV_HEADS
NORM_EPS = 1e-06
ROPE_BASE = 1000000.0
MASKED = -1e30
BF16 = jnp.bfloat16
F32 = jnp.float32
NO_COST = pl.CostEstimate(flops=0, bytes_accessed=0, transcendentals=0)


def rope_tables(positions, head_dim):
    half_dim = head_dim // 2
    inverse = jnp.exp(
        jnp.arange(half_dim, dtype=jnp.float32) * (-math.log(ROPE_BASE) * 2.0 / head_dim)
    )
    angles = positions.astype(jnp.float32)[:, None] * inverse[None, :]
    return (jnp.cos(angles)[:, None, :], jnp.sin(angles)[:, None, :])


def matmul(left_side, right_side):
    return jnp.dot(left_side, right_side, preferred_element_type=F32)


def contract_rows(left_side, right_side):
    return lax.dot_general(
        left_side, right_side, (((0,), (0,)), ((), ())), preferred_element_type=F32
    )


def times_transposed(left_side, right_side):
    return lax.dot_general(
        left_side, right_side, (((1,), (1,)), ((), ())), preferred_element_type=F32
    )


def rms_backward(grad_out, normed, inv_scale, gain_vec):
    scaled = grad_out * gain_vec
    grad_in = inv_scale * (scaled - normed * jnp.mean(scaled * normed, -1, keepdims=True))
    return (grad_in, grad_out * normed)


def cut_heads(ref, head):
    tile = ref[:, (head // 2) * 128 : (head // 2 + 1) * 128].astype(F32)
    group = head // GROUP
    if head % 2 != group:
        tile = jnp.concatenate([tile[:, HEAD:], tile[:, :HEAD]], 1)
    lane = lax.broadcasted_iota(jnp.int32, tile.shape, 1)
    return jnp.where((lane >= HEAD) if group else (lane < HEAD), tile, 0.0)


def split_lanes(column, shape):
    high = column.astype(BF16).astype(F32)
    mid = (column - high).astype(BF16).astype(F32)
    low = column - high - mid
    lane = lax.broadcasted_iota(jnp.int32, shape, 1)
    return jnp.where(
        lane == 0, high, jnp.where(lane == 1, mid, jnp.where(lane == 2, low, 0.0))
    ).astype(BF16)


def piece_shift(at, zed, tokens_here, keys_here):
    pieces = keys_here // tokens_here
    shift = jnp.zeros(at.shape, jnp.int32)
    for k in range(pieces):
        here = (jnp.bitwise_xor(zed, k) - k - zed) * tokens_here
        shift = jnp.where(at >= k * tokens_here, here, shift)
    return shift


def forward_kernel(by_xor, info_ref, q_ref, kv_ref, att_ref, qext_ref, top_ref, acc_ref):
    step = pl.program_id(0)
    last = pl.num_programs(0) - 1
    tokens_here = q_ref.shape[0]
    keys_here = kv_ref.shape[1]
    here = lax.axis_index("ctx")
    zed = lax.axis_index("fsdp")
    own = info_ref[here]
    block = info_ref[jnp.bitwise_xor(here, step) if by_xor else step]

    @pl.when(step == 0)
    def _():
        for h in range(HEADS):
            qext_ref[h * tokens_here : (h + 1) * tokens_here, :128] = cut_heads(q_ref, h).astype(
                BF16
            )
        top_ref[...] = jnp.full(top_ref.shape, MASKED, F32)
        acc_ref[...] = jnp.zeros(acc_ref.shape, F32)

    def attend(masked):
        keys = kv_ref[0, :, :128]
        values = jnp.concatenate(
            [kv_ref[0, :, 128:], jnp.ones((keys_here, 128), BF16)], 1
        )
        if masked:
            row = lax.broadcasted_iota(jnp.int32, (tokens_here, keys_here), 0)
            col = lax.broadcasted_iota(jnp.int32, (tokens_here, keys_here), 1)
            allowed = col + piece_shift(col, zed, tokens_here, keys_here) <= row
        for h in range(HEADS):
            rows = slice(h * tokens_here, (h + 1) * tokens_here)
            scores = times_transposed(qext_ref[rows, :128], keys)
            if masked:
                scores = jnp.where(allowed, scores, MASKED)
            old = top_ref[rows, :]
            top = jnp.maximum(old, jnp.max(scores, -1, keepdims=True))
            probs = jnp.exp(scores - top[:, :1]).astype(BF16)
            shrink = jnp.exp(old - top)
            top_ref[rows, :] = top
            acc_ref[rows, :] = acc_ref[rows, :] * jnp.concatenate([shrink, shrink], 1) + matmul(
                probs, values
            )

    @pl.when(block == own)
    def _():
        attend(True)

    @pl.when(block < own)
    def _():
        attend(False)

    @pl.when(step == last)
    def _():
        lane = lax.broadcasted_iota(jnp.int32, (tokens_here, 128), 1)
        for pair in range(HEADS // 2):
            outs = []
            for h in (2 * pair, 2 * pair + 1):
                rows = slice(h * tokens_here, (h + 1) * tokens_here)
                total = acc_ref[rows, 128:]
                out = acc_ref[rows, :128] / total
                if h // GROUP != h % 2:
                    out = jnp.concatenate([out[:, HEAD:], out[:, :HEAD]], 1)
                outs.append(out)
                log_total = top_ref[rows, :] + jnp.log(total)
                qext_ref[rows, 128:] = split_lanes(-log_total, (tokens_here, 128))
            att_ref[:, pair * 128 : (pair + 1) * 128] = jnp.where(
                lane < HEAD, outs[0], outs[1]
            ).astype(BF16)


def backward_kernel(
    by_xor, info_ref, qext_ref, do_ref, att_ref, cos_ref, sin_ref, kv_ref, dq_ref, dkv_ref,
    doext_ref, dqt_ref
):
    step = pl.program_id(0)
    last = pl.num_programs(0) - 1
    tokens_here = do_ref.shape[0]
    keys_here = kv_ref.shape[1]
    here = lax.axis_index("ctx")
    zed = lax.axis_index("fsdp")
    own = info_ref[here]
    block = info_ref[jnp.bitwise_xor(here, step) if by_xor else step]
    span = 2 * tokens_here

    @pl.when(step == 0)
    def _():
        for h in range(HEADS):
            rows = slice(h * tokens_here, (h + 1) * tokens_here)
            grad = cut_heads(do_ref, h)
            delta = jnp.sum(grad * cut_heads(att_ref, h), -1, keepdims=True)
            doext_ref[rows, :128] = grad.astype(BF16)
            doext_ref[rows, 128:] = split_lanes(-delta, (tokens_here, 128))
        dqt_ref[...] = jnp.zeros(dqt_ref.shape, F32)

    def attend(masked):
        lane = lax.broadcasted_iota(jnp.int32, (keys_here, 128), 1)
        ones = jnp.where(lane < 3, 1.0, 0.0).astype(BF16)
        keys = kv_ref[0, :, :128]
        keys_ext = jnp.concatenate([keys, ones], 1)
        values_ext = jnp.concatenate([kv_ref[0, :, 128:], ones], 1)
        keys_t = keys.astype(F32).T.astype(BF16)
        if masked:
            row = lax.broadcasted_iota(jnp.int32, (keys_here, tokens_here), 0)
            col = lax.broadcasted_iota(jnp.int32, (keys_here, tokens_here), 1)
            allowed = row + piece_shift(row, zed, tokens_here, keys_here) <= col
            allowed = allowed.astype(F32)
            allowed = jnp.concatenate([allowed, allowed], 1) > 0.5
        dk = jnp.zeros((keys_here, 128), F32)
        dv = jnp.zeros((keys_here, 128), F32)
        for pair in range(HEADS // 2):
            rows = slice(pair * span, (pair + 1) * span)
            probs = jnp.exp(times_transposed(keys_ext, qext_ref[rows, :]))
            if masked:
                probs = jnp.where(allowed, probs, 0.0)
            slope = (probs * times_transposed(values_ext, doext_ref[rows, :])).astype(BF16)
            dv = dv + matmul(probs.astype(BF16), doext_ref[rows, :128])
            dk = dk + matmul(slope, qext_ref[rows, :128])
            dqt_ref[pair] = dqt_ref[pair] + matmul(keys_t, slope)
        dkv_ref[0] = jnp.concatenate([dk, dv], 1).astype(BF16)

    @pl.when(block == own)
    def _():
        attend(True)

    @pl.when(block < own)
    def _():
        attend(False)

    @pl.when(block > own)
    def _():
        dkv_ref[...] = jnp.zeros(dkv_ref.shape, BF16)

    @pl.when(step == last)
    def _():
        lane = lax.broadcasted_iota(jnp.int32, (tokens_here, 128), 1)
        for pair in range(HEADS // 2):
            turned = dqt_ref[pair].T
            outs = []
            for j in range(2):
                h = 2 * pair + j
                out = turned[j * tokens_here : (j + 1) * tokens_here]
                if h // GROUP != j:
                    out = jnp.concatenate([out[:, HEAD:], out[:, :HEAD]], 1)
                outs.append(out)
            out = jnp.where(lane < HEAD, outs[0], outs[1]) * HEAD ** (-0.5)
            dq_ref[:, pair * 128 : (pair + 1) * 128] = turn_tile(
                out, cos_ref[...], -sin_ref[...]
            ).astype(BF16)


def whole_spec(shape):
    return pl.BlockSpec(shape, lambda i, info: (0,) * len(shape))


def attend_forward(info, by_xor, queries, kv):
    blocks, block_len, kv_width = kv.shape
    tokens_here, q_width = queries.shape
    rows = HEADS * tokens_here
    return pl.pallas_call(
        functools.partial(forward_kernel, by_xor),
        grid_spec=pltpu.PrefetchScalarGridSpec(
            num_scalar_prefetch=1,
            grid=(blocks,),
            in_specs=[
                whole_spec((tokens_here, q_width)),
                pl.BlockSpec((1, block_len, kv_width), lambda i, info: (i, 0, 0)),
            ],
            out_specs=[whole_spec((tokens_here, q_width)), whole_spec((rows, 256))],
            scratch_shapes=[pltpu.VMEM((rows, 128), F32), pltpu.VMEM((rows, 256), F32)],
        ),
        out_shape=[
            jax.ShapeDtypeStruct((tokens_here, q_width), BF16),
            jax.ShapeDtypeStruct((rows, 256), BF16),
        ],
        compiler_params=pltpu.CompilerParams(
            dimension_semantics=("arbitrary",), vmem_limit_bytes=40 * 2**20
        ),
        cost_estimate=pl.CostEstimate(
            flops=3 * 10**10, bytes_accessed=2**23, transcendentals=0
        ),
        name="attend_forward",
    )(info, queries, kv)


def attend_backward(info, by_xor, queries_ext, grad_att, attended, cos, sin, kv):
    blocks, block_len, kv_width = kv.shape
    tokens_here, q_width = grad_att.shape
    rows = HEADS * tokens_here
    return pl.pallas_call(
        functools.partial(backward_kernel, by_xor),
        grid_spec=pltpu.PrefetchScalarGridSpec(
            num_scalar_prefetch=1,
            grid=(blocks,),
            in_specs=[
                whole_spec((rows, 256)),
                whole_spec((tokens_here, q_width)),
                whole_spec((tokens_here, q_width)),
                whole_spec(cos.shape),
                whole_spec(sin.shape),
                pl.BlockSpec((1, block_len, kv_width), lambda i, info: (i, 0, 0)),
            ],
            out_specs=[
                whole_spec((tokens_here, q_width)),
                pl.BlockSpec((1, block_len, kv_width), lambda i, info: (i, 0, 0)),
            ],
            scratch_shapes=[
                pltpu.VMEM((rows, 256), BF16),
                pltpu.VMEM((HEADS // 2, 128, 2 * tokens_here), F32),
            ],
        ),
        out_shape=[
            jax.ShapeDtypeStruct((tokens_here, q_width), BF16),
            jax.ShapeDtypeStruct(kv.shape, BF16),
        ],
        compiler_params=pltpu.CompilerParams(
            dimension_semantics=("arbitrary",), vmem_limit_bytes=40 * 2**20
        ),
        cost_estimate=pl.CostEstimate(
            flops=5 * 10**10, bytes_accessed=2**23, transcendentals=0
        ),
        name="attend_backward",
    )(info, queries_ext, grad_att, attended, cos, sin, kv)


def part_place(tp, j, k):
    at = jnp.bitwise_xor(lax.rem(lax.axis_index("ctx"), tp), k)
    return jnp.bitwise_xor(lax.axis_index("seq"), j) * tp + at


def spread_columns_kernel(n_z, *refs):
    pieces, outs, held = refs[:2], refs[2:-1], refs[-1]
    tp = pieces[0].shape[0]
    n_part = 2 * tp
    for j in range(2):
        for k in range(tp):
            held[part_place(tp, j, k)] = pieces[j][k].astype(F32)
    half = held.shape[2] // len(outs)
    pad = half // n_z
    for i, out in enumerate(outs):
        piece = out.shape[1] // (n_z * n_part)
        cuts = []
        for j in range(n_z):
            for e in range(n_part):
                start = i * half + j * pad
                cuts.append(held[e, :, start : start + piece])
        out[...] = jnp.concatenate(cuts, 1)


def spread_columns(pieces, n_z, ff, outs):
    tp, rows, cols = pieces[0].shape
    tile = 32
    return pl.pallas_call(
        functools.partial(spread_columns_kernel, n_z),
        grid=(rows // tile,),
        in_specs=[pl.BlockSpec((tp, tile, cols), lambda i: (0, i, 0))] * 2,
        out_specs=[pl.BlockSpec((tile, ff), lambda i: (i, 0))] * outs,
        scratch_shapes=[pltpu.VMEM((2 * tp, tile, cols), F32)],
        out_shape=[jax.ShapeDtypeStruct((rows, ff), F32)] * outs,
        compiler_params=pltpu.CompilerParams(
            dimension_semantics=("arbitrary",), vmem_limit_bytes=40 * 2**20
        ),
        cost_estimate=NO_COST,
        name="spread_columns",
    )(*pieces)


def spread_rows_kernel(piece, *refs):
    pieces, out_ref = refs[:-1], refs[-1]
    room = out_ref.shape[0] // piece
    tp = pieces[0].shape[0]
    for j in range(2):
        for k in range(tp):
            place = part_place(tp, j, k)

            @pl.when(place < room)
            def _():
                start = pl.multiple_of(place * piece, 8)
                out_ref[pl.ds(start, piece), :] = pieces[j][k].astype(F32)[:piece]


def spread_rows(pieces, piece, rows_out):
    tp, rows, cols = pieces[0].shape
    tile = 128
    return pl.pallas_call(
        functools.partial(spread_rows_kernel, piece),
        grid=(cols // tile,),
        in_specs=[pl.BlockSpec((tp, rows, tile), lambda i: (0, 0, i))] * 2,
        out_specs=pl.BlockSpec((rows_out, tile), lambda i: (0, i)),
        out_shape=jax.ShapeDtypeStruct((rows_out, cols), F32),
        compiler_params=pltpu.CompilerParams(
            dimension_semantics=("arbitrary",), vmem_limit_bytes=40 * 2**20
        ),
        cost_estimate=NO_COST,
        name="spread_rows",
    )(*pieces)


def join_weight(own_ref, sib_ref, first, part_rows, out_ref):
    tp, n_z = own_ref.shape[:2]
    room = out_ref.shape[1] // part_rows
    for j, ref in enumerate((own_ref, sib_ref)):
        for k in range(tp):
            place = part_place(tp, j, k)

            @pl.when(place < room)
            def _():
                start = pl.multiple_of(place * part_rows, 16)
                for z in range(n_z):
                    at = jnp.bitwise_xor(lax.axis_index("fsdp"), z)
                    out_ref[at, pl.ds(start, part_rows), :] = ref[k, z, first : first + part_rows]


def whole_weight(ref):
    return jnp.concatenate([ref[z] for z in range(ref.shape[0])], 0)


def turn_tile(tile, cos, sin):
    h = HEAD // 2
    cuts = [tile[:, h : 2 * h], tile[:, :h], tile[:, 3 * h :], tile[:, 2 * h : 3 * h]]
    return tile * cos + jnp.concatenate(cuts, 1) * sin


def normed_rows(values, gain):
    inv = lax.rsqrt(jnp.mean(values * values, -1, keepdims=True) + NORM_EPS)
    return (values * inv * gain).astype(BF16)


def kv_kernel(widths, *refs):
    x_ref, cos_ref, sin_ref = refs[-8:-5]
    pieces, (out_ref, vec_ref, kv_ref, hid_ref, held) = refs[:-8], refs[-5:]
    n_z, rows_here, cols = out_ref.shape
    for k in range(n_z):
        at = jnp.bitwise_xor(lax.axis_index("fsdp"), k)
        out_ref[at] = pieces[k][:rows_here]
        held[at] = pieces[k][rows_here:].astype(F32)
    vec_ref[...] = jnp.zeros(vec_ref.shape, F32)
    for i, size in enumerate(widths):
        row = jnp.concatenate([held[z, i : i + 1, :size] for z in range(n_z)], 1)
        vec_ref[i : i + 1, : n_z * size] = row
    hidden = normed_rows(x_ref[...].astype(F32), vec_ref[0:1, :])
    hid_ref[...] = hidden
    half = cols // 2
    both = matmul(hidden, whole_weight(out_ref))
    keys = both[:, :half] + vec_ref[3:4, :half]
    kv_ref[:, :half] = turn_tile(keys, cos_ref[...], sin_ref[...]).astype(BF16)
    kv_ref[:, half:] = (both[:, half:] + vec_ref[4:5, :half]).astype(BF16)


def project_kv(pieces, tokens, cos, sin, rows_here, widths):
    rows, cols = pieces[0].shape
    n_z = len(pieces)
    vmem = pl.BlockSpec(memory_space=pltpu.VMEM)
    return pl.pallas_call(
        functools.partial(kv_kernel, widths),
        in_specs=[vmem] * (n_z + 3),
        out_specs=[vmem] * 4,
        out_shape=[
            jax.ShapeDtypeStruct((n_z, rows_here, cols), BF16),
            jax.ShapeDtypeStruct((8, n_z * rows_here), F32),
            jax.ShapeDtypeStruct((tokens.shape[0], cols), BF16),
            jax.ShapeDtypeStruct(tokens.shape, BF16),
        ],
        scratch_shapes=[pltpu.VMEM((n_z, rows - rows_here, cols), F32)],
        compiler_params=pltpu.CompilerParams(vmem_limit_bytes=40 * 2**20),
        cost_estimate=NO_COST,
        name="project_kv",
    )(*pieces, tokens, cos, sin)


def query_kernel(own_ref, sib_ref, hid_ref, vec_ref, cos_ref, sin_ref, out_ref, q_ref):
    part_rows = own_ref.shape[2] // 2
    join_weight(own_ref, sib_ref, 0, part_rows, out_ref)
    whole = matmul(hid_ref[...], whole_weight(out_ref)) + vec_ref[2:3, :]
    for pair in range(HEADS // 2):
        lanes = slice(pair * 128, (pair + 1) * 128)
        tile = turn_tile(whole[:, lanes], cos_ref[...], sin_ref[...]).astype(BF16)
        q_ref[:, lanes] = (tile.astype(F32) * HEAD ** (-0.5)).astype(BF16)


def project_query(own, sib, hidden, vecs, cos, sin, rows_here):
    n_z, cols = own.shape[1], own.shape[3]
    vmem = pl.BlockSpec(memory_space=pltpu.VMEM)
    return pl.pallas_call(
        query_kernel,
        in_specs=[vmem] * 6,
        out_specs=[vmem] * 2,
        out_shape=[
            jax.ShapeDtypeStruct((n_z, rows_here, cols), BF16),
            jax.ShapeDtypeStruct((hidden.shape[0], cols), BF16),
        ],
        compiler_params=pltpu.CompilerParams(vmem_limit_bytes=40 * 2**20),
        cost_estimate=NO_COST,
        name="project_query",
    )(own, sib, hidden, vecs, cos, sin)


def out_kernel(own_ref, sib_ref, att_ref, x_ref, vec_ref, out_ref, resid_ref, hid_ref):
    part_rows = own_ref.shape[2] // 2
    join_weight(own_ref, sib_ref, part_rows, part_rows, out_ref)
    resid = x_ref[...].astype(F32) + matmul(att_ref[...], whole_weight(out_ref))
    resid_ref[...] = resid
    hid_ref[...] = normed_rows(resid, vec_ref[1:2, :])


def project_out(own, sib, attended, tokens, vecs, rows_here):
    n_z, cols = own.shape[1], own.shape[3]
    vmem = pl.BlockSpec(memory_space=pltpu.VMEM)
    return pl.pallas_call(
        out_kernel,
        in_specs=[vmem] * 5,
        out_specs=[vmem] * 3,
        out_shape=[
            jax.ShapeDtypeStruct((n_z, rows_here, cols), BF16),
            jax.ShapeDtypeStruct(tokens.shape, F32),
            jax.ShapeDtypeStruct(tokens.shape, BF16),
        ],
        compiler_params=pltpu.CompilerParams(vmem_limit_bytes=40 * 2**20),
        cost_estimate=NO_COST,
        name="project_out",
    )(own, sib, attended, tokens, vecs)


def kv_back_kernel(n_z, *refs):
    terms, rest = refs[:n_z], refs[n_z:]
    cos_ref, sin_ref, gq_ref, hid_ref, wq_ref, wkv_ref, x_ref, res_ref, vec_ref, two_ref = rest[:10]
    tokens_ref, part_ref = rest[10:]
    rows_here, width = x_ref.shape
    total = sum(t[...].astype(F32) for t in terms)
    half = total.shape[1] // 2
    keys = turn_tile(total[:, :half], cos_ref[...], -sin_ref[...]).astype(BF16)
    both = jnp.concatenate([keys, total[:, half:].astype(BF16)], 1)
    grad = times_transposed(gq_ref[...], wq_ref[...]) + times_transposed(both, wkv_ref[...])
    x = x_ref[...].astype(F32)
    inv = lax.rsqrt(jnp.mean(x * x, -1, keepdims=True) + NORM_EPS)
    normed = x * inv
    scaled = grad * vec_ref[0:1, :]
    tokens_ref[...] = res_ref[...] + inv * (
        scaled - normed * jnp.mean(scaled * normed, -1, keepdims=True)
    )
    sums = jnp.sum(both.astype(F32), 0, keepdims=True)
    share = half // n_z
    gap = jnp.zeros((1, width // n_z - share), F32)
    spread = []
    for i in range(2):
        cuts = []
        for z in range(n_z):
            at = i * half + z * share
            cuts += [sums[:, at : at + share], gap]
        spread.append(jnp.concatenate(cuts, 1))
    columns = [
        jnp.sum(grad * normed, 0, keepdims=True),
        two_ref[...],
        jnp.sum(gq_ref[...].astype(F32), 0, keepdims=True),
    ] + spread
    row = lax.broadcasted_iota(jnp.int32, (128, width), 0)
    table = jnp.zeros((128, width), F32)
    for i, v in enumerate(columns):
        table = jnp.where(row == i, v, table)
    part_ref[:, 2 * half :] = table.T.astype(BF16)
    pad = -rows_here % 128
    left = jnp.concatenate([hid_ref[...].astype(F32), jnp.zeros((pad, width), F32)], 0)
    right = jnp.concatenate([both, jnp.zeros((pad, 2 * half), BF16)], 0)
    part_ref[:, : 2 * half] = matmul(left.T.astype(BF16), right).astype(BF16)


def kv_back(terms, cos, sin, gq, hidden, wq, wkv, tokens, resid_grad, vecs, two_sum):
    vmem = pl.BlockSpec(memory_space=pltpu.VMEM)
    width = tokens.shape[1]
    return pl.pallas_call(
        functools.partial(kv_back_kernel, len(terms)),
        in_specs=[vmem] * (len(terms) + 10),
        out_specs=[vmem] * 2,
        out_shape=[
            jax.ShapeDtypeStruct(tokens.shape, F32),
            jax.ShapeDtypeStruct((width, wkv.shape[1] + 128), BF16),
        ],
        compiler_params=pltpu.CompilerParams(vmem_limit_bytes=40 * 2**20),
        cost_estimate=NO_COST,
        name="kv_back",
    )(*terms, cos, sin, gq, hidden, wq, wkv, tokens, resid_grad, vecs, two_sum)


def grad_weight_kernel(left_ref, right_ref, *refs):
    total = matmul(left_ref[...], right_ref[...])
    if len(refs) == 2:
        total = total + refs[0][...].astype(F32)
    refs[-1][...] = total.astype(BF16)


def grad_weight(left, right, other=None):
    rows, depth = left.shape
    cols = right.shape[1]
    tile = rows // 2 if rows % 32 == 0 else rows
    by_rows = lambda width: pl.BlockSpec((tile, width), lambda i: (i, 0))
    in_specs = [by_rows(depth), pl.BlockSpec((depth, cols), lambda i: (0, 0))]
    args = [left, right]
    if other is not None:
        in_specs.append(by_rows(cols))
        args.append(other)
    return pl.pallas_call(
        grad_weight_kernel,
        grid=(rows // tile,),
        in_specs=in_specs,
        out_specs=by_rows(cols),
        out_shape=jax.ShapeDtypeStruct((rows, cols), BF16),
        compiler_params=pltpu.CompilerParams(
            dimension_semantics=("arbitrary",), vmem_limit_bytes=40 * 2**20
        ),
        cost_estimate=NO_COST,
        name="grad_weight",
    )(*args)


def ff_kernel(tp, n_z, *refs):
    hidden, grads, weights = refs[:tp], refs[tp : 2 * tp], refs[2 * tp : 2 * tp + 4]
    rest = refs[2 * tp + 4 :]
    act_refs, back_refs, (hid_t, grad_all) = rest[:2], rest[2:4], rest[4:6]
    dh_outs, outs = rest[6 : 6 + tp], rest[6 + tp : 6 + 2 * tp]
    gu_buf, down_buf, acc, acc_out, sems = rest[6 + 2 * tp :]
    part_rows = weights[2].shape[1]
    gu_copies = [
        pltpu.make_async_copy(weights[i], gu_buf.at[i], sems.at[i]) for i in range(2)
    ]
    down_copies = []
    for i in range(2):
        for z in range(n_z):
            to = down_buf.at[i, pl.ds(z * part_rows, part_rows)]
            sem = sems.at[2 + i * n_z + z]
            down_copies.append(pltpu.make_async_copy(weights[2 + i].at[z], to, sem))
    gu_copies[0].start()
    for c in down_copies[:n_z]:
        c.start()
    gu_copies[1].start()
    for c in down_copies[n_z:]:
        c.start()
    tokens_here = hidden[0].shape[0]
    half = down_buf.shape[1]
    step = 2 if tp % 2 == 0 else 1
    for i in range(2):
        gu_copies[i].wait()
        for t in range(0, tp, step):
            rows = slice(t * tokens_here, (t + step) * tokens_here)
            here = jnp.concatenate([hidden[t + n][...] for n in range(step)], 0)
            grad = jnp.concatenate([grads[t + n][...] for n in range(step)], 0)
            if i == 0:
                hid_t[:, rows] = here.astype(F32).T.astype(BF16)
                grad_all[rows, :] = grad
            gate = matmul(here, gu_buf[i, :, :half])
            up = matmul(here, gu_buf[i, :, half:])
            if t == 0:
                for c in down_copies[i * n_z : (i + 1) * n_z]:
                    c.wait()
            grad_act = times_transposed(grad, down_buf[i])
            sig = 1.0 / (1.0 + jnp.exp(-gate))
            silu = gate * sig
            act = silu * up
            act_refs[i][:, rows] = act.T.astype(BF16)
            grad_gate = (grad_act * up * (sig + silu * (1.0 - sig))).astype(BF16)
            grad_up = (grad_act * silu).astype(BF16)
            back_refs[i][rows, :half] = grad_gate
            back_refs[i][rows, half:] = grad_up
            part = times_transposed(grad_gate, gu_buf[i, :, :half]) + times_transposed(
                grad_up, gu_buf[i, :, half:]
            )
            out = matmul(act.astype(BF16), down_buf[i])
            if i == 0:
                acc[rows, :] = part
                acc_out[rows, :] = out
            else:
                part = (part + acc[rows, :]).astype(BF16)
                out = (out + acc_out[rows, :]).astype(BF16)
                for n in range(step):
                    mine = slice(n * tokens_here, (n + 1) * tokens_here)
                    dh_outs[t + n][...] = part[mine]
                    outs[t + n][...] = out[mine]


def ff_pass(hidden, grads, gu, down):
    tp = len(hidden)
    n_z, part_rows = down[0].shape[:2]
    tokens_here, width = hidden[0].shape
    half = n_z * part_rows
    rows = tp * tokens_here
    vmem = pl.BlockSpec(memory_space=pltpu.VMEM)
    got = pl.pallas_call(
        functools.partial(ff_kernel, tp, n_z),
        in_specs=[vmem] * (2 * tp) + [pl.BlockSpec(memory_space=pl.ANY)] * 4,
        out_specs=[vmem] * (2 * tp + 6),
        out_shape=[jax.ShapeDtypeStruct((half, rows), BF16)] * 2
        + [jax.ShapeDtypeStruct((rows, 2 * half), BF16)] * 2
        + [jax.ShapeDtypeStruct((width, rows), BF16), jax.ShapeDtypeStruct((rows, width), BF16)]
        + [jax.ShapeDtypeStruct((tokens_here, width), BF16)] * (2 * tp),
        scratch_shapes=[
            pltpu.VMEM((2, width, 2 * half), BF16),
            pltpu.VMEM((2, half, width), BF16),
            pltpu.VMEM((rows, width), F32),
            pltpu.VMEM((rows, width), F32),
            pltpu.SemaphoreType.DMA((2 + 2 * n_z,)),
        ],
        compiler_params=pltpu.CompilerParams(vmem_limit_bytes=58 * 2**20),
        cost_estimate=NO_COST,
        name="ff_pass",
    )(*hidden, *grads, *gu, *down)
    return got[:2], got[2:4], got[4], got[5], got[6 : 6 + tp], got[6 + tp :]


def local(
    tokens,
    out_grad,
    block_order,
    norm1_gain,
    q_weight,
    q_bias,
    k_weight,
    k_bias,
    v_weight,
    v_bias,
    o_weight,
    norm2_gain,
    gate_weight,
    up_weight,
    down_weight,
):
    n_ctx = lax.axis_size("ctx")
    n_z = lax.axis_size("fsdp")
    tp = 4 if n_ctx % 4 == 0 else (2 if n_ctx % 2 == 0 else 1)
    here = lax.axis_index("ctx")
    zed = lax.axis_index("fsdp")
    core = lax.axis_index("seq")
    n_part = 2 * tp
    part = core * tp + lax.rem(here, tp)

    def swap(v):
        return lax.ppermute(v, "seq", [(0, 1), (1, 0)])

    def hop(v, k):
        if k == 0:
            return v
        return lax.ppermute(v, "ctx", [(i, i ^ k) for i in range(n_ctx)])

    def hop_z(v, k):
        if k == 0:
            return v
        return lax.ppermute(v, "fsdp", [(i, i ^ k) for i in range(n_z)])

    def gather_z(v):
        return lax.all_gather(v, "fsdp", axis=0, tiled=True)

    def scatter_z(v):
        return lax.psum_scatter(v, "fsdp", scatter_dimension=0, tiled=True)

    tokens_here, width = tokens.shape[1:]
    ff = gate_weight.shape[1]
    rows_here = q_weight.shape[0]
    key_width = KV_HEADS * HEAD
    block_len = tokens_here * n_z

    part_rows = -(-rows_here // (n_part * 32)) * 32

    kb = k_bias.shape[0]
    vectors = (norm1_gain, norm2_gain, q_bias, k_bias, v_bias)
    vec = sum(
        jnp.pad(v[None], ((i, 15 - i), (0, 2 * key_width - v.shape[0])))
        for i, v in enumerate(vectors)
    )
    kv_pack = jnp.concatenate([jnp.concatenate([k_weight, v_weight], 1), vec], 0)
    og_here = out_grad[0]

    def own_part(w):
        return lax.dynamic_slice_in_dim(w, part * part_rows, part_rows, 0)

    ff_z = ff // n_z
    piece = ff_z // n_part
    piece_pad = -(-piece // 32) * 32

    def ff_columns(w):
        cuts = []
        for j in range(n_z):
            cut = lax.dynamic_slice_in_dim(w, j * ff_z + part * piece, piece, 1)
            cuts.append(jnp.pad(cut, ((0, 0), (0, piece_pad - piece))))
        return jnp.concatenate(cuts, 1)

    order_row = block_order[0]
    x_here = tokens[0]
    kv_pack, q_part, o_part, gate_weight, up_weight, down_weight, query_at = (
        lax.optimization_barrier(
            (
                kv_pack,
                own_part(q_weight),
                own_part(o_weight),
                gate_weight,
                up_weight,
                down_weight,
                order_row[here] * block_len + zed * tokens_here,
            )
        )
    )
    pack_rows = kv_pack.shape[0]
    qo_part = jnp.concatenate([q_part, o_part], 0)
    pack = jnp.concatenate([kv_pack, qo_part.reshape(-1, 2 * key_width)], 0)
    got = [hop_z(pack, k) for k in range(n_z)]
    gu_cut = jnp.concatenate([ff_columns(gate_weight), ff_columns(up_weight)], 1)
    down_cut = lax.dynamic_slice_in_dim(down_weight, part * piece, piece, 0)
    down_cut = jnp.pad(down_cut, ((0, piece_pad - piece), (0, 0)))
    query_pos = query_at + jnp.arange(tokens_here, dtype=jnp.int32)
    cosine_table, sine_table = rope_tables(query_pos, HEAD)
    cos_wide = jnp.tile(cosine_table[:, 0], (1, 4))
    sin_wide = jnp.tile(jnp.concatenate([-sine_table[:, 0], sine_table[:, 0]], 1), (1, 2))
    got, cos_wide, sin_wide, gu_cut, down_cut, og_here = lax.optimization_barrier(
        (got, cos_wide, sin_wide, gu_cut, down_cut, og_here)
    )
    kv_got = [v[:pack_rows] for v in got]

    qo_got = jnp.stack([v[pack_rows:].reshape(2 * part_rows, width) for v in got])
    qo_own = [hop(qo_got, k) for k in range(tp)]
    widths = tuple(v.shape[0] for v in vectors)
    w_kv, vecs, kv_local, hidden_one = project_kv(
        kv_got, x_here, cos_wide, sin_wide, rows_here, widths
    )
    w_kv = w_kv.reshape(width, 2 * key_width)
    gain_one = vecs[0:1, :width]
    gain_two = vecs[1:2, :width]
    kv_z = [hop_z(kv_local, k) for k in range(n_z)]
    gu_own = gather_z(gu_cut)
    kv_z, qo_own = lax.optimization_barrier((kv_z, qo_own))

    kv_block = jnp.concatenate(kv_z, 0)
    if n_ctx == tp:
        kv_blocks = [hop(kv_block, k) for k in range(n_ctx)]
    else:
        kv_blocks = lax.all_gather(kv_block, "ctx", axis=0, tiled=False)
    qo_own = jnp.stack(qo_own)
    qo_sib = swap(qo_own)
    w_query, queries = project_query(
        qo_own, qo_sib, hidden_one, vecs, cos_wide, sin_wide, rows_here
    )
    w_query = w_query.reshape(width, width)
    kv_blocks, queries, og_here, down_cut, gu_own = lax.optimization_barrier(
        (kv_blocks, queries, og_here, down_cut, gu_own)
    )

    og_parts = [hop(og_here, k) for k in range(tp)]
    kv_whole = jnp.stack(kv_blocks) if n_ctx == tp else kv_blocks
    attended, queries_ext = attend_forward(order_row, n_ctx == tp, queries, kv_whole)
    down_own = gather_z(down_cut)
    attended, queries_ext, og_parts = lax.optimization_barrier((attended, queries_ext, og_parts))
    w_out, resid, hidden_two = project_out(
        qo_own, qo_sib, attended, x_here, vecs, rows_here
    )
    w_out = w_out.reshape(width, width)
    h2_parts = [hop(hidden_two, k) for k in range(tp)]
    gu_oth = swap(gu_own)
    h2_parts, down_own = lax.optimization_barrier((h2_parts, down_own))
    down_own = down_own.reshape(n_z, piece_pad, width)
    down_oth = swap(down_own)

    acts, ggus, h2_turned, og_all, dh2, ff_out = ff_pass(
        h2_parts, og_parts, (gu_own, gu_oth), (down_own, down_oth)
    )
    grad_h2_parts = [hop(dh2[k], k) for k in range(tp)]

    def share_pieces(mine):
        own = jnp.stack([hop(mine, k) for k in range(tp)])
        return own, swap(own)

    def core_halves(part_sum):
        cols = part_sum.shape[1]
        cut = part_sum.astype(BF16).reshape(n_z, rows_here, cols)
        cut = jnp.pad(cut, ((0, 0), (0, n_part * part_rows - rows_here), (0, 0)))
        own = lax.dynamic_slice_in_dim(cut, core * tp * part_rows, tp * part_rows, 1)
        oth = lax.dynamic_slice_in_dim(cut, (1 - core) * tp * part_rows, tp * part_rows, 1)
        return own, oth

    def core_total(own, sib):
        return (own.astype(F32) + sib.astype(F32)).astype(BF16)

    def scatter_parts(cut):
        cut = cut.reshape(n_z, tp, part_rows, -1)
        at = lax.rem(here, tp)
        return [
            hop(lax.dynamic_index_in_dim(cut, at ^ k, 1, keepdims=False), k) for k in range(tp)
        ]

    def ctx_groups_sum(v):
        if n_ctx == tp:
            return v
        groups = [[g * tp + c for g in range(n_ctx // tp)] for c in range(tp)]
        return lax.psum(v, "ctx", axis_index_groups=groups)

    d_gu = grad_weight(h2_turned, ggus[0], swap(grad_weight(h2_turned, ggus[1])))
    grad_h2_parts, d_gu = lax.optimization_barrier((grad_h2_parts, d_gu))
    grad_h2 = sum(v.astype(F32) for v in grad_h2_parts)
    scale_two = lax.rsqrt(jnp.mean(resid * resid, -1, keepdims=True) + NORM_EPS)
    normed_two = resid * scale_two

    grad_norm_two, gain_two_terms = rms_backward(grad_h2, normed_two, scale_two, gain_two)
    grad_resid = og_here.astype(F32) + grad_norm_two
    grad_proj = grad_resid.astype(BF16)
    grad_att = times_transposed(grad_proj, w_out).astype(BF16)
    grad_att, d_gu, ff_out = lax.optimization_barrier((grad_att, d_gu, ff_out))
    d_gu = scatter_z(d_gu)
    ff_out = [hop(ff_out[k], k) for k in range(tp)]
    grad_q_pre, grad_terms = attend_backward(
        order_row, n_ctx == tp, queries_ext, grad_att, attended, cos_wide, sin_wide, kv_whole
    )
    grad_q_pre, grad_terms, ff_out, acts, grad_proj = lax.optimization_barrier(
        (grad_q_pre, grad_terms, ff_out, acts, grad_proj)
    )
    d_down = grad_weight(acts[0], og_all, swap(grad_weight(acts[1], og_all)))

    qo_own, qo_oth = core_halves(
        jnp.concatenate(
            [contract_rows(hidden_one, grad_q_pre), contract_rows(attended, grad_proj)], 1
        )
    )
    if n_ctx == tp:
        kv_terms = [hop(grad_terms[k], k) for k in range(n_ctx)]
    else:
        kv_terms = [lax.psum_scatter(grad_terms, "ctx", scatter_dimension=0, tiled=False)]
    kv_terms, d_gu, d_down, qo_own, qo_oth, ff_out = lax.optimization_barrier(
        (kv_terms, d_gu, d_down, qo_own, qo_oth, ff_out)
    )

    kv_sum = sum(v.astype(F32) for v in kv_terms).astype(BF16)
    kv_sum = kv_sum.reshape(n_z, tokens_here, 2 * key_width)
    kv_terms = [hop_z(kv_sum[k], k) for k in range(n_z)]
    d_gu = ctx_groups_sum(d_gu)
    gu_pieces = [hop(d_gu, k) for k in range(tp)]
    qo_sib = swap(qo_oth)
    result = resid + sum(v.astype(F32) for v in ff_out)
    layer_out = result.astype(BF16)[None]
    d_down = scatter_z(d_down)
    kv_terms, qo_own, qo_sib = lax.optimization_barrier((kv_terms, qo_own, qo_sib))

    tokens_grad, kv_part = kv_back(
        kv_terms,
        cos_wide,
        sin_wide,
        grad_q_pre,
        hidden_one,
        w_query,
        w_kv,
        x_here,
        grad_resid,
        vecs,
        jnp.sum(gain_two_terms, 0, keepdims=True),
    )
    tokens_grad = tokens_grad[None]
    kv_own, kv_oth = core_halves(kv_part)
    last = core_total(qo_own, qo_sib)
    kv_own, kv_sib, last = lax.optimization_barrier((kv_own, swap(kv_oth), last))

    last = scatter_parts(jnp.concatenate([last, core_total(kv_own, kv_sib)], 2))
    last, d_down, gu_pieces = lax.optimization_barrier((last, d_down, gu_pieces))

    last = sum(v.astype(F32) for v in last).astype(BF16)
    last = [
        hop_z(lax.dynamic_index_in_dim(last, zed ^ k, 0, keepdims=False), k) for k in range(n_z)
    ]
    d_down = ctx_groups_sum(d_down)
    gu_pieces = jnp.stack(gu_pieces)
    gu_sib = swap(gu_pieces)
    last, d_down, gu_pieces, gu_sib = lax.optimization_barrier(
        (last, d_down, gu_pieces, gu_sib)
    )

    last = ctx_groups_sum(sum(v.astype(F32) for v in last).astype(BF16))
    last = lax.optimization_barrier(last)
    last = [hop(last, k) for k in range(tp)]
    down_pieces = [hop(d_down, k) for k in range(tp)]
    down_pieces = jnp.stack(down_pieces)
    down_sib = swap(down_pieces)
    grad_w_gate, grad_w_up = spread_columns((gu_pieces, gu_sib), n_z, ff, 2)
    last, down_pieces, down_sib, grad_w_gate, grad_w_up = lax.optimization_barrier(
        (last, down_pieces, down_sib, grad_w_gate, grad_w_up)
    )
    last = jnp.stack(last)
    grad_w_down = spread_rows((down_pieces, down_sib), piece, ff_z)
    last = spread_rows((last, swap(last)), part_rows, rows_here)
    grad_w_query = last[:, :width]
    grad_w_out = last[:, width : 2 * width]
    grad_w_kv = last[:, 2 * width :]
    sums = grad_w_kv[:, 2 * key_width :]

    return (
        layer_out,
        tokens_grad,
        sums[:, 0],
        grad_w_query,
        sums[:, 2],
        grad_w_kv[:, :key_width],
        sums[:kb, 3],
        grad_w_kv[:, key_width : 2 * key_width],
        sums[:kb, 4],
        grad_w_out,
        sums[:, 1],
        grad_w_gate,
        grad_w_up,
        grad_w_down,
    )


def solution(mesh):
    in_specs = (
        P("seq", ("ctx", "fsdp"), None),
        P("seq", ("ctx", "fsdp"), None),
        P("seq", None),
        P("fsdp"),
        P("fsdp", None),
        P("fsdp"),
        P("fsdp", None),
        P("fsdp"),
        P("fsdp", None),
        P("fsdp"),
        P("fsdp", None),
        P("fsdp"),
        P("fsdp", None),
        P("fsdp", None),
        P("fsdp", None),
    )
    out_specs = (
        P("seq", ("ctx", "fsdp"), None),
        P("seq", ("ctx", "fsdp"), None),
        P("fsdp"),
        P("fsdp", None),
        P("fsdp"),
        P("fsdp", None),
        P("fsdp"),
        P("fsdp", None),
        P("fsdp"),
        P("fsdp", None),
        P("fsdp"),
        P("fsdp", None),
        P("fsdp", None),
        P("fsdp", None),
    )
    return jax.shard_map(local, mesh=mesh, in_specs=in_specs, out_specs=out_specs, check_vma=False)
```

```python
import functools
import math

import jax
import jax.numpy as jnp
from jax import lax
from jax.experimental import pallas as pl
from jax.experimental.pallas import tpu as pltpu
from jax.sharding import PartitionSpec as P

HEADS = 14
KV_HEADS = 2
HEAD = 64
GROUP = HEADS // KV_HEADS
NORM_EPS = 1e-06
ROPE_BASE = 1000000.0
MASKED = -1e30
BF16 = jnp.bfloat16
F32 = jnp.float32
NO_COST = pl.CostEstimate(flops=0, bytes_accessed=0, transcendentals=0)


def rope_tables(positions, head_dim):
    half_dim = head_dim // 2
    inverse = jnp.exp(
        jnp.arange(half_dim, dtype=jnp.float32) * (-math.log(ROPE_BASE) * 2.0 / head_dim)
    )
    angles = positions.astype(jnp.float32)[:, None] * inverse[None, :]
    return (jnp.cos(angles)[:, None, :], jnp.sin(angles)[:, None, :])


def matmul(left_side, right_side):
    return jnp.dot(left_side, right_side, preferred_element_type=F32)


def contract_rows(left_side, right_side):
    return lax.dot_general(
        left_side, right_side, (((0,), (0,)), ((), ())), preferred_element_type=F32
    )


def times_transposed(left_side, right_side):
    return lax.dot_general(
        left_side, right_side, (((1,), (1,)), ((), ())), preferred_element_type=F32
    )


def rms_backward(grad_out, normed, inv_scale, gain_vec):
    scaled = grad_out * gain_vec
    grad_in = inv_scale * (scaled - normed * jnp.mean(scaled * normed, -1, keepdims=True))
    return (grad_in, grad_out * normed)


def cut_heads(ref, head):
    tile = ref[:, (head // 2) * 128 : (head // 2 + 1) * 128].astype(F32)
    group = head // GROUP
    if head % 2 != group:
        tile = jnp.concatenate([tile[:, HEAD:], tile[:, :HEAD]], 1)
    lane = lax.broadcasted_iota(jnp.int32, tile.shape, 1)
    return jnp.where((lane >= HEAD) if group else (lane < HEAD), tile, 0.0)


def split_lanes(column, shape):
    high = column.astype(BF16).astype(F32)
    mid = (column - high).astype(BF16).astype(F32)
    low = column - high - mid
    lane = lax.broadcasted_iota(jnp.int32, shape, 1)
    return jnp.where(
        lane == 0, high, jnp.where(lane == 1, mid, jnp.where(lane == 2, low, 0.0))
    ).astype(BF16)


def piece_shift(at, zed, tokens_here, keys_here):
    pieces = keys_here // tokens_here
    shift = jnp.zeros(at.shape, jnp.int32)
    for k in range(pieces):
        here = (jnp.bitwise_xor(zed, k) - k - zed) * tokens_here
        shift = jnp.where(at >= k * tokens_here, here, shift)
    return shift


def forward_kernel(by_xor, info_ref, q_ref, kv_ref, att_ref, qext_ref, top_ref, acc_ref):
    step = pl.program_id(0)
    last = pl.num_programs(0) - 1
    tokens_here = q_ref.shape[0]
    keys_here = kv_ref.shape[1]
    here = lax.axis_index("ctx")
    zed = lax.axis_index("fsdp")
    own = info_ref[here]
    block = info_ref[jnp.bitwise_xor(here, step) if by_xor else step]

    @pl.when(step == 0)
    def _():
        for h in range(HEADS):
            qext_ref[h * tokens_here : (h + 1) * tokens_here, :128] = cut_heads(q_ref, h).astype(
                BF16
            )
        top_ref[...] = jnp.full(top_ref.shape, MASKED, F32)
        acc_ref[...] = jnp.zeros(acc_ref.shape, F32)

    def attend(masked):
        keys = kv_ref[0, :, :128]
        values = jnp.concatenate(
            [kv_ref[0, :, 128:], jnp.ones((keys_here, 128), BF16)], 1
        )
        if masked:
            row = lax.broadcasted_iota(jnp.int32, (tokens_here, keys_here), 0)
            col = lax.broadcasted_iota(jnp.int32, (tokens_here, keys_here), 1)
            allowed = col + piece_shift(col, zed, tokens_here, keys_here) <= row
        for h in range(HEADS):
            rows = slice(h * tokens_here, (h + 1) * tokens_here)
            scores = times_transposed(qext_ref[rows, :128], keys)
            if masked:
                scores = jnp.where(allowed, scores, MASKED)
            old = top_ref[rows, :]
            top = jnp.maximum(old, jnp.max(scores, -1, keepdims=True))
            probs = jnp.exp(scores - top[:, :1]).astype(BF16)
            shrink = jnp.exp(old - top)
            top_ref[rows, :] = top
            acc_ref[rows, :] = acc_ref[rows, :] * jnp.concatenate([shrink, shrink], 1) + matmul(
                probs, values
            )

    @pl.when(block == own)
    def _():
        attend(True)

    @pl.when(block < own)
    def _():
        attend(False)

    @pl.when(step == last)
    def _():
        lane = lax.broadcasted_iota(jnp.int32, (tokens_here, 128), 1)
        for pair in range(HEADS // 2):
            outs = []
            for h in (2 * pair, 2 * pair + 1):
                rows = slice(h * tokens_here, (h + 1) * tokens_here)
                total = acc_ref[rows, 128:]
                out = acc_ref[rows, :128] / total
                if h // GROUP != h % 2:
                    out = jnp.concatenate([out[:, HEAD:], out[:, :HEAD]], 1)
                outs.append(out)
                log_total = top_ref[rows, :] + jnp.log(total)
                qext_ref[rows, 128:] = split_lanes(-log_total, (tokens_here, 128))
            att_ref[:, pair * 128 : (pair + 1) * 128] = jnp.where(
                lane < HEAD, outs[0], outs[1]
            ).astype(BF16)


def backward_kernel(
    by_xor, info_ref, qext_ref, do_ref, att_ref, cos_ref, sin_ref, kv_ref, dq_ref, dkv_ref,
    doext_ref, dqt_ref
):
    step = pl.program_id(0)
    last = pl.num_programs(0) - 1
    tokens_here = do_ref.shape[0]
    keys_here = kv_ref.shape[1]
    here = lax.axis_index("ctx")
    zed = lax.axis_index("fsdp")
    own = info_ref[here]
    block = info_ref[jnp.bitwise_xor(here, step) if by_xor else step]
    span = 2 * tokens_here

    @pl.when(step == 0)
    def _():
        for h in range(HEADS):
            rows = slice(h * tokens_here, (h + 1) * tokens_here)
            grad = cut_heads(do_ref, h)
            delta = jnp.sum(grad * cut_heads(att_ref, h), -1, keepdims=True)
            doext_ref[rows, :128] = grad.astype(BF16)
            doext_ref[rows, 128:] = split_lanes(-delta, (tokens_here, 128))
        dqt_ref[...] = jnp.zeros(dqt_ref.shape, F32)

    def attend(masked):
        lane = lax.broadcasted_iota(jnp.int32, (keys_here, 128), 1)
        ones = jnp.where(lane < 3, 1.0, 0.0).astype(BF16)
        keys = kv_ref[0, :, :128]
        keys_ext = jnp.concatenate([keys, ones], 1)
        values_ext = jnp.concatenate([kv_ref[0, :, 128:], ones], 1)
        keys_t = keys.astype(F32).T.astype(BF16)
        if masked:
            row = lax.broadcasted_iota(jnp.int32, (keys_here, tokens_here), 0)
            col = lax.broadcasted_iota(jnp.int32, (keys_here, tokens_here), 1)
            allowed = row + piece_shift(row, zed, tokens_here, keys_here) <= col
            allowed = allowed.astype(F32)
            allowed = jnp.concatenate([allowed, allowed], 1) > 0.5
        dk = jnp.zeros((keys_here, 128), F32)
        dv = jnp.zeros((keys_here, 128), F32)
        for pair in range(HEADS // 2):
            rows = slice(pair * span, (pair + 1) * span)
            probs = jnp.exp(times_transposed(keys_ext, qext_ref[rows, :]))
            if masked:
                probs = jnp.where(allowed, probs, 0.0)
            slope = (probs * times_transposed(values_ext, doext_ref[rows, :])).astype(BF16)
            dv = dv + matmul(probs.astype(BF16), doext_ref[rows, :128])
            dk = dk + matmul(slope, qext_ref[rows, :128])
            dqt_ref[pair] = dqt_ref[pair] + matmul(keys_t, slope)
        dkv_ref[0] = jnp.concatenate([dk, dv], 1).astype(BF16)

    @pl.when(block == own)
    def _():
        attend(True)

    @pl.when(block < own)
    def _():
        attend(False)

    @pl.when(block > own)
    def _():
        dkv_ref[...] = jnp.zeros(dkv_ref.shape, BF16)

    @pl.when(step == last)
    def _():
        lane = lax.broadcasted_iota(jnp.int32, (tokens_here, 128), 1)
        for pair in range(HEADS // 2):
            turned = dqt_ref[pair].T
            outs = []
            for j in range(2):
                h = 2 * pair + j
                out = turned[j * tokens_here : (j + 1) * tokens_here]
                if h // GROUP != j:
                    out = jnp.concatenate([out[:, HEAD:], out[:, :HEAD]], 1)
                outs.append(out)
            out = jnp.where(lane < HEAD, outs[0], outs[1]) * HEAD ** (-0.5)
            dq_ref[:, pair * 128 : (pair + 1) * 128] = turn_tile(
                out, cos_ref[...], -sin_ref[...]
            ).astype(BF16)


def whole_spec(shape):
    return pl.BlockSpec(shape, lambda i, info: (0,) * len(shape))


def attend_forward(info, by_xor, queries, kv):
    blocks, block_len, kv_width = kv.shape
    tokens_here, q_width = queries.shape
    rows = HEADS * tokens_here
    return pl.pallas_call(
        functools.partial(forward_kernel, by_xor),
        grid_spec=pltpu.PrefetchScalarGridSpec(
            num_scalar_prefetch=1,
            grid=(blocks,),
            in_specs=[
                whole_spec((tokens_here, q_width)),
                pl.BlockSpec((1, block_len, kv_width), lambda i, info: (i, 0, 0)),
            ],
            out_specs=[whole_spec((tokens_here, q_width)), whole_spec((rows, 256))],
            scratch_shapes=[pltpu.VMEM((rows, 128), F32), pltpu.VMEM((rows, 256), F32)],
        ),
        out_shape=[
            jax.ShapeDtypeStruct((tokens_here, q_width), BF16),
            jax.ShapeDtypeStruct((rows, 256), BF16),
        ],
        compiler_params=pltpu.CompilerParams(
            dimension_semantics=("arbitrary",), vmem_limit_bytes=40 * 2**20
        ),
        cost_estimate=pl.CostEstimate(
            flops=3 * 10**10, bytes_accessed=2**23, transcendentals=0
        ),
        name="attend_forward",
    )(info, queries, kv)


def attend_backward(info, by_xor, queries_ext, grad_att, attended, cos, sin, kv):
    blocks, block_len, kv_width = kv.shape
    tokens_here, q_width = grad_att.shape
    rows = HEADS * tokens_here
    return pl.pallas_call(
        functools.partial(backward_kernel, by_xor),
        grid_spec=pltpu.PrefetchScalarGridSpec(
            num_scalar_prefetch=1,
            grid=(blocks,),
            in_specs=[
                whole_spec((rows, 256)),
                whole_spec((tokens_here, q_width)),
                whole_spec((tokens_here, q_width)),
                whole_spec(cos.shape),
                whole_spec(sin.shape),
                pl.BlockSpec((1, block_len, kv_width), lambda i, info: (i, 0, 0)),
            ],
            out_specs=[
                whole_spec((tokens_here, q_width)),
                pl.BlockSpec((1, block_len, kv_width), lambda i, info: (i, 0, 0)),
            ],
            scratch_shapes=[
                pltpu.VMEM((rows, 256), BF16),
                pltpu.VMEM((HEADS // 2, 128, 2 * tokens_here), F32),
            ],
        ),
        out_shape=[
            jax.ShapeDtypeStruct((tokens_here, q_width), BF16),
            jax.ShapeDtypeStruct(kv.shape, BF16),
        ],
        compiler_params=pltpu.CompilerParams(
            dimension_semantics=("arbitrary",), vmem_limit_bytes=40 * 2**20
        ),
        cost_estimate=pl.CostEstimate(
            flops=5 * 10**10, bytes_accessed=2**23, transcendentals=0
        ),
        name="attend_backward",
    )(info, queries_ext, grad_att, attended, cos, sin, kv)


def part_place(tp, j, k):
    at = jnp.bitwise_xor(lax.rem(lax.axis_index("ctx"), tp), k)
    return jnp.bitwise_xor(lax.axis_index("seq"), j) * tp + at


def spread_columns_kernel(n_z, *refs):
    pieces, outs, held = refs[:2], refs[2:-1], refs[-1]
    tp = pieces[0].shape[0]
    n_part = 2 * tp
    for j in range(2):
        for k in range(tp):
            held[part_place(tp, j, k)] = pieces[j][k].astype(F32)
    half = held.shape[2] // len(outs)
    pad = half // n_z
    for i, out in enumerate(outs):
        piece = out.shape[1] // (n_z * n_part)
        cuts = []
        for j in range(n_z):
            for e in range(n_part):
                start = i * half + j * pad
                cuts.append(held[e, :, start : start + piece])
        out[...] = jnp.concatenate(cuts, 1)


def spread_columns(pieces, n_z, ff, outs):
    tp, rows, cols = pieces[0].shape
    tile = 32
    return pl.pallas_call(
        functools.partial(spread_columns_kernel, n_z),
        grid=(rows // tile,),
        in_specs=[pl.BlockSpec((tp, tile, cols), lambda i: (0, i, 0))] * 2,
        out_specs=[pl.BlockSpec((tile, ff), lambda i: (i, 0))] * outs,
        scratch_shapes=[pltpu.VMEM((2 * tp, tile, cols), F32)],
        out_shape=[jax.ShapeDtypeStruct((rows, ff), F32)] * outs,
        compiler_params=pltpu.CompilerParams(
            dimension_semantics=("arbitrary",), vmem_limit_bytes=40 * 2**20
        ),
        cost_estimate=pl.CostEstimate(
            flops=10**10, bytes_accessed=2**23, transcendentals=0
        ),
        name="spread_columns",
    )(*pieces)


def spread_rows_kernel(piece, *refs):
    pieces, out_ref = refs[:-1], refs[-1]
    room = out_ref.shape[0] // piece
    tp = pieces[0].shape[0]
    for j in range(2):
        for k in range(tp):
            place = part_place(tp, j, k)

            @pl.when(place < room)
            def _():
                start = pl.multiple_of(place * piece, 8)
                out_ref[pl.ds(start, piece), :] = pieces[j][k].astype(F32)[:piece]


def spread_rows(pieces, piece, rows_out):
    tp, rows, cols = pieces[0].shape
    tile = 128
    return pl.pallas_call(
        functools.partial(spread_rows_kernel, piece),
        grid=(cols // tile,),
        in_specs=[pl.BlockSpec((tp, rows, tile), lambda i: (0, 0, i))] * 2,
        out_specs=pl.BlockSpec((rows_out, tile), lambda i: (0, i)),
        out_shape=jax.ShapeDtypeStruct((rows_out, cols), F32),
        compiler_params=pltpu.CompilerParams(
            dimension_semantics=("arbitrary",), vmem_limit_bytes=40 * 2**20
        ),
        cost_estimate=NO_COST,
        name="spread_rows",
    )(*pieces)


def join_weight(own_ref, sib_ref, first, part_rows, out_ref):
    tp, n_z = own_ref.shape[:2]
    room = out_ref.shape[1] // part_rows
    for j, ref in enumerate((own_ref, sib_ref)):
        for k in range(tp):
            place = part_place(tp, j, k)

            @pl.when(place < room)
            def _():
                start = pl.multiple_of(place * part_rows, 16)
                for z in range(n_z):
                    at = jnp.bitwise_xor(lax.axis_index("fsdp"), z)
                    out_ref[at, pl.ds(start, part_rows), :] = ref[k, z, first : first + part_rows]


def whole_weight(ref):
    return jnp.concatenate([ref[z] for z in range(ref.shape[0])], 0)


def turn_tile(tile, cos, sin):
    h = HEAD // 2
    cuts = [tile[:, h : 2 * h], tile[:, :h], tile[:, 3 * h :], tile[:, 2 * h : 3 * h]]
    return tile * cos + jnp.concatenate(cuts, 1) * sin


def normed_rows(values, gain):
    inv = lax.rsqrt(jnp.mean(values * values, -1, keepdims=True) + NORM_EPS)
    return (values * inv * gain).astype(BF16)


def kv_kernel(widths, *refs):
    x_ref, cos_ref, sin_ref = refs[-8:-5]
    pieces, (out_ref, vec_ref, kv_ref, hid_ref, held) = refs[:-8], refs[-5:]
    n_z, rows_here, cols = out_ref.shape
    for k in range(n_z):
        at = jnp.bitwise_xor(lax.axis_index("fsdp"), k)
        out_ref[at] = pieces[k][:rows_here]
        held[at] = pieces[k][rows_here : rows_here + held.shape[1]].astype(F32)
    vec_ref[...] = jnp.zeros(vec_ref.shape, F32)
    for i, size in enumerate(widths):
        row = jnp.concatenate([held[z, i : i + 1, :size] for z in range(n_z)], 1)
        vec_ref[i : i + 1, : n_z * size] = row
    hidden = normed_rows(x_ref[...].astype(F32), vec_ref[0:1, :])
    hid_ref[...] = hidden
    half = cols // 2
    both = matmul(hidden, whole_weight(out_ref))
    keys = both[:, :half] + vec_ref[3:4, :half]
    kv_ref[:, :half] = turn_tile(keys, cos_ref[...], sin_ref[...]).astype(BF16)
    kv_ref[:, half:] = (both[:, half:] + vec_ref[4:5, :half]).astype(BF16)


def project_kv(pieces, tokens, cos, sin, rows_here, vec_rows, widths):
    cols = pieces[0].shape[1]
    n_z = len(pieces)
    vmem = pl.BlockSpec(memory_space=pltpu.VMEM)
    return pl.pallas_call(
        functools.partial(kv_kernel, widths),
        in_specs=[vmem] * (n_z + 3),
        out_specs=[vmem] * 4,
        out_shape=[
            jax.ShapeDtypeStruct((n_z, rows_here, cols), BF16),
            jax.ShapeDtypeStruct((8, n_z * rows_here), F32),
            jax.ShapeDtypeStruct((tokens.shape[0], cols), BF16),
            jax.ShapeDtypeStruct(tokens.shape, BF16),
        ],
        scratch_shapes=[pltpu.VMEM((n_z, vec_rows, cols), F32)],
        compiler_params=pltpu.CompilerParams(vmem_limit_bytes=40 * 2**20),
        cost_estimate=NO_COST,
        name="project_kv",
    )(*pieces, tokens, cos, sin)


def query_kernel(own_ref, sib_ref, hid_ref, vec_ref, cos_ref, sin_ref, out_ref, q_ref):
    part_rows = own_ref.shape[2] // 2
    join_weight(own_ref, sib_ref, 0, part_rows, out_ref)
    whole = matmul(hid_ref[...], whole_weight(out_ref)) + vec_ref[2:3, :]
    for pair in range(HEADS // 2):
        lanes = slice(pair * 128, (pair + 1) * 128)
        tile = turn_tile(whole[:, lanes], cos_ref[...], sin_ref[...]).astype(BF16)
        q_ref[:, lanes] = (tile.astype(F32) * HEAD ** (-0.5)).astype(BF16)


def project_query(own, sib, hidden, vecs, cos, sin, rows_here):
    n_z, cols = own.shape[1], own.shape[3]
    vmem = pl.BlockSpec(memory_space=pltpu.VMEM)
    return pl.pallas_call(
        query_kernel,
        in_specs=[vmem] * 6,
        out_specs=[vmem] * 2,
        out_shape=[
            jax.ShapeDtypeStruct((n_z, rows_here, cols), BF16),
            jax.ShapeDtypeStruct((hidden.shape[0], cols), BF16),
        ],
        compiler_params=pltpu.CompilerParams(vmem_limit_bytes=40 * 2**20),
        cost_estimate=NO_COST,
        name="project_query",
    )(own, sib, hidden, vecs, cos, sin)


def out_kernel(own_ref, sib_ref, att_ref, x_ref, vec_ref, out_ref, resid_ref, hid_ref):
    part_rows = own_ref.shape[2] // 2
    join_weight(own_ref, sib_ref, part_rows, part_rows, out_ref)
    resid = x_ref[...].astype(F32) + matmul(att_ref[...], whole_weight(out_ref))
    resid_ref[...] = resid
    hid_ref[...] = normed_rows(resid, vec_ref[1:2, :])


def project_out(own, sib, attended, tokens, vecs, rows_here):
    n_z, cols = own.shape[1], own.shape[3]
    vmem = pl.BlockSpec(memory_space=pltpu.VMEM)
    return pl.pallas_call(
        out_kernel,
        in_specs=[vmem] * 5,
        out_specs=[vmem] * 3,
        out_shape=[
            jax.ShapeDtypeStruct((n_z, rows_here, cols), BF16),
            jax.ShapeDtypeStruct(tokens.shape, F32),
            jax.ShapeDtypeStruct(tokens.shape, BF16),
        ],
        compiler_params=pltpu.CompilerParams(vmem_limit_bytes=40 * 2**20),
        cost_estimate=NO_COST,
        name="project_out",
    )(own, sib, attended, tokens, vecs)


def kv_back_kernel(n_z, *refs):
    terms, rest = refs[:n_z], refs[n_z:]
    cos_ref, sin_ref, gq_ref, hid_ref, wq_ref, wkv_ref, x_ref, res_ref, vec_ref, two_ref = rest[:10]
    tokens_ref, part_ref = rest[10:]
    rows_here, width = x_ref.shape
    total = sum(t[...].astype(F32) for t in terms)
    half = total.shape[1] // 2
    keys = turn_tile(total[:, :half], cos_ref[...], -sin_ref[...]).astype(BF16)
    both = jnp.concatenate([keys, total[:, half:].astype(BF16)], 1)
    grad = times_transposed(gq_ref[...], wq_ref[...]) + times_transposed(both, wkv_ref[...])
    x = x_ref[...].astype(F32)
    inv = lax.rsqrt(jnp.mean(x * x, -1, keepdims=True) + NORM_EPS)
    normed = x * inv
    scaled = grad * vec_ref[0:1, :]
    tokens_ref[...] = res_ref[...] + inv * (
        scaled - normed * jnp.mean(scaled * normed, -1, keepdims=True)
    )
    sums = jnp.sum(both.astype(F32), 0, keepdims=True)
    share = half // n_z
    gap = jnp.zeros((1, width // n_z - share), F32)
    spread = []
    for i in range(2):
        cuts = []
        for z in range(n_z):
            at = i * half + z * share
            cuts += [sums[:, at : at + share], gap]
        spread.append(jnp.concatenate(cuts, 1))
    columns = [
        jnp.sum(grad * normed, 0, keepdims=True),
        two_ref[...],
        jnp.sum(gq_ref[...].astype(F32), 0, keepdims=True),
    ] + spread
    row = lax.broadcasted_iota(jnp.int32, (128, width), 0)
    table = jnp.zeros((128, width), F32)
    for i, v in enumerate(columns):
        table = jnp.where(row == i, v, table)
    part_ref[:, 2 * half :] = table.T.astype(BF16)
    pad = -rows_here % 128
    left = jnp.concatenate([hid_ref[...].astype(F32), jnp.zeros((pad, width), F32)], 0)
    right = jnp.concatenate([both, jnp.zeros((pad, 2 * half), BF16)], 0)
    part_ref[:, : 2 * half] = matmul(left.T.astype(BF16), right).astype(BF16)


def kv_back(terms, cos, sin, gq, hidden, wq, wkv, tokens, resid_grad, vecs, two_sum):
    vmem = pl.BlockSpec(memory_space=pltpu.VMEM)
    width = tokens.shape[1]
    return pl.pallas_call(
        functools.partial(kv_back_kernel, len(terms)),
        in_specs=[vmem] * (len(terms) + 10),
        out_specs=[vmem] * 2,
        out_shape=[
            jax.ShapeDtypeStruct(tokens.shape, F32),
            jax.ShapeDtypeStruct((width, wkv.shape[1] + 128), BF16),
        ],
        compiler_params=pltpu.CompilerParams(vmem_limit_bytes=40 * 2**20),
        cost_estimate=NO_COST,
        name="kv_back",
    )(*terms, cos, sin, gq, hidden, wq, wkv, tokens, resid_grad, vecs, two_sum)


def grad_weight_kernel(left_ref, right_ref, *refs):
    total = matmul(left_ref[...], right_ref[...])
    if len(refs) == 2:
        total = total + refs[0][...].astype(F32)
    refs[-1][...] = total.astype(BF16)


def grad_weight(left, right, other=None):
    rows, depth = left.shape
    cols = right.shape[1]
    tile = rows // 2 if rows % 32 == 0 else rows
    by_rows = lambda width: pl.BlockSpec((tile, width), lambda i: (i, 0))
    in_specs = [by_rows(depth), pl.BlockSpec((depth, cols), lambda i: (0, 0))]
    args = [left, right]
    if other is not None:
        in_specs.append(by_rows(cols))
        args.append(other)
    return pl.pallas_call(
        grad_weight_kernel,
        grid=(rows // tile,),
        in_specs=in_specs,
        out_specs=by_rows(cols),
        out_shape=jax.ShapeDtypeStruct((rows, cols), BF16),
        compiler_params=pltpu.CompilerParams(
            dimension_semantics=("arbitrary",), vmem_limit_bytes=40 * 2**20
        ),
        cost_estimate=NO_COST,
        name="grad_weight",
    )(*args)


def ff_kernel(tp, n_z, *refs):
    hidden, grads, weights = refs[:tp], refs[tp : 2 * tp], refs[2 * tp : 2 * tp + 4]
    rest = refs[2 * tp + 4 :]
    act_refs, back_refs, (hid_t, grad_all) = rest[:2], rest[2:4], rest[4:6]
    dh_outs, outs = rest[6 : 6 + tp], rest[6 + tp : 6 + 2 * tp]
    gu_buf, down_buf, acc, acc_out, sems = rest[6 + 2 * tp :]
    part_rows = weights[2].shape[1]
    gu_copies = [
        pltpu.make_async_copy(weights[i], gu_buf.at[i], sems.at[i]) for i in range(2)
    ]
    down_copies = []
    for i in range(2):
        for z in range(n_z):
            to = down_buf.at[i, pl.ds(z * part_rows, part_rows)]
            sem = sems.at[2 + i * n_z + z]
            down_copies.append(pltpu.make_async_copy(weights[2 + i].at[z], to, sem))
    gu_copies[0].start()
    for c in down_copies[:n_z]:
        c.start()
    gu_copies[1].start()
    for c in down_copies[n_z:]:
        c.start()
    tokens_here = hidden[0].shape[0]
    half = down_buf.shape[1]
    step = 2 if tp % 2 == 0 else 1
    for i in range(2):
        gu_copies[i].wait()
        for t in range(0, tp, step):
            rows = slice(t * tokens_here, (t + step) * tokens_here)
            here = jnp.concatenate([hidden[t + n][...] for n in range(step)], 0)
            grad = jnp.concatenate([grads[t + n][...] for n in range(step)], 0)
            if i == 0:
                hid_t[:, rows] = here.astype(F32).T.astype(BF16)
                grad_all[rows, :] = grad
            gate = matmul(here, gu_buf[i, :, :half])
            up = matmul(here, gu_buf[i, :, half:])
            if t == 0:
                for c in down_copies[i * n_z : (i + 1) * n_z]:
                    c.wait()
            grad_act = times_transposed(grad, down_buf[i])
            sig = 1.0 / (1.0 + jnp.exp(-gate))
            silu = gate * sig
            act = silu * up
            act_refs[i][:, rows] = act.T.astype(BF16)
            grad_gate = (grad_act * up * (sig + silu * (1.0 - sig))).astype(BF16)
            grad_up = (grad_act * silu).astype(BF16)
            back_refs[i][rows, :half] = grad_gate
            back_refs[i][rows, half:] = grad_up
            part = times_transposed(grad_gate, gu_buf[i, :, :half]) + times_transposed(
                grad_up, gu_buf[i, :, half:]
            )
            out = matmul(act.astype(BF16), down_buf[i])
            if i == 0:
                acc[rows, :] = part
                acc_out[rows, :] = out
            else:
                part = (part + acc[rows, :]).astype(BF16)
                out = (out + acc_out[rows, :]).astype(BF16)
                for n in range(step):
                    mine = slice(n * tokens_here, (n + 1) * tokens_here)
                    dh_outs[t + n][...] = part[mine]
                    outs[t + n][...] = out[mine]


def ff_pass(hidden, grads, gu, down):
    tp = len(hidden)
    n_z, part_rows = down[0].shape[:2]
    tokens_here, width = hidden[0].shape
    half = n_z * part_rows
    rows = tp * tokens_here
    vmem = pl.BlockSpec(memory_space=pltpu.VMEM)
    got = pl.pallas_call(
        functools.partial(ff_kernel, tp, n_z),
        in_specs=[vmem] * (2 * tp) + [pl.BlockSpec(memory_space=pl.ANY)] * 4,
        out_specs=[vmem] * (2 * tp + 6),
        out_shape=[jax.ShapeDtypeStruct((half, rows), BF16)] * 2
        + [jax.ShapeDtypeStruct((rows, 2 * half), BF16)] * 2
        + [jax.ShapeDtypeStruct((width, rows), BF16), jax.ShapeDtypeStruct((rows, width), BF16)]
        + [jax.ShapeDtypeStruct((tokens_here, width), BF16)] * (2 * tp),
        scratch_shapes=[
            pltpu.VMEM((2, width, 2 * half), BF16),
            pltpu.VMEM((2, half, width), BF16),
            pltpu.VMEM((rows, width), F32),
            pltpu.VMEM((rows, width), F32),
            pltpu.SemaphoreType.DMA((2 + 2 * n_z,)),
        ],
        compiler_params=pltpu.CompilerParams(vmem_limit_bytes=58 * 2**20),
        cost_estimate=NO_COST,
        name="ff_pass",
    )(*hidden, *grads, *gu, *down)
    return got[:2], got[2:4], got[4], got[5], got[6 : 6 + tp], got[6 + tp :]


def local(
    tokens,
    out_grad,
    block_order,
    norm1_gain,
    q_weight,
    q_bias,
    k_weight,
    k_bias,
    v_weight,
    v_bias,
    o_weight,
    norm2_gain,
    gate_weight,
    up_weight,
    down_weight,
):
    n_ctx = lax.axis_size("ctx")
    n_z = lax.axis_size("fsdp")
    tp = 4 if n_ctx % 4 == 0 else (2 if n_ctx % 2 == 0 else 1)
    here = lax.axis_index("ctx")
    zed = lax.axis_index("fsdp")
    core = lax.axis_index("seq")
    n_part = 2 * tp
    part = core * tp + lax.rem(here, tp)

    def swap(v):
        return lax.ppermute(v, "seq", [(0, 1), (1, 0)])

    def hop(v, k):
        if k == 0:
            return v
        return lax.ppermute(v, "ctx", [(i, i ^ k) for i in range(n_ctx)])

    def hop_z(v, k):
        if k == 0:
            return v
        return lax.ppermute(v, "fsdp", [(i, i ^ k) for i in range(n_z)])

    def gather_z(v):
        return lax.all_gather(v, "fsdp", axis=0, tiled=True)

    def scatter_z(v):
        return lax.psum_scatter(v, "fsdp", scatter_dimension=0, tiled=True)

    tokens_here, width = tokens.shape[1:]
    ff = gate_weight.shape[1]
    rows_here = q_weight.shape[0]
    key_width = KV_HEADS * HEAD
    block_len = tokens_here * n_z

    part_rows = -(-rows_here // (n_part * 32)) * 32

    kb = k_bias.shape[0]
    vectors = (norm1_gain, norm2_gain, q_bias, k_bias, v_bias)
    vec = sum(
        jnp.pad(v[None], ((i, 15 - i), (0, 2 * key_width - v.shape[0])))
        for i, v in enumerate(vectors)
    )
    kv_pack = jnp.concatenate([jnp.concatenate([k_weight, v_weight], 1), vec], 0)
    og_here = out_grad[0]

    def own_part(w):
        return lax.dynamic_slice_in_dim(w, part * part_rows, part_rows, 0)

    ff_z = ff // n_z
    piece = ff_z // n_part
    piece_pad = -(-piece // 32) * 32

    def ff_columns(w):
        cuts = []
        for j in range(n_z):
            cut = lax.dynamic_slice_in_dim(w, j * ff_z + part * piece, piece, 1)
            cuts.append(jnp.pad(cut, ((0, 0), (0, piece_pad - piece))))
        return jnp.concatenate(cuts, 1)

    order_row = block_order[0]
    x_here = tokens[0]
    kv_pack, q_part, o_part, gate_weight, up_weight, down_weight, query_at = (
        lax.optimization_barrier(
            (
                kv_pack,
                own_part(q_weight),
                own_part(o_weight),
                gate_weight,
                up_weight,
                down_weight,
                order_row[here] * block_len + zed * tokens_here,
            )
        )
    )
    pack_rows = kv_pack.shape[0]
    qo_part = jnp.concatenate([q_part, o_part], 0)
    pack = jnp.concatenate([kv_pack, qo_part.reshape(-1, 2 * key_width)], 0)
    got = [hop_z(pack, k) for k in range(n_z)]
    gu_cut = jnp.concatenate([ff_columns(gate_weight), ff_columns(up_weight)], 1)
    down_cut = lax.dynamic_slice_in_dim(down_weight, part * piece, piece, 0)
    down_cut = jnp.pad(down_cut, ((0, piece_pad - piece), (0, 0)))
    query_pos = query_at + jnp.arange(tokens_here, dtype=jnp.int32)
    cosine_table, sine_table = rope_tables(query_pos, HEAD)
    cos_wide = jnp.tile(cosine_table[:, 0], (1, 4))
    sin_wide = jnp.tile(jnp.concatenate([-sine_table[:, 0], sine_table[:, 0]], 1), (1, 2))
    got, cos_wide, sin_wide, gu_cut, down_cut, og_here = lax.optimization_barrier(
        (got, cos_wide, sin_wide, gu_cut, down_cut, og_here)
    )

    qo_got = jnp.stack([v[pack_rows:].reshape(2 * part_rows, width) for v in got])
    qo_own = [hop(qo_got, k) for k in range(tp)]
    widths = tuple(v.shape[0] for v in vectors)
    w_kv, vecs, kv_local, hidden_one = project_kv(
        got, x_here, cos_wide, sin_wide, rows_here, pack_rows - rows_here, widths
    )
    w_kv = w_kv.reshape(width, 2 * key_width)
    gain_one = vecs[0:1, :width]
    gain_two = vecs[1:2, :width]
    kv_z = [hop_z(kv_local, k) for k in range(n_z)]
    gu_own = gather_z(gu_cut)
    kv_z, qo_own = lax.optimization_barrier((kv_z, qo_own))

    kv_block = jnp.concatenate(kv_z, 0)
    if n_ctx == tp:
        kv_blocks = [hop(kv_block, k) for k in range(n_ctx)]
    else:
        kv_blocks = lax.all_gather(kv_block, "ctx", axis=0, tiled=False)
    qo_own = jnp.stack(qo_own)
    qo_sib = swap(qo_own)
    w_query, queries = project_query(
        qo_own, qo_sib, hidden_one, vecs, cos_wide, sin_wide, rows_here
    )
    w_query = w_query.reshape(width, width)
    kv_blocks, queries, og_here, down_cut, gu_own = lax.optimization_barrier(
        (kv_blocks, queries, og_here, down_cut, gu_own)
    )

    og_parts = [hop(og_here, k) for k in range(tp)]
    kv_whole = jnp.stack(kv_blocks) if n_ctx == tp else kv_blocks
    attended, queries_ext = attend_forward(order_row, n_ctx == tp, queries, kv_whole)
    down_own = gather_z(down_cut)
    attended, queries_ext, og_parts = lax.optimization_barrier((attended, queries_ext, og_parts))
    w_out, resid, hidden_two = project_out(
        qo_own, qo_sib, attended, x_here, vecs, rows_here
    )
    w_out = w_out.reshape(width, width)
    h2_parts = [hop(hidden_two, k) for k in range(tp)]
    gu_oth = swap(gu_own)
    h2_parts, down_own = lax.optimization_barrier((h2_parts, down_own))
    down_own = down_own.reshape(n_z, piece_pad, width)
    down_oth = swap(down_own)

    acts, ggus, h2_turned, og_all, dh2, ff_out = ff_pass(
        h2_parts, og_parts, (gu_own, gu_oth), (down_own, down_oth)
    )
    grad_h2_parts = [hop(dh2[k], k) for k in range(tp)]

    def share_pieces(mine):
        own = jnp.stack([hop(mine, k) for k in range(tp)])
        return own, swap(own)

    def core_halves(part_sum):
        cols = part_sum.shape[1]
        cut = part_sum.astype(BF16).reshape(n_z, rows_here, cols)
        cut = jnp.pad(cut, ((0, 0), (0, n_part * part_rows - rows_here), (0, 0)))
        own = lax.dynamic_slice_in_dim(cut, core * tp * part_rows, tp * part_rows, 1)
        oth = lax.dynamic_slice_in_dim(cut, (1 - core) * tp * part_rows, tp * part_rows, 1)
        return own, oth

    def core_total(own, sib):
        return (own.astype(F32) + sib.astype(F32)).astype(BF16)

    def scatter_parts(cut):
        cut = cut.reshape(n_z, tp, part_rows, -1)
        at = lax.rem(here, tp)
        return [
            hop(lax.dynamic_index_in_dim(cut, at ^ k, 1, keepdims=False), k) for k in range(tp)
        ]

    def ctx_groups_sum(v):
        if n_ctx == tp:
            return v
        groups = [[g * tp + c for g in range(n_ctx // tp)] for c in range(tp)]
        return lax.psum(v, "ctx", axis_index_groups=groups)

    d_gu = grad_weight(h2_turned, ggus[0], swap(grad_weight(h2_turned, ggus[1])))
    grad_h2_parts, d_gu = lax.optimization_barrier((grad_h2_parts, d_gu))
    grad_h2 = sum(v.astype(F32) for v in grad_h2_parts)
    scale_two = lax.rsqrt(jnp.mean(resid * resid, -1, keepdims=True) + NORM_EPS)
    normed_two = resid * scale_two

    grad_norm_two, gain_two_terms = rms_backward(grad_h2, normed_two, scale_two, gain_two)
    grad_resid = og_here.astype(F32) + grad_norm_two
    grad_proj = grad_resid.astype(BF16)
    grad_att = times_transposed(grad_proj, w_out).astype(BF16)
    grad_att, d_gu, ff_out = lax.optimization_barrier((grad_att, d_gu, ff_out))
    d_gu = scatter_z(d_gu)
    ff_out = [hop(ff_out[k], k) for k in range(tp)]
    grad_q_pre, grad_terms = attend_backward(
        order_row, n_ctx == tp, queries_ext, grad_att, attended, cos_wide, sin_wide, kv_whole
    )
    grad_q_pre, grad_terms, ff_out, acts, grad_proj = lax.optimization_barrier(
        (grad_q_pre, grad_terms, ff_out, acts, grad_proj)
    )
    d_down = grad_weight(acts[0], og_all, swap(grad_weight(acts[1], og_all)))

    qo_own, qo_oth = core_halves(
        jnp.concatenate(
            [contract_rows(hidden_one, grad_q_pre), contract_rows(attended, grad_proj)], 1
        )
    )
    if n_ctx == tp:
        kv_terms = [hop(grad_terms[k], k) for k in range(n_ctx)]
    else:
        kv_terms = [lax.psum_scatter(grad_terms, "ctx", scatter_dimension=0, tiled=False)]
    kv_terms, d_gu, d_down, qo_own, qo_oth, ff_out = lax.optimization_barrier(
        (kv_terms, d_gu, d_down, qo_own, qo_oth, ff_out)
    )

    kv_sum = sum(v.astype(F32) for v in kv_terms).astype(BF16)
    kv_sum = kv_sum.reshape(n_z, tokens_here, 2 * key_width)
    kv_terms = [hop_z(kv_sum[k], k) for k in range(n_z)]
    d_gu = ctx_groups_sum(d_gu)
    gu_pieces = [hop(d_gu, k) for k in range(tp)]
    qo_sib = swap(qo_oth)
    result = resid + sum(v.astype(F32) for v in ff_out)
    layer_out = result.astype(BF16)[None]
    d_down = scatter_z(d_down)
    kv_terms, qo_own, qo_sib = lax.optimization_barrier((kv_terms, qo_own, qo_sib))

    tokens_grad, kv_part = kv_back(
        kv_terms,
        cos_wide,
        sin_wide,
        grad_q_pre,
        hidden_one,
        w_query,
        w_kv,
        x_here,
        grad_resid,
        vecs,
        jnp.sum(gain_two_terms, 0, keepdims=True),
    )
    tokens_grad = tokens_grad[None]
    kv_own, kv_oth = core_halves(kv_part)
    last = core_total(qo_own, qo_sib)
    kv_own, kv_sib, last = lax.optimization_barrier((kv_own, swap(kv_oth), last))

    last = scatter_parts(jnp.concatenate([last, core_total(kv_own, kv_sib)], 2))
    last, d_down, gu_pieces = lax.optimization_barrier((last, d_down, gu_pieces))

    last = sum(v.astype(F32) for v in last).astype(BF16)
    last = [
        hop_z(lax.dynamic_index_in_dim(last, zed ^ k, 0, keepdims=False), k) for k in range(n_z)
    ]
    d_down = ctx_groups_sum(d_down)
    gu_pieces = jnp.stack(gu_pieces)
    gu_sib = swap(gu_pieces)
    last, d_down, gu_pieces, gu_sib = lax.optimization_barrier(
        (last, d_down, gu_pieces, gu_sib)
    )

    last = ctx_groups_sum(sum(v.astype(F32) for v in last).astype(BF16))
    last = lax.optimization_barrier(last)
    down_pieces = [hop(d_down, k) for k in range(tp)]
    grad_w_gate, grad_w_up = spread_columns((gu_pieces, gu_sib), n_z, ff, 2)
    last, down_pieces, grad_w_gate, grad_w_up = lax.optimization_barrier(
        (last, down_pieces, grad_w_gate, grad_w_up)
    )
    last = [hop(last, k) for k in range(tp)]
    down_pieces = jnp.stack(down_pieces)
    down_sib = swap(down_pieces)
    last, down_pieces, down_sib = lax.optimization_barrier((last, down_pieces, down_sib))
    last = jnp.stack(last)
    grad_w_down = spread_rows((down_pieces, down_sib), piece, ff_z)
    last = spread_rows((last, swap(last)), part_rows, rows_here)
    grad_w_query = last[:, :width]
    grad_w_out = last[:, width : 2 * width]
    grad_w_kv = last[:, 2 * width :]
    sums = grad_w_kv[:, 2 * key_width :]

    return (
        layer_out,
        tokens_grad,
        sums[:, 0],
        grad_w_query,
        sums[:, 2],
        grad_w_kv[:, :key_width],
        sums[:kb, 3],
        grad_w_kv[:, key_width : 2 * key_width],
        sums[:kb, 4],
        grad_w_out,
        sums[:, 1],
        grad_w_gate,
        grad_w_up,
        grad_w_down,
    )


def solution(mesh):
    in_specs = (
        P("seq", ("ctx", "fsdp"), None),
        P("seq", ("ctx", "fsdp"), None),
        P("seq", None),
        P("fsdp"),
        P("fsdp", None),
        P("fsdp"),
        P("fsdp", None),
        P("fsdp"),
        P("fsdp", None),
        P("fsdp"),
        P("fsdp", None),
        P("fsdp"),
        P("fsdp", None),
        P("fsdp", None),
        P("fsdp", None),
    )
    out_specs = (
        P("seq", ("ctx", "fsdp"), None),
        P("seq", ("ctx", "fsdp"), None),
        P("fsdp"),
        P("fsdp", None),
        P("fsdp"),
        P("fsdp", None),
        P("fsdp"),
        P("fsdp", None),
        P("fsdp"),
        P("fsdp", None),
        P("fsdp"),
        P("fsdp", None),
        P("fsdp", None),
        P("fsdp", None),
    )
    return jax.shard_map(local, mesh=mesh, in_specs=in_specs, out_specs=out_specs, check_vma=False)
```

```python
import functools
import math

import jax
import jax.numpy as jnp
from jax import lax
from jax.experimental import pallas as pl
from jax.experimental.pallas import tpu as pltpu
from jax.sharding import PartitionSpec as P

HEADS = 14
KV_HEADS = 2
HEAD = 64
GROUP = HEADS // KV_HEADS
NORM_EPS = 1e-06
ROPE_BASE = 1000000.0
MASKED = -1e30
BF16 = jnp.bfloat16
F32 = jnp.float32
NO_COST = pl.CostEstimate(flops=0, bytes_accessed=0, transcendentals=0)


def rope_tables(positions, head_dim):
    half_dim = head_dim // 2
    inverse = jnp.exp(
        jnp.arange(half_dim, dtype=jnp.float32) * (-math.log(ROPE_BASE) * 2.0 / head_dim)
    )
    angles = positions.astype(jnp.float32)[:, None] * inverse[None, :]
    return (jnp.cos(angles)[:, None, :], jnp.sin(angles)[:, None, :])


def matmul(left_side, right_side):
    return jnp.dot(left_side, right_side, preferred_element_type=F32)


def contract_rows(left_side, right_side):
    return lax.dot_general(
        left_side, right_side, (((0,), (0,)), ((), ())), preferred_element_type=F32
    )


def times_transposed(left_side, right_side):
    return lax.dot_general(
        left_side, right_side, (((1,), (1,)), ((), ())), preferred_element_type=F32
    )


def rms_backward(grad_out, normed, inv_scale, gain_vec):
    scaled = grad_out * gain_vec
    grad_in = inv_scale * (scaled - normed * jnp.mean(scaled * normed, -1, keepdims=True))
    return (grad_in, grad_out * normed)


def cut_heads(ref, head):
    tile = ref[:, (head // 2) * 128 : (head // 2 + 1) * 128].astype(F32)
    group = head // GROUP
    if head % 2 != group:
        tile = jnp.concatenate([tile[:, HEAD:], tile[:, :HEAD]], 1)
    lane = lax.broadcasted_iota(jnp.int32, tile.shape, 1)
    return jnp.where((lane >= HEAD) if group else (lane < HEAD), tile, 0.0)


def split_lanes(column, shape):
    high = column.astype(BF16).astype(F32)
    mid = (column - high).astype(BF16).astype(F32)
    low = column - high - mid
    lane = lax.broadcasted_iota(jnp.int32, shape, 1)
    return jnp.where(
        lane == 0, high, jnp.where(lane == 1, mid, jnp.where(lane == 2, low, 0.0))
    ).astype(BF16)


def piece_shift(at, zed, tokens_here, keys_here):
    pieces = keys_here // tokens_here
    shift = jnp.zeros(at.shape, jnp.int32)
    for k in range(pieces):
        here = (jnp.bitwise_xor(zed, k) - k - zed) * tokens_here
        shift = jnp.where(at >= k * tokens_here, here, shift)
    return shift


def forward_kernel(by_xor, info_ref, q_ref, kv_ref, att_ref, qext_ref, top_ref, acc_ref):
    step = pl.program_id(0)
    last = pl.num_programs(0) - 1
    tokens_here = q_ref.shape[0]
    keys_here = kv_ref.shape[1]
    here = lax.axis_index("ctx")
    zed = lax.axis_index("fsdp")
    own = info_ref[here]
    block = info_ref[jnp.bitwise_xor(here, step) if by_xor else step]

    @pl.when(step == 0)
    def _():
        for h in range(HEADS):
            qext_ref[h * tokens_here : (h + 1) * tokens_here, :128] = cut_heads(q_ref, h).astype(
                BF16
            )
        top_ref[...] = jnp.full(top_ref.shape, MASKED, F32)
        acc_ref[...] = jnp.zeros(acc_ref.shape, F32)

    def attend(masked):
        keys = kv_ref[0, :, :128]
        values = jnp.concatenate(
            [kv_ref[0, :, 128:], jnp.ones((keys_here, 128), BF16)], 1
        )
        if masked:
            row = lax.broadcasted_iota(jnp.int32, (tokens_here, keys_here), 0)
            col = lax.broadcasted_iota(jnp.int32, (tokens_here, keys_here), 1)
            allowed = col + piece_shift(col, zed, tokens_here, keys_here) <= row
        for h in range(HEADS):
            rows = slice(h * tokens_here, (h + 1) * tokens_here)
            scores = times_transposed(qext_ref[rows, :128], keys)
            if masked:
                scores = jnp.where(allowed, scores, MASKED)
            old = top_ref[rows, :]
            top = jnp.maximum(old, jnp.max(scores, -1, keepdims=True))
            probs = jnp.exp(scores - top[:, :1]).astype(BF16)
            shrink = jnp.exp(old - top)
            top_ref[rows, :] = top
            acc_ref[rows, :] = acc_ref[rows, :] * jnp.concatenate([shrink, shrink], 1) + matmul(
                probs, values
            )

    @pl.when(block == own)
    def _():
        attend(True)

    @pl.when(block < own)
    def _():
        attend(False)

    @pl.when(step == last)
    def _():
        lane = lax.broadcasted_iota(jnp.int32, (tokens_here, 128), 1)
        for pair in range(HEADS // 2):
            outs = []
            for h in (2 * pair, 2 * pair + 1):
                rows = slice(h * tokens_here, (h + 1) * tokens_here)
                total = acc_ref[rows, 128:]
                out = acc_ref[rows, :128] / total
                if h // GROUP != h % 2:
                    out = jnp.concatenate([out[:, HEAD:], out[:, :HEAD]], 1)
                outs.append(out)
                log_total = top_ref[rows, :] + jnp.log(total)
                qext_ref[rows, 128:] = split_lanes(-log_total, (tokens_here, 128))
            att_ref[:, pair * 128 : (pair + 1) * 128] = jnp.where(
                lane < HEAD, outs[0], outs[1]
            ).astype(BF16)


def backward_kernel(
    by_xor, info_ref, qext_ref, do_ref, att_ref, cos_ref, sin_ref, kv_ref, dq_ref, dkv_ref,
    doext_ref, dqt_ref
):
    step = pl.program_id(0)
    last = pl.num_programs(0) - 1
    tokens_here = do_ref.shape[0]
    keys_here = kv_ref.shape[1]
    here = lax.axis_index("ctx")
    zed = lax.axis_index("fsdp")
    own = info_ref[here]
    block = info_ref[jnp.bitwise_xor(here, step) if by_xor else step]
    span = 2 * tokens_here

    @pl.when(step == 0)
    def _():
        for h in range(HEADS):
            rows = slice(h * tokens_here, (h + 1) * tokens_here)
            grad = cut_heads(do_ref, h)
            delta = jnp.sum(grad * cut_heads(att_ref, h), -1, keepdims=True)
            doext_ref[rows, :128] = grad.astype(BF16)
            doext_ref[rows, 128:] = split_lanes(-delta, (tokens_here, 128))
        dqt_ref[...] = jnp.zeros(dqt_ref.shape, F32)

    def attend(masked):
        lane = lax.broadcasted_iota(jnp.int32, (keys_here, 128), 1)
        ones = jnp.where(lane < 3, 1.0, 0.0).astype(BF16)
        keys = kv_ref[0, :, :128]
        keys_ext = jnp.concatenate([keys, ones], 1)
        values_ext = jnp.concatenate([kv_ref[0, :, 128:], ones], 1)
        keys_t = keys.astype(F32).T.astype(BF16)
        if masked:
            row = lax.broadcasted_iota(jnp.int32, (keys_here, tokens_here), 0)
            col = lax.broadcasted_iota(jnp.int32, (keys_here, tokens_here), 1)
            allowed = row + piece_shift(row, zed, tokens_here, keys_here) <= col
            allowed = allowed.astype(F32)
            allowed = jnp.concatenate([allowed, allowed], 1) > 0.5
        dk = jnp.zeros((keys_here, 128), F32)
        dv = jnp.zeros((keys_here, 128), F32)
        for pair in range(HEADS // 2):
            rows = slice(pair * span, (pair + 1) * span)
            probs = jnp.exp(times_transposed(keys_ext, qext_ref[rows, :]))
            if masked:
                probs = jnp.where(allowed, probs, 0.0)
            slope = (probs * times_transposed(values_ext, doext_ref[rows, :])).astype(BF16)
            dv = dv + matmul(probs.astype(BF16), doext_ref[rows, :128])
            dk = dk + matmul(slope, qext_ref[rows, :128])
            dqt_ref[pair] = dqt_ref[pair] + matmul(keys_t, slope)
        dkv_ref[0] = jnp.concatenate([dk, dv], 1).astype(BF16)

    @pl.when(block == own)
    def _():
        attend(True)

    @pl.when(block < own)
    def _():
        attend(False)

    @pl.when(block > own)
    def _():
        dkv_ref[...] = jnp.zeros(dkv_ref.shape, BF16)

    @pl.when(step == last)
    def _():
        lane = lax.broadcasted_iota(jnp.int32, (tokens_here, 128), 1)
        for pair in range(HEADS // 2):
            turned = dqt_ref[pair].T
            outs = []
            for j in range(2):
                h = 2 * pair + j
                out = turned[j * tokens_here : (j + 1) * tokens_here]
                if h // GROUP != j:
                    out = jnp.concatenate([out[:, HEAD:], out[:, :HEAD]], 1)
                outs.append(out)
            out = jnp.where(lane < HEAD, outs[0], outs[1]) * HEAD ** (-0.5)
            dq_ref[:, pair * 128 : (pair + 1) * 128] = turn_tile(
                out, cos_ref[...], -sin_ref[...]
            ).astype(BF16)


def whole_spec(shape):
    return pl.BlockSpec(shape, lambda i, info: (0,) * len(shape))


def attend_forward(info, by_xor, queries, kv):
    blocks, block_len, kv_width = kv.shape
    tokens_here, q_width = queries.shape
    rows = HEADS * tokens_here
    return pl.pallas_call(
        functools.partial(forward_kernel, by_xor),
        grid_spec=pltpu.PrefetchScalarGridSpec(
            num_scalar_prefetch=1,
            grid=(blocks,),
            in_specs=[
                whole_spec((tokens_here, q_width)),
                pl.BlockSpec((1, block_len, kv_width), lambda i, info: (i, 0, 0)),
            ],
            out_specs=[whole_spec((tokens_here, q_width)), whole_spec((rows, 256))],
            scratch_shapes=[pltpu.VMEM((rows, 128), F32), pltpu.VMEM((rows, 256), F32)],
        ),
        out_shape=[
            jax.ShapeDtypeStruct((tokens_here, q_width), BF16),
            jax.ShapeDtypeStruct((rows, 256), BF16),
        ],
        compiler_params=pltpu.CompilerParams(
            dimension_semantics=("arbitrary",), vmem_limit_bytes=40 * 2**20
        ),
        cost_estimate=pl.CostEstimate(
            flops=3 * 10**10, bytes_accessed=2**23, transcendentals=0
        ),
        name="attend_forward",
    )(info, queries, kv)


def attend_backward(info, by_xor, queries_ext, grad_att, attended, cos, sin, kv):
    blocks, block_len, kv_width = kv.shape
    tokens_here, q_width = grad_att.shape
    rows = HEADS * tokens_here
    return pl.pallas_call(
        functools.partial(backward_kernel, by_xor),
        grid_spec=pltpu.PrefetchScalarGridSpec(
            num_scalar_prefetch=1,
            grid=(blocks,),
            in_specs=[
                whole_spec((rows, 256)),
                whole_spec((tokens_here, q_width)),
                whole_spec((tokens_here, q_width)),
                whole_spec(cos.shape),
                whole_spec(sin.shape),
                pl.BlockSpec((1, block_len, kv_width), lambda i, info: (i, 0, 0)),
            ],
            out_specs=[
                whole_spec((tokens_here, q_width)),
                pl.BlockSpec((1, block_len, kv_width), lambda i, info: (i, 0, 0)),
            ],
            scratch_shapes=[
                pltpu.VMEM((rows, 256), BF16),
                pltpu.VMEM((HEADS // 2, 128, 2 * tokens_here), F32),
            ],
        ),
        out_shape=[
            jax.ShapeDtypeStruct((tokens_here, q_width), BF16),
            jax.ShapeDtypeStruct(kv.shape, BF16),
        ],
        compiler_params=pltpu.CompilerParams(
            dimension_semantics=("arbitrary",), vmem_limit_bytes=40 * 2**20
        ),
        cost_estimate=pl.CostEstimate(
            flops=5 * 10**10, bytes_accessed=2**23, transcendentals=0
        ),
        name="attend_backward",
    )(info, queries_ext, grad_att, attended, cos, sin, kv)


def part_place(tp, j, k):
    at = jnp.bitwise_xor(lax.rem(lax.axis_index("ctx"), tp), k)
    return jnp.bitwise_xor(lax.axis_index("seq"), j) * tp + at


def spread_columns_kernel(n_z, *refs):
    pieces, outs, held = refs[:2], refs[2:-1], refs[-1]
    tp = pieces[0].shape[0]
    n_part = 2 * tp
    for j in range(2):
        for k in range(tp):
            held[part_place(tp, j, k)] = pieces[j][k].astype(F32)
    half = held.shape[2] // len(outs)
    pad = half // n_z
    for i, out in enumerate(outs):
        piece = out.shape[1] // (n_z * n_part)
        cuts = []
        for j in range(n_z):
            for e in range(n_part):
                start = i * half + j * pad
                cuts.append(held[e, :, start : start + piece])
        out[...] = jnp.concatenate(cuts, 1)


def spread_columns(pieces, n_z, ff, outs):
    tp, rows, cols = pieces[0].shape
    tile = 32
    return pl.pallas_call(
        functools.partial(spread_columns_kernel, n_z),
        grid=(rows // tile,),
        in_specs=[pl.BlockSpec((tp, tile, cols), lambda i: (0, i, 0))] * 2,
        out_specs=[pl.BlockSpec((tile, ff), lambda i: (i, 0))] * outs,
        scratch_shapes=[pltpu.VMEM((2 * tp, tile, cols), F32)],
        out_shape=[jax.ShapeDtypeStruct((rows, ff), F32)] * outs,
        compiler_params=pltpu.CompilerParams(
            dimension_semantics=("arbitrary",), vmem_limit_bytes=40 * 2**20
        ),
        cost_estimate=pl.CostEstimate(
            flops=10**10, bytes_accessed=2**23, transcendentals=0
        ),
        name="spread_columns",
    )(*pieces)


def spread_rows_kernel(piece, *refs):
    pieces, out_ref = refs[:-1], refs[-1]
    room = out_ref.shape[0] // piece
    tp = pieces[0].shape[0]
    for j in range(2):
        for k in range(tp):
            place = part_place(tp, j, k)

            @pl.when(place < room)
            def _():
                start = pl.multiple_of(place * piece, 8)
                out_ref[pl.ds(start, piece), :] = pieces[j][k].astype(F32)[:piece]


def spread_rows(pieces, piece, rows_out):
    tp, rows, cols = pieces[0].shape
    tile = 128
    return pl.pallas_call(
        functools.partial(spread_rows_kernel, piece),
        grid=(cols // tile,),
        in_specs=[pl.BlockSpec((tp, rows, tile), lambda i: (0, 0, i))] * 2,
        out_specs=pl.BlockSpec((rows_out, tile), lambda i: (0, i)),
        out_shape=jax.ShapeDtypeStruct((rows_out, cols), F32),
        compiler_params=pltpu.CompilerParams(
            dimension_semantics=("arbitrary",), vmem_limit_bytes=40 * 2**20
        ),
        cost_estimate=NO_COST,
        name="spread_rows",
    )(*pieces)


def join_weight(own_ref, sib_ref, first, part_rows, out_ref):
    tp, n_z = own_ref.shape[:2]
    room = out_ref.shape[1] // part_rows
    for j, ref in enumerate((own_ref, sib_ref)):
        for k in range(tp):
            place = part_place(tp, j, k)

            @pl.when(place < room)
            def _():
                start = pl.multiple_of(place * part_rows, 16)
                for z in range(n_z):
                    at = jnp.bitwise_xor(lax.axis_index("fsdp"), z)
                    out_ref[at, pl.ds(start, part_rows), :] = ref[k, z, first : first + part_rows]


def whole_weight(ref):
    return jnp.concatenate([ref[z] for z in range(ref.shape[0])], 0)


def turn_tile(tile, cos, sin):
    h = HEAD // 2
    cuts = [tile[:, h : 2 * h], tile[:, :h], tile[:, 3 * h :], tile[:, 2 * h : 3 * h]]
    return tile * cos + jnp.concatenate(cuts, 1) * sin


def normed_rows(values, gain):
    inv = lax.rsqrt(jnp.mean(values * values, -1, keepdims=True) + NORM_EPS)
    return (values * inv * gain).astype(BF16)


def kv_kernel(widths, *refs):
    x_ref, cos_ref, sin_ref = refs[-8:-5]
    pieces, (out_ref, vec_ref, kv_ref, hid_ref, held) = refs[:-8], refs[-5:]
    n_z, rows_here, cols = out_ref.shape
    for k in range(n_z):
        at = jnp.bitwise_xor(lax.axis_index("fsdp"), k)
        out_ref[at] = pieces[k][:rows_here]
        held[at] = pieces[k][rows_here : rows_here + held.shape[1]].astype(F32)
    vec_ref[...] = jnp.zeros(vec_ref.shape, F32)
    for i, size in enumerate(widths):
        row = jnp.concatenate([held[z, i : i + 1, :size] for z in range(n_z)], 1)
        vec_ref[i : i + 1, : n_z * size] = row
    hidden = normed_rows(x_ref[...].astype(F32), vec_ref[0:1, :])
    hid_ref[...] = hidden
    half = cols // 2
    both = matmul(hidden, whole_weight(out_ref))
    keys = both[:, :half] + vec_ref[3:4, :half]
    kv_ref[:, :half] = turn_tile(keys, cos_ref[...], sin_ref[...]).astype(BF16)
    kv_ref[:, half:] = (both[:, half:] + vec_ref[4:5, :half]).astype(BF16)


def project_kv(pieces, tokens, cos, sin, rows_here, vec_rows, widths):
    cols = pieces[0].shape[1]
    n_z = len(pieces)
    vmem = pl.BlockSpec(memory_space=pltpu.VMEM)
    return pl.pallas_call(
        functools.partial(kv_kernel, widths),
        in_specs=[vmem] * (n_z + 3),
        out_specs=[vmem] * 4,
        out_shape=[
            jax.ShapeDtypeStruct((n_z, rows_here, cols), BF16),
            jax.ShapeDtypeStruct((8, n_z * rows_here), F32),
            jax.ShapeDtypeStruct((tokens.shape[0], cols), BF16),
            jax.ShapeDtypeStruct(tokens.shape, BF16),
        ],
        scratch_shapes=[pltpu.VMEM((n_z, vec_rows, cols), F32)],
        compiler_params=pltpu.CompilerParams(vmem_limit_bytes=40 * 2**20),
        cost_estimate=NO_COST,
        name="project_kv",
    )(*pieces, tokens, cos, sin)


def query_kernel(own_ref, sib_ref, hid_ref, vec_ref, cos_ref, sin_ref, out_ref, q_ref):
    part_rows = own_ref.shape[2] // 2
    join_weight(own_ref, sib_ref, 0, part_rows, out_ref)
    whole = matmul(hid_ref[...], whole_weight(out_ref)) + vec_ref[2:3, :]
    for pair in range(HEADS // 2):
        lanes = slice(pair * 128, (pair + 1) * 128)
        tile = turn_tile(whole[:, lanes], cos_ref[...], sin_ref[...]).astype(BF16)
        q_ref[:, lanes] = (tile.astype(F32) * HEAD ** (-0.5)).astype(BF16)


def project_query(own, sib, hidden, vecs, cos, sin, rows_here):
    n_z, cols = own.shape[1], own.shape[3]
    vmem = pl.BlockSpec(memory_space=pltpu.VMEM)
    return pl.pallas_call(
        query_kernel,
        in_specs=[vmem] * 6,
        out_specs=[vmem] * 2,
        out_shape=[
            jax.ShapeDtypeStruct((n_z, rows_here, cols), BF16),
            jax.ShapeDtypeStruct((hidden.shape[0], cols), BF16),
        ],
        compiler_params=pltpu.CompilerParams(vmem_limit_bytes=40 * 2**20),
        cost_estimate=NO_COST,
        name="project_query",
    )(own, sib, hidden, vecs, cos, sin)


def out_kernel(own_ref, sib_ref, att_ref, x_ref, vec_ref, out_ref, resid_ref, hid_ref):
    part_rows = own_ref.shape[2] // 2
    join_weight(own_ref, sib_ref, part_rows, part_rows, out_ref)
    resid = x_ref[...].astype(F32) + matmul(att_ref[...], whole_weight(out_ref))
    resid_ref[...] = resid
    hid_ref[...] = normed_rows(resid, vec_ref[1:2, :])


def project_out(own, sib, attended, tokens, vecs, rows_here):
    n_z, cols = own.shape[1], own.shape[3]
    vmem = pl.BlockSpec(memory_space=pltpu.VMEM)
    return pl.pallas_call(
        out_kernel,
        in_specs=[vmem] * 5,
        out_specs=[vmem] * 3,
        out_shape=[
            jax.ShapeDtypeStruct((n_z, rows_here, cols), BF16),
            jax.ShapeDtypeStruct(tokens.shape, F32),
            jax.ShapeDtypeStruct(tokens.shape, BF16),
        ],
        compiler_params=pltpu.CompilerParams(vmem_limit_bytes=40 * 2**20),
        cost_estimate=NO_COST,
        name="project_out",
    )(own, sib, attended, tokens, vecs)


def kv_back_kernel(n_z, *refs):
    terms, rest = refs[:n_z], refs[n_z:]
    cos_ref, sin_ref, gq_ref, hid_ref, wq_ref, wkv_ref, x_ref, res_ref, vec_ref, two_ref = rest[:10]
    tokens_ref, part_ref = rest[10:]
    rows_here, width = x_ref.shape
    total = sum(t[...].astype(F32) for t in terms)
    half = total.shape[1] // 2
    keys = turn_tile(total[:, :half], cos_ref[...], -sin_ref[...]).astype(BF16)
    both = jnp.concatenate([keys, total[:, half:].astype(BF16)], 1)
    grad = times_transposed(gq_ref[...], wq_ref[...]) + times_transposed(both, wkv_ref[...])
    x = x_ref[...].astype(F32)
    inv = lax.rsqrt(jnp.mean(x * x, -1, keepdims=True) + NORM_EPS)
    normed = x * inv
    scaled = grad * vec_ref[0:1, :]
    tokens_ref[...] = res_ref[...] + inv * (
        scaled - normed * jnp.mean(scaled * normed, -1, keepdims=True)
    )
    sums = jnp.sum(both.astype(F32), 0, keepdims=True)
    share = half // n_z
    gap = jnp.zeros((1, width // n_z - share), F32)
    spread = []
    for i in range(2):
        cuts = []
        for z in range(n_z):
            at = i * half + z * share
            cuts += [sums[:, at : at + share], gap]
        spread.append(jnp.concatenate(cuts, 1))
    columns = [
        jnp.sum(grad * normed, 0, keepdims=True),
        two_ref[...],
        jnp.sum(gq_ref[...].astype(F32), 0, keepdims=True),
    ] + spread
    row = lax.broadcasted_iota(jnp.int32, (128, width), 0)
    table = jnp.zeros((128, width), F32)
    for i, v in enumerate(columns):
        table = jnp.where(row == i, v, table)
    part_ref[:, 2 * half :] = table.T.astype(BF16)
    pad = -rows_here % 128
    left = jnp.concatenate([hid_ref[...].astype(F32), jnp.zeros((pad, width), F32)], 0)
    right = jnp.concatenate([both, jnp.zeros((pad, 2 * half), BF16)], 0)
    part_ref[:, : 2 * half] = matmul(left.T.astype(BF16), right).astype(BF16)


def kv_back(terms, cos, sin, gq, hidden, wq, wkv, tokens, resid_grad, vecs, two_sum):
    vmem = pl.BlockSpec(memory_space=pltpu.VMEM)
    width = tokens.shape[1]
    return pl.pallas_call(
        functools.partial(kv_back_kernel, len(terms)),
        in_specs=[vmem] * (len(terms) + 10),
        out_specs=[vmem] * 2,
        out_shape=[
            jax.ShapeDtypeStruct(tokens.shape, F32),
            jax.ShapeDtypeStruct((width, wkv.shape[1] + 128), BF16),
        ],
        compiler_params=pltpu.CompilerParams(vmem_limit_bytes=40 * 2**20),
        cost_estimate=NO_COST,
        name="kv_back",
    )(*terms, cos, sin, gq, hidden, wq, wkv, tokens, resid_grad, vecs, two_sum)


def grad_weight_kernel(left_ref, right_ref, *refs):
    total = matmul(left_ref[...], right_ref[...])
    if len(refs) == 2:
        total = total + refs[0][...].astype(F32)
    refs[-1][...] = total.astype(BF16)


def grad_weight(left, right, other=None):
    rows, depth = left.shape
    cols = right.shape[1]
    tile = rows // 2 if rows % 32 == 0 else rows
    by_rows = lambda width: pl.BlockSpec((tile, width), lambda i: (i, 0))
    in_specs = [by_rows(depth), pl.BlockSpec((depth, cols), lambda i: (0, 0))]
    args = [left, right]
    if other is not None:
        in_specs.append(by_rows(cols))
        args.append(other)
    return pl.pallas_call(
        grad_weight_kernel,
        grid=(rows // tile,),
        in_specs=in_specs,
        out_specs=by_rows(cols),
        out_shape=jax.ShapeDtypeStruct((rows, cols), BF16),
        compiler_params=pltpu.CompilerParams(
            dimension_semantics=("arbitrary",), vmem_limit_bytes=40 * 2**20
        ),
        cost_estimate=NO_COST,
        name="grad_weight",
    )(*args)


def ff_kernel(tp, n_z, *refs):
    hidden, grads, weights = refs[:tp], refs[tp : 2 * tp], refs[2 * tp : 2 * tp + 4]
    rest = refs[2 * tp + 4 :]
    act_refs, back_refs, (hid_t, grad_all) = rest[:2], rest[2:4], rest[4:6]
    dh_outs, outs = rest[6 : 6 + tp], rest[6 + tp : 6 + 2 * tp]
    gu_buf, down_buf, acc, acc_out, sems = rest[6 + 2 * tp :]
    part_rows = weights[2].shape[1]
    gu_copies = [
        pltpu.make_async_copy(weights[i], gu_buf.at[i], sems.at[i]) for i in range(2)
    ]
    down_copies = []
    for i in range(2):
        for z in range(n_z):
            to = down_buf.at[i, pl.ds(z * part_rows, part_rows)]
            sem = sems.at[2 + i * n_z + z]
            down_copies.append(pltpu.make_async_copy(weights[2 + i].at[z], to, sem))
    gu_copies[0].start()
    for c in down_copies[:n_z]:
        c.start()
    gu_copies[1].start()
    for c in down_copies[n_z:]:
        c.start()
    tokens_here = hidden[0].shape[0]
    half = down_buf.shape[1]
    step = 2 if tp % 2 == 0 else 1
    for i in range(2):
        gu_copies[i].wait()
        for t in range(0, tp, step):
            rows = slice(t * tokens_here, (t + step) * tokens_here)
            here = jnp.concatenate([hidden[t + n][...] for n in range(step)], 0)
            grad = jnp.concatenate([grads[t + n][...] for n in range(step)], 0)
            if i == 0:
                hid_t[:, rows] = here.astype(F32).T.astype(BF16)
                grad_all[rows, :] = grad
            gate = matmul(here, gu_buf[i, :, :half])
            up = matmul(here, gu_buf[i, :, half:])
            if t == 0:
                for c in down_copies[i * n_z : (i + 1) * n_z]:
                    c.wait()
            grad_act = times_transposed(grad, down_buf[i])
            sig = 1.0 / (1.0 + jnp.exp(-gate))
            silu = gate * sig
            act = silu * up
            act_refs[i][:, rows] = act.T.astype(BF16)
            grad_gate = (grad_act * up * (sig + silu * (1.0 - sig))).astype(BF16)
            grad_up = (grad_act * silu).astype(BF16)
            back_refs[i][rows, :half] = grad_gate
            back_refs[i][rows, half:] = grad_up
            part = times_transposed(grad_gate, gu_buf[i, :, :half]) + times_transposed(
                grad_up, gu_buf[i, :, half:]
            )
            out = matmul(act.astype(BF16), down_buf[i])
            if i == 0:
                acc[rows, :] = part
                acc_out[rows, :] = out
            else:
                part = (part + acc[rows, :]).astype(BF16)
                out = (out + acc_out[rows, :]).astype(BF16)
                for n in range(step):
                    mine = slice(n * tokens_here, (n + 1) * tokens_here)
                    dh_outs[t + n][...] = part[mine]
                    outs[t + n][...] = out[mine]


def ff_pass(hidden, grads, gu, down):
    tp = len(hidden)
    n_z, part_rows = down[0].shape[:2]
    tokens_here, width = hidden[0].shape
    half = n_z * part_rows
    rows = tp * tokens_here
    vmem = pl.BlockSpec(memory_space=pltpu.VMEM)
    got = pl.pallas_call(
        functools.partial(ff_kernel, tp, n_z),
        in_specs=[vmem] * (2 * tp) + [pl.BlockSpec(memory_space=pl.ANY)] * 4,
        out_specs=[vmem] * (2 * tp + 6),
        out_shape=[jax.ShapeDtypeStruct((half, rows), BF16)] * 2
        + [jax.ShapeDtypeStruct((rows, 2 * half), BF16)] * 2
        + [jax.ShapeDtypeStruct((width, rows), BF16), jax.ShapeDtypeStruct((rows, width), BF16)]
        + [jax.ShapeDtypeStruct((tokens_here, width), BF16)] * (2 * tp),
        scratch_shapes=[
            pltpu.VMEM((2, width, 2 * half), BF16),
            pltpu.VMEM((2, half, width), BF16),
            pltpu.VMEM((rows, width), F32),
            pltpu.VMEM((rows, width), F32),
            pltpu.SemaphoreType.DMA((2 + 2 * n_z,)),
        ],
        compiler_params=pltpu.CompilerParams(vmem_limit_bytes=58 * 2**20),
        cost_estimate=NO_COST,
        name="ff_pass",
    )(*hidden, *grads, *gu, *down)
    return got[:2], got[2:4], got[4], got[5], got[6 : 6 + tp], got[6 + tp :]


def local(
    tokens,
    out_grad,
    block_order,
    norm1_gain,
    q_weight,
    q_bias,
    k_weight,
    k_bias,
    v_weight,
    v_bias,
    o_weight,
    norm2_gain,
    gate_weight,
    up_weight,
    down_weight,
):
    n_ctx = lax.axis_size("ctx")
    n_z = lax.axis_size("fsdp")
    tp = 4 if n_ctx % 4 == 0 else (2 if n_ctx % 2 == 0 else 1)
    here = lax.axis_index("ctx")
    zed = lax.axis_index("fsdp")
    core = lax.axis_index("seq")
    n_part = 2 * tp
    part = core * tp + lax.rem(here, tp)

    def swap(v):
        return lax.ppermute(v, "seq", [(0, 1), (1, 0)])

    def hop(v, k):
        if k == 0:
            return v
        return lax.ppermute(v, "ctx", [(i, i ^ k) for i in range(n_ctx)])

    def hop_z(v, k):
        if k == 0:
            return v
        return lax.ppermute(v, "fsdp", [(i, i ^ k) for i in range(n_z)])

    def gather_z(v):
        return lax.all_gather(v, "fsdp", axis=0, tiled=True)

    def scatter_z(v):
        return lax.psum_scatter(v, "fsdp", scatter_dimension=0, tiled=True)

    tokens_here, width = tokens.shape[1:]
    ff = gate_weight.shape[1]
    rows_here = q_weight.shape[0]
    key_width = KV_HEADS * HEAD
    block_len = tokens_here * n_z

    part_rows = -(-rows_here // (n_part * 32)) * 32

    kb = k_bias.shape[0]
    vectors = (norm1_gain, norm2_gain, q_bias, k_bias, v_bias)
    vec = sum(
        jnp.pad(v[None], ((i, 15 - i), (0, 2 * key_width - v.shape[0])))
        for i, v in enumerate(vectors)
    )
    kv_pack = jnp.concatenate([jnp.concatenate([k_weight, v_weight], 1), vec], 0)
    og_here = out_grad[0]

    def own_part(w):
        return lax.dynamic_slice_in_dim(w, part * part_rows, part_rows, 0)

    ff_z = ff // n_z
    piece = ff_z // n_part
    piece_pad = -(-piece // 32) * 32

    def ff_columns(w):
        cuts = []
        for j in range(n_z):
            cut = lax.dynamic_slice_in_dim(w, j * ff_z + part * piece, piece, 1)
            cuts.append(jnp.pad(cut, ((0, 0), (0, piece_pad - piece))))
        return jnp.concatenate(cuts, 1)

    order_row = block_order[0]
    x_here = tokens[0]
    kv_pack, q_part, o_part, gate_weight, up_weight, down_weight, query_at = (
        lax.optimization_barrier(
            (
                kv_pack,
                own_part(q_weight),
                own_part(o_weight),
                gate_weight,
                up_weight,
                down_weight,
                order_row[here] * block_len + zed * tokens_here,
            )
        )
    )
    pack_rows = kv_pack.shape[0]
    qo_part = jnp.concatenate([q_part, o_part], 0)
    pack = jnp.concatenate([kv_pack, qo_part.reshape(-1, 2 * key_width)], 0)
    got = [hop_z(pack, k) for k in range(n_z)]
    gu_cut = jnp.concatenate([ff_columns(gate_weight), ff_columns(up_weight)], 1)
    down_cut = lax.dynamic_slice_in_dim(down_weight, part * piece, piece, 0)
    down_cut = jnp.pad(down_cut, ((0, piece_pad - piece), (0, 0)))
    query_pos = query_at + jnp.arange(tokens_here, dtype=jnp.int32)
    cosine_table, sine_table = rope_tables(query_pos, HEAD)
    cos_wide = jnp.tile(cosine_table[:, 0], (1, 4))
    sin_wide = jnp.tile(jnp.concatenate([-sine_table[:, 0], sine_table[:, 0]], 1), (1, 2))
    got, cos_wide, sin_wide, gu_cut, down_cut, og_here = lax.optimization_barrier(
        (got, cos_wide, sin_wide, gu_cut, down_cut, og_here)
    )

    qo_got = jnp.stack([v[pack_rows:].reshape(2 * part_rows, width) for v in got])
    qo_own = [hop(qo_got, k) for k in range(tp)]
    widths = tuple(v.shape[0] for v in vectors)
    w_kv, vecs, kv_local, hidden_one = project_kv(
        got, x_here, cos_wide, sin_wide, rows_here, pack_rows - rows_here, widths
    )
    w_kv = w_kv.reshape(width, 2 * key_width)
    gain_one = vecs[0:1, :width]
    gain_two = vecs[1:2, :width]
    kv_z = [hop_z(kv_local, k) for k in range(n_z)]
    gu_own = gather_z(gu_cut)
    kv_z, qo_own = lax.optimization_barrier((kv_z, qo_own))

    kv_block = jnp.concatenate(kv_z, 0)
    if n_ctx == tp:
        kv_blocks = [hop(kv_block, k) for k in range(n_ctx)]
    else:
        kv_blocks = lax.all_gather(kv_block, "ctx", axis=0, tiled=False)
    qo_own = jnp.stack(qo_own)
    qo_sib = swap(qo_own)
    w_query, queries = project_query(
        qo_own, qo_sib, hidden_one, vecs, cos_wide, sin_wide, rows_here
    )
    w_query = w_query.reshape(width, width)
    kv_blocks, queries, og_here, down_cut, gu_own = lax.optimization_barrier(
        (kv_blocks, queries, og_here, down_cut, gu_own)
    )

    og_parts = [hop(og_here, k) for k in range(tp)]
    kv_whole = jnp.stack(kv_blocks) if n_ctx == tp else kv_blocks
    attended, queries_ext = attend_forward(order_row, n_ctx == tp, queries, kv_whole)
    down_own = gather_z(down_cut)
    attended, queries_ext, og_parts = lax.optimization_barrier((attended, queries_ext, og_parts))
    w_out, resid, hidden_two = project_out(
        qo_own, qo_sib, attended, x_here, vecs, rows_here
    )
    w_out = w_out.reshape(width, width)
    h2_parts = [hop(hidden_two, k) for k in range(tp)]
    gu_oth = swap(gu_own)
    h2_parts, down_own = lax.optimization_barrier((h2_parts, down_own))
    down_own = down_own.reshape(n_z, piece_pad, width)
    down_oth = swap(down_own)

    acts, ggus, h2_turned, og_all, dh2, ff_out = ff_pass(
        h2_parts, og_parts, (gu_own, gu_oth), (down_own, down_oth)
    )
    grad_h2_parts = [hop(dh2[k], k) for k in range(tp)]

    def share_pieces(mine):
        own = jnp.stack([hop(mine, k) for k in range(tp)])
        return own, swap(own)

    def core_halves(part_sum):
        cols = part_sum.shape[1]
        cut = part_sum.astype(BF16).reshape(n_z, rows_here, cols)
        cut = jnp.pad(cut, ((0, 0), (0, n_part * part_rows - rows_here), (0, 0)))
        own = lax.dynamic_slice_in_dim(cut, core * tp * part_rows, tp * part_rows, 1)
        oth = lax.dynamic_slice_in_dim(cut, (1 - core) * tp * part_rows, tp * part_rows, 1)
        return own, oth

    def core_total(own, sib):
        return (own.astype(F32) + sib.astype(F32)).astype(BF16)

    def scatter_parts(cut):
        cut = cut.reshape(n_z, tp, part_rows, -1)
        at = lax.rem(here, tp)
        return [
            hop(lax.dynamic_index_in_dim(cut, at ^ k, 1, keepdims=False), k) for k in range(tp)
        ]

    def ctx_groups_sum(v):
        if n_ctx == tp:
            return v
        groups = [[g * tp + c for g in range(n_ctx // tp)] for c in range(tp)]
        return lax.psum(v, "ctx", axis_index_groups=groups)

    d_gu = grad_weight(h2_turned, ggus[0], swap(grad_weight(h2_turned, ggus[1])))
    grad_h2_parts, d_gu = lax.optimization_barrier((grad_h2_parts, d_gu))
    grad_h2 = sum(v.astype(F32) for v in grad_h2_parts)
    scale_two = lax.rsqrt(jnp.mean(resid * resid, -1, keepdims=True) + NORM_EPS)
    normed_two = resid * scale_two

    grad_norm_two, gain_two_terms = rms_backward(grad_h2, normed_two, scale_two, gain_two)
    grad_resid = og_here.astype(F32) + grad_norm_two
    grad_proj = grad_resid.astype(BF16)
    grad_att = times_transposed(grad_proj, w_out).astype(BF16)
    grad_att, d_gu = lax.optimization_barrier((grad_att, d_gu))
    d_gu = scatter_z(d_gu)
    grad_q_pre, grad_terms = attend_backward(
        order_row, n_ctx == tp, queries_ext, grad_att, attended, cos_wide, sin_wide, kv_whole
    )
    grad_q_pre, grad_terms, ff_out, acts, grad_proj = lax.optimization_barrier(
        (grad_q_pre, grad_terms, ff_out, acts, grad_proj)
    )
    d_down = grad_weight(acts[0], og_all, swap(grad_weight(acts[1], og_all)))

    qo_own, qo_oth = core_halves(
        jnp.concatenate(
            [contract_rows(hidden_one, grad_q_pre), contract_rows(attended, grad_proj)], 1
        )
    )
    if n_ctx == tp:
        kv_terms = [hop(grad_terms[k], k) for k in range(n_ctx)]
    else:
        kv_terms = [lax.psum_scatter(grad_terms, "ctx", scatter_dimension=0, tiled=False)]
    kv_terms, d_gu, d_down, qo_own, qo_oth, ff_out = lax.optimization_barrier(
        (kv_terms, d_gu, d_down, qo_own, qo_oth, ff_out)
    )

    kv_sum = sum(v.astype(F32) for v in kv_terms).astype(BF16)
    kv_sum = kv_sum.reshape(n_z, tokens_here, 2 * key_width)
    kv_terms = [hop_z(kv_sum[k], k) for k in range(n_z)]
    d_gu = ctx_groups_sum(d_gu)
    gu_pieces = [hop(d_gu, k) for k in range(tp)]
    qo_sib = swap(qo_oth)
    d_down = scatter_z(d_down)
    kv_terms, qo_own, qo_sib = lax.optimization_barrier((kv_terms, qo_own, qo_sib))

    tokens_grad, kv_part = kv_back(
        kv_terms,
        cos_wide,
        sin_wide,
        grad_q_pre,
        hidden_one,
        w_query,
        w_kv,
        x_here,
        grad_resid,
        vecs,
        jnp.sum(gain_two_terms, 0, keepdims=True),
    )
    tokens_grad = tokens_grad[None]
    kv_own, kv_oth = core_halves(kv_part)
    last = core_total(qo_own, qo_sib)
    kv_own, kv_sib, last = lax.optimization_barrier((kv_own, swap(kv_oth), last))

    last = scatter_parts(jnp.concatenate([last, core_total(kv_own, kv_sib)], 2))
    last, d_down, gu_pieces, ff_out = lax.optimization_barrier((last, d_down, gu_pieces, ff_out))
    ff_out = [hop(ff_out[k], k) for k in range(tp)]

    last = sum(v.astype(F32) for v in last).astype(BF16)
    last = [
        hop_z(lax.dynamic_index_in_dim(last, zed ^ k, 0, keepdims=False), k) for k in range(n_z)
    ]
    d_down = ctx_groups_sum(d_down)
    gu_pieces = jnp.stack(gu_pieces)
    gu_sib = swap(gu_pieces)
    last, d_down, gu_pieces, gu_sib = lax.optimization_barrier(
        (last, d_down, gu_pieces, gu_sib)
    )

    result = resid + sum(v.astype(F32) for v in ff_out)
    layer_out = result.astype(BF16)[None]

    last = ctx_groups_sum(sum(v.astype(F32) for v in last).astype(BF16))
    last = lax.optimization_barrier(last)
    down_pieces = [hop(d_down, k) for k in range(tp)]
    grad_w_gate, grad_w_up = spread_columns((gu_pieces, gu_sib), n_z, ff, 2)
    last, down_pieces, grad_w_gate, grad_w_up = lax.optimization_barrier(
        (last, down_pieces, grad_w_gate, grad_w_up)
    )
    last = [hop(last, k) for k in range(tp)]
    down_pieces = jnp.stack(down_pieces)
    down_sib = swap(down_pieces)
    last, down_pieces, down_sib = lax.optimization_barrier((last, down_pieces, down_sib))
    last = jnp.stack(last)
    grad_w_down = spread_rows((down_pieces, down_sib), piece, ff_z)
    last = spread_rows((last, swap(last)), part_rows, rows_here)
    grad_w_query = last[:, :width]
    grad_w_out = last[:, width : 2 * width]
    grad_w_kv = last[:, 2 * width :]
    sums = grad_w_kv[:, 2 * key_width :]

    return (
        layer_out,
        tokens_grad,
        sums[:, 0],
        grad_w_query,
        sums[:, 2],
        grad_w_kv[:, :key_width],
        sums[:kb, 3],
        grad_w_kv[:, key_width : 2 * key_width],
        sums[:kb, 4],
        grad_w_out,
        sums[:, 1],
        grad_w_gate,
        grad_w_up,
        grad_w_down,
    )


def solution(mesh):
    in_specs = (
        P("seq", ("ctx", "fsdp"), None),
        P("seq", ("ctx", "fsdp"), None),
        P("seq", None),
        P("fsdp"),
        P("fsdp", None),
        P("fsdp"),
        P("fsdp", None),
        P("fsdp"),
        P("fsdp", None),
        P("fsdp"),
        P("fsdp", None),
        P("fsdp"),
        P("fsdp", None),
        P("fsdp", None),
        P("fsdp", None),
    )
    out_specs = (
        P("seq", ("ctx", "fsdp"), None),
        P("seq", ("ctx", "fsdp"), None),
        P("fsdp"),
        P("fsdp", None),
        P("fsdp"),
        P("fsdp", None),
        P("fsdp"),
        P("fsdp", None),
        P("fsdp"),
        P("fsdp", None),
        P("fsdp"),
        P("fsdp", None),
        P("fsdp", None),
        P("fsdp", None),
    )
    return jax.shard_map(local, mesh=mesh, in_specs=in_specs, out_specs=out_specs, check_vma=False)
```
